32 devices in a mesh: piece: 8 (over y, x, core), col: 4 (over z).
Axes of the slice: x: 2, y: 2, z: 4, core: 2. Of those that a mesh axis runs over, the one named last changes fastest.
Arguments:
- positions: float32 [3, 1024, 128], P(None, 'piece'), as said below
- phase: int32 [1024, 128], P('piece'), may hold values from 0 to 2
- neighbours: int32 [1024, 28], P('piece', 'col'), may hold values from -1 to 1023, as said below
- counts: int32 [8], replicated, may hold values from 64 to 128, as said below
- phase_density: float32 [3], replicated, may hold values from 0.1 to 1
- right_side: float32 [1024, 128], P(('piece', 'col')), may hold values from -6 to 6
Outputs:
- solution_field: float32 [1024, 128], P(('piece', 'col'))
- residual: float32 [1024, 128], P(('piece', 'col'))
The draws below stay inside these ranges and needn't reach their ends.
Inputs may be any that keep to these rules, and one draw needn't show every extreme that they name: `neighbours`: the slots of each piece at or past its count hold no block. Live blocks, taken in slot order piece after piece, form layers of 16 blocks in Morton order of a 4 x 4 grid. Block q lists n exactly when n lists q; every listed block lies on q's own piece or the piece just before or after it, and its place in that order of live blocks differs from q's by less than 32; empty slots and the last column list only -1. `counts`: some piece holds exactly 128 live blocks. `positions`: the particles of one live block lie in one unit cell; particles of two live blocks that do not list each other are 1 or more apart.
All inputs are finite; a program needn't handle non-finite values.
Results may differ from the reference program's by a relative error of at most 0.0003.
Values sent between devices are 32-bit elements; how exact they have to be, the bound alone decides.
No kernel may reach another device: no remote copies, remote signals or barrier semaphores. Data moves between devices by JAX's collectives and lax.ppermute only.
A program may use at most 64 MiB of HBM per device.

```python
import math
import jax
import jax.numpy as jnp
from jax import lax

BLK = 128
SIDE = 4
LAYER = 16
CAP = 128
NEIGHBOUR_SLOTS = 28
ITERS = 2
NBLK = 1024
N_PIECE = 8


def layout_counts(key):
    first_key = jax.random.fold_in(key, 101)
    second_key = jax.random.fold_in(key, 102)
    extra = jax.random.randint(first_key, (N_PIECE,), 0, CAP // 2 + 1)
    filled = CAP // 2 + extra
    chosen = jax.random.randint(second_key, (), 0, N_PIECE)
    filled = jnp.where(jnp.arange(N_PIECE, dtype=jnp.int32) == chosen, CAP, filled).astype(jnp.int32)
    starts = (jnp.cumsum(filled) - filled).astype(jnp.int32)
    return (filled, starts)


def morton_cell(code):
    levels = SIDE.bit_length() - 1
    across = jnp.zeros_like(code)
    along = jnp.zeros_like(code)
    for level in range(levels):
        across = across + code // 4 ** level % 2 * 2 ** level
        along = along + code // (2 * 4 ** level) % 2 * 2 ** level
    return (across, along)


def morton_code(across, along):
    levels = SIDE.bit_length() - 1
    code = jnp.zeros_like(across)
    for level in range(levels):
        code = code + across // 2 ** level % 2 * 4 ** level
        code = code + along // 2 ** level % 2 * (2 * 4 ** level)
    return code


def slot_cells(key):
    filled, starts = layout_counts(key)
    slots = jnp.arange(NBLK, dtype=jnp.int32)
    owner = slots // CAP
    within = slots % CAP
    live = within < filled[owner]
    dense = starts[owner] + within
    height = dense // LAYER
    across, along = morton_cell(dense % LAYER)
    return (filled, starts, live, height, across, along)


def draw_counts(key, part):
    return layout_counts(key)[0]


def draw_neighbours(key, part):
    filled, starts, live, height, across, along = slot_cells(key)
    total = jnp.sum(filled)
    columns = []
    for step_z in (-1, 0, 1):
        for step_y in (-1, 0, 1):
            for step_x in (-1, 0, 1):
                next_x = across + step_x
                next_y = along + step_y
                next_z = height + step_z
                inside = (next_x >= 0) & (next_x < SIDE) & (next_y >= 0) & (next_y < SIDE) & (next_z >= 0)
                target = next_z * LAYER + morton_code(jnp.clip(next_x, 0, SIDE - 1), jnp.clip(next_y, 0, SIDE - 1))
                inside = inside & (target < total) & live
                holder = jnp.sum((starts[None, :] <= target[:, None]).astype(jnp.int32), axis=1) - 1
                holder = jnp.clip(holder, 0, N_PIECE - 1)
                worldwide_slot = holder * CAP + target - starts[holder]
                columns.append(jnp.where(inside, worldwide_slot, -1))
    columns.append(jnp.full((NBLK,), -1, jnp.int32))
    return jnp.stack(columns, axis=1).astype(jnp.int32)


def draw_positions(key, part):
    filled, starts, live, height, across, along = slot_cells(key)
    offsets = jax.random.uniform(jax.random.fold_in(key, 103), (3, NBLK, BLK), jnp.float32)
    corner = jnp.stack([across, along, height], 0).astype(jnp.float32)
    return (corner[:, :, None] + offsets).astype(jnp.float32)


def touch_ends(array, own_key, least, top_value):
    shape = array.shape
    index_at = [jax.random.randint(jax.random.fold_in(own_key, axis), (), 0, shape[axis]) for axis in range(len(shape))]
    array = array.at[tuple(index_at)].set(least)
    longest = shape.index(max(shape))
    index_at[longest] = (index_at[longest] + 1) % shape[longest]
    return array.at[tuple(index_at)].set(top_value)


def block_scale(stream_key, shape, shards, least, largest):
    def one(position, blocks):
        draws = jax.random.uniform(jax.random.fold_in(jax.random.fold_in(stream_key, 6), position), (blocks,), jnp.float32, least / len(shards), largest / len(shards))
        return jnp.repeat(jnp.exp(draws), shape[position] // blocks).reshape((-1,) + (1,) * (len(shape) - position - 1))

    factor_of = one(*shards[0])
    for cut in shards[1:]:
        factor_of = factor_of * one(*cut)
    return factor_of


def scatter_about(stream_key, extent, spread, most, pieces=(), kind=jnp.bfloat16):
    gain = block_scale(stream_key, extent, pieces, -0.22, 0.18) if pieces else 1.0
    entries = jax.random.normal(stream_key, extent, jnp.float32) * spread * gain
    return jnp.minimum(jnp.maximum(entries, -most), most).astype(kind)


def setup_inputs(seed: int = 0) -> dict:
    key_list = jax.random.split(jax.random.key(seed), 7)
    positions = draw_positions(jax.random.fold_in(key_list[6], 71), 0)
    phase = touch_ends(jax.random.randint(key_list[1], (NBLK, BLK), 0, 3), jax.random.fold_in(key_list[1], 1), 0, 2).astype(jnp.int32)
    neighbours = draw_neighbours(jax.random.fold_in(key_list[6], 71), 0)
    counts = draw_counts(jax.random.fold_in(key_list[6], 71), 0)
    phase_density = jnp.clip(jnp.exp(jax.random.uniform(key_list[4], (3,), jnp.float32, math.log(0.1), math.log(1.0))), 0.1, 1.0)
    right_side = scatter_about(key_list[5], (NBLK, BLK), 1.0, 6.0, ((0, 32),), jnp.float32)
    return dict(positions=positions, phase=phase, neighbours=neighbours, counts=counts, phase_density=phase_density, right_side=right_side)


def fetch_phase_density(phase, phase_density):
    labels = jnp.arange(3, dtype=jnp.int32)
    return jnp.sum(jnp.where(phase[..., None] == labels, phase_density, 0.0), axis=-1).astype(jnp.float32)


def pair_term(own_pos, own_rho, own_ids, slot_ids, hood_state, hood_field, base):
    valid = slot_ids >= 0
    where_at = jnp.clip(slot_ids - base, 0, hood_field.shape[0] - 1).astype(jnp.int32)
    other = hood_state[:, where_at]
    remote = hood_field[where_at]
    squared = jnp.zeros((own_rho.shape[0], own_rho.shape[1], own_rho.shape[1]), jnp.float32)
    for component in range(3):
        slot_displacement = own_pos[component][:, :, None] - other[component][:, None, :]
        squared = squared + slot_displacement * slot_displacement
    kernel = jnp.square(jnp.maximum(1.0 - squared, 0.0)) / (squared + 0.01)
    weight = 2.0 / (own_rho[:, :, None] + other[3][:, None, :])
    particles = jnp.arange(own_rho.shape[1], dtype=jnp.int32)
    same = (slot_ids == own_ids)[:, None, None] & (particles[:, None] == particles[None, :])[None]
    keep = valid[:, None, None] & jnp.logical_not(same)
    tile = jnp.where(keep, kernel * weight / own_rho.shape[1], 0.0)
    return jnp.einsum("gij,gj->gi", tile, remote, precision=lax.Precision.HIGHEST)


def reference(positions, phase, neighbours, counts, phase_density, right_side):
    density = fetch_phase_density(phase, phase_density)
    state = jnp.concatenate([positions, density[None]], 0)
    slots = jnp.arange(NBLK, dtype=jnp.int32)
    live = (slots % CAP) < counts[slots // CAP]
    source = jnp.where(live[:, None], right_side, 0.0)
    group = 16

    def apply_pairs(field):
        def group_sum(start):
            own_pos = lax.dynamic_slice_in_dim(positions, start, group, 1)
            own_rho = lax.dynamic_slice_in_dim(density, start, group, 0)
            own_ids = start + jnp.arange(group, dtype=jnp.int32)
            lists = lax.dynamic_slice_in_dim(neighbours, start, group, 0)
            running = jnp.zeros((group, BLK), jnp.float32)
            for neighbour_slot in range(NEIGHBOUR_SLOTS):
                running = running + pair_term(own_pos, own_rho, own_ids, lists[:, neighbour_slot], state, field, 0)
            return running
        starts = jnp.arange(NBLK // group, dtype=jnp.int32) * group
        return lax.map(group_sum, starts).reshape(NBLK, BLK)

    diagonal = 1.0 / density + apply_pairs(jnp.ones((NBLK, BLK), jnp.float32))
    solution_field = jnp.zeros((NBLK, BLK), jnp.float32)
    residual = source
    precond = residual / diagonal
    direction = precond
    weighted = jnp.sum(residual * precond)
    for step in range(ITERS):
        image = diagonal * direction - apply_pairs(direction)
        advance = weighted / jnp.sum(direction * image)
        solution_field = solution_field + advance * direction
        residual = residual - advance * image
        precond = residual / diagonal
        weighted_next = jnp.sum(residual * precond)
        direction = precond + (weighted_next / weighted) * direction
        weighted = weighted_next
    return solution_field, residual
```

```python
import functools
import math

import jax
import jax.numpy as jnp
import numpy as np
from jax import lax
from jax.experimental import pallas as pl
from jax.experimental.pallas import tpu as pltpu
from jax.sharding import PartitionSpec as P

ITERS = 2
SIDE = 4
LAYER = SIDE * SIDE
REACH = 2 * LAYER
SUB = 8
VMEM = pl.BlockSpec(memory_space=pltpu.VMEM)
SMEM = pl.BlockSpec(memory_space=pltpu.SMEM)


def stencil_tables():
    levels = SIDE.bit_length() - 1

    def cell(code):
        across = sum((code >> (2 * level) & 1) << level for level in range(levels))
        along = sum((code >> (2 * level + 1) & 1) << level for level in range(levels))
        return across, along

    place = {cell(code): code for code in range(LAYER)}
    rows = []
    for code in range(LAYER):
        across, along = cell(code)
        rows.append(
            sorted(
                step_z * LAYER + place[across + step_x, along + step_y] - code
                for step_z in (-1, 0, 1)
                for step_y in (-1, 0, 1)
                for step_x in (-1, 0, 1)
                if (across + step_x, along + step_y) in place
            )
        )
    longest = max(len(row) for row in rows)
    offsets = np.zeros((LAYER, longest), np.int32)
    below = np.zeros((LAYER, 2 * REACH + 1), np.int32)
    for code, row in enumerate(rows):
        offsets[code, : len(row)] = row
        for t in range(-REACH, REACH + 1):
            below[code, t + REACH] = sum(offset < t for offset in row)
    return offsets, below


OFFSETS, BELOW = stencil_tables()


def tile_bounds(share):
    inner = outer = 0
    for first in range(LAYER):
        for live in range(1, share + 1):
            near = far = 0
            for a in range(live):
                code = (first + a) % LAYER
                row = [int(o) for o in OFFSETS[code][: BELOW[code, -1]]]
                near += sum(0 <= a + o and o <= 0 for o in row)
                far += sum(a + o < 0 or a + o >= live for o in row)
            inner, outer = max(inner, near), max(outer, far)
    return inner, outer


def padded(cells, sides, width):
    for axis, dim in sides:
        count = lax.axis_size(axis)
        ends = count - 1
        head = lax.slice_in_dim(cells, 0, width, axis=dim)
        tail = lax.slice_in_dim(cells, cells.shape[dim] - width, cells.shape[dim], axis=dim)
        cells = jnp.concatenate(
            [
                lax.ppermute(tail, axis, [(i, (i + 1) % count) for i in range(ends)]),
                cells,
                lax.ppermute(head, axis, [((i + 1) % count, i) for i in range(ends)]),
            ],
            axis=dim,
        )
    return cells


def fetch_phase_density(phase, phase_density):
    labels = jnp.arange(3, dtype=jnp.int32)
    return jnp.sum(jnp.where(phase[..., None] == labels, phase_density, 0.0), axis=-1)


def literal_pair_term(own_pos, own_rho, own_ids, slot_ids, hood_state, hood_field, base):
    valid = slot_ids >= 0
    where_at = jnp.clip(slot_ids - base, 0, hood_field.shape[0] - 1)
    other = hood_state[:, where_at]
    remote = hood_field[where_at]
    squared = jnp.zeros((own_rho.shape[0], own_rho.shape[1], own_rho.shape[1]), jnp.float32)
    for component in range(3):
        slot_displacement = own_pos[component][:, :, None] - other[component][:, None, :]
        squared = squared + slot_displacement * slot_displacement
    kernel = jnp.square(jnp.maximum(1.0 - squared, 0.0)) / (squared + 0.01)
    weight = 2.0 / (own_rho[:, :, None] + other[3][:, None, :])
    particles = jnp.arange(own_rho.shape[1], dtype=jnp.int32)
    same = (slot_ids == own_ids)[:, None, None] & (particles[:, None] == particles[None, :])[None]
    keep = valid[:, None, None] & jnp.logical_not(same)
    tile = jnp.where(keep, kernel * weight / own_rho.shape[1], 0.0)
    return jnp.einsum("gij,gj->gi", tile, remote, precision=lax.Precision.HIGHEST)


def literal(positions, phase, neighbours, counts, phase_density, right_side):
    capacity = positions.shape[1]
    per_block = positions.shape[2]
    columns = lax.axis_size("col")
    share = capacity // columns
    piece = lax.axis_index("piece")
    column = lax.axis_index("col")
    density = fetch_phase_density(phase, phase_density)
    state = jnp.concatenate([positions, density[None]], 0)
    filled = counts[piece]
    hood_state = padded(state, (("piece", 1),), capacity)

    def remap(ids):
        return jnp.where(ids >= 0, ids - (piece - 1) * capacity, -1)

    def surround(whole):
        return padded(whole, (("piece", 0),), capacity)

    hood_size = hood_state.shape[1]
    live = jnp.arange(capacity, dtype=jnp.int32) < filled
    group = math.gcd(16, capacity)
    ngroup = capacity // group

    def group_sum(field_hood, start):
        own_pos = lax.dynamic_slice_in_dim(positions, start, group, 1)
        own_rho = lax.dynamic_slice_in_dim(density, start, group, 0)
        own_ids = capacity + start + jnp.arange(group, dtype=jnp.int32)
        lists = remap(lax.dynamic_slice_in_dim(neighbours, start, group, 0))
        running = jnp.zeros((group, per_block), jnp.float32)
        for neighbour_slot in range(lists.shape[1]):
            running = running + literal_pair_term(
                own_pos, own_rho, own_ids, lists[:, neighbour_slot], hood_state, field_hood, 0
            )
        return running

    def own_terms(field_hood):
        starts = jnp.arange(ngroup, dtype=jnp.int32) * group
        output_blocks = lax.map(lambda start: group_sum(field_hood, start), starts)
        return output_blocks.reshape(capacity, per_block)

    def mine(values):
        return lax.dynamic_slice_in_dim(values, column * share, share, 0)

    def totals(part_sum):
        return lax.psum_scatter(part_sum, "col", scatter_dimension=0, tiled=True)

    def hood_of(column_vector):
        return surround(lax.all_gather(column_vector, "col", axis=0, tiled=True))

    source = jnp.where(mine(live)[:, None], right_side, 0.0)
    rho_vector = mine(density)

    def inner(first, second):
        return jnp.sum(first * second)

    diagonal = 1.0 / rho_vector + totals(own_terms(jnp.ones((hood_size, per_block), jnp.float32)))

    def operate(column_vector):
        return diagonal * column_vector - totals(own_terms(hood_of(column_vector)))

    solution_field = jnp.zeros_like(source)
    residual = source

    def paired_sums(first, second, third):
        return lax.psum((inner(first, second), inner(second, third)), ("piece", "col"))

    precond = residual / diagonal
    image = operate(precond)
    weighted, curved = paired_sums(residual, precond, image)
    advance = weighted / curved
    direction = precond
    along = image
    for step in range(ITERS):
        solution_field = solution_field + advance * direction
        residual = residual - advance * along
        if step + 1 < ITERS:
            precond = residual / diagonal
            image = operate(precond)
            weighted_next, curved = paired_sums(residual, precond, image)
            blend = weighted_next / weighted
            advance = weighted_next / (curved - blend * weighted_next / advance)
            direction = precond + blend * direction
            along = image + blend * along
            weighted = weighted_next
    return (solution_field, residual)


def rank(table, code, t):
    return table[code, jnp.clip(t, -REACH, REACH) + REACH]


def inner_range(meta, below, a):
    code = lax.rem(meta[1] + a, LAYER)
    return code, rank(below, code, -a), rank(below, code, 0)


def outer_ranges(meta, below, a):
    code = lax.rem(meta[1] + a, LAYER)
    place = meta[1] + a
    before = (rank(below, code, -place), rank(below, code, -a))
    after = (rank(below, code, meta[0] - a), rank(below, code, meta[2] - place))
    return code, before, after


def pair_chunk(own, other):
    dx = own[0] - other[0]
    dy = own[1] - other[1]
    dz = own[2] - other[2]
    squared = dx * dx + dy * dy + dz * dz
    rest = jnp.maximum(1.0 - squared, 0.0)
    return rest * rest * pltpu.reciprocal((squared + 0.01) * (own[3] + other[3]), approx=True)


def spread_columns(out, index, rows):
    count, width = rows.shape
    turned = rows.T
    for a in range(count):
        out[index(a)] = jnp.broadcast_to(turned[:, a : a + 1], (width, width))


def lane_sums(parts, count, width):
    lanes = lax.broadcasted_iota(jnp.int32, (width, width), 1)
    turned = jnp.zeros((width, width), jnp.float32)
    for a in range(count):
        turned = jnp.where(lanes == a, jnp.sum(parts[a], axis=1, keepdims=True), turned)
    return turned.T[:count]


def totals(live, rows_ref, cols_ref, count, width):
    rows = lane_sums(rows_ref, count, width)
    cols = jnp.sum(cols_ref[...].reshape(count, SUB, width), axis=1)
    alive = lax.broadcasted_iota(jnp.int32, (count, width), 0) < live
    return jnp.where(alive, rows + cols, 0.0)


def build_inner(meta, offsets, below, position, density, tiles, spread, rows_ref, cols_ref, weight):
    share, width = rows_ref.shape[0], rows_ref.shape[2]
    chunks = width // SUB
    base = meta[3]
    weight[...] = density[...] * (width / 2.0)
    own_rows = pl.ds(pl.multiple_of(base, SUB), share)
    for k in range(4):
        values = position[k, own_rows, :] if k < 3 else weight[own_rows, :]
        spread_columns(spread, lambda a: (a, k), values)
    cols_ref[...] = jnp.zeros_like(cols_ref)

    def other_rows(row):
        here = pl.ds(row, 1)
        return [position[k, here, :] for k in range(3)] + [weight[here, :]]

    def block(a, at):
        code, low, high = inner_range(meta, below, a)

        def pair(j, carry):
            at, sums = carry
            n = a + offsets[code, j]
            other = other_rows(base + n)
            down = jnp.zeros((SUB, width), jnp.float32)
            after = []
            for c in range(chunks):
                here = slice(c * SUB, (c + 1) * SUB)
                tile = pair_chunk([spread[a, k, here, :] for k in range(4)], other)
                tiles[at, here, :] = tile
                down = down + tile
                after.append(sums[c] + tile)
            there = pl.ds(pl.multiple_of(n * SUB, SUB), SUB)
            cols_ref[there, :] = cols_ref[there, :] + down
            return at + 1, tuple(after)

        zero = jnp.zeros((SUB, width), jnp.float32)
        at, sums = lax.fori_loop(low, high, pair, (at, (zero,) * chunks))
        other = other_rows(base + a)
        lane = lax.broadcasted_iota(jnp.int32, (SUB, width), 1)
        sublane = lax.broadcasted_iota(jnp.int32, (SUB, width), 0)
        for c in range(chunks):
            here = slice(c * SUB, (c + 1) * SUB)
            tile = pair_chunk([spread[a, k, here, :] for k in range(4)], other)
            tile = jnp.where(lane == sublane + c * SUB, 0.0, tile)
            tiles[at, here, :] = tile
            rows_ref[a, here, :] = sums[c] + tile
        return at + 1

    lax.fori_loop(0, meta[0], block, 0)


def build_outer(
    meta, offsets, below, position, density, before, after, right_side, spread, rows_ref, cols_ref,
    tiles, diagonal_ref, precond_ref, hood,
):
    share, width = right_side.shape
    chunks = width // SUB
    capacity = density.shape[0]
    base, filled = meta[3], meta[4]
    scale = width / 2.0
    for k in range(4):
        gain = 1.0 if k < 3 else scale
        hood[k, 0:share, :] = before[k] * gain
        hood[k, share : share + capacity, :] = position[k] if k < 3 else density[...] * gain
        hood[k, share + capacity :, :] = after[k] * gain
    edge = share + filled - base

    def block(a, at):
        code, (low, high), (low_next, high_next) = outer_ranges(meta, below, a)

        def pair(j, carry):
            at, sums = carry
            w = share + a + offsets[code, j]
            row = jnp.where(w < edge, base + w, share + capacity + w - edge)
            here = pl.ds(row, 1)
            other = [hood[k, here, :] for k in range(4)]
            result = []
            for c in range(chunks):
                here = slice(c * SUB, (c + 1) * SUB)
                tile = pair_chunk([spread[a, k, here, :] for k in range(4)], other)
                tiles[at, here, :] = tile
                result.append(sums[c] + tile)
            return at + 1, tuple(result)

        start = tuple(rows_ref[a, c * SUB : (c + 1) * SUB, :] for c in range(chunks))
        carry = lax.fori_loop(low, high, pair, (at, start))
        at, sums = lax.fori_loop(low_next, high_next, pair, carry)
        for c in range(chunks):
            rows_ref[a, c * SUB : (c + 1) * SUB, :] = sums[c]
        return at

    lax.fori_loop(0, meta[0], block, 0)
    own_rows = pl.ds(pl.multiple_of(base, SUB), share)
    alive = lax.broadcasted_iota(jnp.int32, (share, width), 0) < meta[0]
    diagonal = 1.0 / density[own_rows, :] + totals(meta[0], rows_ref, cols_ref, share, width)
    diagonal_ref[...] = diagonal
    precond_ref[...] = jnp.where(alive, right_side[...], 0.0) / diagonal


def apply_inner(meta, offsets, below, field, tiles, rows_ref, cols_ref, spread):
    share, width = field.shape
    chunks = width // SUB
    spread_columns(spread, lambda a: a, field[...])
    cols_ref[...] = jnp.zeros_like(cols_ref)

    def block(a, at):
        code, low, high = inner_range(meta, below, a)

        def pair(j, carry):
            at, sums = carry
            n = a + offsets[code, j]
            value = field[pl.ds(n, 1), :]
            down = jnp.zeros((SUB, width), jnp.float32)
            after = []
            for c in range(chunks):
                here = slice(c * SUB, (c + 1) * SUB)
                tile = tiles[at, here, :]
                down = down + tile * spread[a, here, :]
                after.append(sums[c] + tile * value)
            there = pl.ds(pl.multiple_of(n * SUB, SUB), SUB)
            cols_ref[there, :] = cols_ref[there, :] + down
            return at + 1, tuple(after)

        zero = jnp.zeros((SUB, width), jnp.float32)
        at, sums = lax.fori_loop(low, high, pair, (at, (zero,) * chunks))
        value = field[pl.ds(a, 1), :]
        for c in range(chunks):
            here = slice(c * SUB, (c + 1) * SUB)
            rows_ref[a, here, :] = sums[c] + tiles[at, here, :] * value
        return at + 1

    lax.fori_loop(0, meta[0], block, 0)


def apply_outer(meta, offsets, below, received, tiles, rows_ref, cols_ref, hood):
    heres = received
    columns = len(heres)
    share, width = heres[0].shape
    chunks = width // SUB
    base, filled = meta[3], meta[4]
    for k, ref in enumerate(heres):
        hood[k * share : (k + 1) * share, :] = ref[...]
    column = lax.div(base, share)
    last = columns - 2
    edge = share + filled - base
    before_at = jnp.where(column == 0, meta[5] - 2 * share, last * share)
    after_at = (last + 1) * share - 2 * share
    head_at = jnp.where(column == last + 1, (last + 1) * share, (column - 1) * share) - edge

    def block(a, at):
        code, (low, high), (low_next, high_next) = outer_ranges(meta, below, a)

        def pair(j, carry):
            at, sums = carry
            w = share + a + offsets[code, j]
            row = w + jnp.where(w < share, before_at, jnp.where(w < edge, after_at, head_at))
            value = hood[pl.ds(row, 1), :]
            result = []
            for c in range(chunks):
                here = slice(c * SUB, (c + 1) * SUB)
                result.append(sums[c] + tiles[at, here, :] * value)
            return at + 1, tuple(result)

        start = tuple(rows_ref[a, c * SUB : (c + 1) * SUB, :] for c in range(chunks))
        carry = lax.fori_loop(low, high, pair, (at, start))
        at, sums = lax.fori_loop(low_next, high_next, pair, carry)
        for c in range(chunks):
            rows_ref[a, c * SUB : (c + 1) * SUB, :] = sums[c]
        return at

    lax.fori_loop(0, meta[0], block, 0)
    return totals(meta[0], rows_ref, cols_ref, share, width)


def build_inner_kernel(meta, offsets, below, position, density, tiles, spread, rows_ref, cols_ref, weight):
    build_inner(meta, offsets, below, position, density, tiles, spread, rows_ref, cols_ref, weight)


def apply_first_kernel(
    meta, offsets, below, right_side, precond, diagonal, *rest
):
    *received, tiles, rows_ref, cols_ref, spill_ref, scaled_ref, work, hood = rest
    work[...] = rows_ref[...]
    spill = apply_outer(meta, offsets, below, received, tiles, work, cols_ref, hood)
    spill_ref[...] = spill
    scaled_ref[...] = spill / diagonal[...]


def apply_second_kernel(
    meta, offsets, below, listed, right_side, precond, spill, scaled, *rest
):
    *received, tiles, rows_ref, cols_ref, twice_ref, sums_ref, work, hood = rest
    work[...] = rows_ref[...]
    twice = apply_outer(meta, offsets, below, received, tiles, work, cols_ref, hood)
    twice_ref[...] = twice
    share, width = twice.shape
    alive = lax.broadcasted_iota(jnp.int32, (share, width), 0) < meta[0]
    source = jnp.where(alive, right_side[...], 0.0)
    lane = lax.broadcasted_iota(jnp.int32, (1, width), 1)
    sums = jnp.where(lane == 4, listed[0], 0.0)
    pairs = ((source, precond[...]), (spill[...], precond[...]), (spill[...], scaled[...]), (scaled[...], twice))
    for k, (first, second) in enumerate(pairs):
        along = jnp.sum(first * second, axis=0, keepdims=True)
        sums = jnp.where(lane == k, jnp.sum(along, axis=1, keepdims=True), sums)
    sums_ref[...] = jnp.broadcast_to(sums, (SUB, width))


def finish_kernel(meta, right_side, precond, diagonal, spill, scaled, twice, mine, other, solution_ref, residual_ref, count_ref):
    share, width = precond.shape
    sums = mine[...] + other[...]
    count_ref[...] = sums

    def pick(k):
        return sums[0:1, k : k + 1]

    weighted, cross, square, last = pick(0), pick(1), pick(2), pick(3)
    part = cross / weighted
    advance = 1.0 / (1.0 - part)
    keep = -part * advance
    weighted_next = advance * advance * (square - cross * part)
    bent = keep * keep * cross + 2.0 * keep * advance * square + advance * advance * last
    blend = weighted_next / weighted
    advance_next = weighted_next / (weighted_next - bent - blend * weighted_next / advance)
    alive = lax.broadcasted_iota(jnp.int32, (share, width), 0) < meta[0]
    source = jnp.where(alive, right_side[...], 0.0)
    residual = keep * source + advance * spill[...]
    next_precond = keep * precond[...] + advance * scaled[...]
    direction = next_precond + blend * precond[...]
    image = residual - keep * spill[...] - advance * twice[...] + blend * (source - spill[...])
    solution_ref[...] = advance * precond[...] + advance_next * direction
    residual_ref[...] = residual - advance_next * image


def cost(pairs, each):
    return pl.CostEstimate(flops=pairs * each, bytes_accessed=pairs * 4, transcendentals=0)


def held(array):
    return pltpu.with_memory_space_constraint(array, pltpu.VMEM)


def body(positions, phase, neighbours, counts, phase_density, right_side):
    capacity, width = phase.shape
    columns = lax.axis_size("col")
    pieces = lax.axis_size("piece")
    share = capacity // columns
    piece = lax.axis_index("piece")
    column = lax.axis_index("col")
    density = fetch_phase_density(phase, phase_density)
    state = jnp.concatenate([positions, density[None]], 0)
    filled = counts[piece]
    onward = [(i, i + 1) for i in range(pieces - 1)]
    back = [(i + 1, i) for i in range(pieces - 1)]
    tail = lax.dynamic_slice_in_dim(state, filled - share, share, 1)
    before = lax.ppermute(tail, "piece", onward)
    after = lax.ppermute(state[:, :share], "piece", back)

    ranks = jnp.arange(pieces, dtype=jnp.int32)
    live = jnp.clip(filled - column * share, 0, share)
    first = jnp.sum(jnp.where(ranks < piece, counts, 0)) + column * share
    total = jnp.sum(counts)
    ahead = counts[jnp.maximum(piece - 1, 0)]
    meta = jnp.stack([live, first, total, column * share, filled, ahead]).astype(jnp.int32)
    slots = piece * capacity + jnp.arange(capacity, dtype=jnp.int32)
    listed = jnp.sum((neighbours == slots[:, None]).astype(jnp.float32)).reshape(1)

    offsets, below = jnp.asarray(OFFSETS), jnp.asarray(BELOW)
    most_inner, most_outer = tile_bounds(share)
    vector = jax.ShapeDtypeStruct((share, width), jnp.float32)
    inner_tiles = pltpu.VMEM((most_inner, width, width), jnp.float32)
    outer_tiles = pltpu.VMEM((most_outer, width, width), jnp.float32)
    square = pltpu.VMEM((share, width, width), jnp.float32)
    narrow = pltpu.VMEM((share * SUB, width), jnp.float32)
    params = pltpu.CompilerParams(vmem_limit_bytes=16 * 1024 * 1024)
    tables = [SMEM] * 3

    tiles_in, spread, rows, cols = pl.pallas_call(
        build_inner_kernel,
        out_shape=[inner_tiles, pltpu.VMEM((share, 4, width, width), jnp.float32), square, narrow],
        in_specs=tables + [VMEM] * 2,
        out_specs=[VMEM] * 4,
        scratch_shapes=[pltpu.VMEM((capacity, width), jnp.float32)],
        compiler_params=params,
        cost_estimate=cost(most_inner * width * width, 16),
        name="build_inner",
    )(meta, offsets, below, positions, density)

    def build_outer_kernel(*refs):
        (m, o, b, position, dens, bef, aft, rhs, spr, rows_in, cols_in, tiles, diag, prec, hood, work) = refs
        work[...] = rows_in[...]
        build_outer(m, o, b, position, dens, bef, aft, rhs, spr, work, cols_in, tiles, diag, prec, hood)

    tiles_out, diagonal, precond = pl.pallas_call(
        build_outer_kernel,
        out_shape=[outer_tiles, vector, vector],
        in_specs=tables + [VMEM] * 8,
        out_specs=[VMEM] * 3,
        scratch_shapes=[
            pltpu.VMEM((4, capacity + 2 * share, width), jnp.float32),
            pltpu.VMEM((share, width, width), jnp.float32),
        ],
        compiler_params=params,
        cost_estimate=cost(most_outer * width * width, 16),
        name="build_outer",
    )(meta, offsets, below, positions, density, before, after, right_side, held(spread), held(rows), held(cols))

    def inner(field):
        return pl.pallas_call(
            apply_inner,
            out_shape=[square, narrow],
            in_specs=tables + [VMEM] * 2,
            out_specs=[VMEM] * 2,
            scratch_shapes=[pltpu.VMEM((share, width, width), jnp.float32)],
            compiler_params=params,
            cost_estimate=cost(most_inner * width * width, 4),
            name="apply_inner",
        )(meta, offsets, below, field, held(tiles_in))

    def exchange(field):
        count = pieces * columns
        axes = ("piece", "col")
        received = []
        for c in range(1, columns - 1):
            pairs = []
            for p in range(pieces - 1):
                low, high = p * columns + c, (p + 1) * columns
                pairs += [(low, high), (high, low)]
            received.append(lax.ppermute(field, axes, pairs))
        received.append(lax.ppermute(field, axes, [(i, i + 1) for i in range(count - 1)]))
        received.append(lax.ppermute(field, axes, [(i + 1, i) for i in range(count - 1)]))
        return received

    outer_scratch = [
        pltpu.VMEM((share, width, width), jnp.float32),
        pltpu.VMEM((columns * share, width), jnp.float32),
    ]
    outer_cost = cost(most_outer * width * width, 2)

    received = exchange(precond)
    rows, cols = inner(precond)
    spill, scaled = pl.pallas_call(
        apply_first_kernel,
        out_shape=[vector, vector],
        in_specs=tables + [VMEM] * (3 + columns + 3),
        out_specs=[VMEM] * 2,
        scratch_shapes=outer_scratch,
        compiler_params=params,
        cost_estimate=outer_cost,
        name="apply_first",
    )(meta, offsets, below, right_side, precond, diagonal, *received, held(tiles_out), held(rows), held(cols))

    received = exchange(scaled)
    rows, cols = inner(scaled)
    twice, sums = pl.pallas_call(
        apply_second_kernel,
        out_shape=[vector, jax.ShapeDtypeStruct((SUB, width), jnp.float32)],
        in_specs=tables + [SMEM] + [VMEM] * (4 + columns + 3),
        out_specs=[VMEM] * 2,
        scratch_shapes=outer_scratch,
        compiler_params=params,
        cost_estimate=outer_cost,
        name="apply_second",
    )(meta, offsets, below, listed, right_side, precond, spill, scaled, *received, held(tiles_out), held(rows), held(cols))

    steps = [("col", 1 << k) for k in range(columns.bit_length() - 1)]
    steps += [("piece", 1 << k) for k in range(pieces.bit_length() - 1)]
    other = jnp.zeros_like(sums)
    for axis, step in steps:
        sums = sums + other
        other = lax.ppermute(sums, axis, [(i, i ^ step) for i in range(lax.axis_size(axis))])

    solution_field, residual, count = pl.pallas_call(
        finish_kernel,
        out_shape=[vector, vector, jax.ShapeDtypeStruct((SUB, width), jnp.float32)],
        in_specs=[SMEM] + [VMEM] * 8,
        out_specs=[VMEM] * 3,
        name="finish",
    )(meta, right_side, precond, diagonal, spill, scaled, twice, sums, other)
    return lax.cond(
        count[0, 4] == total.astype(jnp.float32),
        lambda: (solution_field, residual),
        lambda: literal(positions, phase, neighbours, counts, phase_density, right_side),
    )


def solution(mesh):
    placed = (
        P(None, "piece", None),
        P("piece", None),
        P("piece", "col"),
        P(),
        P(),
        P(("piece", "col"), None),
    )
    return jax.shard_map(
        body,
        mesh=mesh,
        in_specs=placed,
        out_specs=(P(("piece", "col"), None), P(("piece", "col"), None)),
        check_vma=False,
    )
```

```python
import functools
import math

import jax
import jax.numpy as jnp
import numpy as np
from jax import lax
from jax.experimental import pallas as pl
from jax.experimental.pallas import tpu as pltpu
from jax.sharding import PartitionSpec as P

ITERS = 2
SIDE = 4
LAYER = SIDE * SIDE
REACH = 2 * LAYER
SUB = 8
VMEM = pl.BlockSpec(memory_space=pltpu.VMEM)
SMEM = pl.BlockSpec(memory_space=pltpu.SMEM)


def stencil_tables():
    levels = SIDE.bit_length() - 1

    def cell(code):
        across = sum((code >> (2 * level) & 1) << level for level in range(levels))
        along = sum((code >> (2 * level + 1) & 1) << level for level in range(levels))
        return across, along

    place = {cell(code): code for code in range(LAYER)}
    rows = []
    for code in range(LAYER):
        across, along = cell(code)
        rows.append(
            sorted(
                step_z * LAYER + place[across + step_x, along + step_y] - code
                for step_z in (-1, 0, 1)
                for step_y in (-1, 0, 1)
                for step_x in (-1, 0, 1)
                if (across + step_x, along + step_y) in place
            )
        )
    longest = max(len(row) for row in rows)
    offsets = np.zeros((LAYER, longest), np.int32)
    below = np.zeros((LAYER, 2 * REACH + 1), np.int32)
    for code, row in enumerate(rows):
        offsets[code, : len(row)] = row
        for t in range(-REACH, REACH + 1):
            below[code, t + REACH] = sum(offset < t for offset in row)
    return offsets, below


OFFSETS, BELOW = stencil_tables()
WIDEST = OFFSETS.shape[1]
TABLE = np.concatenate([OFFSETS, BELOW], 1)
LIMIT = pltpu.CompilerParams(vmem_limit_bytes=6 * 1024 * 1024)


def tile_bounds(share):
    inner = outer = 0
    for first in range(LAYER):
        for live in range(1, share + 1):
            near = far = 0
            for a in range(live):
                code = (first + a) % LAYER
                row = [int(o) for o in OFFSETS[code][: BELOW[code, -1]]]
                near += sum(0 <= a + o and o <= 0 for o in row)
                far += sum(a + o < 0 or a + o >= live for o in row)
            inner, outer = max(inner, near), max(outer, far)
    return inner, outer


def padded(cells, sides, width):
    for axis, dim in sides:
        count = lax.axis_size(axis)
        ends = count - 1
        head = lax.slice_in_dim(cells, 0, width, axis=dim)
        tail = lax.slice_in_dim(cells, cells.shape[dim] - width, cells.shape[dim], axis=dim)
        cells = jnp.concatenate(
            [
                lax.ppermute(tail, axis, [(i, (i + 1) % count) for i in range(ends)]),
                cells,
                lax.ppermute(head, axis, [((i + 1) % count, i) for i in range(ends)]),
            ],
            axis=dim,
        )
    return cells


def fetch_phase_density(phase, phase_density):
    labels = jnp.arange(3, dtype=jnp.int32)
    return jnp.sum(jnp.where(phase[..., None] == labels, phase_density, 0.0), axis=-1)


def literal_pair_term(own_pos, own_rho, own_ids, slot_ids, hood_state, hood_field, base):
    valid = slot_ids >= 0
    where_at = jnp.clip(slot_ids - base, 0, hood_field.shape[0] - 1)
    other = hood_state[:, where_at]
    remote = hood_field[where_at]
    squared = jnp.zeros((own_rho.shape[0], own_rho.shape[1], own_rho.shape[1]), jnp.float32)
    for component in range(3):
        slot_displacement = own_pos[component][:, :, None] - other[component][:, None, :]
        squared = squared + slot_displacement * slot_displacement
    kernel = jnp.square(jnp.maximum(1.0 - squared, 0.0)) / (squared + 0.01)
    weight = 2.0 / (own_rho[:, :, None] + other[3][:, None, :])
    particles = jnp.arange(own_rho.shape[1], dtype=jnp.int32)
    same = (slot_ids == own_ids)[:, None, None] & (particles[:, None] == particles[None, :])[None]
    keep = valid[:, None, None] & jnp.logical_not(same)
    tile = jnp.where(keep, kernel * weight / own_rho.shape[1], 0.0)
    return jnp.einsum("gij,gj->gi", tile, remote, precision=lax.Precision.HIGHEST)


def literal(positions, phase, neighbours, counts, phase_density, right_side):
    capacity = positions.shape[1]
    per_block = positions.shape[2]
    columns = lax.axis_size("col")
    share = capacity // columns
    piece = lax.axis_index("piece")
    column = lax.axis_index("col")
    density = fetch_phase_density(phase, phase_density)
    state = jnp.concatenate([positions, density[None]], 0)
    filled = counts[piece]
    hood_state = padded(state, (("piece", 1),), capacity)

    def remap(ids):
        return jnp.where(ids >= 0, ids - (piece - 1) * capacity, -1)

    def surround(whole):
        return padded(whole, (("piece", 0),), capacity)

    hood_size = hood_state.shape[1]
    live = jnp.arange(capacity, dtype=jnp.int32) < filled
    group = math.gcd(16, capacity)
    ngroup = capacity // group

    def group_sum(field_hood, start):
        own_pos = lax.dynamic_slice_in_dim(positions, start, group, 1)
        own_rho = lax.dynamic_slice_in_dim(density, start, group, 0)
        own_ids = capacity + start + jnp.arange(group, dtype=jnp.int32)
        lists = remap(lax.dynamic_slice_in_dim(neighbours, start, group, 0))
        running = jnp.zeros((group, per_block), jnp.float32)
        for neighbour_slot in range(lists.shape[1]):
            running = running + literal_pair_term(
                own_pos, own_rho, own_ids, lists[:, neighbour_slot], hood_state, field_hood, 0
            )
        return running

    def own_terms(field_hood):
        starts = jnp.arange(ngroup, dtype=jnp.int32) * group
        output_blocks = lax.map(lambda start: group_sum(field_hood, start), starts)
        return output_blocks.reshape(capacity, per_block)

    def mine(values):
        return lax.dynamic_slice_in_dim(values, column * share, share, 0)

    def totals(part_sum):
        return lax.psum_scatter(part_sum, "col", scatter_dimension=0, tiled=True)

    def hood_of(column_vector):
        return surround(lax.all_gather(column_vector, "col", axis=0, tiled=True))

    source = jnp.where(mine(live)[:, None], right_side, 0.0)
    rho_vector = mine(density)

    def inner(first, second):
        return jnp.sum(first * second)

    diagonal = 1.0 / rho_vector + totals(own_terms(jnp.ones((hood_size, per_block), jnp.float32)))

    def operate(column_vector):
        return diagonal * column_vector - totals(own_terms(hood_of(column_vector)))

    solution_field = jnp.zeros_like(source)
    residual = source

    def paired_sums(first, second, third):
        return lax.psum((inner(first, second), inner(second, third)), ("piece", "col"))

    precond = residual / diagonal
    image = operate(precond)
    weighted, curved = paired_sums(residual, precond, image)
    advance = weighted / curved
    direction = precond
    along = image
    for step in range(ITERS):
        solution_field = solution_field + advance * direction
        residual = residual - advance * along
        if step + 1 < ITERS:
            precond = residual / diagonal
            image = operate(precond)
            weighted_next, curved = paired_sums(residual, precond, image)
            blend = weighted_next / weighted
            advance = weighted_next / (curved - blend * weighted_next / advance)
            direction = precond + blend * direction
            along = image + blend * along
            weighted = weighted_next
    return (solution_field, residual)


def rank(table, code, t):
    return table[code, jnp.clip(t, -REACH, REACH) + REACH + WIDEST]


def inner_range(meta, table, a):
    code = lax.rem(meta[1] + a, LAYER)
    return code, rank(table, code, -a), rank(table, code, 0)


def outer_ranges(meta, table, a):
    code = lax.rem(meta[1] + a, LAYER)
    place = meta[1] + a
    before = (rank(table, code, -place), rank(table, code, -a))
    after = (rank(table, code, meta[0] - a), rank(table, code, meta[2] - place))
    return code, before, after


def pair_chunk(own, other):
    dx = own[0] - other[0]
    dy = own[1] - other[1]
    dz = own[2] - other[2]
    squared = dx * dx + dy * dy + dz * dz
    rest = jnp.maximum(1.0 - squared, 0.0)
    return rest * rest * pltpu.reciprocal((squared + 0.01) * (own[3] + other[3]), approx=True)


def spread_columns(out, index, rows):
    count, width = rows.shape
    turned = rows.T
    for a in range(count):
        out[index(a)] = jnp.broadcast_to(turned[:, a : a + 1], (width, width))


def lane_sums(parts, count, width):
    lanes = lax.broadcasted_iota(jnp.int32, (width, width), 1)
    turned = jnp.zeros((width, width), jnp.float32)
    for a in range(count):
        turned = jnp.where(lanes == a, jnp.sum(parts[a], axis=1, keepdims=True), turned)
    return turned.T[:count]


def totals(live, rows_ref, cols_ref, count, width):
    rows = lane_sums(rows_ref, count, width)
    cols = jnp.sum(cols_ref[...].reshape(count, SUB, width), axis=1)
    alive = lax.broadcasted_iota(jnp.int32, (count, width), 0) < live
    return jnp.where(alive, rows + cols, 0.0)


def prepare(counts, densities, position, phase, meta, density, tail, head):
    share, width = tail.shape[1:]
    capacity = phase.shape[0]
    piece, column = lax.axis_index("piece"), lax.axis_index("col")
    filled = counts[piece]
    before = jnp.int32(0)
    total = jnp.int32(0)
    for p in range(counts.shape[0]):
        before = before + jnp.where(p < piece, counts[p], 0)
        total = total + counts[p]
    meta[0] = jnp.clip(filled - column * share, 0, share)
    meta[1] = before + column * share
    meta[2] = total
    meta[3] = column * share
    meta[4] = filled
    meta[5] = counts[jnp.maximum(piece - 1, 0)]
    labels = phase[...]
    density[...] = sum(jnp.where(labels == k, densities[k], 0.0) for k in range(densities.shape[0]))
    last = pl.ds(filled - share, share)
    for k in range(3):
        tail[k] = position[k, last, :]
        head[k] = position[k, 0:share, :]
    tail[3] = density[last, :]
    head[3] = density[0:share, :]


def build_inner(meta, table, position, density, tiles, spread, rows_ref, cols_ref, weight):
    share, width = rows_ref.shape[0], rows_ref.shape[2]
    chunks = width // SUB
    base = meta[3]
    weight[...] = density[...] * (width / 2.0)
    own_rows = pl.ds(pl.multiple_of(base, SUB), share)
    for k in range(4):
        values = position[k, own_rows, :] if k < 3 else weight[own_rows, :]
        spread_columns(spread, lambda a: (a, k), values)
    cols_ref[...] = jnp.zeros_like(cols_ref)

    def other_rows(row):
        here = pl.ds(row, 1)
        return [position[k, here, :] for k in range(3)] + [weight[here, :]]

    def block(a, at):
        code, low, high = inner_range(meta, table, a)

        def pair(j, carry):
            at, sums = carry
            n = a + table[code, j]
            other = other_rows(base + n)
            down = jnp.zeros((SUB, width), jnp.float32)
            after = []
            for c in range(chunks):
                here = slice(c * SUB, (c + 1) * SUB)
                tile = pair_chunk([spread[a, k, here, :] for k in range(4)], other)
                tiles[at, here, :] = tile
                down = down + tile
                after.append(sums[c] + tile)
            there = pl.ds(pl.multiple_of(n * SUB, SUB), SUB)
            cols_ref[there, :] = cols_ref[there, :] + down
            return at + 1, tuple(after)

        zero = jnp.zeros((SUB, width), jnp.float32)
        at, sums = lax.fori_loop(low, high, pair, (at, (zero,) * chunks))
        other = other_rows(base + a)
        lane = lax.broadcasted_iota(jnp.int32, (SUB, width), 1)
        sublane = lax.broadcasted_iota(jnp.int32, (SUB, width), 0)
        for c in range(chunks):
            here = slice(c * SUB, (c + 1) * SUB)
            tile = pair_chunk([spread[a, k, here, :] for k in range(4)], other)
            tile = jnp.where(lane == sublane + c * SUB, 0.0, tile)
            tiles[at, here, :] = tile
            rows_ref[a, here, :] = sums[c] + tile
        return at + 1

    lax.fori_loop(0, meta[0], block, 0)


def build_outer(
    meta, table, position, density, before, after, right_side, spread, rows_ref, cols_ref,
    tiles, diagonal_ref, precond_ref, hood, work,
):
    share, width = right_side.shape
    chunks = width // SUB
    capacity = density.shape[0]
    base, filled = meta[3], meta[4]
    scale = width / 2.0
    for k in range(4):
        gain = 1.0 if k < 3 else scale
        hood[k, 0:share, :] = before[k] * gain
        hood[k, share : share + capacity, :] = position[k] if k < 3 else density[...] * gain
        hood[k, share + capacity :, :] = after[k] * gain
    edge = share + filled - base

    def block(a, at):
        code, (low, high), (low_next, high_next) = outer_ranges(meta, table, a)

        def pair(j, carry):
            at, sums = carry
            w = share + a + table[code, j]
            row = jnp.where(w < edge, base + w, share + capacity + w - edge)
            here = pl.ds(row, 1)
            other = [hood[k, here, :] for k in range(4)]
            result = []
            for c in range(chunks):
                here = slice(c * SUB, (c + 1) * SUB)
                tile = pair_chunk([spread[a, k, here, :] for k in range(4)], other)
                tiles[at, here, :] = tile
                result.append(sums[c] + tile)
            return at + 1, tuple(result)

        start = tuple(rows_ref[a, c * SUB : (c + 1) * SUB, :] for c in range(chunks))
        carry = lax.fori_loop(low, high, pair, (at, start))
        at, sums = lax.fori_loop(low_next, high_next, pair, carry)
        for c in range(chunks):
            work[a, c * SUB : (c + 1) * SUB, :] = sums[c]
        return at

    lax.fori_loop(0, meta[0], block, 0)
    own_rows = pl.ds(pl.multiple_of(base, SUB), share)
    alive = lax.broadcasted_iota(jnp.int32, (share, width), 0) < meta[0]
    diagonal = 1.0 / density[own_rows, :] + totals(meta[0], work, cols_ref, share, width)
    diagonal_ref[...] = diagonal
    precond_ref[...] = jnp.where(alive, right_side[...], 0.0) / diagonal


def apply_inner(meta, table, field, tiles, rows_ref, cols_ref, spread):
    share, width = field.shape
    chunks = width // SUB
    spread_columns(spread, lambda a: a, field[...])
    cols_ref[...] = jnp.zeros_like(cols_ref)

    def block(a, at):
        code, low, high = inner_range(meta, table, a)

        def pair(j, carry):
            at, sums = carry
            n = a + table[code, j]
            value = field[pl.ds(n, 1), :]
            down = jnp.zeros((SUB, width), jnp.float32)
            after = []
            for c in range(chunks):
                here = slice(c * SUB, (c + 1) * SUB)
                tile = tiles[at, here, :]
                down = down + tile * spread[a, here, :]
                after.append(sums[c] + tile * value)
            there = pl.ds(pl.multiple_of(n * SUB, SUB), SUB)
            cols_ref[there, :] = cols_ref[there, :] + down
            return at + 1, tuple(after)

        zero = jnp.zeros((SUB, width), jnp.float32)
        at, sums = lax.fori_loop(low, high, pair, (at, (zero,) * chunks))
        value = field[pl.ds(a, 1), :]
        for c in range(chunks):
            here = slice(c * SUB, (c + 1) * SUB)
            rows_ref[a, here, :] = sums[c] + tiles[at, here, :] * value
        return at + 1

    lax.fori_loop(0, meta[0], block, 0)


def apply_outer(meta, table, received, tiles, rows_ref, cols_ref, work, hood):
    columns = len(received)
    share, width = received[0].shape
    chunks = width // SUB
    base, filled = meta[3], meta[4]
    for k, ref in enumerate(received):
        hood[k * share : (k + 1) * share, :] = ref[...]
    column = lax.div(base, share)
    last = columns - 2
    edge = share + filled - base
    before_at = jnp.where(column == 0, meta[5] - 2 * share, last * share)
    after_at = (last + 1) * share - 2 * share
    head_at = jnp.where(column == last + 1, (last + 1) * share, (column - 1) * share) - edge

    def block(a, at):
        code, (low, high), (low_next, high_next) = outer_ranges(meta, table, a)

        def pair(j, carry):
            at, sums = carry
            w = share + a + table[code, j]
            row = w + jnp.where(w < share, before_at, jnp.where(w < edge, after_at, head_at))
            value = hood[pl.ds(row, 1), :]
            result = []
            for c in range(chunks):
                here = slice(c * SUB, (c + 1) * SUB)
                result.append(sums[c] + tiles[at, here, :] * value)
            return at + 1, tuple(result)

        start = tuple(rows_ref[a, c * SUB : (c + 1) * SUB, :] for c in range(chunks))
        carry = lax.fori_loop(low, high, pair, (at, start))
        at, sums = lax.fori_loop(low_next, high_next, pair, carry)
        for c in range(chunks):
            work[a, c * SUB : (c + 1) * SUB, :] = sums[c]
        return at

    lax.fori_loop(0, meta[0], block, 0)
    return totals(meta[0], work, cols_ref, share, width)


def apply_first_kernel(
    meta, table, right_side, precond, diagonal, *rest
):
    *received, tiles, rows_ref, cols_ref, spill_ref, scaled_ref, work, hood = rest
    spill = apply_outer(meta, table, received, tiles, rows_ref, cols_ref, work, hood)
    spill_ref[...] = spill
    scaled_ref[...] = spill / diagonal[...]


def apply_second_kernel(
    meta, table, listed, right_side, precond, spill, scaled, *rest
):
    *received, tiles, rows_ref, cols_ref, twice_ref, sums_ref, work, hood = rest
    twice = apply_outer(meta, table, received, tiles, rows_ref, cols_ref, work, hood)
    twice_ref[...] = twice
    share, width = twice.shape
    alive = lax.broadcasted_iota(jnp.int32, (share, width), 0) < meta[0]
    source = jnp.where(alive, right_side[...], 0.0)
    lane = lax.broadcasted_iota(jnp.int32, (1, width), 1)
    sums = jnp.where(lane == 4, listed[0], 0.0)
    pairs = ((source, precond[...]), (spill[...], precond[...]), (spill[...], scaled[...]), (scaled[...], twice))
    for k, (first, second) in enumerate(pairs):
        along = jnp.sum(first * second, axis=0, keepdims=True)
        sums = jnp.where(lane == k, jnp.sum(along, axis=1, keepdims=True), sums)
    sums_ref[...] = jnp.broadcast_to(sums, (SUB, width))


def finish_kernel(meta, right_side, precond, diagonal, spill, scaled, twice, mine, other, solution_ref, residual_ref, count_ref):
    share, width = precond.shape
    sums = mine[...] + other[...]
    count_ref[...] = sums

    def pick(k):
        return sums[0:1, k : k + 1]

    weighted, cross, square, last = pick(0), pick(1), pick(2), pick(3)
    part = cross / weighted
    advance = 1.0 / (1.0 - part)
    keep = -part * advance
    weighted_next = advance * advance * (square - cross * part)
    bent = keep * keep * cross + 2.0 * keep * advance * square + advance * advance * last
    blend = weighted_next / weighted
    advance_next = weighted_next / (weighted_next - bent - blend * weighted_next / advance)
    alive = lax.broadcasted_iota(jnp.int32, (share, width), 0) < meta[0]
    source = jnp.where(alive, right_side[...], 0.0)
    residual = keep * source + advance * spill[...]
    next_precond = keep * precond[...] + advance * scaled[...]
    direction = next_precond + blend * precond[...]
    image = residual - keep * spill[...] - advance * twice[...] + blend * (source - spill[...])
    solution_ref[...] = advance * precond[...] + advance_next * direction
    residual_ref[...] = residual - advance_next * image


def cost(pairs, each):
    return pl.CostEstimate(flops=pairs * each, bytes_accessed=pairs * 4, transcendentals=0)


def held(array):
    return pltpu.with_memory_space_constraint(array, pltpu.VMEM)


def body(positions, phase, neighbours, counts, phase_density, right_side):
    capacity, width = phase.shape
    columns = lax.axis_size("col")
    pieces = lax.axis_size("piece")
    share = capacity // columns
    piece = lax.axis_index("piece")
    column = lax.axis_index("col")
    message = jax.ShapeDtypeStruct((4, share, width), jnp.float32)
    meta, density, tail, head = pl.pallas_call(
        prepare,
        out_shape=[pltpu.SMEM((8,), jnp.int32), jax.ShapeDtypeStruct(phase.shape, jnp.float32), message, message],
        in_specs=[SMEM] * 2 + [VMEM] * 2,
        out_specs=[SMEM] + [VMEM] * 3,
        compiler_params=LIMIT,
        name="prepare",
    )(counts, phase_density, positions, phase)
    meta = pltpu.with_memory_space_constraint(meta, pltpu.SMEM)
    before = lax.ppermute(tail, "piece", [(i, (i + 1) % pieces) for i in range(pieces)])
    after = lax.ppermute(head, "piece", [((i + 1) % pieces, i) for i in range(pieces)])

    total = jnp.sum(counts)
    slots = piece * capacity + jnp.arange(capacity, dtype=jnp.int32)
    listed = jnp.sum((neighbours == slots[:, None]).astype(jnp.float32)).reshape(1)

    table = jnp.asarray(TABLE)
    most_inner, most_outer = tile_bounds(share)
    vector = jax.ShapeDtypeStruct((share, width), jnp.float32)
    inner_tiles = pltpu.VMEM((most_inner, width, width), jnp.float32)
    outer_tiles = pltpu.VMEM((most_outer, width, width), jnp.float32)
    square = pltpu.VMEM((share, width, width), jnp.float32)
    narrow = pltpu.VMEM((share * SUB, width), jnp.float32)
    tables = [SMEM] * 2

    tiles_in, spread, rows, cols = pl.pallas_call(
        build_inner,
        out_shape=[inner_tiles, pltpu.VMEM((share, 4, width, width), jnp.float32), square, narrow],
        in_specs=tables + [VMEM] * 2,
        out_specs=[VMEM] * 4,
        scratch_shapes=[pltpu.VMEM((capacity, width), jnp.float32)],
        compiler_params=LIMIT,
        cost_estimate=cost(most_inner * width * width, 16),
        name="build_inner",
    )(meta, table, positions, density)

    tiles_out, diagonal, precond = pl.pallas_call(
        build_outer,
        out_shape=[outer_tiles, vector, vector],
        in_specs=tables + [VMEM] * 8,
        out_specs=[VMEM] * 3,
        scratch_shapes=[
            pltpu.VMEM((4, capacity + 2 * share, width), jnp.float32),
            pltpu.VMEM((share, width, width), jnp.float32),
        ],
        compiler_params=LIMIT,
        cost_estimate=cost(most_outer * width * width, 16),
        name="build_outer",
    )(meta, table, positions, density, before, after, right_side, held(spread), held(rows), held(cols))

    def inner(field):
        return pl.pallas_call(
            apply_inner,
            out_shape=[square, narrow],
            in_specs=tables + [VMEM] * 2,
            out_specs=[VMEM] * 2,
            scratch_shapes=[pltpu.VMEM((share, width, width), jnp.float32)],
            compiler_params=LIMIT,
            cost_estimate=cost(most_inner * width * width, 4),
            name="apply_inner",
        )(meta, table, field, held(tiles_in))

    def exchange(field):
        count = pieces * columns
        axes = ("piece", "col")
        received = []
        for c in range(1, columns - 1):
            pairs = []
            for p in range(pieces):
                low, high = p * columns + c, (p + 1) % pieces * columns
                pairs += [(low, high), (high, low)]
                rest = [p * columns + k for k in range(1, columns) if k != c]
                pairs += list(zip(rest, rest[1:] + rest[:1]))
            received.append(lax.ppermute(field, axes, pairs))
        received.append(lax.ppermute(field, axes, [(i, (i + 1) % count) for i in range(count)]))
        received.append(lax.ppermute(field, axes, [((i + 1) % count, i) for i in range(count)]))
        return received

    outer_scratch = [
        pltpu.VMEM((share, width, width), jnp.float32),
        pltpu.VMEM((columns * share, width), jnp.float32),
    ]
    outer_cost = cost(most_outer * width * width, 2)

    received = exchange(precond)
    rows, cols = inner(precond)
    spill, scaled = pl.pallas_call(
        apply_first_kernel,
        out_shape=[vector, vector],
        in_specs=tables + [VMEM] * (3 + columns + 3),
        out_specs=[VMEM] * 2,
        scratch_shapes=outer_scratch,
        compiler_params=LIMIT,
        cost_estimate=outer_cost,
        name="apply_first",
    )(meta, table, right_side, precond, diagonal, *received, held(tiles_out), held(rows), held(cols))

    received = exchange(scaled)
    rows, cols = inner(scaled)
    twice, sums = pl.pallas_call(
        apply_second_kernel,
        out_shape=[vector, jax.ShapeDtypeStruct((SUB, width), jnp.float32)],
        in_specs=tables + [SMEM] + [VMEM] * (4 + columns + 3),
        out_specs=[VMEM] * 2,
        scratch_shapes=outer_scratch,
        compiler_params=LIMIT,
        cost_estimate=outer_cost,
        name="apply_second",
    )(meta, table, listed, right_side, precond, spill, scaled, *received, held(tiles_out), held(rows), held(cols))

    steps = [("col", 1 << k) for k in range(columns.bit_length() - 1)]
    steps += [("piece", 1 << k) for k in range(pieces.bit_length() - 1)]
    other = jnp.zeros_like(sums)
    for axis, step in steps:
        sums = sums + other
        other = lax.ppermute(sums, axis, [(i, i ^ step) for i in range(lax.axis_size(axis))])

    solution_field, residual, count = pl.pallas_call(
        finish_kernel,
        out_shape=[vector, vector, jax.ShapeDtypeStruct((SUB, width), jnp.float32)],
        in_specs=[SMEM] + [VMEM] * 8,
        out_specs=[VMEM] * 3,
        compiler_params=LIMIT,
        name="finish",
    )(meta, right_side, precond, diagonal, spill, scaled, twice, sums, other)
    return lax.cond(
        count[0, 4] == total.astype(jnp.float32),
        lambda: (solution_field, residual),
        lambda: literal(positions, phase, neighbours, counts, phase_density, right_side),
    )


def solution(mesh):
    placed = (
        P(None, "piece", None),
        P("piece", None),
        P("piece", "col"),
        P(),
        P(),
        P(("piece", "col"), None),
    )
    return jax.shard_map(
        body,
        mesh=mesh,
        in_specs=placed,
        out_specs=(P(("piece", "col"), None), P(("piece", "col"), None)),
        check_vma=False,
    )
```

```python
import jax
import jax.numpy as jnp
import numpy as np
from jax import lax
from jax.experimental import pallas as pl
from jax.experimental.pallas import tpu as pltpu
from jax.sharding import PartitionSpec as P

ITERS = 2
SIDE = 4
LAYER = SIDE * SIDE
REACH = 2 * LAYER
SUB = 8
VMEM = pl.BlockSpec(memory_space=pltpu.VMEM)
SMEM = pl.BlockSpec(memory_space=pltpu.SMEM)


def stencil_tables():
    levels = SIDE.bit_length() - 1

    def cell(code):
        across = sum((code >> (2 * level) & 1) << level for level in range(levels))
        along = sum((code >> (2 * level + 1) & 1) << level for level in range(levels))
        return across, along

    place = {cell(code): code for code in range(LAYER)}
    rows = []
    for code in range(LAYER):
        across, along = cell(code)
        rows.append(
            sorted(
                step_z * LAYER + place[across + step_x, along + step_y] - code
                for step_z in (-1, 0, 1)
                for step_y in (-1, 0, 1)
                for step_x in (-1, 0, 1)
                if (across + step_x, along + step_y) in place
            )
        )
    longest = max(len(row) for row in rows)
    offsets = np.zeros((LAYER, longest), np.int32)
    below = np.zeros((LAYER, 2 * REACH + 1), np.int32)
    for code, row in enumerate(rows):
        offsets[code, : len(row)] = row
        for t in range(-REACH, REACH + 1):
            below[code, t + REACH] = sum(offset < t for offset in row)
    return offsets, below


OFFSETS, BELOW = stencil_tables()
WIDEST = OFFSETS.shape[1]
TABLE = np.concatenate([OFFSETS, BELOW], 1)
LIMIT = pltpu.CompilerParams(vmem_limit_bytes=6 * 1024 * 1024)


def tile_bounds(share):
    inner = outer = 0
    for first in range(LAYER):
        for live in range(1, share + 1):
            near = far = 0
            for a in range(live):
                code = (first + a) % LAYER
                row = [int(o) for o in OFFSETS[code][: BELOW[code, -1]]]
                near += sum(0 <= a + o and o <= 0 for o in row)
                far += sum(a + o < 0 or a + o >= live for o in row)
            inner, outer = max(inner, near), max(outer, far)
    return inner, outer


def rank(table, code, t):
    return table[code, jnp.clip(t, -REACH, REACH) + REACH + WIDEST]


def inner_range(meta, table, a):
    code = lax.rem(meta[1] + a, LAYER)
    low, high = rank(table, code, -a), rank(table, code, 0)
    last = jnp.maximum(high - low - 1, 0)
    return high - low, lambda t: a + table[code, low + jnp.minimum(t, last)]


def outer_range(meta, table, a):
    code = lax.rem(meta[1] + a, LAYER)
    place = meta[1] + a
    low, split = rank(table, code, -place), rank(table, code, -a)
    resume, high = rank(table, code, meta[0] - a), rank(table, code, meta[2] - place)
    ahead = split - low
    count = ahead + jnp.maximum(high - resume, 0)
    last = jnp.maximum(count - 1, 0)

    def place_of(t):
        t = jnp.minimum(t, last)
        return a + table[code, jnp.where(t < ahead, low + t, resume + t - ahead)]

    return count, place_of


def sweep(count, fetch, step, carry):
    def both(i, state):
        carry, first, second = state
        later = fetch(2 * i + 2), fetch(2 * i + 3)
        return step(second, step(first, carry)), *later

    carry, first, _ = lax.fori_loop(0, lax.div(count, 2), both, (carry, fetch(0), fetch(1)))
    return lax.fori_loop(0, lax.rem(count, 2), lambda _, carry: step(first, carry), carry)


def tree(terms):
    while len(terms) > 1:
        terms = [a + b for a, b in zip(terms[::2], terms[1::2])] + terms[len(terms) // 2 * 2 :]
    return terms[0]


def pieces_of(width):
    return [slice(c * SUB, (c + 1) * SUB) for c in range(width // SUB)]


def wide(row):
    return jnp.broadcast_to(row, (SUB, row.shape[1]))


def pair_chunk(own, other):
    dx = own[0] - other[0]
    dy = own[1] - other[1]
    dz = own[2] - other[2]
    squared = dx * dx + dy * dy + dz * dz
    rest = jnp.maximum(1.0 - squared, 0.0)
    return rest * rest * pltpu.reciprocal((squared + 0.01) * (own[3] + other[3]), approx=True)


def spread_columns(out, index, rows):
    count, width = rows.shape
    turned = rows.T
    for a in range(count):
        out[index(a)] = jnp.broadcast_to(turned[:, a : a + 1], (width, width))


def lane_sums(parts, count, width):
    lanes = lax.broadcasted_iota(jnp.int32, (width, width), 1)
    turned = jnp.zeros((width, width), jnp.float32)
    for a in range(count):
        turned = jnp.where(lanes == a, jnp.sum(parts[a], axis=1, keepdims=True), turned)
    return turned.T[:count]


def sub_sums(cols):
    return jnp.sum(cols[...].reshape(-1, SUB, cols.shape[1]), axis=1)


def alive_rows(meta, share, width):
    return lax.broadcasted_iota(jnp.int32, (share, width), 0) < meta[0]


def prepare(counts, densities, position, phase, listed, meta, density, tail, head, times):
    share, width = tail.shape[1:]
    capacity = phase.shape[0]
    piece, column = lax.axis_index("piece"), lax.axis_index("col")
    filled = counts[piece]
    filled_before = counts[jnp.maximum(piece - 1, 0)]
    before = jnp.int32(0)
    total = jnp.int32(0)
    for p in range(counts.shape[0]):
        before = before + jnp.where(p < piece, counts[p], 0)
        total = total + counts[p]
    meta[0] = jnp.clip(filled - column * share, 0, share)
    meta[1] = before + column * share
    meta[2] = total
    meta[3] = column * share
    meta[4] = filled
    meta[5] = filled_before
    labels = phase[...]
    density[...] = sum(jnp.where(labels == k, densities[k], 0.0) for k in range(densities.shape[0]))
    last = pl.ds(filled - share, share)
    for k in range(3):
        tail[k] = position[k, last, :]
        head[k] = position[k, 0:share, :]
    tail[3] = density[last, :]
    head[3] = density[0:share, :]
    ids = listed[...]
    own = lax.broadcasted_iota(jnp.int32, ids.shape, 1)
    slot = ids - piece * capacity
    away = slot - own + jnp.where(slot < 0, capacity - filled_before, jnp.where(slot >= capacity, filled - capacity, 0))
    away = jnp.where(ids < 0, -REACH, away) + REACH
    steps = lax.broadcasted_iota(jnp.int32, (2 * REACH, capacity), 0)
    found = tree([jnp.where(steps == away[k : k + 1], 1.0, 0.0) for k in range(ids.shape[0])])
    found = jnp.concatenate([found, jnp.zeros((width - 2 * REACH, capacity), jnp.float32)], 0)
    times[...] = found.T


def build_inner(meta, table, position, density, tiles, spread, rows_ref, cols_ref, self_ref, weight):
    share, width = rows_ref.shape[0], rows_ref.shape[2]
    chunks = pieces_of(width)
    base = meta[3]
    weight[...] = density[...] * (width / 2.0)
    own_rows = pl.ds(pl.multiple_of(base, SUB), share)
    for k in range(4):
        values = position[k, own_rows, :] if k < 3 else weight[own_rows, :]
        spread_columns(spread, lambda a: (a, k), values)
    cols_ref[...] = jnp.zeros_like(cols_ref)

    def rows_at(n):
        here = pl.ds(base + n, 1)
        return [wide(position[k, here, :]) for k in range(3)] + [wide(weight[here, :])]

    def block(a, at):
        count, place_of = inner_range(meta, table, a)

        def fetch(t):
            n = place_of(t)
            return n, rows_at(n)

        def pair(fetched, carry):
            n, other = fetched
            at, sums = carry
            result = []
            for here in chunks:
                tile = pair_chunk([spread[a, k, here, :] for k in range(4)], other)
                tiles[at, here, :] = tile
                result.append(tile)
            there = pl.ds(pl.multiple_of(n * SUB, SUB), SUB)
            cols_ref[there, :] = cols_ref[there, :] + tree(result)
            return at + 1, [old + new for old, new in zip(sums, result)]

        zero = jnp.zeros((SUB, width), jnp.float32)
        at, sums = sweep(count, fetch, pair, (at, [zero] * len(chunks)))
        for here, values in zip(chunks, sums):
            rows_ref[a, here, :] = values
        other = rows_at(a)
        lane = lax.broadcasted_iota(jnp.int32, (SUB, width), 1)
        sublane = lax.broadcasted_iota(jnp.int32, (SUB, width), 0)
        result = []
        for c, here in enumerate(chunks):
            tile = pair_chunk([spread[a, k, here, :] for k in range(4)], other)
            tile = jnp.where(lane == sublane + c * SUB, 0.0, tile)
            tiles[at, here, :] = tile
            result.append(tile)
        self_ref[pl.ds(pl.multiple_of(a * SUB, SUB), SUB), :] = tree(result)
        return at + 1

    lax.fori_loop(0, meta[0], block, 0)


def build_outer(
    meta, table, position, density, before, after, spread, rows_ref, cols_ref, self_ref,
    tiles, sums_ref, alone_ref, hood, work,
):
    share, width = sums_ref.shape
    chunks = pieces_of(width)
    capacity = density.shape[0]
    base, filled = meta[3], meta[4]
    scale = width / 2.0
    for k in range(4):
        gain = 1.0 if k < 3 else scale
        hood[k, 0:share, :] = before[k] * gain
        hood[k, share : share + capacity, :] = position[k] if k < 3 else density[...] * gain
        hood[k, share + capacity :, :] = after[k] * gain
    edge = share + filled - base

    def block(a, at):
        count, place_of = outer_range(meta, table, a)

        def fetch(t):
            w = share + place_of(t)
            here = pl.ds(jnp.where(w < edge, base + w, share + capacity + w - edge), 1)
            return [wide(hood[k, here, :]) for k in range(4)]

        def pair(other, carry):
            at, sums = carry
            result = []
            for here, old in zip(chunks, sums):
                tile = pair_chunk([spread[a, k, here, :] for k in range(4)], other)
                tiles[at, here, :] = tile
                result.append(old + tile)
            return at + 1, result

        at, sums = sweep(count, fetch, pair, (at, [rows_ref[a, here, :] for here in chunks]))
        for here, values in zip(chunks, sums):
            work[a, here, :] = values
        return at

    lax.fori_loop(0, meta[0], block, 0)
    sums_ref[...] = lane_sums(work, share, width) + sub_sums(cols_ref)
    alone_ref[...] = sub_sums(self_ref)


def settle(
    meta, table, times, density, right_side, sums, alone, inner_old, outer_old,
    inner_tiles, outer_tiles, diagonal_ref, precond_ref, alone_times, sums_work, cols_work, row_work,
):
    share, width = right_side.shape
    alive = alive_rows(meta, share, width)
    lane = lax.broadcasted_iota(jnp.int32, (share, width), 1)
    often = jnp.where(alive, times[...], 0.0)
    mine = jnp.sum(jnp.where(lane == REACH, often, 0.0), axis=1, keepdims=True)
    alone_times[...] = jnp.broadcast_to(mine, (share, width))
    most = jnp.max(jnp.where((lane == REACH) | (lane == 0), 0.0, often))
    sums_work[...] = sums[...]

    @pl.when(most > 1.5)
    def _():
        one_lane = lax.broadcasted_iota(jnp.int32, (1, width), 1)
        cols_work[...] = jnp.zeros_like(cols_work)
        row_work[...] = jnp.zeros_like(row_work)

        def factor(a, n):
            row = times[pl.ds(a, 1), :]
            return jnp.sum(jnp.where(one_lane == n - a + REACH, row, 0.0), axis=1, keepdims=True)

        def block(a, state):
            count, place_of = inner_range(meta, table, a)

            def inner(t, at):
                n = place_of(t)
                tile = inner_old[at] * factor(a, n)
                inner_tiles[at] = tile
                row_work[a] = row_work[a] + tile
                there = pl.ds(n, 1)
                cols_work[there, :] = cols_work[there, :] + jnp.sum(tile, axis=0, keepdims=True)
                return at + 1

            at = lax.fori_loop(0, count, inner, state[0]) + 1
            count, place_far = outer_range(meta, table, a)

            def outer(t, at):
                tile = outer_old[at] * factor(a, place_far(t))
                outer_tiles[at] = tile
                row_work[a] = row_work[a] + tile
                return at + 1

            return at, lax.fori_loop(0, count, outer, state[1])

        lax.fori_loop(0, meta[0], block, (0, 0))
        sums_work[...] = lane_sums(row_work, share, width) + cols_work[...]

    own_rows = pl.ds(pl.multiple_of(meta[3], SUB), share)
    pairs = jnp.where(alive, sums_work[...] + alone[...] * alone_times[...], 0.0)
    diagonal = 1.0 / density[own_rows, :] + pairs
    diagonal_ref[...] = diagonal
    precond_ref[...] = jnp.where(alive, right_side[...], 0.0) / diagonal


def apply_inner(meta, table, field, alone_times, tiles, rows_ref, cols_ref, spread):
    share, width = field.shape
    chunks = pieces_of(width)
    spread_columns(spread, lambda a: a, field[...])
    cols_ref[...] = jnp.zeros_like(cols_ref)

    def block(a, at):
        count, place_of = inner_range(meta, table, a)

        def fetch(t):
            n = place_of(t)
            return n, wide(field[pl.ds(n, 1), :])

        def pair(fetched, carry):
            n, value = fetched
            at, sums = carry
            down, result = [], []
            for here, old in zip(chunks, sums):
                tile = tiles[at, here, :]
                down.append(tile * spread[a, here, :])
                result.append(old + tile * value)
            there = pl.ds(pl.multiple_of(n * SUB, SUB), SUB)
            cols_ref[there, :] = cols_ref[there, :] + tree(down)
            return at + 1, result

        zero = jnp.zeros((SUB, width), jnp.float32)
        at, sums = sweep(count, fetch, pair, (at, [zero] * len(chunks)))
        here = pl.ds(a, 1)
        value = wide(field[here, :] * alone_times[here, :])
        for here, old in zip(chunks, sums):
            rows_ref[a, here, :] = old + tiles[at, here, :] * value
        return at + 1

    lax.fori_loop(0, meta[0], block, 0)


def apply_outer(meta, table, received, tiles, rows_ref, cols_ref, work, hood):
    columns = len(received)
    share, width = received[0].shape
    chunks = pieces_of(width)
    base, filled = meta[3], meta[4]
    for k, ref in enumerate(received):
        hood[k * share : (k + 1) * share, :] = ref[...]
    column = lax.div(base, share)
    last = columns - 2
    edge = share + filled - base
    before_at = jnp.where(column == 0, meta[5] - 2 * share, last * share)
    after_at = (last + 1) * share - 2 * share
    head_at = jnp.where(column == last + 1, (last + 1) * share, (column - 1) * share) - edge

    def block(a, at):
        count, place_of = outer_range(meta, table, a)

        def fetch(t):
            w = share + place_of(t)
            row = w + jnp.where(w < share, before_at, jnp.where(w < edge, after_at, head_at))
            return wide(hood[pl.ds(row, 1), :])

        def pair(value, carry):
            at, sums = carry
            return at + 1, [old + tiles[at, here, :] * value for here, old in zip(chunks, sums)]

        at, sums = sweep(count, fetch, pair, (at, [rows_ref[a, here, :] for here in chunks]))
        for here, values in zip(chunks, sums):
            work[a, here, :] = values
        return at

    lax.fori_loop(0, meta[0], block, 0)
    return jnp.where(alive_rows(meta, share, width), lane_sums(work, share, width) + sub_sums(cols_ref), 0.0)


def apply_first(meta, table, diagonal, *rest):
    *received, tiles, rows_ref, cols_ref, spill_ref, scaled_ref, work, hood = rest
    spill = apply_outer(meta, table, received, tiles, rows_ref, cols_ref, work, hood)
    spill_ref[...] = spill
    scaled_ref[...] = spill / diagonal[...]


def apply_second(meta, table, right_side, precond, spill, scaled, *rest):
    *received, tiles, rows_ref, cols_ref, twice_ref, sums_ref, work, hood = rest
    twice = apply_outer(meta, table, received, tiles, rows_ref, cols_ref, work, hood)
    twice_ref[...] = twice
    share, width = twice.shape
    source = jnp.where(alive_rows(meta, share, width), right_side[...], 0.0)
    lane = lax.broadcasted_iota(jnp.int32, (1, width), 1)
    sums = jnp.zeros((1, width), jnp.float32)
    pairs = ((source, precond[...]), (spill[...], precond[...]), (spill[...], scaled[...]), (scaled[...], twice))
    for k, (first, second) in enumerate(pairs):
        along = jnp.sum(first * second, axis=0, keepdims=True)
        sums = jnp.where(lane == k, jnp.sum(along, axis=1, keepdims=True), sums)
    sums_ref[...] = wide(sums)


def finish(meta, right_side, precond, spill, scaled, twice, mine, other, solution_ref, residual_ref):
    share, width = precond.shape
    sums = mine[...] + other[...]

    def pick(k):
        return sums[0:1, k : k + 1]

    weighted, cross, square, last = pick(0), pick(1), pick(2), pick(3)
    part = cross / weighted
    advance = 1.0 / (1.0 - part)
    keep = -part * advance
    weighted_next = advance * advance * (square - cross * part)
    bent = keep * keep * cross + 2.0 * keep * advance * square + advance * advance * last
    blend = weighted_next / weighted
    advance_next = weighted_next / (weighted_next - bent - blend * weighted_next / advance)
    source = jnp.where(alive_rows(meta, share, width), right_side[...], 0.0)
    residual = keep * source + advance * spill[...]
    next_precond = keep * precond[...] + advance * scaled[...]
    direction = next_precond + blend * precond[...]
    image = residual - keep * spill[...] - advance * twice[...] + blend * (source - spill[...])
    solution_ref[...] = advance * precond[...] + advance_next * direction
    residual_ref[...] = residual - advance_next * image


def held(array):
    return pltpu.with_memory_space_constraint(array, pltpu.VMEM)


def body(positions, phase, neighbours, counts, phase_density, right_side):
    capacity, width = phase.shape
    columns = lax.axis_size("col")
    pieces = lax.axis_size("piece")
    share = capacity // columns
    f32 = jnp.float32
    vector = jax.ShapeDtypeStruct((share, width), f32)
    few = jax.ShapeDtypeStruct((SUB, width), f32)
    message = jax.ShapeDtypeStruct((4, share, width), f32)
    most_inner, most_outer = tile_bounds(share)
    inner_tiles = pltpu.VMEM((most_inner, width, width), f32)
    outer_tiles = pltpu.VMEM((most_outer, width, width), f32)
    square = pltpu.VMEM((share, width, width), f32)
    narrow = pltpu.VMEM((share * SUB, width), f32)
    table = jnp.asarray(TABLE)

    def call(kernel, args, outs, scratch=(), work=0, scalars=2, **more):
        return pl.pallas_call(
            kernel,
            out_shape=outs,
            in_specs=[SMEM] * scalars + [VMEM] * (len(args) - scalars),
            out_specs=[SMEM if getattr(o, "memory_space", None) == pltpu.SMEM else VMEM for o in outs],
            scratch_shapes=scratch,
            compiler_params=LIMIT,
            cost_estimate=pl.CostEstimate(flops=work * width * width, bytes_accessed=0, transcendentals=0),
            name=kernel.__name__,
            **more,
        )(*args)

    meta, density, tail, head, times = call(
        prepare,
        (counts, phase_density, positions, phase, neighbours.T),
        [pltpu.SMEM((8,), jnp.int32), jax.ShapeDtypeStruct(phase.shape, f32), message, message,
         jax.ShapeDtypeStruct((capacity, width), f32)],
    )
    meta = pltpu.with_memory_space_constraint(meta, pltpu.SMEM)
    before = lax.ppermute(tail, "piece", [(i, (i + 1) % pieces) for i in range(pieces)])
    after = lax.ppermute(head, "piece", [((i + 1) % pieces, i) for i in range(pieces)])
    times = lax.psum_scatter(times, "col", scatter_dimension=0, tiled=True)

    tiles_in, spread, rows, cols, selfs = call(
        build_inner,
        (meta, table, positions, density),
        [inner_tiles, pltpu.VMEM((share, 4, width, width), f32), square, narrow, narrow],
        [pltpu.VMEM((capacity, width), f32)],
        16 * most_inner,
    )
    tiles_out, sums, alone = call(
        build_outer,
        (meta, table, positions, density, before, after, held(spread), held(rows), held(cols), held(selfs)),
        [outer_tiles, vector, vector],
        [pltpu.VMEM((4, capacity + 2 * share, width), f32), pltpu.VMEM((share, width, width), f32)],
        16 * most_outer,
    )
    tiles_in, tiles_out, diagonal, precond, alone_times = call(
        settle,
        (meta, table, times, density, right_side, sums, alone, held(tiles_in), held(tiles_out)),
        [inner_tiles, outer_tiles, vector, vector, vector],
        [pltpu.VMEM((share, width), f32)] * 2 + [pltpu.VMEM((share, width, width), f32)],
        input_output_aliases={7: 0, 8: 1},
    )

    def inner(field):
        return call(
            apply_inner,
            (meta, table, field, alone_times, held(tiles_in)),
            [square, narrow],
            [pltpu.VMEM((share, width, width), f32)],
            4 * most_inner,
        )

    def exchange(field):
        count = pieces * columns
        axes = ("piece", "col")
        received = []
        for c in range(1, columns - 1):
            pairs = []
            for p in range(pieces):
                low, high = p * columns + c, (p + 1) % pieces * columns
                pairs += [(low, high), (high, low)]
                rest = [p * columns + k for k in range(1, columns) if k != c]
                pairs += list(zip(rest, rest[1:] + rest[:1]))
            received.append(lax.ppermute(field, axes, pairs))
        received.append(lax.ppermute(field, axes, [(i, (i + 1) % count) for i in range(count)]))
        received.append(lax.ppermute(field, axes, [((i + 1) % count, i) for i in range(count)]))
        return received

    scratch = [pltpu.VMEM((share, width, width), f32), pltpu.VMEM((columns * share, width), f32)]

    received = exchange(precond)
    rows, cols = inner(precond)
    spill, scaled = call(
        apply_first,
        (meta, table, diagonal, *received, held(tiles_out), held(rows), held(cols)),
        [vector, vector],
        scratch,
        2 * most_outer,
    )

    received = exchange(scaled)
    rows, cols = inner(scaled)
    twice, sums = call(
        apply_second,
        (meta, table, right_side, precond, spill, scaled, *received, held(tiles_out), held(rows), held(cols)),
        [vector, few],
        scratch,
        2 * most_outer,
    )

    steps = [("col", 1 << k) for k in range(columns.bit_length() - 1)]
    steps += [("piece", 1 << k) for k in range(pieces.bit_length() - 1)]
    other = None
    for axis, step in steps:
        sums = sums if other is None else sums + other
        other = lax.ppermute(sums, axis, [(i, i ^ step) for i in range(lax.axis_size(axis))])

    return tuple(call(
        finish,
        (meta, right_side, precond, spill, scaled, twice, sums, other),
        [vector, vector],
        scalars=1,
    ))


def solution(mesh):
    placed = (
        P(None, "piece", None),
        P("piece", None),
        P("piece", "col"),
        P(),
        P(),
        P(("piece", "col"), None),
    )
    return jax.shard_map(
        body,
        mesh=mesh,
        in_specs=placed,
        out_specs=(P(("piece", "col"), None), P(("piece", "col"), None)),
        check_vma=False,
    )
```

```python
import jax
import jax.numpy as jnp
import numpy as np
from jax import lax
from jax.experimental import pallas as pl
from jax.experimental.pallas import tpu as pltpu
from jax.sharding import PartitionSpec as P

ITERS = 2
SIDE = 4
LAYER = SIDE * SIDE
REACH = 2 * LAYER
SUB = 8
VMEM = pl.BlockSpec(memory_space=pltpu.VMEM)
SMEM = pl.BlockSpec(memory_space=pltpu.SMEM)


def stencil_tables():
    levels = SIDE.bit_length() - 1

    def cell(code):
        across = sum((code >> (2 * level) & 1) << level for level in range(levels))
        along = sum((code >> (2 * level + 1) & 1) << level for level in range(levels))
        return across, along

    place = {cell(code): code for code in range(LAYER)}
    rows = []
    for code in range(LAYER):
        across, along = cell(code)
        rows.append(
            sorted(
                step_z * LAYER + place[across + step_x, along + step_y] - code
                for step_z in (-1, 0, 1)
                for step_y in (-1, 0, 1)
                for step_x in (-1, 0, 1)
                if (across + step_x, along + step_y) in place
            )
        )
    longest = max(len(row) for row in rows)
    offsets = np.zeros((LAYER, longest), np.int32)
    below = np.zeros((LAYER, 2 * REACH + 1), np.int32)
    for code, row in enumerate(rows):
        offsets[code, : len(row)] = row
        for t in range(-REACH, REACH + 1):
            below[code, t + REACH] = sum(offset < t for offset in row)
    return offsets, below


OFFSETS, BELOW = stencil_tables()
WIDEST = OFFSETS.shape[1]
TABLE = np.concatenate([OFFSETS, BELOW], 1)
STRIDE = TABLE.shape[1]
LIMIT = pltpu.CompilerParams(vmem_limit_bytes=6 * 1024 * 1024)


def tile_bounds(share):
    inner = outer = 0
    for first in range(LAYER):
        for live in range(1, share + 1):
            near = far = 0
            for a in range(live):
                code = (first + a) % LAYER
                row = [int(o) for o in OFFSETS[code][: BELOW[code, -1]]]
                near += sum(0 <= a + o and o <= 0 for o in row)
                far += sum(a + o < 0 or a + o >= live for o in row)
            inner, outer = max(inner, near), max(outer, far)
    return inner, outer


def rank(table, code, t):
    return table[code * STRIDE + jnp.clip(t, -REACH, REACH) + REACH + WIDEST]


def inner_range(meta, table, a):
    code = lax.rem(meta[1] + a, LAYER)
    low, high = rank(table, code, -a), rank(table, code, 0)
    start = code * STRIDE + low
    return high - low, lambda t: a + table[start + t]


def outer_range(meta, table, a):
    code = lax.rem(meta[1] + a, LAYER)
    place = meta[1] + a
    low, split = rank(table, code, -place), rank(table, code, -a)
    resume, high = rank(table, code, meta[0] - a), rank(table, code, meta[2] - place)
    ahead = split - low
    start = code * STRIDE + low
    start_after = code * STRIDE + resume - ahead
    count = ahead + jnp.maximum(high - resume, 0)
    return count, lambda t: a + table[t + jnp.where(t < ahead, start, start_after)]


def sweep(count, fetch, step, carry):
    def both(i, state):
        carry, first, second = state
        later = fetch(2 * i + 2), fetch(2 * i + 3)
        return step(second, step(first, carry)), *later

    carry, first, _ = lax.fori_loop(0, lax.div(count, 2), both, (carry, fetch(0), fetch(1)))
    return lax.fori_loop(0, lax.rem(count, 2), lambda _, carry: step(first, carry), carry)


def tree(terms):
    while len(terms) > 1:
        terms = [a + b for a, b in zip(terms[::2], terms[1::2])] + terms[len(terms) // 2 * 2 :]
    return terms[0]


def pieces_of(width):
    return [slice(c * SUB, (c + 1) * SUB) for c in range(width // SUB)]


def wide(row):
    return jnp.broadcast_to(row, (SUB, row.shape[1]))


def pair_chunk(own, other):
    dx = own[0] - other[0]
    dy = own[1] - other[1]
    dz = own[2] - other[2]
    squared = dx * dx + dy * dy + dz * dz
    rest = jnp.maximum(1.0 - squared, 0.0)
    return rest * rest * pltpu.reciprocal((squared + 0.01) * (own[3] + other[3]), approx=True)


def spread_columns(out, index, rows):
    count, width = rows.shape
    turned = rows.T
    for a in range(count):
        out[index(a)] = jnp.broadcast_to(turned[:, a : a + 1], (width, width))


def lane_sums(parts, count, width):
    lanes = lax.broadcasted_iota(jnp.int32, (width, width), 1)
    turned = jnp.zeros((width, width), jnp.float32)
    for a in range(count):
        turned = jnp.where(lanes == a, jnp.sum(parts[a], axis=1, keepdims=True), turned)
    return turned.T[:count]


def sub_sums(cols):
    return jnp.sum(cols[...].reshape(-1, SUB, cols.shape[1]), axis=1)


def alive_rows(meta, share, width):
    return lax.broadcasted_iota(jnp.int32, (share, width), 0) < meta[0]


def prepare(counts, densities, position, phase, listed, meta, density, first_swap, second_swap, times, *times_out):
    share, width = first_swap.shape[1:]
    capacity = phase.shape[0]
    piece, column = lax.axis_index("piece"), lax.axis_index("col")
    filled = counts[piece]
    filled_before = counts[jnp.maximum(piece - 1, 0)]
    before = jnp.int32(0)
    total = jnp.int32(0)
    for p in range(counts.shape[0]):
        before = before + jnp.where(p < piece, counts[p], 0)
        total = total + counts[p]
    meta[0] = jnp.clip(filled - column * share, 0, share)
    meta[1] = before + column * share
    meta[2] = total
    meta[3] = column * share
    meta[4] = filled
    meta[5] = filled_before
    labels = phase[...]
    density[...] = sum(jnp.where(labels == k, densities[k], 0.0) for k in range(densities.shape[0]))
    last = pl.ds(filled - share, share)
    even = lax.rem(piece, 2) == 0
    for k in range(4):
        rows = position.at[k] if k < 3 else density
        tail, head = rows[last, :], rows[0:share, :]
        first_swap[k] = jnp.where(even, tail, head)
        second_swap[k] = jnp.where(even, head, tail)
    ids = listed[...]
    own = lax.broadcasted_iota(jnp.int32, ids.shape, 1)
    slot = ids - piece * capacity
    away = slot - own + jnp.where(slot < 0, capacity - filled_before, jnp.where(slot >= capacity, filled - capacity, 0))
    away = jnp.where(ids < 0, -REACH, away) + REACH
    steps = lax.broadcasted_iota(jnp.int32, (2 * REACH, capacity), 0)
    found = tree([jnp.where(steps == away[k : k + 1], 1.0, 0.0) for k in range(ids.shape[0])])
    found = jnp.concatenate([found, jnp.zeros((width - 2 * REACH, capacity), jnp.float32)], 0)
    times[...] = found.T
    for k, out in enumerate(times_out):
        out[...] = times[pl.ds(pl.multiple_of((column ^ k) * share, SUB), share), :]


def build_inner(meta, table, position, density, tiles, spread, rows_ref, cols_ref, self_ref, near):
    share, width = rows_ref.shape[0], rows_ref.shape[2]
    chunks = pieces_of(width)
    base = meta[3]
    own_rows = pl.ds(pl.multiple_of(base, SUB), share)
    for k in range(4):
        values = position[k, own_rows, :] if k < 3 else density[own_rows, :] * (width / 2.0)
        near[k, 0:share, :] = values
        spread_columns(spread, lambda a: (a, k), values)
    cols_ref[...] = jnp.zeros_like(cols_ref)

    def rows_at(n):
        return [wide(near[k, pl.ds(n, 1), :]) for k in range(4)]

    def block(a, at):
        count, place_of = inner_range(meta, table, a)

        def fetch(t):
            n = place_of(t)
            return n, rows_at(n)

        def pair(fetched, carry):
            n, other = fetched
            at, sums = carry
            result = []
            for here in chunks:
                tile = pair_chunk([spread[a, k, here, :] for k in range(4)], other)
                tiles[at, here, :] = tile
                result.append(tile)
            there = pl.ds(pl.multiple_of(n * SUB, SUB), SUB)
            cols_ref[there, :] = cols_ref[there, :] + tree(result)
            return at + 1, [old + new for old, new in zip(sums, result)]

        zero = jnp.zeros((SUB, width), jnp.float32)
        at, sums = sweep(count, fetch, pair, (at, [zero] * len(chunks)))
        for here, values in zip(chunks, sums):
            rows_ref[a, here, :] = values
        other = rows_at(a)
        lane = lax.broadcasted_iota(jnp.int32, (SUB, width), 1)
        sublane = lax.broadcasted_iota(jnp.int32, (SUB, width), 0)
        result = []
        for c, here in enumerate(chunks):
            tile = pair_chunk([spread[a, k, here, :] for k in range(4)], other)
            tile = jnp.where(lane == sublane + c * SUB, 0.0, tile)
            tiles[at, here, :] = tile
            result.append(tile)
        self_ref[pl.ds(pl.multiple_of(a * SUB, SUB), SUB), :] = tree(result)
        return at + 1

    lax.fori_loop(0, meta[0], block, 0)


def factor(times, a, n):
    lane = lax.broadcasted_iota(jnp.int32, (1, times.shape[1]), 1)
    return jnp.sum(jnp.where(lane == n - a + REACH, times[pl.ds(a, 1), :], 0.0), axis=1, keepdims=True)


def either(flag, run):
    @pl.when(flag == 0)
    def _():
        run(False)

    @pl.when(flag != 0)
    def _():
        run(True)


def build_outer(
    meta, table, position, density, first, second, right_side, tiles_in, spread, rows_ref, cols_ref, self_ref, *rest
):
    *times_in, again_ref, tiles, diagonal_ref, precond_ref, times, hood, work, sums_ref, extra = rest
    share, width = diagonal_ref.shape
    chunks = pieces_of(width)
    capacity = density.shape[0]
    base, filled = meta[3], meta[4]
    scale = width / 2.0
    even = lax.rem(lax.axis_index("piece"), 2) == 0
    for k in range(4):
        gain = 1.0 if k < 3 else scale
        before = jnp.where(even, second[k], first[k]) * gain
        after = jnp.where(even, first[k], second[k]) * gain
        hood[k, 0:share, :] = before
        hood[k, share : share + capacity, :] = position[k] if k < 3 else density[...] * gain
        hood[k, pl.ds(share + filled, share), :] = after
    alive = alive_rows(meta, share, width)
    often = jnp.where(alive, tree([ref[...] for ref in times_in]), 0.0)
    times[...] = often
    lane = lax.broadcasted_iota(jnp.int32, (share, width), 1)
    again = jnp.max(jnp.where((lane == REACH) | (lane == 0), 0.0, often)) > 1.5
    again_ref[0] = again.astype(jnp.int32)

    def block(a, at):
        count, place_of = outer_range(meta, table, a)

        def fetch(t):
            here = pl.ds(base + share + place_of(t), 1)
            return [wide(hood[k, here, :]) for k in range(4)]

        def pair(other, carry):
            at, sums = carry
            result = []
            for here, old in zip(chunks, sums):
                tile = pair_chunk([spread[a, k, here, :] for k in range(4)], other)
                tiles[at, here, :] = tile
                result.append(old + tile)
            return at + 1, result

        at, sums = sweep(count, fetch, pair, (at, [rows_ref[a, here, :] for here in chunks]))
        for here, values in zip(chunks, sums):
            work[a, here, :] = values
        return at

    lax.fori_loop(0, meta[0], block, 0)
    sums_ref[...] = lane_sums(work, share, width) + sub_sums(cols_ref)

    @pl.when(again)
    def _():
        extra[...] = jnp.zeros_like(extra)
        work[...] = jnp.zeros_like(work)

        def block(a, state):
            count, place_of = inner_range(meta, table, a)

            def inner(t, at):
                n = place_of(t)
                tile = tiles_in[at]
                work[a] = work[a] + tile * factor(times, a, n)
                there = pl.ds(n, 1)
                down = jnp.sum(tile, axis=0, keepdims=True)
                extra[there, :] = extra[there, :] + down * factor(times, n, a)
                return at + 1

            at = lax.fori_loop(0, count, inner, state[0]) + 1
            count, place_far = outer_range(meta, table, a)

            def outer(t, at):
                work[a] = work[a] + tiles[at] * factor(times, a, place_far(t))
                return at + 1

            return at, lax.fori_loop(0, count, outer, state[1])

        lax.fori_loop(0, meta[0], block, (0, 0))
        sums_ref[...] = lane_sums(work, share, width) + extra[...]

    alone = jnp.sum(jnp.where(lane == REACH, often, 0.0), axis=1, keepdims=True)
    pairs = jnp.where(alive, sums_ref[...] + sub_sums(self_ref) * alone, 0.0)
    diagonal = 1.0 / density[pl.ds(pl.multiple_of(base, SUB), share), :] + pairs
    diagonal_ref[...] = diagonal
    precond_ref[...] = jnp.where(alive, right_side[...], 0.0) / diagonal


def apply_inner(meta, table, again, field, times, tiles, rows_ref, cols_ref, spread, near):
    share, width = field.shape
    chunks = pieces_of(width)
    near[0:share, :] = field[...]
    spread_columns(spread, lambda a: a, field[...])
    cols_ref[...] = jnp.zeros_like(cols_ref)

    def run(weighted):
        def block(a, at):
            count, place_of = inner_range(meta, table, a)

            def fetch(t):
                n = place_of(t)
                return n, wide(near[pl.ds(n, 1), :])

            def pair(fetched, carry):
                n, value = fetched
                at, sums = carry
                if weighted:
                    value = value * factor(times, a, n)
                down, result = [], []
                for here, old in zip(chunks, sums):
                    tile = tiles[at, here, :]
                    down.append(tile * spread[a, here, :])
                    result.append(old + tile * value)
                there = pl.ds(pl.multiple_of(n * SUB, SUB), SUB)
                down = tree(down)
                if weighted:
                    down = down * factor(times, n, a)
                cols_ref[there, :] = cols_ref[there, :] + down
                return at + 1, result

            zero = jnp.zeros((SUB, width), jnp.float32)
            at, sums = sweep(count, fetch, pair, (at, [zero] * len(chunks)))
            value = wide(near[pl.ds(a, 1), :] * factor(times, a, a))
            for here, old in zip(chunks, sums):
                rows_ref[a, here, :] = old + tiles[at, here, :] * value
            return at + 1

        lax.fori_loop(0, meta[0], block, 0)

    either(again[0], run)


def apply_outer(meta, table, again, received, times, tiles, rows_ref, cols_ref, work, hood):
    first, second, *ends = received
    columns = len(received)
    share, width = first.shape
    chunks = pieces_of(width)
    base, filled = meta[3], meta[4]
    column = lax.div(base, share)
    odd = lax.rem(column, 2) == 1
    before = jnp.where(odd, first[...], second[...])
    after = jnp.where(odd, second[...], first[...])
    own = 3 * share
    for c, end in enumerate(ends, 1):
        hood[pl.ds(own - meta[5] + c * share, share), :] = end[...]
    from_last = own - meta[5] + (columns - 1) * share
    hood[pl.ds(jnp.where(column == 0, from_last, own - share), share), :] = before
    hood[own + share : own + 2 * share, :] = after
    head = after
    for c, end in enumerate(ends, 1):
        head = jnp.where(column == c, end[...], head)
    hood[pl.ds(own + jnp.clip(filled - base, 0, 2 * share), share), :] = head

    def run(weighted):
        def block(a, at):
            count, place_of = outer_range(meta, table, a)

            def fetch(t):
                place = place_of(t)
                value = hood[pl.ds(own + place, 1), :]
                if weighted:
                    value = value * factor(times, a, place)
                return wide(value)

            def pair(value, carry):
                at, sums = carry
                return at + 1, [old + tiles[at, here, :] * value for here, old in zip(chunks, sums)]

            at, sums = sweep(count, fetch, pair, (at, [rows_ref[a, here, :] for here in chunks]))
            for here, values in zip(chunks, sums):
                work[a, here, :] = values
            return at

        lax.fori_loop(0, meta[0], block, 0)

    either(again[0], run)
    return jnp.where(alive_rows(meta, share, width), lane_sums(work, share, width) + sub_sums(cols_ref), 0.0)


def apply_first(meta, table, again, diagonal, times, *rest):
    *received, tiles, rows_ref, cols_ref, spill_ref, scaled_ref, work, hood = rest
    spill = apply_outer(meta, table, again, received, times, tiles, rows_ref, cols_ref, work, hood)
    spill_ref[...] = spill
    scaled_ref[...] = spill / diagonal[...]


def apply_second(meta, table, again, right_side, precond, spill, scaled, times, *rest):
    *received, tiles, rows_ref, cols_ref, twice_ref, sums_ref, work, hood = rest
    twice = apply_outer(meta, table, again, received, times, tiles, rows_ref, cols_ref, work, hood)
    twice_ref[...] = twice
    share, width = twice.shape
    source = jnp.where(alive_rows(meta, share, width), right_side[...], 0.0)
    lane = lax.broadcasted_iota(jnp.int32, (1, width), 1)
    sums = jnp.zeros((1, width), jnp.float32)
    pairs = ((source, precond[...]), (spill[...], precond[...]), (spill[...], scaled[...]), (scaled[...], twice))
    for k, (first, second) in enumerate(pairs):
        along = jnp.sum(first * second, axis=0, keepdims=True)
        sums = jnp.where(lane == k, jnp.sum(along, axis=1, keepdims=True), sums)
    sums_ref[...] = wide(sums)


def finish(meta, right_side, precond, spill, scaled, twice, mine, other, solution_ref, residual_ref):
    share, width = precond.shape
    sums = mine[...] + other[...]

    def pick(k):
        return sums[0:1, k : k + 1]

    weighted, cross, square, last = pick(0), pick(1), pick(2), pick(3)
    part = cross / weighted
    advance = 1.0 / (1.0 - part)
    keep = -part * advance
    weighted_next = advance * advance * (square - cross * part)
    bent = keep * keep * cross + 2.0 * keep * advance * square + advance * advance * last
    blend = weighted_next / weighted
    advance_next = weighted_next / (weighted_next - bent - blend * weighted_next / advance)
    source = jnp.where(alive_rows(meta, share, width), right_side[...], 0.0)
    residual = keep * source + advance * spill[...]
    next_precond = keep * precond[...] + advance * scaled[...]
    direction = next_precond + blend * precond[...]
    image = residual - keep * spill[...] - advance * twice[...] + blend * (source - spill[...])
    solution_ref[...] = advance * precond[...] + advance_next * direction
    residual_ref[...] = residual - advance_next * image


def held(array):
    return pltpu.with_memory_space_constraint(array, pltpu.VMEM)


def body(positions, phase, neighbours, counts, phase_density, right_side):
    capacity, width = phase.shape
    columns = lax.axis_size("col")
    pieces = lax.axis_size("piece")
    share = capacity // columns
    f32 = jnp.float32
    vector = jax.ShapeDtypeStruct((share, width), f32)
    few = jax.ShapeDtypeStruct((SUB, width), f32)
    message = jax.ShapeDtypeStruct((4, share, width), f32)
    most_inner, most_outer = tile_bounds(share)
    inner_tiles = pltpu.VMEM((most_inner, width, width), f32)
    outer_tiles = pltpu.VMEM((most_outer, width, width), f32)
    square = pltpu.VMEM((share, width, width), f32)
    narrow = pltpu.VMEM((share * SUB, width), f32)
    table = jnp.asarray(TABLE.reshape(-1))

    def call(kernel, args, outs, scratch=(), work=0, scalars=2, **more):
        return pl.pallas_call(
            kernel,
            out_shape=outs,
            in_specs=[SMEM] * scalars + [VMEM] * (len(args) - scalars),
            out_specs=[SMEM if getattr(o, "memory_space", None) == pltpu.SMEM else VMEM for o in outs],
            scratch_shapes=scratch,
            compiler_params=LIMIT,
            cost_estimate=pl.CostEstimate(flops=work * width * width, bytes_accessed=0, transcendentals=0),
            name=kernel.__name__,
            **more,
        )(*args)

    meta, density, first, second, _, *times = call(
        prepare,
        (counts, phase_density, positions, phase, neighbours.T),
        [pltpu.SMEM((8,), jnp.int32), jax.ShapeDtypeStruct(phase.shape, f32), message, message,
         jax.ShapeDtypeStruct((capacity, width), f32)] + [vector] * columns,
    )
    meta = pltpu.with_memory_space_constraint(meta, pltpu.SMEM)
    first = lax.ppermute(first, "piece", [(i, i ^ 1) for i in range(pieces)])
    second = lax.ppermute(second, "piece", [(i, ((i ^ 1) + (1 if i % 2 else -1) * 2) % pieces) for i in range(pieces)])
    times = [lax.ppermute(t, "col", [(i, i ^ k) for i in range(columns)]) if k else t for k, t in enumerate(times)]

    tiles_in, spread, rows, cols, selfs = call(
        build_inner,
        (meta, table, positions, density),
        [inner_tiles, pltpu.VMEM((share, 4, width, width), f32), square, narrow, narrow],
        [pltpu.VMEM((4, 2 * share, width), f32)],
        16 * most_inner,
    )
    again, tiles_out, diagonal, precond, times = call(
        build_outer,
        (meta, table, positions, density, first, second, right_side,
         held(tiles_in), held(spread), held(rows), held(cols), held(selfs), *times),
        [pltpu.SMEM((1,), jnp.int32), outer_tiles, vector, vector, vector],
        [pltpu.VMEM((4, capacity + 2 * share, width), f32), pltpu.VMEM((share, width, width), f32)]
        + [pltpu.VMEM((share, width), f32)] * 2,
        16 * most_outer,
    )
    again = pltpu.with_memory_space_constraint(again, pltpu.SMEM)

    def inner(field):
        return call(
            apply_inner,
            (meta, table, again, field, times, held(tiles_in)),
            [square, narrow],
            [pltpu.VMEM((share, width, width), f32), pltpu.VMEM((2 * share, width), f32)],
            4 * most_inner,
            scalars=3,
        )

    def exchange(field):
        axes = ("piece", "col")
        count = pieces * columns
        swaps = [[i ^ 1 for i in range(count)], [i - 1 if i % 2 == 0 else i + 1 for i in range(count)]]
        swaps[1][0], swaps[1][-1] = count - 1, 0
        for c in range(1, columns - 1):
            to = {}
            for p in range(pieces - 1):
                low, high = p * columns + c, (p + 1) * columns
                to[low], to[high] = high, low
            for p in range(pieces):
                rest = [i for i in range(p * columns, (p + 1) * columns) if i not in to]
                to.update(zip(rest, rest[1:] + rest[:1]))
            swaps.append([to[i] for i in range(count)])
        return [lax.ppermute(field, axes, list(enumerate(to))) for to in swaps]

    scratch = [pltpu.VMEM((share, width, width), f32), pltpu.VMEM((8 * share, width), f32)]

    received = exchange(precond)
    rows, cols = inner(precond)
    spill, scaled = call(
        apply_first,
        (meta, table, again, diagonal, times, *received, held(tiles_out), held(rows), held(cols)),
        [vector, vector],
        scratch,
        2 * most_outer,
        scalars=3,
    )

    received = exchange(scaled)
    rows, cols = inner(scaled)
    twice, sums = call(
        apply_second,
        (meta, table, again, right_side, precond, spill, scaled, times, *received, held(tiles_out), held(rows), held(cols)),
        [vector, few],
        scratch,
        2 * most_outer,
        scalars=3,
    )

    def swap(values, axis, step):
        return lax.ppermute(values, axis, [(i, i ^ step) for i in range(lax.axis_size(axis))])

    sums = tree([sums] + [swap(sums, "col", k) for k in range(1, columns)])
    steps = [1 << k for k in range(pieces.bit_length() - 1)]
    for step in steps[:-1]:
        sums = sums + swap(sums, "piece", step)
    other = swap(sums, "piece", steps[-1])

    return tuple(call(
        finish,
        (meta, right_side, precond, spill, scaled, twice, sums, other),
        [vector, vector],
        scalars=1,
    ))


def solution(mesh):
    placed = (
        P(None, "piece", None),
        P("piece", None),
        P("piece", "col"),
        P(),
        P(),
        P(("piece", "col"), None),
    )
    return jax.shard_map(
        body,
        mesh=mesh,
        in_specs=placed,
        out_specs=(P(("piece", "col"), None), P(("piece", "col"), None)),
        check_vma=False,
    )
```

```python
import jax
import jax.numpy as jnp
import numpy as np
from jax import lax
from jax.experimental import pallas as pl
from jax.experimental.pallas import tpu as pltpu
from jax.sharding import PartitionSpec as P

ITERS = 2
SIDE = 4
LAYER = SIDE * SIDE
REACH = 2 * LAYER
SUB = 8
VMEM = pl.BlockSpec(memory_space=pltpu.VMEM)
SMEM = pl.BlockSpec(memory_space=pltpu.SMEM)
HBM = pl.BlockSpec(memory_space=pltpu.HBM)


def stencil_tables():
    levels = SIDE.bit_length() - 1

    def cell(code):
        across = sum((code >> (2 * level) & 1) << level for level in range(levels))
        along = sum((code >> (2 * level + 1) & 1) << level for level in range(levels))
        return across, along

    place = {cell(code): code for code in range(LAYER)}
    rows = []
    for code in range(LAYER):
        across, along = cell(code)
        rows.append(
            sorted(
                step_z * LAYER + place[across + step_x, along + step_y] - code
                for step_z in (-1, 0, 1)
                for step_y in (-1, 0, 1)
                for step_x in (-1, 0, 1)
                if (across + step_x, along + step_y) in place
            )
        )
    longest = max(len(row) for row in rows)
    offsets = np.zeros((LAYER, longest), np.int32)
    below = np.zeros((LAYER, 2 * REACH + 1), np.int32)
    for code, row in enumerate(rows):
        offsets[code, : len(row)] = row
        for t in range(-REACH, REACH + 1):
            below[code, t + REACH] = sum(offset < t for offset in row)
    return offsets, below


OFFSETS, BELOW = stencil_tables()
WIDEST = OFFSETS.shape[1]
TABLE = np.concatenate([OFFSETS, BELOW], 1)
STRIDE = TABLE.shape[1]
LIMIT = pltpu.CompilerParams(vmem_limit_bytes=6 * 1024 * 1024)


def tile_bounds(share):
    inner = outer = 0
    for first in range(LAYER):
        for live in range(1, share + 1):
            near = far = 0
            for a in range(live):
                code = (first + a) % LAYER
                row = [int(o) for o in OFFSETS[code][: BELOW[code, -1]]]
                near += sum(0 <= a + o and o <= 0 for o in row)
                far += sum(a + o < 0 or a + o >= live for o in row)
            inner, outer = max(inner, near), max(outer, far)
    return inner, outer


def rank(table, code, t):
    return table[code * STRIDE + jnp.clip(t, -REACH, REACH) + REACH + WIDEST]


def inner_range(meta, table, a):
    code = lax.rem(meta[1] + a, LAYER)
    low, high = rank(table, code, -a), rank(table, code, 0)
    start = code * STRIDE + low
    return high - low, lambda t: a + table[start + t]


def outer_range(meta, table, a):
    code = lax.rem(meta[1] + a, LAYER)
    place = meta[1] + a
    low, split = rank(table, code, -place), rank(table, code, -a)
    resume, high = rank(table, code, meta[0] - a), rank(table, code, meta[2] - place)
    ahead = split - low
    start = code * STRIDE + low
    start_after = code * STRIDE + resume - ahead
    count = ahead + jnp.maximum(high - resume, 0)
    return count, lambda t: a + table[t + jnp.where(t < ahead, start, start_after)]


def sweep(count, fetch, step, carry):
    def both(i, state):
        carry, *now = state
        later = fetch(2 * i + 2), fetch(2 * i + 3)
        return step(now, carry), *later

    carry, first, _ = lax.fori_loop(0, lax.div(count, 2), both, (carry, fetch(0), fetch(1)))
    return lax.fori_loop(0, lax.rem(count, 2), lambda _, carry: step([first], carry), carry)


def tree(terms):
    while len(terms) > 1:
        terms = [a + b for a, b in zip(terms[::2], terms[1::2])] + terms[len(terms) // 2 * 2 :]
    return terms[0]


def gather(partial, c, term):
    if c < len(partial):
        partial[c] = term
    else:
        partial[c % len(partial)] = partial[c % len(partial)] + term


def pieces_of(width):
    return [slice(c * SUB, (c + 1) * SUB) for c in range(width // SUB)]


def wide(row):
    return jnp.broadcast_to(row, (SUB, row.shape[1]))


def pair_chunk(own, other):
    dx = own[0] - other[0]
    dy = own[1] - other[1]
    dz = own[2] - other[2]
    squared = dx * dx + dy * dy + dz * dz
    rest = jnp.maximum(1.0 - squared, 0.0)
    return rest * rest * pltpu.reciprocal((squared + 0.01) * (own[3] + other[3]), approx=True)


def spread_columns(out, index, rows):
    count, width = rows.shape
    turned = rows.T
    for a in range(count):
        out[index(a)] = jnp.broadcast_to(turned[:, a : a + 1], (width, width))


def lane_sums(parts, count, width):
    lanes = lax.broadcasted_iota(jnp.int32, (width, width), 1)
    turned = jnp.zeros((width, width), jnp.float32)
    for a in range(count):
        turned = jnp.where(lanes == a, jnp.sum(parts[a], axis=1, keepdims=True), turned)
    return turned.T[:count]


def sub_sums(cols):
    return jnp.sum(cols[...].reshape(-1, SUB, cols.shape[1]), axis=1)


def alive_rows(meta, share, width):
    return lax.broadcasted_iota(jnp.int32, (share, width), 0) < meta[0]


def prepare(
    counts, densities, position_in, phase_in, listed_in, right_side_in, table_in,
    meta, table, hood, near, density, source, first_swap, second_swap, *rest
):
    *times_out, phase, listed, right_side, times, sems = rest
    share, width = source.shape
    capacity = phase.shape[0]
    body_rows = pl.ds(share, capacity)
    copies = [
        pltpu.make_async_copy(phase_in, phase, sems.at[0]),
        pltpu.make_async_copy(position_in, hood.at[pl.ds(0, 3), body_rows, :], sems.at[1]),
        pltpu.make_async_copy(listed_in, listed, sems.at[2]),
        pltpu.make_async_copy(right_side_in, right_side, sems.at[3]),
        pltpu.make_async_copy(table_in, table, sems.at[4]),
    ]
    for copy in copies:
        copy.start()
    piece, column = lax.axis_index("piece"), lax.axis_index("col")
    filled = counts[piece]
    filled_before = counts[jnp.maximum(piece - 1, 0)]
    before = jnp.int32(0)
    total = jnp.int32(0)
    for p in range(counts.shape[0]):
        before = before + jnp.where(p < piece, counts[p], 0)
        total = total + counts[p]
    meta[0] = jnp.clip(filled - column * share, 0, share)
    meta[1] = before + column * share
    meta[2] = total
    meta[3] = column * share
    meta[4] = filled
    meta[5] = filled_before
    own_rows = pl.ds(pl.multiple_of(share + column * share, SUB), share)
    copies[0].wait()
    labels = phase[...]
    whole = sum(jnp.where(labels == k, densities[k], 0.0) for k in range(densities.shape[0]))
    hood[3, body_rows, :] = whole * (width / 2.0)
    density[...] = hood[3, own_rows, :] * (2.0 / width)
    copies[1].wait()
    even = lax.rem(piece, 2) == 0
    for k in range(4):
        tail, head = hood[k, pl.ds(filled, share), :], hood[k, share : 2 * share, :]
        first_swap[k] = jnp.where(even, tail, head)
        second_swap[k] = jnp.where(even, head, tail)
        near[k, 0:share, :] = hood[k, own_rows, :]
    for copy in copies[2:]:
        copy.wait()
    source[...] = jnp.where(alive_rows(meta, share, width), right_side[...], 0.0)
    ids = listed[...]
    own = lax.broadcasted_iota(jnp.int32, ids.shape, 1)
    slot = ids - piece * capacity
    away = slot - own + jnp.where(slot < 0, capacity - filled_before, jnp.where(slot >= capacity, filled - capacity, 0))
    away = jnp.where(ids < 0, -REACH, away) + REACH
    steps = lax.broadcasted_iota(jnp.int32, (2 * REACH, capacity), 0)
    found = tree([jnp.where(steps == away[k : k + 1], 1.0, 0.0) for k in range(ids.shape[0])])
    found = jnp.concatenate([found, jnp.zeros((width - 2 * REACH, capacity), jnp.float32)], 0)
    times[...] = found.T
    for k, out in enumerate(times_out):
        out[...] = times[pl.ds(pl.multiple_of((column ^ k) * share, SUB), share), :]


def build_inner(meta, table, near, tiles, spread, rows_ref, cols_ref, self_ref):
    share, width = rows_ref.shape[0], rows_ref.shape[2]
    chunks = pieces_of(width)
    for k in range(4):
        spread_columns(spread, lambda a: (a, k), near[k, 0:share, :])
    cols_ref[...] = jnp.zeros_like(cols_ref)

    def rows_at(n):
        return [wide(near[k, pl.ds(n, 1), :]) for k in range(4)]

    def block(a, at):
        count, place_of = inner_range(meta, table, a)

        def fetch(t):
            n = place_of(t)
            return n, rows_at(n)

        def pairs(fetched, carry):
            at, sums = carry
            down = [[None] * 4 for _ in fetched]
            result = []
            for c, (here, total) in enumerate(zip(chunks, sums)):
                own = [spread[a, k, here, :] for k in range(4)]
                for t, (_, other) in enumerate(fetched):
                    tile = pair_chunk(own, other)
                    tiles[at + t, here, :] = tile
                    gather(down[t], c, tile)
                    total = total + tile
                result.append(total)
            for (n, _), partial in zip(fetched, down):
                there = pl.ds(pl.multiple_of(n * SUB, SUB), SUB)
                cols_ref[there, :] = cols_ref[there, :] + tree(partial)
            return at + len(fetched), result

        zero = jnp.zeros((SUB, width), jnp.float32)
        at, sums = sweep(count, fetch, pairs, (at, [zero] * len(chunks)))
        for here, values in zip(chunks, sums):
            rows_ref[a, here, :] = values
        other = rows_at(a)
        lane = lax.broadcasted_iota(jnp.int32, (SUB, width), 1)
        sublane = lax.broadcasted_iota(jnp.int32, (SUB, width), 0)
        down = [None] * 4
        for c, here in enumerate(chunks):
            tile = pair_chunk([spread[a, k, here, :] for k in range(4)], other)
            tile = jnp.where(lane == sublane + c * SUB, 0.0, tile)
            tiles[at, here, :] = tile
            gather(down, c, tile)
        self_ref[pl.ds(pl.multiple_of(a * SUB, SUB), SUB), :] = tree(down)
        return at + 1

    lax.fori_loop(0, meta[0], block, 0)


def factor(times, a, n):
    lane = lax.broadcasted_iota(jnp.int32, (1, times.shape[1]), 1)
    return jnp.sum(jnp.where(lane == n - a + REACH, times[pl.ds(a, 1), :], 0.0), axis=1, keepdims=True)


def either(flag, run):
    @pl.when(flag == 0)
    def _():
        run(False)

    @pl.when(flag != 0)
    def _():
        run(True)


def build_outer(
    meta, table, around, first, second, density, source, tiles_in, spread, rows_ref, cols_ref, self_ref, *rest
):
    *times_in, again_ref, tiles, diagonal_ref, precond_ref, times, alone_ref, hood, work, sums_ref, extra = rest
    share, width = diagonal_ref.shape
    chunks = pieces_of(width)
    base, filled = meta[3], meta[4]
    even = lax.rem(lax.axis_index("piece"), 2) == 0
    for k in range(4):
        hood[k, 0:share, :] = jnp.where(even, second[k], first[k])
        hood[k, share:, :] = around[k, share:, :]
        hood[k, pl.ds(share + filled, share), :] = jnp.where(even, first[k], second[k])
    alive = alive_rows(meta, share, width)
    often = jnp.where(alive, tree([ref[...] for ref in times_in]), 0.0)
    times[...] = often
    lane = lax.broadcasted_iota(jnp.int32, (share, width), 1)
    again = jnp.max(jnp.where((lane == REACH) | (lane == 0), 0.0, often)) > 1.5
    again_ref[0] = again.astype(jnp.int32)

    def block(a, at):
        count, place_of = outer_range(meta, table, a)

        def fetch(t):
            here = pl.ds(base + share + place_of(t), 1)
            return [wide(hood[k, here, :]) for k in range(4)]

        def pairs(fetched, carry):
            at, sums = carry
            result = []
            for here, total in zip(chunks, sums):
                own = [spread[a, k, here, :] for k in range(4)]
                for t, other in enumerate(fetched):
                    tile = pair_chunk(own, other)
                    tiles[at + t, here, :] = tile
                    total = total + tile
                result.append(total)
            return at + len(fetched), result

        at, sums = sweep(count, fetch, pairs, (at, [rows_ref[a, here, :] for here in chunks]))
        for here, values in zip(chunks, sums):
            work[a, here, :] = values
        return at

    lax.fori_loop(0, meta[0], block, 0)
    sums_ref[...] = lane_sums(work, share, width) + sub_sums(cols_ref)

    @pl.when(again)
    def _():
        extra[...] = jnp.zeros_like(extra)
        work[...] = jnp.zeros_like(work)

        def block(a, state):
            count, place_of = inner_range(meta, table, a)

            def inner(t, at):
                n = place_of(t)
                tile = tiles_in[at]
                work[a] = work[a] + tile * factor(times, a, n)
                there = pl.ds(n, 1)
                down = jnp.sum(tile, axis=0, keepdims=True)
                extra[there, :] = extra[there, :] + down * factor(times, n, a)
                return at + 1

            at = lax.fori_loop(0, count, inner, state[0]) + 1
            count, place_far = outer_range(meta, table, a)

            def outer(t, at):
                work[a] = work[a] + tiles[at] * factor(times, a, place_far(t))
                return at + 1

            return at, lax.fori_loop(0, count, outer, state[1])

        lax.fori_loop(0, meta[0], block, (0, 0))
        sums_ref[...] = lane_sums(work, share, width) + extra[...]

    alone = jnp.sum(jnp.where(lane == REACH, often, 0.0), axis=1, keepdims=True)
    alone_ref[...] = jnp.broadcast_to(alone, (share, width))
    pairs = jnp.where(alive, sums_ref[...] + sub_sums(self_ref) * alone, 0.0)
    diagonal = 1.0 / density[...] + pairs
    diagonal_ref[...] = diagonal
    precond_ref[...] = source[...] / diagonal


def apply_inner(meta, table, again, field, alone, times, tiles, rows_ref, cols_ref, spread, near, lone):
    share, width = field.shape
    chunks = pieces_of(width)
    near[0:share, :] = field[...]
    lone[...] = field[...] * alone[...]
    spread_columns(spread, lambda a: a, field[...])
    cols_ref[...] = jnp.zeros_like(cols_ref)

    def run(weighted):
        def block(a, at):
            count, place_of = inner_range(meta, table, a)

            def fetch(t):
                n = place_of(t)
                return n, wide(near[pl.ds(n, 1), :])

            def pairs(fetched, carry):
                at, sums = carry
                if weighted:
                    fetched = [(n, value * factor(times, a, n)) for n, value in fetched]
                down = [[None] * 4 for _ in fetched]
                result = []
                for c, (here, total) in enumerate(zip(chunks, sums)):
                    own = spread[a, here, :]
                    for t, (_, value) in enumerate(fetched):
                        tile = tiles[at + t, here, :]
                        gather(down[t], c, tile * own)
                        total = total + tile * value
                    result.append(total)
                for (n, _), partial in zip(fetched, down):
                    there = pl.ds(pl.multiple_of(n * SUB, SUB), SUB)
                    partial = tree(partial)
                    if weighted:
                        partial = partial * factor(times, n, a)
                    cols_ref[there, :] = cols_ref[there, :] + partial
                return at + len(fetched), result

            zero = jnp.zeros((SUB, width), jnp.float32)
            at, sums = sweep(count, fetch, pairs, (at, [zero] * len(chunks)))
            value = wide(lone[pl.ds(a, 1), :])
            for here, old in zip(chunks, sums):
                rows_ref[a, here, :] = old + tiles[at, here, :] * value
            return at + 1

        lax.fori_loop(0, meta[0], block, 0)

    either(again[0], run)


def apply_outer(meta, table, again, received, times, tiles, rows_ref, cols_ref, work, hood):
    first, second, *ends = received
    columns = len(received)
    share, width = first.shape
    chunks = pieces_of(width)
    base, filled = meta[3], meta[4]
    column = lax.div(base, share)
    odd = lax.rem(column, 2) == 1
    before = jnp.where(odd, first[...], second[...])
    after = jnp.where(odd, second[...], first[...])
    own = 3 * share
    for c, end in enumerate(ends, 1):
        hood[pl.ds(own - meta[5] + c * share, share), :] = end[...]
    from_last = own - meta[5] + (columns - 1) * share
    hood[pl.ds(jnp.where(column == 0, from_last, own - share), share), :] = before
    hood[own + share : own + 2 * share, :] = after
    head = after
    for c, end in enumerate(ends, 1):
        head = jnp.where(column == c, end[...], head)
    hood[pl.ds(own + jnp.clip(filled - base, 0, 2 * share), share), :] = head

    def run(weighted):
        def block(a, at):
            count, place_of = outer_range(meta, table, a)

            def fetch(t):
                place = place_of(t)
                value = hood[pl.ds(own + place, 1), :]
                if weighted:
                    value = value * factor(times, a, place)
                return wide(value)

            def pairs(values, carry):
                at, sums = carry
                result = []
                for here, total in zip(chunks, sums):
                    for t, value in enumerate(values):
                        total = total + tiles[at + t, here, :] * value
                    result.append(total)
                return at + len(values), result

            at, sums = sweep(count, fetch, pairs, (at, [rows_ref[a, here, :] for here in chunks]))
            for here, values in zip(chunks, sums):
                work[a, here, :] = values
            return at

        lax.fori_loop(0, meta[0], block, 0)

    either(again[0], run)
    return jnp.where(alive_rows(meta, share, width), lane_sums(work, share, width) + sub_sums(cols_ref), 0.0)


def apply_first(meta, table, again, diagonal, times, *rest):
    *received, tiles, rows_ref, cols_ref, spill_ref, scaled_ref, work, hood = rest
    spill = apply_outer(meta, table, again, received, times, tiles, rows_ref, cols_ref, work, hood)
    spill_ref[...] = spill
    scaled_ref[...] = spill / diagonal[...]


def apply_second(meta, table, again, source, precond, spill, scaled, times, *rest):
    *received, tiles, rows_ref, cols_ref, twice_ref, sums_ref, work, hood = rest
    twice = apply_outer(meta, table, again, received, times, tiles, rows_ref, cols_ref, work, hood)
    twice_ref[...] = twice
    share, width = twice.shape
    lane = lax.broadcasted_iota(jnp.int32, (1, width), 1)
    sums = jnp.zeros((1, width), jnp.float32)
    pairs = ((source[...], precond[...]), (spill[...], precond[...]), (spill[...], scaled[...]), (scaled[...], twice))
    for k, (first, second) in enumerate(pairs):
        along = jnp.sum(first * second, axis=0, keepdims=True)
        sums = jnp.where(lane == k, jnp.sum(along, axis=1, keepdims=True), sums)
    sums_ref[...] = wide(sums)


def finish(source, precond, spill, scaled, twice, mine, other, solution_ref, residual_ref):
    sums = mine[...] + other[...]

    def pick(k):
        return sums[0:1, k : k + 1]

    weighted, cross, square, last = pick(0), pick(1), pick(2), pick(3)
    part = cross / weighted
    advance = 1.0 / (1.0 - part)
    keep = -part * advance
    weighted_next = advance * advance * (square - cross * part)
    bent = keep * keep * cross + 2.0 * keep * advance * square + advance * advance * last
    blend = weighted_next / weighted
    advance_next = weighted_next / (weighted_next - bent - blend * weighted_next / advance)
    residual = keep * source[...] + advance * spill[...]
    next_precond = keep * precond[...] + advance * scaled[...]
    direction = next_precond + blend * precond[...]
    image = residual - keep * spill[...] - advance * twice[...] + blend * (source[...] - spill[...])
    solution_ref[...] = advance * precond[...] + advance_next * direction
    residual_ref[...] = residual - advance_next * image


def held(array):
    return pltpu.with_memory_space_constraint(array, pltpu.VMEM)


def body(positions, phase, neighbours, counts, phase_density, right_side):
    capacity, width = phase.shape
    columns = lax.axis_size("col")
    pieces = lax.axis_size("piece")
    share = capacity // columns
    f32 = jnp.float32
    vector = jax.ShapeDtypeStruct((share, width), f32)
    few = jax.ShapeDtypeStruct((SUB, width), f32)
    message = jax.ShapeDtypeStruct((4, share, width), f32)
    most_inner, most_outer = tile_bounds(share)
    inner_tiles = pltpu.VMEM((most_inner, width, width), f32)
    outer_tiles = pltpu.VMEM((most_outer, width, width), f32)
    square = pltpu.VMEM((share, width, width), f32)
    narrow = pltpu.VMEM((share * SUB, width), f32)
    table = jnp.asarray(TABLE.reshape(-1))

    def call(kernel, args, outs, scratch=(), work=0, scalars=2, far=0, **more):
        return pl.pallas_call(
            kernel,
            out_shape=outs,
            in_specs=[SMEM] * scalars + [HBM] * far + [VMEM] * (len(args) - scalars - far),
            out_specs=[SMEM if getattr(o, "memory_space", None) == pltpu.SMEM else VMEM for o in outs],
            scratch_shapes=scratch,
            compiler_params=LIMIT,
            cost_estimate=pl.CostEstimate(flops=work * width * width, bytes_accessed=0, transcendentals=0),
            name=kernel.__name__,
            **more,
        )(*args)

    def away(array):
        return pltpu.with_memory_space_constraint(array, pltpu.HBM)

    around = jax.ShapeDtypeStruct((4, capacity + 2 * share, width), f32)
    near = jax.ShapeDtypeStruct((4, 2 * share, width), f32)
    far = [away(array) for array in (positions, phase, neighbours.T, right_side, table)]
    meta, table, around, near, density, source, first, second, *times = call(
        prepare,
        (away(counts), away(phase_density), *far),
        [pltpu.SMEM((8,), jnp.int32), pltpu.SMEM(table.shape, jnp.int32), around, near, vector, vector, message, message]
        + [vector] * columns,
        [pltpu.VMEM(phase.shape, jnp.int32), pltpu.VMEM(far[2].shape, jnp.int32), pltpu.VMEM((share, width), f32),
         pltpu.VMEM((capacity, width), f32), pltpu.SemaphoreType.DMA((5,))],
        far=len(far),
    )
    meta, table = (pltpu.with_memory_space_constraint(array, pltpu.SMEM) for array in (meta, table))
    first = lax.ppermute(first, "piece", [(i, i ^ 1) for i in range(pieces)])
    second = lax.ppermute(second, "piece", [(i, ((i ^ 1) + (1 if i % 2 else -1) * 2) % pieces) for i in range(pieces)])
    times = [lax.ppermute(t, "col", [(i, i ^ k) for i in range(columns)]) if k else t for k, t in enumerate(times)]

    tiles_in, spread, rows, cols, selfs = call(
        build_inner,
        (meta, table, near),
        [inner_tiles, pltpu.VMEM((share, 4, width, width), f32), square, narrow, narrow],
        work=16 * most_inner,
    )
    again, tiles_out, diagonal, precond, times, alone = call(
        build_outer,
        (meta, table, around, first, second, density, source,
         held(tiles_in), held(spread), held(rows), held(cols), held(selfs), *times),
        [pltpu.SMEM((1,), jnp.int32), outer_tiles, vector, vector, vector, vector],
        [pltpu.VMEM((4, capacity + 2 * share, width), f32), pltpu.VMEM((share, width, width), f32)]
        + [pltpu.VMEM((share, width), f32)] * 2,
        16 * most_outer,
    )
    again = pltpu.with_memory_space_constraint(again, pltpu.SMEM)

    def inner(field):
        return call(
            apply_inner,
            (meta, table, again, field, alone, times, held(tiles_in)),
            [square, narrow],
            [pltpu.VMEM((share, width, width), f32), pltpu.VMEM((2 * share, width), f32), pltpu.VMEM((share, width), f32)],
            4 * most_inner,
            scalars=3,
        )

    def exchange(field):
        axes = ("piece", "col")
        count = pieces * columns
        swaps = [[i ^ 1 for i in range(count)], [i - 1 if i % 2 == 0 else i + 1 for i in range(count)]]
        swaps[1][0], swaps[1][-1] = count - 1, 0
        for c in range(1, columns - 1):
            to = {}
            for p in range(pieces - 1):
                low, high = p * columns + c, (p + 1) * columns
                to[low], to[high] = high, low
            for p in range(pieces):
                rest = [i for i in range(p * columns, (p + 1) * columns) if i not in to]
                to.update(zip(rest, rest[1:] + rest[:1]))
            swaps.append([to[i] for i in range(count)])
        return [lax.ppermute(field, axes, list(enumerate(to))) for to in swaps]

    scratch = [pltpu.VMEM((share, width, width), f32), pltpu.VMEM((8 * share, width), f32)]

    received = exchange(precond)
    rows, cols = inner(precond)
    spill, scaled = call(
        apply_first,
        (meta, table, again, diagonal, times, *received, held(tiles_out), held(rows), held(cols)),
        [vector, vector],
        scratch,
        2 * most_outer,
        scalars=3,
    )

    received = exchange(scaled)
    rows, cols = inner(scaled)
    twice, sums = call(
        apply_second,
        (meta, table, again, source, precond, spill, scaled, times, *received, held(tiles_out), held(rows), held(cols)),
        [vector, few],
        scratch,
        2 * most_outer,
        scalars=3,
    )

    def swap(values, axis, step):
        return lax.ppermute(values, axis, [(i, i ^ step) for i in range(lax.axis_size(axis))])

    sums = tree([sums] + [swap(sums, "col", k) for k in range(1, columns)])
    steps = [1 << k for k in range(pieces.bit_length() - 1)]
    for step in steps[:-1]:
        sums = sums + swap(sums, "piece", step)
    other = swap(sums, "piece", steps[-1])

    return tuple(call(
        finish,
        (source, precond, spill, scaled, twice, sums, other),
        [vector, vector],
        scalars=0,
    ))


def solution(mesh):
    placed = (
        P(None, "piece", None),
        P("piece", None),
        P("piece", "col"),
        P(),
        P(),
        P(("piece", "col"), None),
    )
    return jax.shard_map(
        body,
        mesh=mesh,
        in_specs=placed,
        out_specs=(P(("piece", "col"), None), P(("piece", "col"), None)),
        check_vma=False,
    )
```

```python
import jax
import jax.numpy as jnp
import numpy as np
from jax import lax
from jax.experimental import pallas as pl
from jax.experimental.pallas import tpu as pltpu
from jax.sharding import PartitionSpec as P

ITERS = 2
SIDE = 4
LAYER = SIDE * SIDE
REACH = 2 * LAYER
SUB = 8
VMEM = pl.BlockSpec(memory_space=pltpu.VMEM)
SMEM = pl.BlockSpec(memory_space=pltpu.SMEM)
HBM = pl.BlockSpec(memory_space=pltpu.HBM)


def stencil_tables():
    levels = SIDE.bit_length() - 1

    def cell(code):
        across = sum((code >> (2 * level) & 1) << level for level in range(levels))
        along = sum((code >> (2 * level + 1) & 1) << level for level in range(levels))
        return across, along

    place = {cell(code): code for code in range(LAYER)}
    rows = []
    for code in range(LAYER):
        across, along = cell(code)
        rows.append(
            sorted(
                step_z * LAYER + place[across + step_x, along + step_y] - code
                for step_z in (-1, 0, 1)
                for step_y in (-1, 0, 1)
                for step_x in (-1, 0, 1)
                if (across + step_x, along + step_y) in place
            )
        )
    longest = max(len(row) for row in rows)
    offsets = np.zeros((LAYER, longest), np.int32)
    below = np.zeros((LAYER, 2 * REACH + 1), np.int32)
    for code, row in enumerate(rows):
        offsets[code, : len(row)] = row
        for t in range(-REACH, REACH + 1):
            below[code, t + REACH] = sum(offset < t for offset in row)
    return offsets, below


OFFSETS, BELOW = stencil_tables()
WIDEST = OFFSETS.shape[1]
TABLE = np.concatenate([OFFSETS, BELOW], 1)
STRIDE = TABLE.shape[1]
LIMIT = pltpu.CompilerParams(vmem_limit_bytes=6 * 1024 * 1024)


def tile_bounds(share):
    inner = outer = 0
    for first in range(LAYER):
        for live in range(1, share + 1):
            near = far = 0
            for a in range(live):
                code = (first + a) % LAYER
                row = [int(o) for o in OFFSETS[code][: BELOW[code, -1]]]
                near += sum(0 <= a + o and o <= 0 for o in row)
                far += sum(a + o < 0 or a + o >= live for o in row)
            inner, outer = max(inner, near), max(outer, far)
    return inner, outer


def rank(table, code, t):
    return table[code * STRIDE + jnp.clip(t, -REACH, REACH) + REACH + WIDEST]


FIELDS = 6


def write_plan(meta, table, plan, a):
    code = lax.bitwise_and(meta[1] + a, LAYER - 1)
    place = meta[1] + a
    low, split, middle = rank(table, code, -place), rank(table, code, -a), rank(table, code, 0)
    resume, high = rank(table, code, meta[0] - a), rank(table, code, meta[2] - place)
    row = code * STRIDE
    ahead = split - low
    plan[a * FIELDS] = middle - split
    plan[a * FIELDS + 1] = row + split
    plan[a * FIELDS + 2] = ahead + jnp.maximum(high - resume, 0)
    plan[a * FIELDS + 3] = ahead
    plan[a * FIELDS + 4] = row + low
    plan[a * FIELDS + 5] = row + resume - ahead


def inner_range(plan, table, a):
    start = plan[a * FIELDS + 1]
    return plan[a * FIELDS], lambda t: a + table[start + t]


def outer_range(plan, table, a):
    ahead, start, start_after = (plan[a * FIELDS + k] for k in (3, 4, 5))
    return plan[a * FIELDS + 2], lambda t: a + table[t + jnp.where(t < ahead, start, start_after)]


def sweep(count, place_of, step, carry):
    def both(i, state):
        carry, *now = state
        later = place_of(2 * i + 2), place_of(2 * i + 3)
        return step(now, carry), *later

    carry, first, _ = lax.fori_loop(0, lax.div(count, 2), both, (carry, place_of(0), place_of(1)))
    return lax.fori_loop(0, lax.rem(count, 2), lambda _, carry: step([first], carry), carry)


TURN = 4


def padded_sweep(count, fetch, step, carry):
    def turn(i, state):
        carry, *now = state
        later = [fetch(TURN * (i + 1) + k) for k in range(TURN)]
        return step(now, carry), *later

    state = (carry, *(fetch(k) for k in range(TURN)))
    return lax.fori_loop(0, lax.div(count + (TURN - 1), TURN), turn, state)[0]


def tree(terms):
    while len(terms) > 1:
        terms = [a + b for a, b in zip(terms[::2], terms[1::2])] + terms[len(terms) // 2 * 2 :]
    return terms[0]


def gather(partial, c, term):
    if c < len(partial):
        partial[c] = term
    else:
        partial[c % len(partial)] = partial[c % len(partial)] + term


def pieces_of(width):
    return [slice(c * SUB, (c + 1) * SUB) for c in range(width // SUB)]


def wide(row):
    return jnp.broadcast_to(row, (SUB, row.shape[1]))


def pair_chunk(own, other):
    dx = own[0] - other[0]
    dy = own[1] - other[1]
    dz = own[2] - other[2]
    squared = dx * dx + dy * dy + dz * dz
    rest = jnp.maximum(1.0 - squared, 0.0)
    return rest * rest * pltpu.reciprocal((squared + 0.01) * (own[3] + other[3]), approx=True)


def spread_columns(out, index, rows):
    count, width = rows.shape
    turned = rows.T
    for a in range(count):
        out[index(a)] = jnp.broadcast_to(turned[:, a : a + 1], (width, width))


def lane_sums(parts, count, width):
    lanes = lax.broadcasted_iota(jnp.int32, (width, width), 1)
    turned = jnp.zeros((width, width), jnp.float32)
    for a in range(count):
        turned = jnp.where(lanes == a, jnp.sum(parts[a], axis=1, keepdims=True), turned)
    return turned.T[:count]


def sub_sums(cols):
    return jnp.sum(cols[...].reshape(-1, SUB, cols.shape[1]), axis=1)


def alive_rows(meta, share, width):
    return lax.broadcasted_iota(jnp.int32, (share, width), 0) < meta[0]


def prepare(
    counts, densities, position_in, phase_in, listed_in, right_side_in, table_in,
    meta, table, hood, near, density, source, first_swap, second_swap, *rest
):
    *times_out, phase, listed, right_side, times, sems = rest
    share, width = source.shape
    capacity = phase.shape[0]
    body_rows = pl.ds(share, capacity)
    copies = [
        pltpu.make_async_copy(phase_in, phase, sems.at[0]),
        pltpu.make_async_copy(position_in, hood.at[pl.ds(0, 3), body_rows, :], sems.at[1]),
        pltpu.make_async_copy(listed_in, listed, sems.at[2]),
        pltpu.make_async_copy(right_side_in, right_side, sems.at[3]),
        pltpu.make_async_copy(table_in, table, sems.at[4]),
    ]
    for copy in copies:
        copy.start()
    piece, column = lax.axis_index("piece"), lax.axis_index("col")
    filled = counts[piece]
    filled_before = counts[jnp.maximum(piece - 1, 0)]
    before = jnp.int32(0)
    total = jnp.int32(0)
    for p in range(counts.shape[0]):
        before = before + jnp.where(p < piece, counts[p], 0)
        total = total + counts[p]
    meta[0] = jnp.clip(filled - column * share, 0, share)
    meta[1] = before + column * share
    meta[2] = total
    meta[3] = column * share
    meta[4] = filled
    meta[5] = filled_before
    own_rows = pl.ds(pl.multiple_of(share + column * share, SUB), share)
    copies[0].wait()
    labels = phase[...]
    whole = sum(jnp.where(labels == k, densities[k], 0.0) for k in range(densities.shape[0]))
    hood[3, body_rows, :] = whole * (width / 2.0)
    density[...] = hood[3, own_rows, :] * (2.0 / width)
    copies[1].wait()
    even = lax.rem(piece, 2) == 0
    for k in range(4):
        tail, head = hood[k, pl.ds(filled, share), :], hood[k, share : 2 * share, :]
        first_swap[k] = jnp.where(even, tail, head)
        second_swap[k] = jnp.where(even, head, tail)
        near[k, 0:share, :] = hood[k, own_rows, :]
    for copy in copies[2:]:
        copy.wait()
    source[...] = jnp.where(alive_rows(meta, share, width), right_side[...], 0.0)
    ids = listed[...]
    own = lax.broadcasted_iota(jnp.int32, ids.shape, 1)
    slot = ids - piece * capacity
    away = slot - own + jnp.where(slot < 0, capacity - filled_before, jnp.where(slot >= capacity, filled - capacity, 0))
    away = jnp.where(ids < 0, -REACH, away) + REACH
    steps = lax.broadcasted_iota(jnp.int32, (2 * REACH, capacity), 0)
    found = tree([jnp.where(steps == away[k : k + 1], 1.0, 0.0) for k in range(ids.shape[0])])
    found = jnp.concatenate([found, jnp.zeros((width - 2 * REACH, capacity), jnp.float32)], 0)
    times[...] = found.T
    for k, out in enumerate(times_out):
        out[...] = times[pl.ds(pl.multiple_of((column ^ k) * share, SUB), share), :]


def finish_tiles(tiles, end):
    for t in range(TURN):
        tiles[end + t] = jnp.zeros(tiles.shape[1:], jnp.float32)


def build_inner(meta, table, near, plan, tiles, spread, rows_ref, cols_ref, self_ref):
    share, width = rows_ref.shape[0], rows_ref.shape[2]
    chunks = pieces_of(width)
    for a in range(share):
        write_plan(meta, table, plan, a)
    for k in range(4):
        spread_columns(spread, lambda a: (a, k), near[k, 0:share, :])
    cols_ref[...] = jnp.zeros_like(cols_ref)

    def rows_at(n):
        return [wide(near[k, pl.ds(n, 1), :]) for k in range(4)]

    def block(a, at):
        count, place_of = inner_range(plan, table, a)
        rows_ref[a] = jnp.zeros((width, width), jnp.float32)

        def pairs(places, at):
            others = [rows_at(n) for n in places]
            down = [[None] * 2 for _ in places]
            for c, here in enumerate(chunks):
                own = [spread[a, k, here, :] for k in range(4)]
                found = []
                for t, other in enumerate(others):
                    tile = pair_chunk(own, other)
                    tiles[at + t, here, :] = tile
                    gather(down[t], c, tile)
                    found.append(tile)
                rows_ref[a, here, :] = rows_ref[a, here, :] + tree(found)
            for n, partial in zip(places, down):
                there = pl.ds(pl.multiple_of(n * SUB, SUB), SUB)
                cols_ref[there, :] = cols_ref[there, :] + tree(partial)
            return at + len(places)

        at = sweep(count, place_of, pairs, at)
        other = rows_at(a)
        lane = lax.broadcasted_iota(jnp.int32, (SUB, width), 1)
        sublane = lax.broadcasted_iota(jnp.int32, (SUB, width), 0)
        down = [None] * 4
        for c, here in enumerate(chunks):
            tile = pair_chunk([spread[a, k, here, :] for k in range(4)], other)
            tile = jnp.where(lane == sublane + c * SUB, 0.0, tile)
            tiles[at, here, :] = tile
            gather(down, c, tile)
        self_ref[pl.ds(pl.multiple_of(a * SUB, SUB), SUB), :] = tree(down)
        return at + 1

    finish_tiles(tiles, lax.fori_loop(0, meta[0], block, 0))


def factor(times, a, n):
    lane = lax.broadcasted_iota(jnp.int32, (1, times.shape[1]), 1)
    return jnp.sum(jnp.where(lane == n - a + REACH, times[pl.ds(a, 1), :], 0.0), axis=1, keepdims=True)


def either(flag, run):
    @pl.when(flag == 0)
    def _():
        run(False)

    @pl.when(flag != 0)
    def _():
        run(True)


def build_outer(
    meta, table, plan, around, first, second, density, source, tiles_in, spread, rows_ref, cols_ref, self_ref, *rest
):
    *times_in, again_ref, tiles, diagonal_ref, precond_ref, times, alone_ref, hood, work, sums_ref, extra = rest
    share, width = diagonal_ref.shape
    chunks = pieces_of(width)
    base, filled = meta[3], meta[4]
    even = lax.rem(lax.axis_index("piece"), 2) == 0
    for k in range(4):
        hood[k, 0:share, :] = jnp.where(even, second[k], first[k])
        hood[k, share:, :] = around[k, share:, :]
        hood[k, pl.ds(share + filled, share), :] = jnp.where(even, first[k], second[k])
    alive = alive_rows(meta, share, width)
    often = jnp.where(alive, tree([ref[...] for ref in times_in]), 0.0)
    times[...] = often
    lane = lax.broadcasted_iota(jnp.int32, (share, width), 1)
    again = jnp.max(jnp.where((lane == REACH) | (lane == 0), 0.0, often)) > 1.5
    again_ref[0] = again.astype(jnp.int32)


    def block(a, at):
        count, place_of = outer_range(plan, table, a)
        work[a] = rows_ref[a]

        def pairs(places, at):
            others = [[wide(hood[k, pl.ds(base + share + n, 1), :]) for k in range(4)] for n in places]
            for here in chunks:
                own = [spread[a, k, here, :] for k in range(4)]
                found = []
                for t, other in enumerate(others):
                    tile = pair_chunk(own, other)
                    tiles[at + t, here, :] = tile
                    found.append(tile)
                work[a, here, :] = work[a, here, :] + tree(found)
            return at + len(places)

        return sweep(count, place_of, pairs, at)

    finish_tiles(tiles, lax.fori_loop(0, meta[0], block, 0))
    sums_ref[...] = lane_sums(work, share, width) + sub_sums(cols_ref)

    @pl.when(again)
    def _():
        extra[...] = jnp.zeros_like(extra)
        work[...] = jnp.zeros_like(work)

        def block(a, state):
            count, place_of = inner_range(plan, table, a)

            def inner(t, at):
                n = place_of(t)
                tile = tiles_in[at]
                work[a] = work[a] + tile * factor(times, a, n)
                there = pl.ds(n, 1)
                down = jnp.sum(tile, axis=0, keepdims=True)
                extra[there, :] = extra[there, :] + down * factor(times, n, a)
                return at + 1

            at = lax.fori_loop(0, count, inner, state[0]) + 1
            count, place_far = outer_range(plan, table, a)

            def outer(t, at):
                work[a] = work[a] + tiles[at] * factor(times, a, place_far(t))
                return at + 1

            return at, lax.fori_loop(0, count, outer, state[1])

        lax.fori_loop(0, meta[0], block, (0, 0))
        sums_ref[...] = lane_sums(work, share, width) + extra[...]

    alone = jnp.sum(jnp.where(lane == REACH, often, 0.0), axis=1, keepdims=True)
    alone_ref[...] = jnp.broadcast_to(alone, (share, width))
    pairs = jnp.where(alive, sums_ref[...] + sub_sums(self_ref) * alone, 0.0)
    diagonal = 1.0 / density[...] + pairs
    diagonal_ref[...] = diagonal
    precond_ref[...] = source[...] / diagonal


def apply_inner(meta, table, plan, again, field, alone, times, tiles, rows_ref, cols_ref, spread, near, lone, cols):
    share, width = field.shape
    chunks = pieces_of(width)
    near[0:share, :] = field[...]
    near[share:, :] = jnp.zeros((SUB, width), jnp.float32)
    lone[...] = field[...] * alone[...]
    spread_columns(spread, lambda a: a, field[...])
    cols[...] = jnp.zeros_like(cols)

    def run(weighted):
        def block(a, at):
            count, place_of = inner_range(plan, table, a)

            def fetch(t):
                n = jnp.where(t < count, place_of(t), share)
                return n, wide(near[pl.ds(n, 1), :])

            def pairs(fetched, carry):
                at, sums = carry
                if weighted:
                    fetched = [(n, value * factor(times, a, jnp.minimum(n, share - 1))) for n, value in fetched]
                down = [[None] * 2 for _ in fetched]
                result = []
                for c, (here, total) in enumerate(zip(chunks, sums)):
                    own = spread[a, here, :]
                    found = []
                    for t, (_, value) in enumerate(fetched):
                        tile = tiles[at + t, here, :]
                        gather(down[t], c, tile * own)
                        found.append(tile * value)
                    result.append(total + tree(found))
                for (n, _), partial in zip(fetched, down):
                    there = pl.ds(pl.multiple_of(n * SUB, SUB), SUB)
                    partial = tree(partial)
                    if weighted:
                        partial = partial * factor(times, jnp.minimum(n, share - 1), a)
                    cols[there, :] = cols[there, :] + partial
                return at + len(fetched), result

            zero = jnp.zeros((SUB, width), jnp.float32)
            _, sums = padded_sweep(count, fetch, pairs, (at, [zero] * len(chunks)))
            at = at + count
            value = wide(lone[pl.ds(a, 1), :])
            for here, old in zip(chunks, sums):
                rows_ref[a, here, :] = old + tiles[at, here, :] * value
            return at + 1

        lax.fori_loop(0, meta[0], block, 0)

    either(again[0], run)
    cols_ref[...] = cols[0 : share * SUB, :]


def apply_outer(meta, table, plan, again, received, times, tiles, rows_ref, cols_ref, work, hood):
    first, second, *ends = received
    columns = len(received)
    share, width = first.shape
    chunks = pieces_of(width)
    base, filled = meta[3], meta[4]
    column = lax.div(base, share)
    odd = lax.rem(column, 2) == 1
    before = jnp.where(odd, first[...], second[...])
    after = jnp.where(odd, second[...], first[...])
    own = 3 * share
    for c, end in enumerate(ends, 1):
        hood[pl.ds(own - meta[5] + c * share, share), :] = end[...]
    from_last = own - meta[5] + (columns - 1) * share
    hood[pl.ds(jnp.where(column == 0, from_last, own - share), share), :] = before
    hood[own + share : own + 2 * share, :] = after
    head = after
    for c, end in enumerate(ends, 1):
        head = jnp.where(column == c, end[...], head)
    hood[pl.ds(own + jnp.clip(filled - base, 0, 2 * share), share), :] = head
    nothing = hood.shape[0] - SUB
    hood[nothing:, :] = jnp.zeros((SUB, width), jnp.float32)

    def run(weighted):
        def block(a, at):
            count, place_of = outer_range(plan, table, a)

            def fetch(t):
                place = place_of(t)
                value = hood[pl.ds(jnp.where(t < count, own + place, nothing), 1), :]
                if weighted:
                    value = value * factor(times, a, place)
                return wide(value)

            def pairs(values, carry):
                at, sums = carry
                result = []
                for here, total in zip(chunks, sums):
                    result.append(total + tree([tiles[at + t, here, :] * value for t, value in enumerate(values)]))
                return at + len(values), result

            _, sums = padded_sweep(count, fetch, pairs, (at, [rows_ref[a, here, :] for here in chunks]))
            for here, values in zip(chunks, sums):
                work[a, here, :] = values
            return at + count

        lax.fori_loop(0, meta[0], block, 0)

    either(again[0], run)
    return jnp.where(alive_rows(meta, share, width), lane_sums(work, share, width) + sub_sums(cols_ref), 0.0)


def apply_first(meta, table, plan, again, diagonal, times, *rest):
    *received, tiles, rows_ref, cols_ref, spill_ref, scaled_ref, work, hood = rest
    spill = apply_outer(meta, table, plan, again, received, times, tiles, rows_ref, cols_ref, work, hood)
    spill_ref[...] = spill
    scaled_ref[...] = spill / diagonal[...]


def apply_second(meta, table, plan, again, source, precond, spill, scaled, times, *rest):
    *received, tiles, rows_ref, cols_ref, twice_ref, sums_ref, work, hood = rest
    twice = apply_outer(meta, table, plan, again, received, times, tiles, rows_ref, cols_ref, work, hood)
    twice_ref[...] = twice
    share, width = twice.shape
    lane = lax.broadcasted_iota(jnp.int32, (1, width), 1)
    sums = jnp.zeros((1, width), jnp.float32)
    pairs = ((source[...], precond[...]), (spill[...], precond[...]), (spill[...], scaled[...]), (scaled[...], twice))
    for k, (first, second) in enumerate(pairs):
        along = jnp.sum(first * second, axis=0, keepdims=True)
        sums = jnp.where(lane == k, jnp.sum(along, axis=1, keepdims=True), sums)
    sums_ref[...] = wide(sums)


def finish(source, precond, spill, scaled, twice, *rest):
    *parts, solution_ref, residual_ref = rest
    sums = tree([ref[...] for ref in parts])

    def pick(k):
        return sums[0:1, k : k + 1]

    weighted, cross, square, last = pick(0), pick(1), pick(2), pick(3)
    part = cross / weighted
    advance = 1.0 / (1.0 - part)
    keep = -part * advance
    weighted_next = advance * advance * (square - cross * part)
    bent = keep * keep * cross + 2.0 * keep * advance * square + advance * advance * last
    blend = weighted_next / weighted
    advance_next = weighted_next / (weighted_next - bent - blend * weighted_next / advance)
    residual = keep * source[...] + advance * spill[...]
    next_precond = keep * precond[...] + advance * scaled[...]
    direction = next_precond + blend * precond[...]
    image = residual - keep * spill[...] - advance * twice[...] + blend * (source[...] - spill[...])
    solution_ref[...] = advance * precond[...] + advance_next * direction
    residual_ref[...] = residual - advance_next * image


def held(array):
    return pltpu.with_memory_space_constraint(array, pltpu.VMEM)


def body(positions, phase, neighbours, counts, phase_density, right_side):
    capacity, width = phase.shape
    columns = lax.axis_size("col")
    pieces = lax.axis_size("piece")
    share = capacity // columns
    f32 = jnp.float32
    vector = jax.ShapeDtypeStruct((share, width), f32)
    few = jax.ShapeDtypeStruct((SUB, width), f32)
    message = jax.ShapeDtypeStruct((4, share, width), f32)
    most_inner, most_outer = tile_bounds(share)
    inner_tiles = pltpu.VMEM((most_inner + TURN, width, width), f32)
    outer_tiles = pltpu.VMEM((most_outer + TURN, width, width), f32)
    square = pltpu.VMEM((share, width, width), f32)
    narrow = pltpu.VMEM((share * SUB, width), f32)
    table = jnp.asarray(TABLE.reshape(-1))

    def call(kernel, args, outs, scratch=(), work=0, scalars=2, far=0, **more):
        return pl.pallas_call(
            kernel,
            out_shape=outs,
            in_specs=[SMEM] * scalars + [HBM] * far + [VMEM] * (len(args) - scalars - far),
            out_specs=[SMEM if getattr(o, "memory_space", None) == pltpu.SMEM else VMEM for o in outs],
            scratch_shapes=scratch,
            compiler_params=LIMIT,
            cost_estimate=pl.CostEstimate(flops=work * width * width, bytes_accessed=0, transcendentals=0),
            name=kernel.__name__,
            **more,
        )(*args)

    def away(array):
        return pltpu.with_memory_space_constraint(array, pltpu.HBM)

    around = jax.ShapeDtypeStruct((4, capacity + 2 * share, width), f32)
    near = jax.ShapeDtypeStruct((4, 2 * share, width), f32)
    far = [away(array) for array in (positions, phase, neighbours.T, right_side, table)]
    meta, table, around, near, density, source, first, second, *times = call(
        prepare,
        (away(counts), away(phase_density), *far),
        [pltpu.SMEM((8,), jnp.int32), pltpu.SMEM(table.shape, jnp.int32), around, near, vector, vector, message, message]
        + [vector] * columns,
        [pltpu.VMEM(phase.shape, jnp.int32), pltpu.VMEM(far[2].shape, jnp.int32), pltpu.VMEM((share, width), f32),
         pltpu.VMEM((capacity, width), f32), pltpu.SemaphoreType.DMA((5,))],
        far=len(far),
    )
    meta, table = (pltpu.with_memory_space_constraint(array, pltpu.SMEM) for array in (meta, table))
    first = lax.ppermute(first, "piece", [(i, i ^ 1) for i in range(pieces)])
    second = lax.ppermute(second, "piece", [(i, ((i ^ 1) + (1 if i % 2 else -1) * 2) % pieces) for i in range(pieces)])
    times = [lax.ppermute(t, "col", [(i, i ^ k) for i in range(columns)]) if k else t for k, t in enumerate(times)]

    plan, tiles_in, spread, rows, cols, selfs = call(
        build_inner,
        (meta, table, near),
        [pltpu.SMEM((share * FIELDS,), jnp.int32), inner_tiles, pltpu.VMEM((share, 4, width, width), f32),
         square, narrow, narrow],
        work=16 * most_inner,
    )
    plan = pltpu.with_memory_space_constraint(plan, pltpu.SMEM)
    again, tiles_out, diagonal, precond, times, alone = call(
        build_outer,
        (meta, table, plan, around, first, second, density, source,
         held(tiles_in), held(spread), held(rows), held(cols), held(selfs), *times),
        [pltpu.SMEM((1,), jnp.int32), outer_tiles, vector, vector, vector, vector],
        [pltpu.VMEM((4, capacity + 2 * share, width), f32), pltpu.VMEM((share, width, width), f32)]
        + [pltpu.VMEM((share, width), f32)] * 2,
        16 * most_outer,
        scalars=3,
    )
    again = pltpu.with_memory_space_constraint(again, pltpu.SMEM)

    def inner(field):
        return call(
            apply_inner,
            (meta, table, plan, again, field, alone, times, held(tiles_in)),
            [square, narrow],
            [pltpu.VMEM((share, width, width), f32), pltpu.VMEM((share + SUB, width), f32), pltpu.VMEM((share, width), f32),
             pltpu.VMEM(((share + 1) * SUB, width), f32)],
            4 * most_inner,
            scalars=4,
        )

    def exchange(field):
        axes = ("piece", "col")
        count = pieces * columns
        swaps = [[i ^ 1 for i in range(count)], [i - 1 if i % 2 == 0 else i + 1 for i in range(count)]]
        swaps[1][0], swaps[1][-1] = count - 1, 0
        for c in range(1, columns - 1):
            to = {}
            for p in range(pieces - 1):
                low, high = p * columns + c, (p + 1) * columns
                to[low], to[high] = high, low
            for p in range(pieces):
                rest = [i for i in range(p * columns, (p + 1) * columns) if i not in to]
                to.update(zip(rest, rest[1:] + rest[:1]))
            swaps.append([to[i] for i in range(count)])
        return [lax.ppermute(field, axes, list(enumerate(to))) for to in swaps]

    scratch = [pltpu.VMEM((share, width, width), f32), pltpu.VMEM((8 * share, width), f32)]

    received = exchange(precond)
    rows, cols = inner(precond)
    spill, scaled = call(
        apply_first,
        (meta, table, plan, again, diagonal, times, *received, held(tiles_out), held(rows), held(cols)),
        [vector, vector],
        scratch,
        2 * most_outer,
        scalars=4,
    )

    received = exchange(scaled)
    rows, cols = inner(scaled)
    twice, sums = call(
        apply_second,
        (meta, table, plan, again, source, precond, spill, scaled, times, *received, held(tiles_out), held(rows), held(cols)),
        [vector, few],
        scratch,
        2 * most_outer,
        scalars=4,
    )

    def swap(values, axis, step):
        return lax.ppermute(values, axis, [(i, i ^ step) for i in range(lax.axis_size(axis))])

    def together(values, axis, low, size):
        return tree([values] + [swap(values, axis, low * k) for k in range(1, size)])

    sums = together(sums, "col", 1, columns)
    step = 1
    while pieces // step > 8:
        sums = together(sums, "piece", step, 8)
        step *= 8
    others = [swap(sums, "piece", step * k) for k in range(1, pieces // step)]

    return tuple(call(
        finish,
        (source, precond, spill, scaled, twice, sums, *others),
        [vector, vector],
        scalars=0,
    ))


def solution(mesh):
    placed = (
        P(None, "piece", None),
        P("piece", None),
        P("piece", "col"),
        P(),
        P(),
        P(("piece", "col"), None),
    )
    return jax.shard_map(
        body,
        mesh=mesh,
        in_specs=placed,
        out_specs=(P(("piece", "col"), None), P(("piece", "col"), None)),
        check_vma=False,
    )
```

```python
import jax
import jax.numpy as jnp
import numpy as np
from jax import lax
from jax.experimental import pallas as pl
from jax.experimental.pallas import tpu as pltpu
from jax.sharding import PartitionSpec as P

ITERS = 2
SIDE = 4
LAYER = SIDE * SIDE
REACH = 2 * LAYER
SUB = 8
VMEM = pl.BlockSpec(memory_space=pltpu.VMEM)
SMEM = pl.BlockSpec(memory_space=pltpu.SMEM)
HBM = pl.BlockSpec(memory_space=pltpu.HBM)


def stencil_tables():
    levels = SIDE.bit_length() - 1

    def cell(code):
        across = sum((code >> (2 * level) & 1) << level for level in range(levels))
        along = sum((code >> (2 * level + 1) & 1) << level for level in range(levels))
        return across, along

    place = {cell(code): code for code in range(LAYER)}
    rows = []
    for code in range(LAYER):
        across, along = cell(code)
        rows.append(
            sorted(
                step_z * LAYER + place[across + step_x, along + step_y] - code
                for step_z in (-1, 0, 1)
                for step_y in (-1, 0, 1)
                for step_x in (-1, 0, 1)
                if (across + step_x, along + step_y) in place
            )
        )
    longest = max(len(row) for row in rows)
    offsets = np.zeros((LAYER, longest), np.int32)
    below = np.zeros((LAYER, 2 * REACH + 1), np.int32)
    for code, row in enumerate(rows):
        offsets[code, : len(row)] = row
        for t in range(-REACH, REACH + 1):
            below[code, t + REACH] = sum(offset < t for offset in row)
    return offsets, below


OFFSETS, BELOW = stencil_tables()
WIDEST = OFFSETS.shape[1]
TABLE = np.concatenate([OFFSETS, BELOW], 1)
STRIDE = TABLE.shape[1]
LIMIT = pltpu.CompilerParams(vmem_limit_bytes=6 * 1024 * 1024)


def tile_bounds(share):
    inner = outer = 0
    for first in range(LAYER):
        for live in range(1, share + 1):
            near = far = 0
            for a in range(live):
                code = (first + a) % LAYER
                row = [int(o) for o in OFFSETS[code][: BELOW[code, -1]]]
                near += sum(0 <= a + o and o <= 0 for o in row)
                far += sum(a + o < 0 or a + o >= live for o in row)
            inner, outer = max(inner, near), max(outer, far)
    return inner, outer


def rank(table, code, t):
    return table[code * STRIDE + jnp.clip(t, -REACH, REACH) + REACH + WIDEST]


FIELDS = 6


def write_plan(meta, table, plan, a):
    code = lax.bitwise_and(meta[1] + a, LAYER - 1)
    place = meta[1] + a
    low, split, middle = rank(table, code, -place), rank(table, code, -a), rank(table, code, 0)
    resume, high = rank(table, code, meta[0] - a), rank(table, code, meta[2] - place)
    row = code * STRIDE
    ahead = split - low
    plan[a * FIELDS] = middle - split
    plan[a * FIELDS + 1] = row + split
    plan[a * FIELDS + 2] = ahead + jnp.maximum(high - resume, 0)
    plan[a * FIELDS + 3] = ahead
    plan[a * FIELDS + 4] = row + low
    plan[a * FIELDS + 5] = row + resume - ahead


def inner_range(plan, table, a):
    start = plan[a * FIELDS + 1]
    return plan[a * FIELDS], lambda t: a + table[start + t]


def outer_range(plan, table, a):
    ahead, start, start_after = (plan[a * FIELDS + k] for k in (3, 4, 5))
    return plan[a * FIELDS + 2], lambda t: a + table[t + jnp.where(t < ahead, start, start_after)]


def sweep(count, place_of, step, carry):
    def both(i, state):
        carry, *now = state
        later = place_of(2 * i + 2), place_of(2 * i + 3)
        return step(now, carry), *later

    carry, first, _ = lax.fori_loop(0, lax.div(count, 2), both, (carry, place_of(0), place_of(1)))
    return lax.fori_loop(0, lax.rem(count, 2), lambda _, carry: step([first], carry), carry)


TURN = 4


def padded_sweep(count, fetch, step, carry):
    def turn(i, state):
        carry, *now = state
        later = [fetch(TURN * (i + 1) + k) for k in range(TURN)]
        return step(now, carry), *later

    state = (carry, *(fetch(k) for k in range(TURN)))
    return lax.fori_loop(0, lax.div(count + (TURN - 1), TURN), turn, state)[0]


def tree(terms):
    while len(terms) > 1:
        terms = [a + b for a, b in zip(terms[::2], terms[1::2])] + terms[len(terms) // 2 * 2 :]
    return terms[0]


def gather(partial, c, term):
    if c < len(partial):
        partial[c] = term
    else:
        partial[c % len(partial)] = partial[c % len(partial)] + term


def pieces_of(width):
    return [slice(c * SUB, (c + 1) * SUB) for c in range(width // SUB)]


def wide(row):
    return jnp.broadcast_to(row, (SUB, row.shape[1]))


def pair_parts(own, other):
    dx = own[0] - other[0]
    dy = own[1] - other[1]
    dz = own[2] - other[2]
    squared = dx * dx + dy * dy + dz * dz
    rest = jnp.maximum(1.0 - squared, 0.0)
    return rest * rest, (squared + 0.01) * (own[3] + other[3])


def pair_weights(first, second):
    inverse = pltpu.reciprocal(first[1] * second[1], approx=True)
    return first[0] * (inverse * second[1]), second[0] * (inverse * first[1])


def tile_chunks(own_of, others, chunks):
    for c in range(0, len(chunks), 2):
        parts = [[pair_parts(own, other) for other in others] for own in (own_of(chunks[c]), own_of(chunks[c + 1]))]
        if len(others) == 2:
            yield c, pair_weights(*parts[0])
            yield c + 1, pair_weights(*parts[1])
        else:
            low, high = pair_weights(parts[0][0], parts[1][0])
            yield c, [low]
            yield c + 1, [high]


def spread_columns(out, index, rows):
    count, width = rows.shape
    turned = rows.T
    for a in range(count):
        out[index(a)] = jnp.broadcast_to(turned[:, a : a + 1], (width, width))


def lane_sums(parts, count, width):
    lanes = lax.broadcasted_iota(jnp.int32, (width, width), 1)
    turned = jnp.zeros((width, width), jnp.float32)
    for a in range(count):
        turned = jnp.where(lanes == a, jnp.sum(parts[a], axis=1, keepdims=True), turned)
    return turned.T[:count]


def sub_sums(cols):
    return jnp.sum(cols[...].reshape(-1, SUB, cols.shape[1]), axis=1)


def alive_rows(meta, share, width):
    return lax.broadcasted_iota(jnp.int32, (share, width), 0) < meta[0]


def prepare(
    counts, densities, position_in, phase_in, listed_in, right_side_in, table_in,
    meta, table, hood, near, density, source, first_swap, second_swap, *rest
):
    *times_out, phase, listed, right_side, times, sems = rest
    share, width = source.shape
    capacity = phase.shape[0]
    body_rows = pl.ds(share, capacity)
    copies = [
        pltpu.make_async_copy(phase_in, phase, sems.at[0]),
        pltpu.make_async_copy(position_in, hood.at[pl.ds(0, 3), body_rows, :], sems.at[1]),
        pltpu.make_async_copy(listed_in, listed, sems.at[2]),
        pltpu.make_async_copy(right_side_in, right_side, sems.at[3]),
        pltpu.make_async_copy(table_in, table, sems.at[4]),
    ]
    for copy in copies:
        copy.start()
    piece, column = lax.axis_index("piece"), lax.axis_index("col")
    filled = counts[piece]
    filled_before = counts[jnp.maximum(piece - 1, 0)]
    before = jnp.int32(0)
    total = jnp.int32(0)
    for p in range(counts.shape[0]):
        before = before + jnp.where(p < piece, counts[p], 0)
        total = total + counts[p]
    meta[0] = jnp.clip(filled - column * share, 0, share)
    meta[1] = before + column * share
    meta[2] = total
    meta[3] = column * share
    meta[4] = filled
    meta[5] = filled_before
    own_rows = pl.ds(pl.multiple_of(share + column * share, SUB), share)
    copies[0].wait()
    labels = phase[...]
    whole = sum(jnp.where(labels == k, densities[k], 0.0) for k in range(densities.shape[0]))
    hood[3, body_rows, :] = whole * (width / 2.0)
    density[...] = hood[3, own_rows, :] * (2.0 / width)
    copies[1].wait()
    even = lax.rem(piece, 2) == 0
    for k in range(4):
        tail, head = hood[k, pl.ds(filled, share), :], hood[k, share : 2 * share, :]
        first_swap[k] = jnp.where(even, tail, head)
        second_swap[k] = jnp.where(even, head, tail)
        near[k, 0:share, :] = hood[k, own_rows, :]
    for copy in copies[2:]:
        copy.wait()
    source[...] = jnp.where(alive_rows(meta, share, width), right_side[...], 0.0)
    ids = listed[...]
    own = lax.broadcasted_iota(jnp.int32, ids.shape, 1)
    slot = ids - piece * capacity
    away = slot - own + jnp.where(slot < 0, capacity - filled_before, jnp.where(slot >= capacity, filled - capacity, 0))
    away = jnp.where(ids < 0, -REACH, away) + REACH
    steps = lax.broadcasted_iota(jnp.int32, (2 * REACH, capacity), 0)
    found = tree([jnp.where(steps == away[k : k + 1], 1.0, 0.0) for k in range(ids.shape[0])])
    found = jnp.concatenate([found, jnp.zeros((width - 2 * REACH, capacity), jnp.float32)], 0)
    times[...] = found.T
    for k, out in enumerate(times_out):
        out[...] = times[pl.ds(pl.multiple_of((column ^ k) * share, SUB), share), :]


def finish_tiles(tiles, end):
    for t in range(TURN):
        tiles[end + t] = jnp.zeros(tiles.shape[1:], jnp.float32)


def build_inner(meta, table, near, plan, tiles, spread, rows_ref, cols_ref, self_ref):
    share, width = rows_ref.shape[0], rows_ref.shape[2]
    chunks = pieces_of(width)
    for a in range(share):
        write_plan(meta, table, plan, a)
    for k in range(4):
        spread_columns(spread, lambda a: (a, k), near[k, 0:share, :])
    cols_ref[...] = jnp.zeros_like(cols_ref)

    def rows_at(n):
        return [wide(near[k, pl.ds(n, 1), :]) for k in range(4)]

    def block(a, at):
        count, place_of = inner_range(plan, table, a)
        rows_ref[a] = jnp.zeros((width, width), jnp.float32)

        def own_of(here):
            return [spread[a, k, here, :] for k in range(4)]

        def pairs(places, at):
            others = [rows_at(n) for n in places]
            down = [[None] * 2 for _ in places]
            for c, found in tile_chunks(own_of, others, chunks):
                here = chunks[c]
                for t, tile in enumerate(found):
                    tiles[at + t, here, :] = tile
                    gather(down[t], c, tile)
                rows_ref[a, here, :] = rows_ref[a, here, :] + tree(list(found))
            for n, partial in zip(places, down):
                there = pl.ds(pl.multiple_of(n * SUB, SUB), SUB)
                cols_ref[there, :] = cols_ref[there, :] + tree(partial)
            return at + len(places)

        at = sweep(count, place_of, pairs, at)
        other = rows_at(a)
        lane = lax.broadcasted_iota(jnp.int32, (SUB, width), 1)
        sublane = lax.broadcasted_iota(jnp.int32, (SUB, width), 0)
        down = [None] * 4
        for c, (tile,) in tile_chunks(own_of, [other], chunks):
            tile = jnp.where(lane == sublane + c * SUB, 0.0, tile)
            tiles[at, chunks[c], :] = tile
            gather(down, c, tile)
        self_ref[pl.ds(pl.multiple_of(a * SUB, SUB), SUB), :] = tree(down)
        return at + 1

    finish_tiles(tiles, lax.fori_loop(0, meta[0], block, 0))


def factor(times, a, n):
    lane = lax.broadcasted_iota(jnp.int32, (1, times.shape[1]), 1)
    return jnp.sum(jnp.where(lane == n - a + REACH, times[pl.ds(a, 1), :], 0.0), axis=1, keepdims=True)


def either(flag, run):
    @pl.when(flag == 0)
    def _():
        run(False)

    @pl.when(flag != 0)
    def _():
        run(True)


def build_outer(
    meta, table, plan, around, first, second, density, source, tiles_in, spread, rows_ref, cols_ref, self_ref, *rest
):
    *times_in, again_ref, tiles, diagonal_ref, precond_ref, times, alone_ref, hood, work, sums_ref, extra = rest
    share, width = diagonal_ref.shape
    chunks = pieces_of(width)
    base, filled = meta[3], meta[4]
    even = lax.rem(lax.axis_index("piece"), 2) == 0
    for k in range(4):
        hood[k, 0:share, :] = jnp.where(even, second[k], first[k])
        hood[k, share:, :] = around[k, share:, :]
        hood[k, pl.ds(share + filled, share), :] = jnp.where(even, first[k], second[k])
    alive = alive_rows(meta, share, width)
    often = jnp.where(alive, tree([ref[...] for ref in times_in]), 0.0)
    times[...] = often
    lane = lax.broadcasted_iota(jnp.int32, (share, width), 1)
    again = jnp.max(jnp.where((lane == REACH) | (lane == 0), 0.0, often)) > 1.5
    again_ref[0] = again.astype(jnp.int32)


    def block(a, at):
        count, place_of = outer_range(plan, table, a)
        work[a] = rows_ref[a]

        def own_of(here):
            return [spread[a, k, here, :] for k in range(4)]

        def pairs(places, at):
            others = [[wide(hood[k, pl.ds(base + share + n, 1), :]) for k in range(4)] for n in places]
            for c, found in tile_chunks(own_of, others, chunks):
                here = chunks[c]
                for t, tile in enumerate(found):
                    tiles[at + t, here, :] = tile
                work[a, here, :] = work[a, here, :] + tree(list(found))
            return at + len(places)

        return sweep(count, place_of, pairs, at)

    finish_tiles(tiles, lax.fori_loop(0, meta[0], block, 0))
    sums_ref[...] = lane_sums(work, share, width) + sub_sums(cols_ref)

    @pl.when(again)
    def _():
        extra[...] = jnp.zeros_like(extra)
        work[...] = jnp.zeros_like(work)

        def block(a, state):
            count, place_of = inner_range(plan, table, a)

            def inner(t, at):
                n = place_of(t)
                tile = tiles_in[at]
                work[a] = work[a] + tile * factor(times, a, n)
                there = pl.ds(n, 1)
                down = jnp.sum(tile, axis=0, keepdims=True)
                extra[there, :] = extra[there, :] + down * factor(times, n, a)
                return at + 1

            at = lax.fori_loop(0, count, inner, state[0]) + 1
            count, place_far = outer_range(plan, table, a)

            def outer(t, at):
                work[a] = work[a] + tiles[at] * factor(times, a, place_far(t))
                return at + 1

            return at, lax.fori_loop(0, count, outer, state[1])

        lax.fori_loop(0, meta[0], block, (0, 0))
        sums_ref[...] = lane_sums(work, share, width) + extra[...]

    alone = jnp.sum(jnp.where(lane == REACH, often, 0.0), axis=1, keepdims=True)
    alone_ref[...] = jnp.broadcast_to(alone, (share, width))
    pairs = jnp.where(alive, sums_ref[...] + sub_sums(self_ref) * alone, 0.0)
    diagonal = 1.0 / density[...] + pairs
    diagonal_ref[...] = diagonal
    precond_ref[...] = source[...] / diagonal


def apply_inner(meta, table, plan, again, field, alone, times, tiles, rows_ref, cols_ref, spread, near, lone, cols):
    share, width = field.shape
    chunks = pieces_of(width)
    near[0:share, :] = field[...]
    near[share:, :] = jnp.zeros((SUB, width), jnp.float32)
    lone[...] = field[...] * alone[...]
    spread_columns(spread, lambda a: a, field[...])
    cols[...] = jnp.zeros_like(cols)

    def run(weighted):
        def block(a, at):
            count, place_of = inner_range(plan, table, a)

            def fetch(t):
                n = jnp.where(t < count, place_of(t), share)
                return n, wide(near[pl.ds(n, 1), :])

            def pairs(fetched, carry):
                at, sums = carry
                if weighted:
                    fetched = [(n, value * factor(times, a, jnp.minimum(n, share - 1))) for n, value in fetched]
                down = [[None] * 2 for _ in fetched]
                result = []
                for c, (here, total) in enumerate(zip(chunks, sums)):
                    own = spread[a, here, :]
                    found = []
                    for t, (_, value) in enumerate(fetched):
                        tile = tiles[at + t, here, :]
                        gather(down[t], c, tile * own)
                        found.append(tile * value)
                    result.append(total + tree(found))
                for (n, _), partial in zip(fetched, down):
                    there = pl.ds(pl.multiple_of(n * SUB, SUB), SUB)
                    partial = tree(partial)
                    if weighted:
                        partial = partial * factor(times, jnp.minimum(n, share - 1), a)
                    cols[there, :] = cols[there, :] + partial
                return at + len(fetched), result

            zero = jnp.zeros((SUB, width), jnp.float32)
            _, sums = padded_sweep(count, fetch, pairs, (at, [zero] * len(chunks)))
            at = at + count
            value = wide(lone[pl.ds(a, 1), :])
            for here, old in zip(chunks, sums):
                rows_ref[a, here, :] = old + tiles[at, here, :] * value
            return at + 1

        lax.fori_loop(0, meta[0], block, 0)

    either(again[0], run)
    cols_ref[...] = cols[0 : share * SUB, :]


def apply_outer(meta, table, plan, again, received, times, tiles, rows_ref, cols_ref, work, hood):
    first, second, *ends = received
    columns = len(received)
    share, width = first.shape
    chunks = pieces_of(width)
    base, filled = meta[3], meta[4]
    column = lax.div(base, share)
    odd = lax.rem(column, 2) == 1
    before = jnp.where(odd, first[...], second[...])
    after = jnp.where(odd, second[...], first[...])
    own = 3 * share
    for c, end in enumerate(ends, 1):
        hood[pl.ds(own - meta[5] + c * share, share), :] = end[...]
    from_last = own - meta[5] + (columns - 1) * share
    hood[pl.ds(jnp.where(column == 0, from_last, own - share), share), :] = before
    hood[own + share : own + 2 * share, :] = after
    head = after
    for c, end in enumerate(ends, 1):
        head = jnp.where(column == c, end[...], head)
    hood[pl.ds(own + jnp.clip(filled - base, 0, 2 * share), share), :] = head
    nothing = hood.shape[0] - SUB
    hood[nothing:, :] = jnp.zeros((SUB, width), jnp.float32)

    def run(weighted):
        def block(a, at):
            count, place_of = outer_range(plan, table, a)

            def fetch(t):
                place = place_of(t)
                value = hood[pl.ds(jnp.where(t < count, own + place, nothing), 1), :]
                if weighted:
                    value = value * factor(times, a, place)
                return wide(value)

            def pairs(values, carry):
                at, sums = carry
                result = []
                for here, total in zip(chunks, sums):
                    result.append(total + tree([tiles[at + t, here, :] * value for t, value in enumerate(values)]))
                return at + len(values), result

            _, sums = padded_sweep(count, fetch, pairs, (at, [rows_ref[a, here, :] for here in chunks]))
            for here, values in zip(chunks, sums):
                work[a, here, :] = values
            return at + count

        lax.fori_loop(0, meta[0], block, 0)

    either(again[0], run)
    return jnp.where(alive_rows(meta, share, width), lane_sums(work, share, width) + sub_sums(cols_ref), 0.0)


def apply_first(meta, table, plan, again, diagonal, times, *rest):
    *received, tiles, rows_ref, cols_ref, spill_ref, scaled_ref, work, hood = rest
    spill = apply_outer(meta, table, plan, again, received, times, tiles, rows_ref, cols_ref, work, hood)
    spill_ref[...] = spill
    scaled_ref[...] = spill / diagonal[...]


def apply_second(meta, table, plan, again, source, precond, spill, scaled, times, *rest):
    *received, tiles, rows_ref, cols_ref, twice_ref, sums_ref, work, hood = rest
    twice = apply_outer(meta, table, plan, again, received, times, tiles, rows_ref, cols_ref, work, hood)
    twice_ref[...] = twice
    share, width = twice.shape
    lane = lax.broadcasted_iota(jnp.int32, (1, width), 1)
    sums = jnp.zeros((1, width), jnp.float32)
    pairs = ((source[...], precond[...]), (spill[...], precond[...]), (spill[...], scaled[...]), (scaled[...], twice))
    for k, (first, second) in enumerate(pairs):
        along = jnp.sum(first * second, axis=0, keepdims=True)
        sums = jnp.where(lane == k, jnp.sum(along, axis=1, keepdims=True), sums)
    sums_ref[...] = wide(sums)


def finish(source, precond, spill, scaled, twice, *rest):
    *parts, solution_ref, residual_ref = rest
    sums = tree([ref[...] for ref in parts])

    def pick(k):
        return sums[0:1, k : k + 1]

    weighted, cross, square, last = pick(0), pick(1), pick(2), pick(3)
    part = cross / weighted
    advance = 1.0 / (1.0 - part)
    keep = -part * advance
    weighted_next = advance * advance * (square - cross * part)
    bent = keep * keep * cross + 2.0 * keep * advance * square + advance * advance * last
    blend = weighted_next / weighted
    advance_next = weighted_next / (weighted_next - bent - blend * weighted_next / advance)
    residual = keep * source[...] + advance * spill[...]
    next_precond = keep * precond[...] + advance * scaled[...]
    direction = next_precond + blend * precond[...]
    image = residual - keep * spill[...] - advance * twice[...] + blend * (source[...] - spill[...])
    solution_ref[...] = advance * precond[...] + advance_next * direction
    residual_ref[...] = residual - advance_next * image


def held(array):
    return pltpu.with_memory_space_constraint(array, pltpu.VMEM)


def body(positions, phase, neighbours, counts, phase_density, right_side):
    capacity, width = phase.shape
    columns = lax.axis_size("col")
    pieces = lax.axis_size("piece")
    share = capacity // columns
    f32 = jnp.float32
    vector = jax.ShapeDtypeStruct((share, width), f32)
    few = jax.ShapeDtypeStruct((SUB, width), f32)
    message = jax.ShapeDtypeStruct((4, share, width), f32)
    most_inner, most_outer = tile_bounds(share)
    inner_tiles = pltpu.VMEM((most_inner + TURN, width, width), f32)
    outer_tiles = pltpu.VMEM((most_outer + TURN, width, width), f32)
    square = pltpu.VMEM((share, width, width), f32)
    narrow = pltpu.VMEM((share * SUB, width), f32)
    table = jnp.asarray(TABLE.reshape(-1))

    def call(kernel, args, outs, scratch=(), work=0, scalars=2, far=0, **more):
        return pl.pallas_call(
            kernel,
            out_shape=outs,
            in_specs=[SMEM] * scalars + [HBM] * far + [VMEM] * (len(args) - scalars - far),
            out_specs=[SMEM if getattr(o, "memory_space", None) == pltpu.SMEM else VMEM for o in outs],
            scratch_shapes=scratch,
            compiler_params=LIMIT,
            cost_estimate=pl.CostEstimate(flops=work * width * width, bytes_accessed=0, transcendentals=0),
            name=kernel.__name__,
            **more,
        )(*args)

    def away(array):
        return pltpu.with_memory_space_constraint(array, pltpu.HBM)

    around = jax.ShapeDtypeStruct((4, capacity + 2 * share, width), f32)
    near = jax.ShapeDtypeStruct((4, 2 * share, width), f32)
    far = [away(array) for array in (positions, phase, neighbours.T, right_side, table)]
    meta, table, around, near, density, source, first, second, *times = call(
        prepare,
        (away(counts), away(phase_density), *far),
        [pltpu.SMEM((8,), jnp.int32), pltpu.SMEM(table.shape, jnp.int32), around, near, vector, vector, message, message]
        + [vector] * columns,
        [pltpu.VMEM(phase.shape, jnp.int32), pltpu.VMEM(far[2].shape, jnp.int32), pltpu.VMEM((share, width), f32),
         pltpu.VMEM((capacity, width), f32), pltpu.SemaphoreType.DMA((5,))],
        far=len(far),
    )
    meta, table = (pltpu.with_memory_space_constraint(array, pltpu.SMEM) for array in (meta, table))
    first = lax.ppermute(first, "piece", [(i, i ^ 1) for i in range(pieces)])
    second = lax.ppermute(second, "piece", [(i, ((i ^ 1) + (1 if i % 2 else -1) * 2) % pieces) for i in range(pieces)])
    times = [lax.ppermute(t, "col", [(i, i ^ k) for i in range(columns)]) if k else t for k, t in enumerate(times)]

    plan, tiles_in, spread, rows, cols, selfs = call(
        build_inner,
        (meta, table, near),
        [pltpu.SMEM((share * FIELDS,), jnp.int32), inner_tiles, pltpu.VMEM((share, 4, width, width), f32),
         square, narrow, narrow],
        work=16 * most_inner,
    )
    plan = pltpu.with_memory_space_constraint(plan, pltpu.SMEM)
    again, tiles_out, diagonal, precond, times, alone = call(
        build_outer,
        (meta, table, plan, around, first, second, density, source,
         held(tiles_in), held(spread), held(rows), held(cols), held(selfs), *times),
        [pltpu.SMEM((1,), jnp.int32), outer_tiles, vector, vector, vector, vector],
        [pltpu.VMEM((4, capacity + 2 * share, width), f32), pltpu.VMEM((share, width, width), f32)]
        + [pltpu.VMEM((share, width), f32)] * 2,
        16 * most_outer,
        scalars=3,
    )
    again = pltpu.with_memory_space_constraint(again, pltpu.SMEM)

    def inner(field):
        return call(
            apply_inner,
            (meta, table, plan, again, field, alone, times, held(tiles_in)),
            [square, narrow],
            [pltpu.VMEM((share, width, width), f32), pltpu.VMEM((share + SUB, width), f32), pltpu.VMEM((share, width), f32),
             pltpu.VMEM(((share + 1) * SUB, width), f32)],
            4 * most_inner,
            scalars=4,
        )

    def exchange(field):
        axes = ("piece", "col")
        count = pieces * columns
        swaps = [[i ^ 1 for i in range(count)], [i - 1 if i % 2 == 0 else i + 1 for i in range(count)]]
        swaps[1][0], swaps[1][-1] = count - 1, 0
        for c in range(1, columns - 1):
            to = {}
            for p in range(pieces - 1):
                low, high = p * columns + c, (p + 1) * columns
                to[low], to[high] = high, low
            for p in range(pieces):
                rest = [i for i in range(p * columns, (p + 1) * columns) if i not in to]
                to.update(zip(rest, rest[1:] + rest[:1]))
            swaps.append([to[i] for i in range(count)])
        return [lax.ppermute(field, axes, list(enumerate(to))) for to in swaps]

    scratch = [pltpu.VMEM((share, width, width), f32), pltpu.VMEM((8 * share, width), f32)]

    received = exchange(precond)
    rows, cols = inner(precond)
    spill, scaled = call(
        apply_first,
        (meta, table, plan, again, diagonal, times, *received, held(tiles_out), held(rows), held(cols)),
        [vector, vector],
        scratch,
        2 * most_outer,
        scalars=4,
    )

    received = exchange(scaled)
    rows, cols = inner(scaled)
    twice, sums = call(
        apply_second,
        (meta, table, plan, again, source, precond, spill, scaled, times, *received, held(tiles_out), held(rows), held(cols)),
        [vector, few],
        scratch,
        2 * most_outer,
        scalars=4,
    )

    def swap(values, axis, step):
        return lax.ppermute(values, axis, [(i, i ^ step) for i in range(lax.axis_size(axis))])

    def together(values, axis, low, size):
        return tree([values] + [swap(values, axis, low * k) for k in range(1, size)])

    sums = together(sums, "col", 1, columns)
    step = 1
    while pieces // step > 8:
        sums = together(sums, "piece", step, 8)
        step *= 8
    others = [swap(sums, "piece", step * k) for k in range(1, pieces // step)]

    return tuple(call(
        finish,
        (source, precond, spill, scaled, twice, sums, *others),
        [vector, vector],
        scalars=0,
    ))


def solution(mesh):
    placed = (
        P(None, "piece", None),
        P("piece", None),
        P("piece", "col"),
        P(),
        P(),
        P(("piece", "col"), None),
    )
    return jax.shard_map(
        body,
        mesh=mesh,
        in_specs=placed,
        out_specs=(P(("piece", "col"), None), P(("piece", "col"), None)),
        check_vma=False,
    )
```

```python
import jax
import jax.numpy as jnp
import numpy as np
from jax import lax
from jax.experimental import pallas as pl
from jax.experimental.pallas import tpu as pltpu
from jax.sharding import PartitionSpec as P

ITERS = 2
SIDE = 4
LAYER = SIDE * SIDE
REACH = 2 * LAYER
SUB = 8
VMEM = pl.BlockSpec(memory_space=pltpu.VMEM)
SMEM = pl.BlockSpec(memory_space=pltpu.SMEM)
HBM = pl.BlockSpec(memory_space=pltpu.HBM)


def stencil_tables():
    levels = SIDE.bit_length() - 1

    def cell(code):
        across = sum((code >> (2 * level) & 1) << level for level in range(levels))
        along = sum((code >> (2 * level + 1) & 1) << level for level in range(levels))
        return across, along

    place = {cell(code): code for code in range(LAYER)}
    rows = []
    for code in range(LAYER):
        across, along = cell(code)
        rows.append(
            sorted(
                step_z * LAYER + place[across + step_x, along + step_y] - code
                for step_z in (-1, 0, 1)
                for step_y in (-1, 0, 1)
                for step_x in (-1, 0, 1)
                if (across + step_x, along + step_y) in place
            )
        )
    longest = max(len(row) for row in rows)
    offsets = np.zeros((LAYER, longest), np.int32)
    below = np.zeros((LAYER, 2 * REACH + 1), np.int32)
    for code, row in enumerate(rows):
        offsets[code, : len(row)] = row
        for t in range(-REACH, REACH + 1):
            below[code, t + REACH] = sum(offset < t for offset in row)
    return offsets, below


OFFSETS, BELOW = stencil_tables()
WIDEST = OFFSETS.shape[1]
TABLE = np.concatenate([OFFSETS, BELOW], 1)
STRIDE = TABLE.shape[1]
FLAT = np.concatenate([TABLE.reshape(-1), np.zeros(8, np.int32)])
LIMIT = pltpu.CompilerParams(vmem_limit_bytes=8 * 1024 * 1024)


def tile_bounds(share):
    inner = outer = 0
    for first in range(LAYER):
        for live in range(1, share + 1):
            near = far = 0
            for a in range(live):
                code = (first + a) % LAYER
                row = [int(o) for o in OFFSETS[code][: BELOW[code, -1]]]
                near += sum(0 <= a + o and o <= 0 for o in row)
                far += sum(a + o < 0 or a + o >= live for o in row)
            inner, outer = max(inner, near), max(outer, far)
    return inner, outer


def rank(table, code, t):
    return table[code * STRIDE + jnp.clip(t, -REACH, REACH) + REACH + WIDEST]


FIELDS = 6


def write_plan(meta, table, plan, a):
    code = lax.bitwise_and(meta[1] + a, LAYER - 1)
    place = meta[1] + a
    low, split, middle = rank(table, code, -place), rank(table, code, -a), rank(table, code, 0)
    resume, high = rank(table, code, meta[0] - a), rank(table, code, meta[2] - place)
    row = code * STRIDE
    ahead = split - low
    plan[a * FIELDS] = middle - split
    plan[a * FIELDS + 1] = row + split
    plan[a * FIELDS + 2] = ahead + jnp.maximum(high - resume, 0)
    plan[a * FIELDS + 3] = ahead
    plan[a * FIELDS + 4] = row + low
    plan[a * FIELDS + 5] = row + resume - ahead


def write_run(runs, at, a, start, count):
    runs[3 * at], runs[3 * at + 1], runs[3 * at + 2] = a, start, count
    return at + (count > 0).astype(jnp.int32)


def write_runs(meta, table, plan, inner_runs, outer_runs, share):
    inner = outer = total = far = jnp.int32(0)
    for a in range(share):
        write_plan(meta, table, plan, a)
        alive = a < meta[0]
        count, start, count_far, ahead, start_far, start_after = (plan[a * FIELDS + k] for k in range(FIELDS))
        inner = write_run(inner_runs, inner, a, start, jnp.where(alive, count + 1, 0))
        outer = write_run(outer_runs, outer, a, start_far, jnp.where(alive, ahead, 0))
        outer = write_run(outer_runs, outer, a, start_after + ahead, jnp.where(alive, count_far - ahead, 0))
        total = total + jnp.where(alive, count + 1, 0)
        far = far + jnp.where(alive, count_far, 0)
    for runs, at in ((inner_runs, inner), (outer_runs, outer)):
        write_run(runs, at, share, len(FLAT) - 8, jnp.int32(1))
    plan[share * FIELDS] = total
    plan[share * FIELDS + 1] = far
    plan[share * FIELDS + 2] = inner
    plan[share * FIELDS + 3] = outer


def inner_range(plan, table, a):
    start = plan[a * FIELDS + 1]
    return plan[a * FIELDS], lambda t: a + table[start + t]


def outer_range(plan, table, a):
    ahead, start, start_after = (plan[a * FIELDS + k] for k in (3, 4, 5))
    return plan[a * FIELDS + 2], lambda t: a + table[t + jnp.where(t < ahead, start, start_after)]


TURN = 4


def padded_sweep(count, fetch, step, carry):
    def turn(i, state):
        carry, *now = state
        later = [fetch(TURN * (i + 1) + k) for k in range(TURN)]
        return step(now, carry), *later

    state = (carry, *(fetch(k) for k in range(TURN)))
    return lax.fori_loop(0, lax.div(count + (TURN - 1), TURN), turn, state)[0]


def tree(terms):
    while len(terms) > 1:
        terms = [a + b for a, b in zip(terms[::2], terms[1::2])] + terms[len(terms) // 2 * 2 :]
    return terms[0]


def gather(partial, c, term):
    if c < len(partial):
        partial[c] = term
    else:
        partial[c % len(partial)] = partial[c % len(partial)] + term


def pieces_of(width):
    return [slice(c * SUB, (c + 1) * SUB) for c in range(width // SUB)]


def wide(row):
    return jnp.broadcast_to(row, (SUB, row.shape[1]))


def three_parts(values):
    high = values.astype(jnp.bfloat16).astype(jnp.float32)
    rest = values - high
    middle = rest.astype(jnp.bfloat16).astype(jnp.float32)
    return high, middle, rest - middle


def stacked(rows):
    sublane = lax.broadcasted_iota(jnp.int32, rows[0].shape, 0)
    result = jnp.zeros(rows[0].shape, jnp.float32)
    for k, row in enumerate(rows):
        result = jnp.where(sublane == k, row, result)
    return result


def own_side(x):
    size = x[0] * x[0] + x[1] * x[1] + x[2] * x[2]
    one = jnp.ones_like(size)
    high, middle, low = three_parts(stacked([2.0 * x[0], 2.0 * x[1], 2.0 * x[2], one, 0.5 - size]))
    width = size.shape[1]
    rest = jnp.zeros((width - 6 * SUB, width), jnp.float32)
    return jnp.concatenate([high, high, middle, middle, high, low, rest], 0).T.astype(jnp.bfloat16)


def other_side(y):
    size = y[0] * y[0] + y[1] * y[1] + y[2] * y[2]
    one = jnp.ones_like(size)
    high, middle, low = three_parts(stacked([y[0], y[1], y[2], 0.5 - size, one]))
    first = jnp.concatenate([high, middle], 0).astype(jnp.bfloat16)
    last = jnp.concatenate([low, high], 0).astype(jnp.bfloat16)
    width = size.shape[1]
    rest = jnp.zeros((width - 6 * SUB, width), jnp.bfloat16)
    return jnp.concatenate([first, first, last, rest], 0)


GROUP = 6


def flat_tiles(count, runs, most, table, sides, middles, weights, other_at, ahead, tiles, rows_ref, cols_ref):
    share, width = rows_ref.shape[0] - 1, rows_ref.shape[2]
    chunks = pieces_of(width)

    def steps(state):
        found = []
        for _ in range(GROUP):
            run, t = state
            a, start, size = (runs[3 * run + k] for k in range(3))
            found.append((a, a + table[start + t]))
            over = t + 1 >= size
            state = jnp.minimum(run + over.astype(jnp.int32), most), jnp.where(over, 0, t + 1)
        return state, found

    def products(found):
        for k, (a, n) in enumerate(found):
            here = pl.ds(jnp.minimum(a, share - 1), 1)
            near = [wide(other_at(c, n)) - wide(middles[c, here, :]) for c in range(3)]
            side = sides[jnp.minimum(a, share - 1)]
            ahead[k] = jnp.dot(side, other_side(near), preferred_element_type=jnp.float32)

    def turn(i, carry):
        state, found = carry
        state, later = steps(state)
        for k, (a, n) in enumerate(found):
            alone = a == n
            row = jnp.where(alone, share, a)
            own = jnp.minimum(a, share - 1)
            other = wide(other_at(3, n))
            down = [None] * 2
            for c, here in enumerate(chunks):
                left = ahead[k, here, :]
                rest = jnp.maximum(left, 0.0)
                inverse = pltpu.reciprocal((1.01 - left) * (weights[own, here, :] + other), approx=True)
                tile = rest * rest * inverse
                tiles[i * GROUP + k, here, :] = tile
                rows_ref[row, here, :] = rows_ref[row, here, :] + tile
                if cols_ref is not None:
                    gather(down, c, tile)
            if cols_ref is not None:
                there = pl.ds(pl.multiple_of(jnp.where(alone, share, n) * SUB, SUB), SUB)
                cols_ref[there, :] = cols_ref[there, :] + tree(down)
        products(later)
        return state, later

    state, found = steps((jnp.int32(0), jnp.int32(0)))
    products(found)
    lax.fori_loop(0, lax.div(count + (GROUP - 1), GROUP), turn, (state, found))


def spread_columns(out, index, rows):
    count, width = rows.shape
    turned = rows.T
    for a in range(count):
        out[index(a)] = jnp.broadcast_to(turned[:, a : a + 1], (width, width))


def lane_sums(parts, count, width):
    lanes = lax.broadcasted_iota(jnp.int32, (width, width), 1)
    turned = jnp.zeros((width, width), jnp.float32)
    for a in range(count):
        turned = jnp.where(lanes == a, jnp.sum(parts[a], axis=1, keepdims=True), turned)
    return turned.T[:count]


def sub_sums(cols):
    return jnp.sum(cols[...].reshape(-1, SUB, cols.shape[1]), axis=1)


def alive_rows(meta, share, width):
    return lax.broadcasted_iota(jnp.int32, (share, width), 0) < meta[0]


def prepare(
    counts, densities, position_in, phase_in, listed_in, right_side_in, table_in,
    meta, table, hood, near, density, source, first_swap, second_swap, *rest
):
    *times_out, phase, listed, right_side, times, sems = rest
    share, width = source.shape
    capacity = phase.shape[0]
    body_rows = pl.ds(share, capacity)
    copies = [
        pltpu.make_async_copy(phase_in, phase, sems.at[0]),
        pltpu.make_async_copy(position_in, hood.at[pl.ds(0, 3), body_rows, :], sems.at[1]),
        pltpu.make_async_copy(listed_in, listed, sems.at[2]),
        pltpu.make_async_copy(right_side_in, right_side, sems.at[3]),
        pltpu.make_async_copy(table_in, table, sems.at[4]),
    ]
    for copy in copies:
        copy.start()
    piece, column = lax.axis_index("piece"), lax.axis_index("col")
    filled = counts[piece]
    filled_before = counts[jnp.maximum(piece - 1, 0)]
    before = jnp.int32(0)
    total = jnp.int32(0)
    for p in range(counts.shape[0]):
        before = before + jnp.where(p < piece, counts[p], 0)
        total = total + counts[p]
    meta[0] = jnp.clip(filled - column * share, 0, share)
    meta[1] = before + column * share
    meta[2] = total
    meta[3] = column * share
    meta[4] = filled
    meta[5] = filled_before
    own_rows = pl.ds(pl.multiple_of(share + column * share, SUB), share)
    copies[0].wait()
    labels = phase[...]
    whole = sum(jnp.where(labels == k, densities[k], 0.0) for k in range(densities.shape[0]))
    hood[3, body_rows, :] = whole * (width / 2.0)
    density[...] = hood[3, own_rows, :] * (2.0 / width)
    copies[1].wait()
    even = lax.rem(piece, 2) == 0
    for k in range(4):
        tail, head = hood[k, pl.ds(filled, share), :], hood[k, share : 2 * share, :]
        first_swap[k] = jnp.where(even, tail, head)
        second_swap[k] = jnp.where(even, head, tail)
        near[k, 0:share, :] = hood[k, own_rows, :]
    for copy in copies[2:]:
        copy.wait()
    source[...] = jnp.where(alive_rows(meta, share, width), right_side[...], 0.0)
    ids = listed[...]
    own = lax.broadcasted_iota(jnp.int32, ids.shape, 1)
    slot = ids - piece * capacity
    away = slot - own + jnp.where(slot < 0, capacity - filled_before, jnp.where(slot >= capacity, filled - capacity, 0))
    away = jnp.where(ids < 0, -REACH, away) + REACH
    steps = lax.broadcasted_iota(jnp.int32, (2 * REACH, capacity), 0)
    found = tree([jnp.where(steps == away[k : k + 1], 1.0, 0.0) for k in range(ids.shape[0])])
    found = jnp.concatenate([found, jnp.zeros((width - 2 * REACH, capacity), jnp.float32)], 0)
    times[...] = found.T
    for k, out in enumerate(times_out):
        out[...] = times[pl.ds(pl.multiple_of((column ^ k) * share, SUB), share), :]


def finish_tiles(tiles, end):
    for t in range(TURN):
        tiles[end + t] = jnp.zeros(tiles.shape[1:], jnp.float32)


def build_inner(
    meta, table, near, plan, outer_runs, tiles, sides, middles, weights, rows_out, cols_out, self_ref,
    inner_runs, rows_ref, cols_ref, ahead,
):
    share, width = rows_out.shape[0], rows_out.shape[2]
    chunks = pieces_of(width)
    write_runs(meta, table, plan, inner_runs, outer_runs, share)
    for k in range(3):
        first = near[k, 0:share, 0:1]
        middles[k] = jnp.broadcast_to(jnp.floor(first) + 0.5, (share, width))
    for a in range(share):
        here = slice(a, a + 1)
        sides[a] = own_side([wide(near[k, here, :] - middles[k, here, :]) for k in range(3)])
    spread_columns(weights, lambda a: a, near[3, 0:share, :])
    cols_ref[...] = jnp.zeros_like(cols_ref)
    rows_ref[...] = jnp.zeros_like(rows_ref)
    count = plan[share * FIELDS]
    flat_tiles(
        count, inner_runs, plan[share * FIELDS + 2], table, sides, middles, weights,
        lambda k, n: near[k, pl.ds(n, 1), :], ahead, tiles, rows_ref, cols_ref,
    )
    finish_tiles(tiles, count)
    lane = lax.broadcasted_iota(jnp.int32, (SUB, width), 1)
    sublane = lax.broadcasted_iota(jnp.int32, (SUB, width), 0)

    def block(a, at):
        at = at + plan[a * FIELDS]
        down = [None] * 4
        for c, here in enumerate(chunks):
            tile = jnp.where(lane == sublane + c * SUB, 0.0, tiles[at, here, :])
            tiles[at, here, :] = tile
            gather(down, c, tile)
        self_ref[pl.ds(pl.multiple_of(a * SUB, SUB), SUB), :] = tree(down)
        return at + 1

    lax.fori_loop(0, meta[0], block, 0)
    rows_out[...] = rows_ref[0:share]
    cols_out[...] = cols_ref[0 : share * SUB, :]


def factor(times, a, n):
    lane = lax.broadcasted_iota(jnp.int32, (1, times.shape[1]), 1)
    return jnp.sum(jnp.where(lane == n - a + REACH, times[pl.ds(a, 1), :], 0.0), axis=1, keepdims=True)


def either(flag, run):
    @pl.when(flag == 0)
    def _():
        run(False)

    @pl.when(flag != 0)
    def _():
        run(True)


def build_outer(
    meta, table, plan, runs, around, first, second, density, source, tiles_in, sides, middles, weights,
    rows_ref, cols_ref, self_ref, *rest
):
    *times_in, again_ref, tiles, diagonal_ref, precond_ref, times, alone_ref, hood, work, sums_ref, extra, ahead = rest
    share, width = diagonal_ref.shape
    base, filled = meta[3], meta[4]
    even = lax.rem(lax.axis_index("piece"), 2) == 0
    for k in range(4):
        hood[k, 0:share, :] = jnp.where(even, second[k], first[k])
        hood[k, share:, :] = around[k, share:, :]
        hood[k, pl.ds(share + filled, share), :] = jnp.where(even, first[k], second[k])
    alive = alive_rows(meta, share, width)
    often = jnp.where(alive, tree([ref[...] for ref in times_in]), 0.0)
    times[...] = often
    lane = lax.broadcasted_iota(jnp.int32, (share, width), 1)
    again = jnp.max(jnp.where((lane == REACH) | (lane == 0), 0.0, often)) > 1.5
    again_ref[0] = again.astype(jnp.int32)


    work[...] = jnp.zeros_like(work)
    count = plan[share * FIELDS + 1]
    flat_tiles(
        count, runs, plan[share * FIELDS + 3], table, sides, middles, weights,
        lambda k, n: hood[k, pl.ds(base + share + n, 1), :], ahead, tiles, work, None,
    )
    finish_tiles(tiles, count)
    sums_ref[...] = lane_sums([rows_ref[a] + work[a] for a in range(share)], share, width) + sub_sums(cols_ref)

    @pl.when(again)
    def _():
        extra[...] = jnp.zeros_like(extra)
        work[...] = jnp.zeros_like(work)

        def block(a, state):
            count, place_of = inner_range(plan, table, a)

            def inner(t, at):
                n = place_of(t)
                tile = tiles_in[at]
                work[a] = work[a] + tile * factor(times, a, n)
                there = pl.ds(n, 1)
                down = jnp.sum(tile, axis=0, keepdims=True)
                extra[there, :] = extra[there, :] + down * factor(times, n, a)
                return at + 1

            at = lax.fori_loop(0, count, inner, state[0]) + 1
            count, place_far = outer_range(plan, table, a)

            def outer(t, at):
                work[a] = work[a] + tiles[at] * factor(times, a, place_far(t))
                return at + 1

            return at, lax.fori_loop(0, count, outer, state[1])

        lax.fori_loop(0, meta[0], block, (0, 0))
        sums_ref[...] = lane_sums(work, share, width) + extra[...]

    alone = jnp.sum(jnp.where(lane == REACH, often, 0.0), axis=1, keepdims=True)
    alone_ref[...] = jnp.broadcast_to(alone, (share, width))
    pairs = jnp.where(alive, sums_ref[...] + sub_sums(self_ref) * alone, 0.0)
    diagonal = 1.0 / density[...] + pairs
    diagonal_ref[...] = diagonal
    precond_ref[...] = source[...] / diagonal


def apply_inner(meta, table, plan, again, field, alone, times, tiles, rows_ref, cols_ref, spread, near, lone, cols):
    share, width = field.shape
    chunks = pieces_of(width)
    near[0:share, :] = field[...]
    near[share:, :] = jnp.zeros((SUB, width), jnp.float32)
    lone[...] = field[...] * alone[...]
    spread_columns(spread, lambda a: a, field[...])
    cols[...] = jnp.zeros_like(cols)

    def run(weighted):
        def block(a, at):
            count, place_of = inner_range(plan, table, a)

            def fetch(t):
                n = jnp.where(t < count, place_of(t), share)
                return n, wide(near[pl.ds(n, 1), :])

            def pairs(fetched, carry):
                at, sums = carry
                if weighted:
                    fetched = [(n, value * factor(times, a, jnp.minimum(n, share - 1))) for n, value in fetched]
                down = [[None] * 2 for _ in fetched]
                result = []
                for c, (here, total) in enumerate(zip(chunks, sums)):
                    own = spread[a, here, :]
                    found = []
                    for t, (_, value) in enumerate(fetched):
                        tile = tiles[at + t, here, :]
                        gather(down[t], c, tile * own)
                        found.append(tile * value)
                    result.append(total + tree(found))
                for (n, _), partial in zip(fetched, down):
                    there = pl.ds(pl.multiple_of(n * SUB, SUB), SUB)
                    partial = tree(partial)
                    if weighted:
                        partial = partial * factor(times, jnp.minimum(n, share - 1), a)
                    cols[there, :] = cols[there, :] + partial
                return at + len(fetched), result

            zero = jnp.zeros((SUB, width), jnp.float32)
            _, sums = padded_sweep(count, fetch, pairs, (at, [zero] * len(chunks)))
            at = at + count
            value = wide(lone[pl.ds(a, 1), :])
            for here, old in zip(chunks, sums):
                rows_ref[a, here, :] = old + tiles[at, here, :] * value
            return at + 1

        lax.fori_loop(0, meta[0], block, 0)

    either(again[0], run)
    cols_ref[...] = cols[0 : share * SUB, :]


def apply_outer(meta, table, plan, again, received, times, tiles, rows_ref, cols_ref, work, hood):
    first, second, *ends = received
    columns = len(received)
    share, width = first.shape
    chunks = pieces_of(width)
    base, filled = meta[3], meta[4]
    column = lax.div(base, share)
    odd = lax.rem(column, 2) == 1
    before = jnp.where(odd, first[...], second[...])
    after = jnp.where(odd, second[...], first[...])
    own = 3 * share
    for c, end in enumerate(ends, 1):
        hood[pl.ds(own - meta[5] + c * share, share), :] = end[...]
    from_last = own - meta[5] + (columns - 1) * share
    hood[pl.ds(jnp.where(column == 0, from_last, own - share), share), :] = before
    hood[own + share : own + 2 * share, :] = after
    head = after
    for c, end in enumerate(ends, 1):
        head = jnp.where(column == c, end[...], head)
    hood[pl.ds(own + jnp.clip(filled - base, 0, 2 * share), share), :] = head
    nothing = hood.shape[0] - SUB
    hood[nothing:, :] = jnp.zeros((SUB, width), jnp.float32)

    def run(weighted):
        def block(a, at):
            count, place_of = outer_range(plan, table, a)

            def fetch(t):
                place = place_of(t)
                value = hood[pl.ds(jnp.where(t < count, own + place, nothing), 1), :]
                if weighted:
                    value = value * factor(times, a, place)
                return wide(value)

            def pairs(values, carry):
                at, sums = carry
                result = []
                for here, total in zip(chunks, sums):
                    result.append(total + tree([tiles[at + t, here, :] * value for t, value in enumerate(values)]))
                return at + len(values), result

            _, sums = padded_sweep(count, fetch, pairs, (at, [rows_ref[a, here, :] for here in chunks]))
            for here, values in zip(chunks, sums):
                work[a, here, :] = values
            return at + count

        lax.fori_loop(0, meta[0], block, 0)

    either(again[0], run)
    return jnp.where(alive_rows(meta, share, width), lane_sums(work, share, width) + sub_sums(cols_ref), 0.0)


def apply_first(meta, table, plan, again, diagonal, times, *rest):
    *received, tiles, rows_ref, cols_ref, spill_ref, scaled_ref, work, hood = rest
    spill = apply_outer(meta, table, plan, again, received, times, tiles, rows_ref, cols_ref, work, hood)
    spill_ref[...] = spill
    scaled_ref[...] = spill / diagonal[...]


def apply_second(meta, table, plan, again, source, precond, spill, scaled, times, *rest):
    *received, tiles, rows_ref, cols_ref, twice_ref, sums_ref, work, hood = rest
    twice = apply_outer(meta, table, plan, again, received, times, tiles, rows_ref, cols_ref, work, hood)
    twice_ref[...] = twice
    share, width = twice.shape
    lane = lax.broadcasted_iota(jnp.int32, (1, width), 1)
    sums = jnp.zeros((1, width), jnp.float32)
    pairs = ((source[...], precond[...]), (spill[...], precond[...]), (spill[...], scaled[...]), (scaled[...], twice))
    for k, (first, second) in enumerate(pairs):
        along = jnp.sum(first * second, axis=0, keepdims=True)
        sums = jnp.where(lane == k, jnp.sum(along, axis=1, keepdims=True), sums)
    sums_ref[...] = wide(sums)


def finish(source, precond, spill, scaled, twice, *rest):
    *parts, solution_ref, residual_ref = rest
    sums = tree([ref[...] for ref in parts])

    def pick(k):
        return sums[0:1, k : k + 1]

    weighted, cross, square, last = pick(0), pick(1), pick(2), pick(3)
    part = cross / weighted
    advance = 1.0 / (1.0 - part)
    keep = -part * advance
    weighted_next = advance * advance * (square - cross * part)
    bent = keep * keep * cross + 2.0 * keep * advance * square + advance * advance * last
    blend = weighted_next / weighted
    advance_next = weighted_next / (weighted_next - bent - blend * weighted_next / advance)
    residual = keep * source[...] + advance * spill[...]
    next_precond = keep * precond[...] + advance * scaled[...]
    direction = next_precond + blend * precond[...]
    image = residual - keep * spill[...] - advance * twice[...] + blend * (source[...] - spill[...])
    solution_ref[...] = advance * precond[...] + advance_next * direction
    residual_ref[...] = residual - advance_next * image


def held(array):
    return pltpu.with_memory_space_constraint(array, pltpu.VMEM)


def body(positions, phase, neighbours, counts, phase_density, right_side):
    capacity, width = phase.shape
    columns = lax.axis_size("col")
    pieces = lax.axis_size("piece")
    share = capacity // columns
    f32 = jnp.float32
    vector = jax.ShapeDtypeStruct((share, width), f32)
    few = jax.ShapeDtypeStruct((SUB, width), f32)
    message = jax.ShapeDtypeStruct((4, share, width), f32)
    most_inner, most_outer = tile_bounds(share)
    inner_tiles = pltpu.VMEM((most_inner + GROUP, width, width), f32)
    outer_tiles = pltpu.VMEM((most_outer + GROUP, width, width), f32)
    ahead = pltpu.VMEM((GROUP, width, width), f32)
    square_more = pltpu.VMEM((share + 1, width, width), f32)
    square = pltpu.VMEM((share, width, width), f32)
    narrow = pltpu.VMEM((share * SUB, width), f32)
    table = jnp.asarray(FLAT)

    def call(kernel, args, outs, scratch=(), work=0, scalars=2, far=0, **more):
        return pl.pallas_call(
            kernel,
            out_shape=outs,
            in_specs=[SMEM] * scalars + [HBM] * far + [VMEM] * (len(args) - scalars - far),
            out_specs=[SMEM if getattr(o, "memory_space", None) == pltpu.SMEM else VMEM for o in outs],
            scratch_shapes=scratch,
            compiler_params=LIMIT,
            cost_estimate=pl.CostEstimate(flops=work * width * width, bytes_accessed=0, transcendentals=0),
            name=kernel.__name__,
            **more,
        )(*args)

    def away(array):
        return pltpu.with_memory_space_constraint(array, pltpu.HBM)

    around = jax.ShapeDtypeStruct((4, capacity + 2 * share, width), f32)
    near = jax.ShapeDtypeStruct((4, 2 * share, width), f32)
    far = [away(array) for array in (positions, phase, neighbours.T, right_side, table)]
    meta, table, around, near, density, source, first, second, *times = call(
        prepare,
        (away(counts), away(phase_density), *far),
        [pltpu.SMEM((8,), jnp.int32), pltpu.SMEM(table.shape, jnp.int32), around, near, vector, vector, message, message]
        + [vector] * columns,
        [pltpu.VMEM(phase.shape, jnp.int32), pltpu.VMEM(far[2].shape, jnp.int32), pltpu.VMEM((share, width), f32),
         pltpu.VMEM((capacity, width), f32), pltpu.SemaphoreType.DMA((5,))],
        far=len(far),
    )
    meta, table = (pltpu.with_memory_space_constraint(array, pltpu.SMEM) for array in (meta, table))
    first = lax.ppermute(first, "piece", [(i, i ^ 1) for i in range(pieces)])
    second = lax.ppermute(second, "piece", [(i, ((i ^ 1) + (1 if i % 2 else -1) * 2) % pieces) for i in range(pieces)])
    times = [lax.ppermute(t, "col", [(i, i ^ k) for i in range(columns)]) if k else t for k, t in enumerate(times)]

    plan, runs, tiles_in, sides, middles, weights, rows, cols, selfs = call(
        build_inner,
        (meta, table, near),
        [pltpu.SMEM((share * FIELDS + 4,), jnp.int32), pltpu.SMEM((6 * share + 3,), jnp.int32), inner_tiles,
         pltpu.VMEM((share, width, width), jnp.bfloat16), pltpu.VMEM((3, share, width), f32), square, square, narrow, narrow],
        [pltpu.SMEM((3 * share + 3,), jnp.int32), square_more, pltpu.VMEM(((share + 1) * SUB, width), f32), ahead],
        16 * most_inner,
    )
    plan, runs = (pltpu.with_memory_space_constraint(array, pltpu.SMEM) for array in (plan, runs))
    again, tiles_out, diagonal, precond, times, alone = call(
        build_outer,
        (meta, table, plan, runs, around, first, second, density, source,
         held(tiles_in), held(sides), held(middles), held(weights), held(rows), held(cols), held(selfs), *times),
        [pltpu.SMEM((1,), jnp.int32), outer_tiles, vector, vector, vector, vector],
        [pltpu.VMEM((4, capacity + 2 * share, width), f32), square_more]
        + [pltpu.VMEM((share, width), f32)] * 2 + [ahead],
        16 * most_outer,
        scalars=4,
    )
    again = pltpu.with_memory_space_constraint(again, pltpu.SMEM)

    def inner(field):
        return call(
            apply_inner,
            (meta, table, plan, again, field, alone, times, held(tiles_in)),
            [square, narrow],
            [pltpu.VMEM((share, width, width), f32), pltpu.VMEM((share + SUB, width), f32), pltpu.VMEM((share, width), f32),
             pltpu.VMEM(((share + 1) * SUB, width), f32)],
            4 * most_inner,
            scalars=4,
        )

    def exchange(field):
        axes = ("piece", "col")
        count = pieces * columns
        swaps = [[i ^ 1 for i in range(count)], [i - 1 if i % 2 == 0 else i + 1 for i in range(count)]]
        swaps[1][0], swaps[1][-1] = count - 1, 0
        for c in range(1, columns - 1):
            to = {}
            for p in range(pieces - 1):
                low, high = p * columns + c, (p + 1) * columns
                to[low], to[high] = high, low
            for p in range(pieces):
                rest = [i for i in range(p * columns, (p + 1) * columns) if i not in to]
                to.update(zip(rest, rest[1:] + rest[:1]))
            swaps.append([to[i] for i in range(count)])
        return [lax.ppermute(field, axes, list(enumerate(to))) for to in swaps]

    scratch = [pltpu.VMEM((share, width, width), f32), pltpu.VMEM((8 * share, width), f32)]

    received = exchange(precond)
    rows, cols = inner(precond)
    spill, scaled = call(
        apply_first,
        (meta, table, plan, again, diagonal, times, *received, held(tiles_out), held(rows), held(cols)),
        [vector, vector],
        scratch,
        2 * most_outer,
        scalars=4,
    )

    received = exchange(scaled)
    rows, cols = inner(scaled)
    twice, sums = call(
        apply_second,
        (meta, table, plan, again, source, precond, spill, scaled, times, *received, held(tiles_out), held(rows), held(cols)),
        [vector, few],
        scratch,
        2 * most_outer,
        scalars=4,
    )

    def swap(values, axis, step):
        return lax.ppermute(values, axis, [(i, i ^ step) for i in range(lax.axis_size(axis))])

    def together(values, axis, low, size):
        return tree([values] + [swap(values, axis, low * k) for k in range(1, size)])

    sums = together(sums, "col", 1, columns)
    step = 1
    while pieces // step > 8:
        sums = together(sums, "piece", step, 8)
        step *= 8
    others = [swap(sums, "piece", step * k) for k in range(1, pieces // step)]

    return tuple(call(
        finish,
        (source, precond, spill, scaled, twice, sums, *others),
        [vector, vector],
        scalars=0,
    ))


def solution(mesh):
    placed = (
        P(None, "piece", None),
        P("piece", None),
        P("piece", "col"),
        P(),
        P(),
        P(("piece", "col"), None),
    )
    return jax.shard_map(
        body,
        mesh=mesh,
        in_specs=placed,
        out_specs=(P(("piece", "col"), None), P(("piece", "col"), None)),
        check_vma=False,
    )
```

```python
import jax
import jax.numpy as jnp
import numpy as np
from jax import lax
from jax.experimental import pallas as pl
from jax.experimental.pallas import tpu as pltpu
from jax.sharding import PartitionSpec as P

ITERS = 2
SIDE = 4
LAYER = SIDE * SIDE
REACH = 2 * LAYER
SUB = 8
VMEM = pl.BlockSpec(memory_space=pltpu.VMEM)
SMEM = pl.BlockSpec(memory_space=pltpu.SMEM)
HBM = pl.BlockSpec(memory_space=pltpu.HBM)


def stencil_tables():
    levels = SIDE.bit_length() - 1

    def cell(code):
        across = sum((code >> (2 * level) & 1) << level for level in range(levels))
        along = sum((code >> (2 * level + 1) & 1) << level for level in range(levels))
        return across, along

    place = {cell(code): code for code in range(LAYER)}
    rows = []
    for code in range(LAYER):
        across, along = cell(code)
        rows.append(
            sorted(
                step_z * LAYER + place[across + step_x, along + step_y] - code
                for step_z in (-1, 0, 1)
                for step_y in (-1, 0, 1)
                for step_x in (-1, 0, 1)
                if (across + step_x, along + step_y) in place
            )
        )
    longest = max(len(row) for row in rows)
    offsets = np.zeros((LAYER, longest), np.int32)
    below = np.zeros((LAYER, 2 * REACH + 1), np.int32)
    for code, row in enumerate(rows):
        offsets[code, : len(row)] = row
        for t in range(-REACH, REACH + 1):
            below[code, t + REACH] = sum(offset < t for offset in row)
    return offsets, below


OFFSETS, BELOW = stencil_tables()
WIDEST = OFFSETS.shape[1]
TABLE = np.concatenate([OFFSETS, BELOW], 1)
STRIDE = TABLE.shape[1]
FLAT = np.concatenate([TABLE.reshape(-1), np.zeros(8, np.int32)])
LIMIT = pltpu.CompilerParams(vmem_limit_bytes=8 * 1024 * 1024)


def tile_bounds(share):
    inner = outer = 0
    for first in range(LAYER):
        for live in range(1, share + 1):
            near = far = 0
            for a in range(live):
                code = (first + a) % LAYER
                row = [int(o) for o in OFFSETS[code][: BELOW[code, -1]]]
                near += sum(0 <= a + o and o <= 0 for o in row)
                far += sum(a + o < 0 or a + o >= live for o in row)
            inner, outer = max(inner, near), max(outer, far)
    return inner, outer


def rank(table, code, t):
    return table[code * STRIDE + jnp.clip(t, -REACH, REACH) + REACH + WIDEST]


FIELDS = 6


def write_plan(meta, table, plan, a):
    code = lax.bitwise_and(meta[1] + a, LAYER - 1)
    place = meta[1] + a
    low, split, middle = rank(table, code, -place), rank(table, code, -a), rank(table, code, 0)
    resume, high = rank(table, code, meta[0] - a), rank(table, code, meta[2] - place)
    row = code * STRIDE
    ahead = split - low
    plan[a * FIELDS] = middle - split
    plan[a * FIELDS + 1] = row + split
    plan[a * FIELDS + 2] = ahead + jnp.maximum(high - resume, 0)
    plan[a * FIELDS + 3] = ahead
    plan[a * FIELDS + 4] = row + low
    plan[a * FIELDS + 5] = row + resume - ahead


def write_run(runs, at, a, start, count):
    runs[3 * at], runs[3 * at + 1], runs[3 * at + 2] = a, start, count
    return at + (count > 0).astype(jnp.int32)


def write_runs(meta, table, plan, inner_runs, outer_runs, share):
    inner = outer = total = far = jnp.int32(0)
    for a in range(share):
        write_plan(meta, table, plan, a)
        alive = a < meta[0]
        count, start, count_far, ahead, start_far, start_after = (plan[a * FIELDS + k] for k in range(FIELDS))
        inner = write_run(inner_runs, inner, a, start, jnp.where(alive, count + 1, 0))
        outer = write_run(outer_runs, outer, a, start_far, jnp.where(alive, ahead, 0))
        outer = write_run(outer_runs, outer, a, start_after + ahead, jnp.where(alive, count_far - ahead, 0))
        total = total + jnp.where(alive, count + 1, 0)
        far = far + jnp.where(alive, count_far, 0)
    for runs, at in ((inner_runs, inner), (outer_runs, outer)):
        write_run(runs, at, share, len(FLAT) - 8, jnp.int32(1))
    plan[share * FIELDS] = total
    plan[share * FIELDS + 1] = far
    plan[share * FIELDS + 2] = inner
    plan[share * FIELDS + 3] = outer


def inner_range(plan, table, a):
    start = plan[a * FIELDS + 1]
    return plan[a * FIELDS], lambda t: a + table[start + t]


def outer_range(plan, table, a):
    ahead, start, start_after = (plan[a * FIELDS + k] for k in (3, 4, 5))
    return plan[a * FIELDS + 2], lambda t: a + table[t + jnp.where(t < ahead, start, start_after)]


TURN = 4


def padded_sweep(count, fetch, step, carry):
    def turn(i, state):
        carry, *now = state
        later = [fetch(TURN * (i + 1) + k) for k in range(TURN)]
        return step(now, carry), *later

    state = (carry, *(fetch(k) for k in range(TURN)))
    return lax.fori_loop(0, lax.div(count + (TURN - 1), TURN), turn, state)[0]


def tree(terms):
    while len(terms) > 1:
        terms = [a + b for a, b in zip(terms[::2], terms[1::2])] + terms[len(terms) // 2 * 2 :]
    return terms[0]


def gather(partial, c, term):
    if c < len(partial):
        partial[c] = term
    else:
        partial[c % len(partial)] = partial[c % len(partial)] + term


def pieces_of(width):
    return [slice(c * SUB, (c + 1) * SUB) for c in range(width // SUB)]


def wide(row):
    return jnp.broadcast_to(row, (SUB, row.shape[1]))


def three_parts(values):
    high = values.astype(jnp.bfloat16).astype(jnp.float32)
    rest = values - high
    middle = rest.astype(jnp.bfloat16).astype(jnp.float32)
    return high, middle, rest - middle


def stacked(rows):
    sublane = lax.broadcasted_iota(jnp.int32, rows[0].shape, 0)
    result = jnp.zeros(rows[0].shape, jnp.float32)
    for k, row in enumerate(rows):
        result = jnp.where(sublane == k, row, result)
    return result


HALF = 64


def own_side(x):
    size = x[0] * x[0] + x[1] * x[1] + x[2] * x[2]
    one = jnp.ones_like(size)
    high, middle, low = three_parts(stacked([2.0 * x[0], 2.0 * x[1], 2.0 * x[2], one, 0.5 - size]))
    rest = jnp.zeros((HALF - 6 * SUB, size.shape[1]), jnp.float32)
    return jnp.concatenate([high, high, middle, middle, high, low, rest], 0)


def other_side(y):
    size = y[0] * y[0] + y[1] * y[1] + y[2] * y[2]
    one = jnp.ones_like(size)
    high, middle, low = three_parts(stacked([y[0], y[1], y[2], 0.5 - size, one]))
    first = jnp.concatenate([high, middle], 0).astype(jnp.bfloat16)
    last = jnp.concatenate([low, high], 0).astype(jnp.bfloat16)
    return jnp.concatenate([first, first, last, jnp.zeros((HALF - 6 * SUB, size.shape[1]), jnp.bfloat16)], 0)


GROUP = 8


def flat_tiles(count, runs, most, table, sides, middles, weights, other_at, ahead, tiles, rows_ref, cols_ref):
    share, width = rows_ref.shape[0] - 1, rows_ref.shape[2]
    chunks = pieces_of(width)

    def steps(state):
        found = []
        for _ in range(GROUP):
            run, t = state
            a, start, size = (runs[3 * run + k] for k in range(3))
            found.append((a, a + table[start + t]))
            over = t + 1 >= size
            state = jnp.minimum(run + over.astype(jnp.int32), most), jnp.where(over, 0, t + 1)
        return state, found

    def other_of(a, n):
        here = pl.ds(a, 1)
        return other_side([wide(other_at(c, n)) - wide(middles[c, here, :]) for c in range(3)])

    def products(found):
        none = jnp.zeros((HALF, width), jnp.bfloat16)
        for k in range(0, GROUP, 2):
            (a, n), (b, m) = ((jnp.minimum(a, share - 1), n) for a, n in found[k : k + 2])
            left = jnp.concatenate([other_of(a, n), none], 0)
            right = jnp.concatenate([none, other_of(b, m)], 0)
            both = jnp.dot(
                sides[0, a] + sides[1, b], jnp.concatenate([left, right], 1), preferred_element_type=jnp.float32
            )
            ahead[k] = both[:, :width]
            ahead[k + 1] = both[:, width:]

    def turn(i, carry):
        state, found = carry
        state, later = steps(state)
        for k, (a, n) in enumerate(found):
            alone = a == n
            row = jnp.where(alone, share, a)
            own = jnp.minimum(a, share - 1)
            other = wide(other_at(3, n))
            down = [None] * 2
            for c, here in enumerate(chunks):
                left = ahead[k, here, :]
                rest = jnp.maximum(left, 0.0)
                inverse = pltpu.reciprocal((1.01 - left) * (weights[own, here, :] + other), approx=True)
                tile = rest * rest * inverse
                tiles[i * GROUP + k, here, :] = tile
                rows_ref[row, here, :] = rows_ref[row, here, :] + tile
                if cols_ref is not None:
                    gather(down, c, tile)
            if cols_ref is not None:
                there = pl.ds(pl.multiple_of(jnp.where(alone, share, n) * SUB, SUB), SUB)
                cols_ref[there, :] = cols_ref[there, :] + tree(down)
        products(later)
        return state, later

    state, found = steps((jnp.int32(0), jnp.int32(0)))
    products(found)
    lax.fori_loop(0, lax.div(count + (GROUP - 1), GROUP), turn, (state, found))


def spread_columns(out, index, rows):
    count, width = rows.shape
    turned = rows.T
    for a in range(count):
        out[index(a)] = jnp.broadcast_to(turned[:, a : a + 1], (width, width))


def lane_sums(parts, count, width):
    lanes = lax.broadcasted_iota(jnp.int32, (width, width), 1)
    turned = jnp.zeros((width, width), jnp.float32)
    for a in range(count):
        turned = jnp.where(lanes == a, jnp.sum(parts[a], axis=1, keepdims=True), turned)
    return turned.T[:count]


def sub_sums(cols):
    return jnp.sum(cols[...].reshape(-1, SUB, cols.shape[1]), axis=1)


def alive_rows(meta, share, width):
    return lax.broadcasted_iota(jnp.int32, (share, width), 0) < meta[0]


def prepare(
    counts, densities, position_in, phase_in, listed_in, right_side_in, table_in,
    meta, table, hood, near, density, source, first_swap, second_swap, *rest
):
    *times_out, phase, listed, right_side, times, sems = rest
    share, width = source.shape
    capacity = phase.shape[0]
    body_rows = pl.ds(share, capacity)
    copies = [
        pltpu.make_async_copy(phase_in, phase, sems.at[0]),
        pltpu.make_async_copy(position_in, hood.at[pl.ds(0, 3), body_rows, :], sems.at[1]),
        pltpu.make_async_copy(listed_in, listed, sems.at[2]),
        pltpu.make_async_copy(right_side_in, right_side, sems.at[3]),
        pltpu.make_async_copy(table_in, table, sems.at[4]),
    ]
    for copy in copies:
        copy.start()
    piece, column = lax.axis_index("piece"), lax.axis_index("col")
    filled = counts[piece]
    filled_before = counts[jnp.maximum(piece - 1, 0)]
    before = jnp.int32(0)
    total = jnp.int32(0)
    for p in range(counts.shape[0]):
        before = before + jnp.where(p < piece, counts[p], 0)
        total = total + counts[p]
    meta[0] = jnp.clip(filled - column * share, 0, share)
    meta[1] = before + column * share
    meta[2] = total
    meta[3] = column * share
    meta[4] = filled
    meta[5] = filled_before
    own_rows = pl.ds(pl.multiple_of(share + column * share, SUB), share)
    copies[0].wait()
    labels = phase[...]
    whole = sum(jnp.where(labels == k, densities[k], 0.0) for k in range(densities.shape[0]))
    hood[3, body_rows, :] = whole * (width / 2.0)
    density[...] = hood[3, own_rows, :] * (2.0 / width)
    copies[1].wait()
    even = lax.rem(piece, 2) == 0
    for k in range(4):
        tail, head = hood[k, pl.ds(filled, share), :], hood[k, share : 2 * share, :]
        first_swap[k] = jnp.where(even, tail, head)
        second_swap[k] = jnp.where(even, head, tail)
        near[k, 0:share, :] = hood[k, own_rows, :]
    for copy in copies[2:]:
        copy.wait()
    source[...] = jnp.where(alive_rows(meta, share, width), right_side[...], 0.0)
    ids = listed[...]
    own = lax.broadcasted_iota(jnp.int32, ids.shape, 1)
    slot = ids - piece * capacity
    away = slot - own + jnp.where(slot < 0, capacity - filled_before, jnp.where(slot >= capacity, filled - capacity, 0))
    away = jnp.where(ids < 0, -REACH, away) + REACH
    steps = lax.broadcasted_iota(jnp.int32, (2 * REACH, capacity), 0)
    found = tree([jnp.where(steps == away[k : k + 1], 1.0, 0.0) for k in range(ids.shape[0])])
    found = jnp.concatenate([found, jnp.zeros((width - 2 * REACH, capacity), jnp.float32)], 0)
    times[...] = found.T
    for k, out in enumerate(times_out):
        out[...] = times[pl.ds(pl.multiple_of((column ^ k) * share, SUB), share), :]


def finish_tiles(tiles, end):
    for t in range(TURN):
        tiles[end + t] = jnp.zeros(tiles.shape[1:], jnp.float32)


def build_inner(
    meta, table, near, plan, outer_runs, tiles, sides, middles, weights, rows_out, cols_out, self_ref,
    inner_runs, rows_ref, cols_ref, ahead,
):
    share, width = rows_out.shape[0], rows_out.shape[2]
    chunks = pieces_of(width)
    write_runs(meta, table, plan, inner_runs, outer_runs, share)
    for k in range(3):
        first = near[k, 0:share, 0:1]
        middles[k] = jnp.broadcast_to(jnp.floor(first) + 0.5, (share, width))
    for a in range(share):
        here = slice(a, a + 1)
        side = own_side([wide(near[k, here, :] - middles[k, here, :]) for k in range(3)])
        none = jnp.zeros((width - HALF, width), jnp.float32)
        sides[0, a] = jnp.concatenate([side, none], 0).T.astype(jnp.bfloat16)
        sides[1, a] = jnp.concatenate([none, side], 0).T.astype(jnp.bfloat16)
    spread_columns(weights, lambda a: a, near[3, 0:share, :])
    cols_ref[...] = jnp.zeros_like(cols_ref)
    rows_ref[...] = jnp.zeros_like(rows_ref)
    count = plan[share * FIELDS]
    flat_tiles(
        count, inner_runs, plan[share * FIELDS + 2], table, sides, middles, weights,
        lambda k, n: near[k, pl.ds(n, 1), :], ahead, tiles, rows_ref, cols_ref,
    )
    finish_tiles(tiles, count)
    lane = lax.broadcasted_iota(jnp.int32, (SUB, width), 1)
    sublane = lax.broadcasted_iota(jnp.int32, (SUB, width), 0)

    def block(a, at):
        at = at + plan[a * FIELDS]
        down = [None] * 4
        for c, here in enumerate(chunks):
            tile = jnp.where(lane == sublane + c * SUB, 0.0, tiles[at, here, :])
            tiles[at, here, :] = tile
            gather(down, c, tile)
        self_ref[pl.ds(pl.multiple_of(a * SUB, SUB), SUB), :] = tree(down)
        return at + 1

    lax.fori_loop(0, meta[0], block, 0)
    rows_out[...] = rows_ref[0:share]
    cols_out[...] = cols_ref[0 : share * SUB, :]


def factor(times, a, n):
    lane = lax.broadcasted_iota(jnp.int32, (1, times.shape[1]), 1)
    return jnp.sum(jnp.where(lane == n - a + REACH, times[pl.ds(a, 1), :], 0.0), axis=1, keepdims=True)


def either(flag, run):
    @pl.when(flag == 0)
    def _():
        run(False)

    @pl.when(flag != 0)
    def _():
        run(True)


def build_outer(
    meta, table, plan, runs, around, first, second, density, source, tiles_in, sides, middles, weights,
    rows_ref, cols_ref, self_ref, *rest
):
    *times_in, again_ref, tiles, diagonal_ref, precond_ref, times, alone_ref, hood, work, sums_ref, extra, ahead = rest
    share, width = diagonal_ref.shape
    base, filled = meta[3], meta[4]
    even = lax.rem(lax.axis_index("piece"), 2) == 0
    for k in range(4):
        hood[k, 0:share, :] = jnp.where(even, second[k], first[k])
        hood[k, share:, :] = around[k, share:, :]
        hood[k, pl.ds(share + filled, share), :] = jnp.where(even, first[k], second[k])
    alive = alive_rows(meta, share, width)
    often = jnp.where(alive, tree([ref[...] for ref in times_in]), 0.0)
    times[...] = often
    lane = lax.broadcasted_iota(jnp.int32, (share, width), 1)
    again = jnp.max(jnp.where((lane == REACH) | (lane == 0), 0.0, often)) > 1.5
    again_ref[0] = again.astype(jnp.int32)


    work[...] = jnp.zeros_like(work)
    count = plan[share * FIELDS + 1]
    flat_tiles(
        count, runs, plan[share * FIELDS + 3], table, sides, middles, weights,
        lambda k, n: hood[k, pl.ds(base + share + n, 1), :], ahead, tiles, work, None,
    )
    finish_tiles(tiles, count)
    sums_ref[...] = lane_sums([rows_ref[a] + work[a] for a in range(share)], share, width) + sub_sums(cols_ref)

    @pl.when(again)
    def _():
        extra[...] = jnp.zeros_like(extra)
        work[...] = jnp.zeros_like(work)

        def block(a, state):
            count, place_of = inner_range(plan, table, a)

            def inner(t, at):
                n = place_of(t)
                tile = tiles_in[at]
                work[a] = work[a] + tile * factor(times, a, n)
                there = pl.ds(n, 1)
                down = jnp.sum(tile, axis=0, keepdims=True)
                extra[there, :] = extra[there, :] + down * factor(times, n, a)
                return at + 1

            at = lax.fori_loop(0, count, inner, state[0]) + 1
            count, place_far = outer_range(plan, table, a)

            def outer(t, at):
                work[a] = work[a] + tiles[at] * factor(times, a, place_far(t))
                return at + 1

            return at, lax.fori_loop(0, count, outer, state[1])

        lax.fori_loop(0, meta[0], block, (0, 0))
        sums_ref[...] = lane_sums(work, share, width) + extra[...]

    alone = jnp.sum(jnp.where(lane == REACH, often, 0.0), axis=1, keepdims=True)
    alone_ref[...] = jnp.broadcast_to(alone, (share, width))
    pairs = jnp.where(alive, sums_ref[...] + sub_sums(self_ref) * alone, 0.0)
    diagonal = 1.0 / density[...] + pairs
    diagonal_ref[...] = diagonal
    precond_ref[...] = source[...] / diagonal


def apply_inner(meta, table, plan, again, field, alone, times, tiles, rows_ref, cols_ref, spread, near, lone, cols):
    share, width = field.shape
    chunks = pieces_of(width)
    near[0:share, :] = field[...]
    near[share:, :] = jnp.zeros((SUB, width), jnp.float32)
    lone[...] = field[...] * alone[...]
    spread_columns(spread, lambda a: a, field[...])
    cols[...] = jnp.zeros_like(cols)

    def run(weighted):
        def block(a, at):
            count, place_of = inner_range(plan, table, a)

            def fetch(t):
                n = jnp.where(t < count, place_of(t), share)
                return n, wide(near[pl.ds(n, 1), :])

            def pairs(fetched, carry):
                at, sums = carry
                if weighted:
                    fetched = [(n, value * factor(times, a, jnp.minimum(n, share - 1))) for n, value in fetched]
                down = [[None] * 2 for _ in fetched]
                result = []
                for c, (here, total) in enumerate(zip(chunks, sums)):
                    own = spread[a, here, :]
                    found = []
                    for t, (_, value) in enumerate(fetched):
                        tile = tiles[at + t, here, :]
                        gather(down[t], c, tile * own)
                        found.append(tile * value)
                    result.append(total + tree(found))
                for (n, _), partial in zip(fetched, down):
                    there = pl.ds(pl.multiple_of(n * SUB, SUB), SUB)
                    partial = tree(partial)
                    if weighted:
                        partial = partial * factor(times, jnp.minimum(n, share - 1), a)
                    cols[there, :] = cols[there, :] + partial
                return at + len(fetched), result

            zero = jnp.zeros((SUB, width), jnp.float32)
            _, sums = padded_sweep(count, fetch, pairs, (at, [zero] * len(chunks)))
            at = at + count
            value = wide(lone[pl.ds(a, 1), :])
            for here, old in zip(chunks, sums):
                rows_ref[a, here, :] = old + tiles[at, here, :] * value
            return at + 1

        lax.fori_loop(0, meta[0], block, 0)

    either(again[0], run)
    cols_ref[...] = cols[0 : share * SUB, :]


def apply_outer(meta, table, plan, again, received, times, tiles, rows_ref, cols_ref, work, hood):
    first, second, *ends = received
    columns = len(received)
    share, width = first.shape
    chunks = pieces_of(width)
    base, filled = meta[3], meta[4]
    column = lax.div(base, share)
    odd = lax.rem(column, 2) == 1
    before = jnp.where(odd, first[...], second[...])
    after = jnp.where(odd, second[...], first[...])
    own = 3 * share
    for c, end in enumerate(ends, 1):
        hood[pl.ds(own - meta[5] + c * share, share), :] = end[...]
    from_last = own - meta[5] + (columns - 1) * share
    hood[pl.ds(jnp.where(column == 0, from_last, own - share), share), :] = before
    hood[own + share : own + 2 * share, :] = after
    head = after
    for c, end in enumerate(ends, 1):
        head = jnp.where(column == c, end[...], head)
    hood[pl.ds(own + jnp.clip(filled - base, 0, 2 * share), share), :] = head
    nothing = hood.shape[0] - SUB
    hood[nothing:, :] = jnp.zeros((SUB, width), jnp.float32)

    def run(weighted):
        def block(a, at):
            count, place_of = outer_range(plan, table, a)

            def fetch(t):
                place = place_of(t)
                value = hood[pl.ds(jnp.where(t < count, own + place, nothing), 1), :]
                if weighted:
                    value = value * factor(times, a, place)
                return wide(value)

            def pairs(values, carry):
                at, sums = carry
                result = []
                for here, total in zip(chunks, sums):
                    result.append(total + tree([tiles[at + t, here, :] * value for t, value in enumerate(values)]))
                return at + len(values), result

            _, sums = padded_sweep(count, fetch, pairs, (at, [rows_ref[a, here, :] for here in chunks]))
            for here, values in zip(chunks, sums):
                work[a, here, :] = values
            return at + count

        lax.fori_loop(0, meta[0], block, 0)

    either(again[0], run)
    return jnp.where(alive_rows(meta, share, width), lane_sums(work, share, width) + sub_sums(cols_ref), 0.0)


def apply_first(meta, table, plan, again, diagonal, times, *rest):
    *received, tiles, rows_ref, cols_ref, spill_ref, scaled_ref, work, hood = rest
    spill = apply_outer(meta, table, plan, again, received, times, tiles, rows_ref, cols_ref, work, hood)
    spill_ref[...] = spill
    scaled_ref[...] = spill / diagonal[...]


def apply_second(meta, table, plan, again, source, precond, spill, scaled, times, *rest):
    *received, tiles, rows_ref, cols_ref, twice_ref, sums_ref, work, hood = rest
    twice = apply_outer(meta, table, plan, again, received, times, tiles, rows_ref, cols_ref, work, hood)
    twice_ref[...] = twice
    share, width = twice.shape
    lane = lax.broadcasted_iota(jnp.int32, (1, width), 1)
    sums = jnp.zeros((1, width), jnp.float32)
    pairs = ((source[...], precond[...]), (spill[...], precond[...]), (spill[...], scaled[...]), (scaled[...], twice))
    for k, (first, second) in enumerate(pairs):
        along = jnp.sum(first * second, axis=0, keepdims=True)
        sums = jnp.where(lane == k, jnp.sum(along, axis=1, keepdims=True), sums)
    sums_ref[...] = wide(sums)


def finish(source, precond, spill, scaled, twice, *rest):
    *parts, solution_ref, residual_ref = rest
    sums = tree([ref[...] for ref in parts])

    def pick(k):
        return sums[0:1, k : k + 1]

    weighted, cross, square, last = pick(0), pick(1), pick(2), pick(3)
    part = cross / weighted
    advance = 1.0 / (1.0 - part)
    keep = -part * advance
    weighted_next = advance * advance * (square - cross * part)
    bent = keep * keep * cross + 2.0 * keep * advance * square + advance * advance * last
    blend = weighted_next / weighted
    advance_next = weighted_next / (weighted_next - bent - blend * weighted_next / advance)
    residual = keep * source[...] + advance * spill[...]
    next_precond = keep * precond[...] + advance * scaled[...]
    direction = next_precond + blend * precond[...]
    image = residual - keep * spill[...] - advance * twice[...] + blend * (source[...] - spill[...])
    solution_ref[...] = advance * precond[...] + advance_next * direction
    residual_ref[...] = residual - advance_next * image


def held(array):
    return pltpu.with_memory_space_constraint(array, pltpu.VMEM)


def body(positions, phase, neighbours, counts, phase_density, right_side):
    capacity, width = phase.shape
    columns = lax.axis_size("col")
    pieces = lax.axis_size("piece")
    share = capacity // columns
    f32 = jnp.float32
    vector = jax.ShapeDtypeStruct((share, width), f32)
    few = jax.ShapeDtypeStruct((SUB, width), f32)
    message = jax.ShapeDtypeStruct((4, share, width), f32)
    most_inner, most_outer = tile_bounds(share)
    inner_tiles = pltpu.VMEM((most_inner + GROUP, width, width), f32)
    outer_tiles = pltpu.VMEM((most_outer + GROUP, width, width), f32)
    ahead = pltpu.VMEM((GROUP, width, width), f32)
    square_more = pltpu.VMEM((share + 1, width, width), f32)
    square = pltpu.VMEM((share, width, width), f32)
    narrow = pltpu.VMEM((share * SUB, width), f32)
    table = jnp.asarray(FLAT)

    def call(kernel, args, outs, scratch=(), work=0, scalars=2, far=0, **more):
        return pl.pallas_call(
            kernel,
            out_shape=outs,
            in_specs=[SMEM] * scalars + [HBM] * far + [VMEM] * (len(args) - scalars - far),
            out_specs=[SMEM if getattr(o, "memory_space", None) == pltpu.SMEM else VMEM for o in outs],
            scratch_shapes=scratch,
            compiler_params=LIMIT,
            cost_estimate=pl.CostEstimate(flops=work * width * width, bytes_accessed=0, transcendentals=0),
            name=kernel.__name__,
            **more,
        )(*args)

    def away(array):
        return pltpu.with_memory_space_constraint(array, pltpu.HBM)

    around = jax.ShapeDtypeStruct((4, capacity + 2 * share, width), f32)
    near = jax.ShapeDtypeStruct((4, 2 * share, width), f32)
    far = [away(array) for array in (positions, phase, neighbours.T, right_side, table)]
    meta, table, around, near, density, source, first, second, *times = call(
        prepare,
        (away(counts), away(phase_density), *far),
        [pltpu.SMEM((8,), jnp.int32), pltpu.SMEM(table.shape, jnp.int32), around, near, vector, vector, message, message]
        + [vector] * columns,
        [pltpu.VMEM(phase.shape, jnp.int32), pltpu.VMEM(far[2].shape, jnp.int32), pltpu.VMEM((share, width), f32),
         pltpu.VMEM((capacity, width), f32), pltpu.SemaphoreType.DMA((5,))],
        far=len(far),
    )
    meta, table = (pltpu.with_memory_space_constraint(array, pltpu.SMEM) for array in (meta, table))
    first = lax.ppermute(first, "piece", [(i, i ^ 1) for i in range(pieces)])
    second = lax.ppermute(second, "piece", [(i, ((i ^ 1) + (1 if i % 2 else -1) * 2) % pieces) for i in range(pieces)])
    times = [lax.ppermute(t, "col", [(i, i ^ k) for i in range(columns)]) if k else t for k, t in enumerate(times)]

    plan, runs, tiles_in, sides, middles, weights, rows, cols, selfs = call(
        build_inner,
        (meta, table, near),
        [pltpu.SMEM((share * FIELDS + 4,), jnp.int32), pltpu.SMEM((6 * share + 3,), jnp.int32), inner_tiles,
         pltpu.VMEM((2, share, width, width), jnp.bfloat16), pltpu.VMEM((3, share, width), f32), square, square, narrow, narrow],
        [pltpu.SMEM((3 * share + 3,), jnp.int32), square_more, pltpu.VMEM(((share + 1) * SUB, width), f32), ahead],
        16 * most_inner,
    )
    plan, runs = (pltpu.with_memory_space_constraint(array, pltpu.SMEM) for array in (plan, runs))
    again, tiles_out, diagonal, precond, times, alone = call(
        build_outer,
        (meta, table, plan, runs, around, first, second, density, source,
         held(tiles_in), held(sides), held(middles), held(weights), held(rows), held(cols), held(selfs), *times),
        [pltpu.SMEM((1,), jnp.int32), outer_tiles, vector, vector, vector, vector],
        [pltpu.VMEM((4, capacity + 2 * share, width), f32), square_more]
        + [pltpu.VMEM((share, width), f32)] * 2 + [ahead],
        16 * most_outer,
        scalars=4,
    )
    again = pltpu.with_memory_space_constraint(again, pltpu.SMEM)

    def inner(field):
        return call(
            apply_inner,
            (meta, table, plan, again, field, alone, times, held(tiles_in)),
            [square, narrow],
            [pltpu.VMEM((share, width, width), f32), pltpu.VMEM((share + SUB, width), f32), pltpu.VMEM((share, width), f32),
             pltpu.VMEM(((share + 1) * SUB, width), f32)],
            4 * most_inner,
            scalars=4,
        )

    def exchange(field):
        axes = ("piece", "col")
        count = pieces * columns
        swaps = [[i ^ 1 for i in range(count)], [i - 1 if i % 2 == 0 else i + 1 for i in range(count)]]
        swaps[1][0], swaps[1][-1] = count - 1, 0
        for c in range(1, columns - 1):
            to = {}
            for p in range(pieces - 1):
                low, high = p * columns + c, (p + 1) * columns
                to[low], to[high] = high, low
            for p in range(pieces):
                rest = [i for i in range(p * columns, (p + 1) * columns) if i not in to]
                to.update(zip(rest, rest[1:] + rest[:1]))
            swaps.append([to[i] for i in range(count)])
        return [lax.ppermute(field, axes, list(enumerate(to))) for to in swaps]

    scratch = [pltpu.VMEM((share, width, width), f32), pltpu.VMEM((8 * share, width), f32)]

    received = exchange(precond)
    rows, cols = inner(precond)
    spill, scaled = call(
        apply_first,
        (meta, table, plan, again, diagonal, times, *received, held(tiles_out), held(rows), held(cols)),
        [vector, vector],
        scratch,
        2 * most_outer,
        scalars=4,
    )

    received = exchange(scaled)
    rows, cols = inner(scaled)
    twice, sums = call(
        apply_second,
        (meta, table, plan, again, source, precond, spill, scaled, times, *received, held(tiles_out), held(rows), held(cols)),
        [vector, few],
        scratch,
        2 * most_outer,
        scalars=4,
    )

    def swap(values, axis, step):
        return lax.ppermute(values, axis, [(i, i ^ step) for i in range(lax.axis_size(axis))])

    def together(values, axis, low, size):
        return tree([values] + [swap(values, axis, low * k) for k in range(1, size)])

    sums = together(sums, "col", 1, columns)
    step = 1
    while pieces // step > 8:
        sums = together(sums, "piece", step, 8)
        step *= 8
    others = [swap(sums, "piece", step * k) for k in range(1, pieces // step)]

    return tuple(call(
        finish,
        (source, precond, spill, scaled, twice, sums, *others),
        [vector, vector],
        scalars=0,
    ))


def solution(mesh):
    placed = (
        P(None, "piece", None),
        P("piece", None),
        P("piece", "col"),
        P(),
        P(),
        P(("piece", "col"), None),
    )
    return jax.shard_map(
        body,
        mesh=mesh,
        in_specs=placed,
        out_specs=(P(("piece", "col"), None), P(("piece", "col"), None)),
        check_vma=False,
    )
```

```python
import jax
import jax.numpy as jnp
import numpy as np
from jax import lax
from jax.experimental import pallas as pl
from jax.experimental.pallas import tpu as pltpu
from jax.sharding import PartitionSpec as P

ITERS = 2
SIDE = 4
LAYER = SIDE * SIDE
REACH = 2 * LAYER
SUB = 8
VMEM = pl.BlockSpec(memory_space=pltpu.VMEM)
SMEM = pl.BlockSpec(memory_space=pltpu.SMEM)
HBM = pl.BlockSpec(memory_space=pltpu.HBM)


def stencil_tables():
    levels = SIDE.bit_length() - 1

    def cell(code):
        across = sum((code >> (2 * level) & 1) << level for level in range(levels))
        along = sum((code >> (2 * level + 1) & 1) << level for level in range(levels))
        return across, along

    place = {cell(code): code for code in range(LAYER)}
    rows = []
    for code in range(LAYER):
        across, along = cell(code)
        rows.append(
            sorted(
                step_z * LAYER + place[across + step_x, along + step_y] - code
                for step_z in (-1, 0, 1)
                for step_y in (-1, 0, 1)
                for step_x in (-1, 0, 1)
                if (across + step_x, along + step_y) in place
            )
        )
    longest = max(len(row) for row in rows)
    offsets = np.zeros((LAYER, longest), np.int32)
    below = np.zeros((LAYER, 2 * REACH + 1), np.int32)
    for code, row in enumerate(rows):
        offsets[code, : len(row)] = row
        for t in range(-REACH, REACH + 1):
            below[code, t + REACH] = sum(offset < t for offset in row)
    return offsets, below


OFFSETS, BELOW = stencil_tables()
WIDEST = OFFSETS.shape[1]
TABLE = np.concatenate([OFFSETS, BELOW], 1)
STRIDE = TABLE.shape[1]
FLAT = np.concatenate([TABLE.reshape(-1), np.zeros(8, np.int32)])
LIMIT = pltpu.CompilerParams(vmem_limit_bytes=8 * 1024 * 1024)


def tile_bounds(share):
    inner = outer = 0
    for first in range(LAYER):
        for live in range(1, share + 1):
            near = far = 0
            for a in range(live):
                code = (first + a) % LAYER
                row = [int(o) for o in OFFSETS[code][: BELOW[code, -1]]]
                near += sum(0 <= a + o and o <= 0 for o in row)
                far += sum(a + o < 0 or a + o >= live for o in row)
            inner, outer = max(inner, near), max(outer, far)
    return inner, outer


def rank(table, code, t):
    return table[code * STRIDE + jnp.clip(t, -REACH, REACH) + REACH + WIDEST]


FIELDS = 6


def write_plan(meta, table, plan, a):
    code = lax.bitwise_and(meta[1] + a, LAYER - 1)
    place = meta[1] + a
    low, split, middle = rank(table, code, -place), rank(table, code, -a), rank(table, code, 0)
    resume, high = rank(table, code, meta[0] - a), rank(table, code, meta[2] - place)
    row = code * STRIDE
    ahead = split - low
    plan[a * FIELDS] = middle - split
    plan[a * FIELDS + 1] = row + split
    plan[a * FIELDS + 2] = ahead + jnp.maximum(high - resume, 0)
    plan[a * FIELDS + 3] = ahead
    plan[a * FIELDS + 4] = row + low
    plan[a * FIELDS + 5] = row + resume - ahead


def write_run(runs, at, a, start, count):
    runs[3 * at], runs[3 * at + 1], runs[3 * at + 2] = a, start, count
    return at + (count > 0).astype(jnp.int32)


def write_runs(meta, table, plan, inner_runs, outer_runs, share):
    inner = outer = total = far = jnp.int32(0)
    for a in range(share):
        write_plan(meta, table, plan, a)
        alive = a < meta[0]
        count, start, count_far, ahead, start_far, start_after = (plan[a * FIELDS + k] for k in range(FIELDS))
        inner = write_run(inner_runs, inner, a, start, jnp.where(alive, count + 1, 0))
        outer = write_run(outer_runs, outer, a, start_far, jnp.where(alive, ahead, 0))
        outer = write_run(outer_runs, outer, a, start_after + ahead, jnp.where(alive, count_far - ahead, 0))
        total = total + jnp.where(alive, count + 1, 0)
        far = far + jnp.where(alive, count_far, 0)
    for runs, at in ((inner_runs, inner), (outer_runs, outer)):
        write_run(runs, at, share, len(FLAT) - 8, jnp.int32(1))
    plan[share * FIELDS] = total
    plan[share * FIELDS + 1] = far
    plan[share * FIELDS + 2] = inner
    plan[share * FIELDS + 3] = outer


def inner_range(plan, table, a):
    start = plan[a * FIELDS + 1]
    return plan[a * FIELDS], lambda t: a + table[start + t]


def outer_range(plan, table, a):
    ahead, start, start_after = (plan[a * FIELDS + k] for k in (3, 4, 5))
    return plan[a * FIELDS + 2], lambda t: a + table[t + jnp.where(t < ahead, start, start_after)]


TURN = 4


def padded_sweep(count, fetch, step, carry):
    def turn(i, state):
        carry, *now = state
        later = [fetch(TURN * (i + 1) + k) for k in range(TURN)]
        return step(now, carry), *later

    state = (carry, *(fetch(k) for k in range(TURN)))
    return lax.fori_loop(0, lax.div(count + (TURN - 1), TURN), turn, state)[0]


def tree(terms):
    while len(terms) > 1:
        terms = [a + b for a, b in zip(terms[::2], terms[1::2])] + terms[len(terms) // 2 * 2 :]
    return terms[0]


def gather(partial, c, term):
    if c < len(partial):
        partial[c] = term
    else:
        partial[c % len(partial)] = partial[c % len(partial)] + term


def pieces_of(width):
    return [slice(c * SUB, (c + 1) * SUB) for c in range(width // SUB)]


def wide(row):
    return jnp.broadcast_to(row, (SUB, row.shape[1]))


def three_parts(values):
    high = values.astype(jnp.bfloat16).astype(jnp.float32)
    rest = values - high
    middle = rest.astype(jnp.bfloat16).astype(jnp.float32)
    return high, middle, rest - middle


def stacked(rows):
    sublane = lax.broadcasted_iota(jnp.int32, rows[0].shape, 0)
    result = jnp.zeros(rows[0].shape, jnp.float32)
    for k, row in enumerate(rows):
        result = jnp.where(sublane == k, row, result)
    return result


HALF = 64


def own_side(x):
    size = x[0] * x[0] + x[1] * x[1] + x[2] * x[2]
    one = jnp.ones_like(size)
    high, middle, low = three_parts(stacked([2.0 * x[0], 2.0 * x[1], 2.0 * x[2], one, 0.5 - size]))
    rest = jnp.zeros((HALF - 6 * SUB, size.shape[1]), jnp.float32)
    return jnp.concatenate([high, high, middle, middle, high, low, rest], 0)


def other_side(y):
    size = y[0] * y[0] + y[1] * y[1] + y[2] * y[2]
    one = jnp.ones_like(size)
    high, middle, low = three_parts(stacked([y[0], y[1], y[2], 0.5 - size, one]))
    first = jnp.concatenate([high, middle], 0).astype(jnp.bfloat16)
    last = jnp.concatenate([low, high], 0).astype(jnp.bfloat16)
    return jnp.concatenate([first, first, last, jnp.zeros((HALF - 6 * SUB, size.shape[1]), jnp.bfloat16)], 0)


GROUP = 4


def flat_tiles(count, runs, most, table, sides, middles, weights, other_at, buffers, tiles, rows_ref, cols_ref):
    share, width = rows_ref.shape[0] - 1, rows_ref.shape[2]
    chunks = pieces_of(width)

    def steps(state):
        found = []
        for _ in range(GROUP):
            run, t = state
            a, start, size = (runs[3 * run + k] for k in range(3))
            found.append((a, a + table[start + t]))
            over = t + 1 >= size
            state = jnp.minimum(run + over.astype(jnp.int32), most), jnp.where(over, 0, t + 1)
        return state, found

    def other_of(a, n):
        here = pl.ds(a, 1)
        return other_side([wide(other_at(c, n)) - wide(middles[c, here, :]) for c in range(3)])

    def products(found, ahead):
        none = jnp.zeros((HALF, width), jnp.bfloat16)
        for k in range(0, GROUP, 2):
            (a, n), (b, m) = ((jnp.minimum(a, share - 1), n) for a, n in found[k : k + 2])
            left = jnp.concatenate([other_of(a, n), none], 0)
            right = jnp.concatenate([none, other_of(b, m)], 0)
            both = jnp.dot(
                sides[0, a] + sides[1, b], jnp.concatenate([left, right], 1), preferred_element_type=jnp.float32
            )
            ahead[k] = both[:, :width]
            ahead[k + 1] = both[:, width:]

    def weigh(at, found, ahead):
        for k, (a, n) in enumerate(found):
            alone = a == n
            row = jnp.where(alone, share, a)
            own = jnp.minimum(a, share - 1)
            other = wide(other_at(3, n))
            down = [None] * 2
            for c, here in enumerate(chunks):
                left = ahead[k, here, :]
                rest = jnp.maximum(left, 0.0)
                inverse = pltpu.reciprocal((1.01 - left) * (weights[own, here, :] + other), approx=True)
                tile = rest * rest * inverse
                tiles[at + k, here, :] = tile
                rows_ref[row, here, :] = rows_ref[row, here, :] + tile
                if cols_ref is not None:
                    gather(down, c, tile)
            if cols_ref is not None:
                there = pl.ds(pl.multiple_of(jnp.where(alone, share, n) * SUB, SUB), SUB)
                cols_ref[there, :] = cols_ref[there, :] + tree(down)

    def turn(i, carry):
        state, found = carry
        at = i * (2 * GROUP)
        state, later = steps(state)
        products(later, buffers[1])
        weigh(at, found, buffers[0])
        state, last = steps(state)
        products(last, buffers[0])
        weigh(at + GROUP, later, buffers[1])
        return state, last

    state, found = steps((jnp.int32(0), jnp.int32(0)))
    products(found, buffers[0])
    lax.fori_loop(0, lax.div(count + (2 * GROUP - 1), 2 * GROUP), turn, (state, found))


def spread_columns(out, index, rows):
    count, width = rows.shape
    turned = rows.T
    for a in range(count):
        out[index(a)] = jnp.broadcast_to(turned[:, a : a + 1], (width, width))


def lane_sums(parts, count, width):
    lanes = lax.broadcasted_iota(jnp.int32, (width, width), 1)
    turned = jnp.zeros((width, width), jnp.float32)
    for a in range(count):
        turned = jnp.where(lanes == a, jnp.sum(parts[a], axis=1, keepdims=True), turned)
    return turned.T[:count]


def sub_sums(cols):
    return jnp.sum(cols[...].reshape(-1, SUB, cols.shape[1]), axis=1)


def alive_rows(meta, share, width):
    return lax.broadcasted_iota(jnp.int32, (share, width), 0) < meta[0]


def prepare(
    counts, densities, position_in, phase_in, listed_in, right_side_in, table_in,
    meta, table, hood, near, density, source, first_swap, second_swap, *rest
):
    *times_out, phase, listed, right_side, times, sems = rest
    share, width = source.shape
    capacity = phase.shape[0]
    body_rows = pl.ds(share, capacity)
    copies = [
        pltpu.make_async_copy(phase_in, phase, sems.at[0]),
        pltpu.make_async_copy(position_in, hood.at[pl.ds(0, 3), body_rows, :], sems.at[1]),
        pltpu.make_async_copy(listed_in, listed, sems.at[2]),
        pltpu.make_async_copy(right_side_in, right_side, sems.at[3]),
        pltpu.make_async_copy(table_in, table, sems.at[4]),
    ]
    for copy in copies:
        copy.start()
    piece, column = lax.axis_index("piece"), lax.axis_index("col")
    filled = counts[piece]
    filled_before = counts[jnp.maximum(piece - 1, 0)]
    before = jnp.int32(0)
    total = jnp.int32(0)
    for p in range(counts.shape[0]):
        before = before + jnp.where(p < piece, counts[p], 0)
        total = total + counts[p]
    meta[0] = jnp.clip(filled - column * share, 0, share)
    meta[1] = before + column * share
    meta[2] = total
    meta[3] = column * share
    meta[4] = filled
    meta[5] = filled_before
    own_rows = pl.ds(pl.multiple_of(share + column * share, SUB), share)
    copies[0].wait()
    labels = phase[...]
    whole = sum(jnp.where(labels == k, densities[k], 0.0) for k in range(densities.shape[0]))
    hood[3, body_rows, :] = whole * (width / 2.0)
    density[...] = hood[3, own_rows, :] * (2.0 / width)
    copies[1].wait()
    even = lax.rem(piece, 2) == 0
    for k in range(4):
        tail, head = hood[k, pl.ds(filled, share), :], hood[k, share : 2 * share, :]
        first_swap[k] = jnp.where(even, tail, head)
        second_swap[k] = jnp.where(even, head, tail)
        near[k, 0:share, :] = hood[k, own_rows, :]
    for copy in copies[2:]:
        copy.wait()
    source[...] = jnp.where(alive_rows(meta, share, width), right_side[...], 0.0)
    ids = listed[...]
    own = lax.broadcasted_iota(jnp.int32, ids.shape, 1)
    slot = ids - piece * capacity
    away = slot - own + jnp.where(slot < 0, capacity - filled_before, jnp.where(slot >= capacity, filled - capacity, 0))
    away = jnp.where(ids < 0, -REACH, away) + REACH
    steps = lax.broadcasted_iota(jnp.int32, (2 * REACH, capacity), 0)
    found = tree([jnp.where(steps == away[k : k + 1], 1.0, 0.0) for k in range(ids.shape[0])])
    found = jnp.concatenate([found, jnp.zeros((width - 2 * REACH, capacity), jnp.float32)], 0)
    times[...] = found.T
    for k, out in enumerate(times_out):
        out[...] = times[pl.ds(pl.multiple_of((column ^ k) * share, SUB), share), :]


def finish_tiles(tiles, end):
    for t in range(TURN):
        tiles[end + t] = jnp.zeros(tiles.shape[1:], jnp.float32)


def build_inner(
    meta, table, near, plan, outer_runs, tiles, sides, middles, weights, rows_out, cols_out, self_ref,
    inner_runs, rows_ref, cols_ref, *buffers,
):
    share, width = rows_out.shape[0], rows_out.shape[2]
    chunks = pieces_of(width)
    write_runs(meta, table, plan, inner_runs, outer_runs, share)
    for k in range(3):
        first = near[k, 0:share, 0:1]
        middles[k] = jnp.broadcast_to(jnp.floor(first) + 0.5, (share, width))
    low = lax.broadcasted_iota(jnp.int32, (width, width), 1) < HALF
    for a in range(0, share, 2):
        pair = []
        for b in (a, a + 1):
            here = slice(b, b + 1)
            pair.append(own_side([wide(near[k, here, :] - middles[k, here, :]) for k in range(3)]))
        turned = jnp.concatenate(pair, 0).T
        moved = pltpu.roll(turned, HALF, 1)
        for at, b, half, side in ((0, a, low, turned), (1, a, ~low, moved), (0, a + 1, low, moved), (1, a + 1, ~low, turned)):
            sides[at, b] = jnp.where(half, side, 0.0).astype(jnp.bfloat16)
    spread_columns(weights, lambda a: a, near[3, 0:share, :])
    cols_ref[...] = jnp.zeros_like(cols_ref)
    rows_ref[...] = jnp.zeros_like(rows_ref)
    count = plan[share * FIELDS]
    flat_tiles(
        count, inner_runs, plan[share * FIELDS + 2], table, sides, middles, weights,
        lambda k, n: near[k, pl.ds(n, 1), :], buffers, tiles, rows_ref, cols_ref,
    )
    finish_tiles(tiles, count)
    lane = lax.broadcasted_iota(jnp.int32, (SUB, width), 1)
    sublane = lax.broadcasted_iota(jnp.int32, (SUB, width), 0)

    def block(a, at):
        at = at + plan[a * FIELDS]
        down = [None] * 4
        for c, here in enumerate(chunks):
            tile = jnp.where(lane == sublane + c * SUB, 0.0, tiles[at, here, :])
            tiles[at, here, :] = tile
            gather(down, c, tile)
        self_ref[pl.ds(pl.multiple_of(a * SUB, SUB), SUB), :] = tree(down)
        return at + 1

    lax.fori_loop(0, meta[0], block, 0)
    rows_out[...] = rows_ref[0:share]
    cols_out[...] = cols_ref[0 : share * SUB, :]


def factor(times, a, n):
    lane = lax.broadcasted_iota(jnp.int32, (1, times.shape[1]), 1)
    return jnp.sum(jnp.where(lane == n - a + REACH, times[pl.ds(a, 1), :], 0.0), axis=1, keepdims=True)


def either(flag, run):
    @pl.when(flag == 0)
    def _():
        run(False)

    @pl.when(flag != 0)
    def _():
        run(True)


TAIL = 12


def build_outer(
    meta, table, plan, runs, around, first, second, density, source, tiles_in, sides, middles, weights,
    rows_ref, cols_ref, self_ref, *rest
):
    times_in, rest = rest[: -TAIL], rest[-TAIL:]
    again_ref, tiles, diagonal_ref, precond_ref, times, alone_ref, hood, work, sums_ref, extra, *buffers = rest
    share, width = diagonal_ref.shape
    base, filled = meta[3], meta[4]
    even = lax.rem(lax.axis_index("piece"), 2) == 0
    for k in range(4):
        hood[k, 0:share, :] = jnp.where(even, second[k], first[k])
        hood[k, share:, :] = around[k, share:, :]
        hood[k, pl.ds(share + filled, share), :] = jnp.where(even, first[k], second[k])
    alive = alive_rows(meta, share, width)
    often = jnp.where(alive, tree([ref[...] for ref in times_in]), 0.0)
    times[...] = often
    lane = lax.broadcasted_iota(jnp.int32, (share, width), 1)
    again = jnp.max(jnp.where((lane == REACH) | (lane == 0), 0.0, often)) > 1.5
    again_ref[0] = again.astype(jnp.int32)


    work[...] = jnp.zeros_like(work)
    count = plan[share * FIELDS + 1]
    flat_tiles(
        count, runs, plan[share * FIELDS + 3], table, sides, middles, weights,
        lambda k, n: hood[k, pl.ds(base + share + n, 1), :], buffers, tiles, work, None,
    )
    finish_tiles(tiles, count)
    sums_ref[...] = lane_sums([rows_ref[a] + work[a] for a in range(share)], share, width) + sub_sums(cols_ref)

    @pl.when(again)
    def _():
        extra[...] = jnp.zeros_like(extra)
        work[...] = jnp.zeros_like(work)

        def block(a, state):
            count, place_of = inner_range(plan, table, a)

            def inner(t, at):
                n = place_of(t)
                tile = tiles_in[at]
                work[a] = work[a] + tile * factor(times, a, n)
                there = pl.ds(n, 1)
                down = jnp.sum(tile, axis=0, keepdims=True)
                extra[there, :] = extra[there, :] + down * factor(times, n, a)
                return at + 1

            at = lax.fori_loop(0, count, inner, state[0]) + 1
            count, place_far = outer_range(plan, table, a)

            def outer(t, at):
                work[a] = work[a] + tiles[at] * factor(times, a, place_far(t))
                return at + 1

            return at, lax.fori_loop(0, count, outer, state[1])

        lax.fori_loop(0, meta[0], block, (0, 0))
        sums_ref[...] = lane_sums(work, share, width) + extra[...]

    alone = jnp.sum(jnp.where(lane == REACH, often, 0.0), axis=1, keepdims=True)
    alone_ref[...] = jnp.broadcast_to(alone, (share, width))
    pairs = jnp.where(alive, sums_ref[...] + sub_sums(self_ref) * alone, 0.0)
    diagonal = 1.0 / density[...] + pairs
    diagonal_ref[...] = diagonal
    precond_ref[...] = source[...] / diagonal


def apply_inner(meta, table, plan, again, field, alone, times, tiles, rows_ref, cols_ref, spread, near, lone, cols):
    share, width = field.shape
    chunks = pieces_of(width)
    near[0:share, :] = field[...]
    near[share:, :] = jnp.zeros((SUB, width), jnp.float32)
    lone[...] = field[...] * alone[...]
    spread_columns(spread, lambda a: a, field[...])
    cols[...] = jnp.zeros_like(cols)

    def run(weighted):
        def block(a, at):
            count, place_of = inner_range(plan, table, a)

            def fetch(t):
                n = jnp.where(t < count, place_of(t), share)
                return n, wide(near[pl.ds(n, 1), :])

            def pairs(fetched, carry):
                at, sums = carry
                if weighted:
                    fetched = [(n, value * factor(times, a, jnp.minimum(n, share - 1))) for n, value in fetched]
                down = [[None] * 2 for _ in fetched]
                result = []
                for c, (here, total) in enumerate(zip(chunks, sums)):
                    own = spread[a, here, :]
                    found = []
                    for t, (_, value) in enumerate(fetched):
                        tile = tiles[at + t, here, :]
                        gather(down[t], c, tile * own)
                        found.append(tile * value)
                    result.append(total + tree(found))
                for (n, _), partial in zip(fetched, down):
                    there = pl.ds(pl.multiple_of(n * SUB, SUB), SUB)
                    partial = tree(partial)
                    if weighted:
                        partial = partial * factor(times, jnp.minimum(n, share - 1), a)
                    cols[there, :] = cols[there, :] + partial
                return at + len(fetched), result

            zero = jnp.zeros((SUB, width), jnp.float32)
            _, sums = padded_sweep(count, fetch, pairs, (at, [zero] * len(chunks)))
            at = at + count
            value = wide(lone[pl.ds(a, 1), :])
            for here, old in zip(chunks, sums):
                rows_ref[a, here, :] = old + tiles[at, here, :] * value
            return at + 1

        lax.fori_loop(0, meta[0], block, 0)

    either(again[0], run)
    cols_ref[...] = cols[0 : share * SUB, :]


def apply_outer(meta, table, plan, again, received, times, tiles, rows_ref, cols_ref, work, hood):
    first, second, *ends = received
    columns = len(received)
    share, width = first.shape
    chunks = pieces_of(width)
    base, filled = meta[3], meta[4]
    column = lax.div(base, share)
    odd = lax.rem(column, 2) == 1
    before = jnp.where(odd, first[...], second[...])
    after = jnp.where(odd, second[...], first[...])
    own = 3 * share
    for c, end in enumerate(ends, 1):
        hood[pl.ds(own - meta[5] + c * share, share), :] = end[...]
    from_last = own - meta[5] + (columns - 1) * share
    hood[pl.ds(jnp.where(column == 0, from_last, own - share), share), :] = before
    hood[own + share : own + 2 * share, :] = after
    head = after
    for c, end in enumerate(ends, 1):
        head = jnp.where(column == c, end[...], head)
    hood[pl.ds(own + jnp.clip(filled - base, 0, 2 * share), share), :] = head
    nothing = hood.shape[0] - SUB
    hood[nothing:, :] = jnp.zeros((SUB, width), jnp.float32)

    def run(weighted):
        def block(a, at):
            count, place_of = outer_range(plan, table, a)

            def fetch(t):
                place = place_of(t)
                value = hood[pl.ds(jnp.where(t < count, own + place, nothing), 1), :]
                if weighted:
                    value = value * factor(times, a, place)
                return wide(value)

            def pairs(values, carry):
                at, sums = carry
                result = []
                for here, total in zip(chunks, sums):
                    result.append(total + tree([tiles[at + t, here, :] * value for t, value in enumerate(values)]))
                return at + len(values), result

            _, sums = padded_sweep(count, fetch, pairs, (at, [rows_ref[a, here, :] for here in chunks]))
            for here, values in zip(chunks, sums):
                work[a, here, :] = values
            return at + count

        lax.fori_loop(0, meta[0], block, 0)

    either(again[0], run)
    return jnp.where(alive_rows(meta, share, width), lane_sums(work, share, width) + sub_sums(cols_ref), 0.0)


def apply_first(meta, table, plan, again, diagonal, times, *rest):
    *received, tiles, rows_ref, cols_ref, spill_ref, scaled_ref, work, hood = rest
    spill = apply_outer(meta, table, plan, again, received, times, tiles, rows_ref, cols_ref, work, hood)
    spill_ref[...] = spill
    scaled_ref[...] = spill / diagonal[...]


def apply_second(meta, table, plan, again, source, precond, spill, scaled, times, *rest):
    *received, tiles, rows_ref, cols_ref, twice_ref, sums_ref, work, hood = rest
    twice = apply_outer(meta, table, plan, again, received, times, tiles, rows_ref, cols_ref, work, hood)
    twice_ref[...] = twice
    share, width = twice.shape
    lane = lax.broadcasted_iota(jnp.int32, (1, width), 1)
    sums = jnp.zeros((1, width), jnp.float32)
    pairs = ((source[...], precond[...]), (spill[...], precond[...]), (spill[...], scaled[...]), (scaled[...], twice))
    for k, (first, second) in enumerate(pairs):
        along = jnp.sum(first * second, axis=0, keepdims=True)
        sums = jnp.where(lane == k, jnp.sum(along, axis=1, keepdims=True), sums)
    sums_ref[...] = wide(sums)


def finish(source, precond, spill, scaled, twice, *rest):
    *parts, solution_ref, residual_ref = rest
    sums = tree([ref[...] for ref in parts])

    def pick(k):
        return sums[0:1, k : k + 1]

    weighted, cross, square, last = pick(0), pick(1), pick(2), pick(3)
    part = cross / weighted
    advance = 1.0 / (1.0 - part)
    keep = -part * advance
    weighted_next = advance * advance * (square - cross * part)
    bent = keep * keep * cross + 2.0 * keep * advance * square + advance * advance * last
    blend = weighted_next / weighted
    advance_next = weighted_next / (weighted_next - bent - blend * weighted_next / advance)
    residual = keep * source[...] + advance * spill[...]
    next_precond = keep * precond[...] + advance * scaled[...]
    direction = next_precond + blend * precond[...]
    image = residual - keep * spill[...] - advance * twice[...] + blend * (source[...] - spill[...])
    solution_ref[...] = advance * precond[...] + advance_next * direction
    residual_ref[...] = residual - advance_next * image


def held(array):
    return pltpu.with_memory_space_constraint(array, pltpu.VMEM)


def body(positions, phase, neighbours, counts, phase_density, right_side):
    capacity, width = phase.shape
    columns = lax.axis_size("col")
    pieces = lax.axis_size("piece")
    share = capacity // columns
    f32 = jnp.float32
    vector = jax.ShapeDtypeStruct((share, width), f32)
    few = jax.ShapeDtypeStruct((SUB, width), f32)
    message = jax.ShapeDtypeStruct((4, share, width), f32)
    most_inner, most_outer = tile_bounds(share)
    inner_tiles = pltpu.VMEM((most_inner + 2 * GROUP, width, width), f32)
    outer_tiles = pltpu.VMEM((most_outer + 2 * GROUP, width, width), f32)
    ahead = pltpu.VMEM((GROUP, width, width), f32)
    square_more = pltpu.VMEM((share + 1, width, width), f32)
    square = pltpu.VMEM((share, width, width), f32)
    narrow = pltpu.VMEM((share * SUB, width), f32)
    table = jnp.asarray(FLAT)

    def call(kernel, args, outs, scratch=(), work=0, scalars=2, far=0, **more):
        return pl.pallas_call(
            kernel,
            out_shape=outs,
            in_specs=[SMEM] * scalars + [HBM] * far + [VMEM] * (len(args) - scalars - far),
            out_specs=[SMEM if getattr(o, "memory_space", None) == pltpu.SMEM else VMEM for o in outs],
            scratch_shapes=scratch,
            compiler_params=LIMIT,
            cost_estimate=pl.CostEstimate(flops=work * width * width, bytes_accessed=0, transcendentals=0),
            name=kernel.__name__,
            **more,
        )(*args)

    def away(array):
        return pltpu.with_memory_space_constraint(array, pltpu.HBM)

    around = jax.ShapeDtypeStruct((4, capacity + 2 * share, width), f32)
    near = jax.ShapeDtypeStruct((4, 2 * share, width), f32)
    far = [away(array) for array in (positions, phase, neighbours.T, right_side, table)]
    meta, table, around, near, density, source, first, second, *times = call(
        prepare,
        (away(counts), away(phase_density), *far),
        [pltpu.SMEM((8,), jnp.int32), pltpu.SMEM(table.shape, jnp.int32), around, near, vector, vector, message, message]
        + [vector] * columns,
        [pltpu.VMEM(phase.shape, jnp.int32), pltpu.VMEM(far[2].shape, jnp.int32), pltpu.VMEM((share, width), f32),
         pltpu.VMEM((capacity, width), f32), pltpu.SemaphoreType.DMA((5,))],
        far=len(far),
    )
    meta, table = (pltpu.with_memory_space_constraint(array, pltpu.SMEM) for array in (meta, table))
    first = lax.ppermute(first, "piece", [(i, i ^ 1) for i in range(pieces)])
    axes = ("piece", "col")
    device = [(p, c) for p in range(pieces) for c in range(columns)]
    partner = [(p + (1 if p % 2 else -1), c) for p, c in device]
    partner = [(q, d) if 0 <= q < pieces else (p, c ^ 1) for (q, d), (p, c) in zip(partner, device)]
    second = lax.ppermute(second, axes, [(i, q * columns + d) for i, (q, d) in enumerate(partner)])
    times = [lax.ppermute(t, "col", [(i, i ^ k) for i in range(columns)]) if k else t for k, t in enumerate(times)]

    plan, runs, tiles_in, sides, middles, weights, rows, cols, selfs = call(
        build_inner,
        (meta, table, near),
        [pltpu.SMEM((share * FIELDS + 4,), jnp.int32), pltpu.SMEM((6 * share + 3,), jnp.int32), inner_tiles,
         pltpu.VMEM((2, share, width, width), jnp.bfloat16), pltpu.VMEM((3, share, width), f32), square, square, narrow, narrow],
        [pltpu.SMEM((3 * share + 3,), jnp.int32), square_more, pltpu.VMEM(((share + 1) * SUB, width), f32), ahead, ahead],
        16 * most_inner,
    )
    plan, runs = (pltpu.with_memory_space_constraint(array, pltpu.SMEM) for array in (plan, runs))
    again, tiles_out, diagonal, precond, times, alone = call(
        build_outer,
        (meta, table, plan, runs, around, first, second, density, source,
         held(tiles_in), held(sides), held(middles), held(weights), held(rows), held(cols), held(selfs), *times),
        [pltpu.SMEM((1,), jnp.int32), outer_tiles, vector, vector, vector, vector],
        [pltpu.VMEM((4, capacity + 2 * share, width), f32), square_more]
        + [pltpu.VMEM((share, width), f32)] * 2 + [ahead, ahead],
        16 * most_outer,
        scalars=4,
    )
    again = pltpu.with_memory_space_constraint(again, pltpu.SMEM)

    def inner(field):
        return call(
            apply_inner,
            (meta, table, plan, again, field, alone, times, held(tiles_in)),
            [square, narrow],
            [pltpu.VMEM((share, width, width), f32), pltpu.VMEM((share + SUB, width), f32), pltpu.VMEM((share, width), f32),
             pltpu.VMEM(((share + 1) * SUB, width), f32)],
            4 * most_inner,
            scalars=4,
        )

    def exchange(field):
        count = pieces * columns
        swaps = [[i ^ 1 for i in range(count)], [i - 1 if i % 2 == 0 else i + 1 for i in range(count)]]
        swaps[1][0], swaps[1][-1] = count - 1, 0
        for c in range(1, columns - 1):
            to = {}
            for p in range(pieces - 1):
                low, high = p * columns + c, (p + 1) * columns
                to[low], to[high] = high, low
            for p in range(pieces):
                rest = [i for i in range(p * columns, (p + 1) * columns) if i not in to]
                to.update(zip(rest, rest[1:] + rest[:1]))
            swaps.append([to[i] for i in range(count)])
        return [lax.ppermute(field, axes, list(enumerate(to))) for to in swaps]

    scratch = [pltpu.VMEM((share, width, width), f32), pltpu.VMEM((8 * share, width), f32)]

    received = exchange(precond)
    rows, cols = inner(precond)
    spill, scaled = call(
        apply_first,
        (meta, table, plan, again, diagonal, times, *received, held(tiles_out), held(rows), held(cols)),
        [vector, vector],
        scratch,
        2 * most_outer,
        scalars=4,
    )

    received = exchange(scaled)
    rows, cols = inner(scaled)
    twice, sums = call(
        apply_second,
        (meta, table, plan, again, source, precond, spill, scaled, times, *received, held(tiles_out), held(rows), held(cols)),
        [vector, few],
        scratch,
        2 * most_outer,
        scalars=4,
    )

    def swap(values, axis, step):
        return lax.ppermute(values, axis, [(i, i ^ step) for i in range(lax.axis_size(axis))])

    def together(values, axis, low, size):
        return tree([values] + [swap(values, axis, low * k) for k in range(1, size)])

    sums = together(sums, "piece", 1, 2)
    sums = together(sums, "col", 1, columns)
    step = 2
    while pieces // step > 4:
        sums = together(sums, "piece", step, 4)
        step *= 4
    others = [swap(sums, "piece", step * k) for k in range(1, pieces // step)]

    return tuple(call(
        finish,
        (source, precond, spill, scaled, twice, sums, *others),
        [vector, vector],
        scalars=0,
    ))


def solution(mesh):
    placed = (
        P(None, "piece", None),
        P("piece", None),
        P("piece", "col"),
        P(),
        P(),
        P(("piece", "col"), None),
    )
    return jax.shard_map(
        body,
        mesh=mesh,
        in_specs=placed,
        out_specs=(P(("piece", "col"), None), P(("piece", "col"), None)),
        check_vma=False,
    )
```

```python
import jax
import jax.numpy as jnp
import numpy as np
from jax import lax
from jax.experimental import pallas as pl
from jax.experimental.pallas import tpu as pltpu
from jax.sharding import PartitionSpec as P

ITERS = 2
SIDE = 4
LAYER = SIDE * SIDE
REACH = 2 * LAYER
SUB = 8
VMEM = pl.BlockSpec(memory_space=pltpu.VMEM)
SMEM = pl.BlockSpec(memory_space=pltpu.SMEM)
HBM = pl.BlockSpec(memory_space=pltpu.HBM)


def stencil_tables():
    levels = SIDE.bit_length() - 1

    def cell(code):
        across = sum((code >> (2 * level) & 1) << level for level in range(levels))
        along = sum((code >> (2 * level + 1) & 1) << level for level in range(levels))
        return across, along

    place = {cell(code): code for code in range(LAYER)}
    rows = []
    for code in range(LAYER):
        across, along = cell(code)
        rows.append(
            sorted(
                step_z * LAYER + place[across + step_x, along + step_y] - code
                for step_z in (-1, 0, 1)
                for step_y in (-1, 0, 1)
                for step_x in (-1, 0, 1)
                if (across + step_x, along + step_y) in place
            )
        )
    longest = max(len(row) for row in rows)
    offsets = np.zeros((LAYER, longest), np.int32)
    below = np.zeros((LAYER, 2 * REACH + 1), np.int32)
    for code, row in enumerate(rows):
        offsets[code, : len(row)] = row
        for t in range(-REACH, REACH + 1):
            below[code, t + REACH] = sum(offset < t for offset in row)
    return offsets, below


OFFSETS, BELOW = stencil_tables()
WIDEST = OFFSETS.shape[1]
TABLE = np.concatenate([OFFSETS, BELOW], 1)
STRIDE = TABLE.shape[1]
FLAT = np.concatenate([TABLE.reshape(-1), np.zeros(8, np.int32)])
LIMIT = pltpu.CompilerParams(vmem_limit_bytes=8 * 1024 * 1024)


def tile_bounds(share):
    inner = outer = 0
    for first in range(LAYER):
        for live in range(1, share + 1):
            near = far = 0
            for a in range(live):
                code = (first + a) % LAYER
                row = [int(o) for o in OFFSETS[code][: BELOW[code, -1]]]
                near += sum(0 <= a + o and o <= 0 for o in row)
                far += sum(a + o < 0 or a + o >= live for o in row)
            inner, outer = max(inner, near), max(outer, far)
    return inner, outer


def rank(table, code, t):
    return table[code * STRIDE + jnp.clip(t, -REACH, REACH) + REACH + WIDEST]


FIELDS = 6


def write_plan(meta, table, plan, a):
    code = lax.bitwise_and(meta[1] + a, LAYER - 1)
    place = meta[1] + a
    low, split, middle = rank(table, code, -place), rank(table, code, -a), rank(table, code, 0)
    resume, high = rank(table, code, meta[0] - a), rank(table, code, meta[2] - place)
    row = code * STRIDE
    ahead = split - low
    plan[a * FIELDS] = middle - split
    plan[a * FIELDS + 1] = row + split
    plan[a * FIELDS + 2] = ahead + jnp.maximum(high - resume, 0)
    plan[a * FIELDS + 3] = ahead
    plan[a * FIELDS + 4] = row + low
    plan[a * FIELDS + 5] = row + resume - ahead


def write_run(runs, at, a, start, count):
    runs[3 * at], runs[3 * at + 1], runs[3 * at + 2] = a, start, count
    return at + (count > 0).astype(jnp.int32)


def write_runs(meta, table, plan, inner_runs, outer_runs, share):
    inner = outer = total = far = jnp.int32(0)
    for a in range(share):
        write_plan(meta, table, plan, a)
        alive = a < meta[0]
        count, start, count_far, ahead, start_far, start_after = (plan[a * FIELDS + k] for k in range(FIELDS))
        inner = write_run(inner_runs, inner, a, start, jnp.where(alive, count + 1, 0))
        outer = write_run(outer_runs, outer, a, start_far, jnp.where(alive, ahead, 0))
        outer = write_run(outer_runs, outer, a, start_after + ahead, jnp.where(alive, count_far - ahead, 0))
        total = total + jnp.where(alive, count + 1, 0)
        far = far + jnp.where(alive, count_far, 0)
    for runs, at in ((inner_runs, inner), (outer_runs, outer)):
        write_run(runs, at, share, len(FLAT) - 8, jnp.int32(1))
    plan[share * FIELDS] = total
    plan[share * FIELDS + 1] = far
    plan[share * FIELDS + 2] = inner
    plan[share * FIELDS + 3] = outer


def inner_range(plan, table, a):
    start = plan[a * FIELDS + 1]
    return plan[a * FIELDS], lambda t: a + table[start + t]


def outer_range(plan, table, a):
    ahead, start, start_after = (plan[a * FIELDS + k] for k in (3, 4, 5))
    return plan[a * FIELDS + 2], lambda t: a + table[t + jnp.where(t < ahead, start, start_after)]


TURN = 4


def padded_sweep(count, fetch, step, carry):
    def turn(i, state):
        carry, *now = state
        later = [fetch(TURN * (i + 1) + k) for k in range(TURN)]
        return step(now, carry), *later

    state = (carry, *(fetch(k) for k in range(TURN)))
    return lax.fori_loop(0, lax.div(count + (TURN - 1), TURN), turn, state)[0]


def tree(terms):
    while len(terms) > 1:
        terms = [a + b for a, b in zip(terms[::2], terms[1::2])] + terms[len(terms) // 2 * 2 :]
    return terms[0]


def gather(partial, c, term):
    if c < len(partial):
        partial[c] = term
    else:
        partial[c % len(partial)] = partial[c % len(partial)] + term


def pieces_of(width):
    return [slice(c * SUB, (c + 1) * SUB) for c in range(width // SUB)]


def wide(row):
    return jnp.broadcast_to(row, (SUB, row.shape[1]))


def three_parts(values):
    high = values.astype(jnp.bfloat16).astype(jnp.float32)
    rest = values - high
    middle = rest.astype(jnp.bfloat16).astype(jnp.float32)
    return high, middle, rest - middle


def stacked(rows):
    sublane = lax.broadcasted_iota(jnp.int32, rows[0].shape, 0)
    result = jnp.zeros(rows[0].shape, jnp.float32)
    for k, row in enumerate(rows):
        result = jnp.where(sublane == k, row, result)
    return result


HALF = 64


def own_side(x):
    size = x[0] * x[0] + x[1] * x[1] + x[2] * x[2]
    one = jnp.ones_like(size)
    high, middle, low = three_parts(stacked([2.0 * x[0], 2.0 * x[1], 2.0 * x[2], one, 0.5 - size]))
    rest = jnp.zeros((HALF - 6 * SUB, size.shape[1]), jnp.float32)
    return jnp.concatenate([high, high, middle, middle, high, low, rest], 0)


def other_side(y):
    size = y[0] * y[0] + y[1] * y[1] + y[2] * y[2]
    one = jnp.ones_like(size)
    high, middle, low = three_parts(stacked([y[0], y[1], y[2], 0.5 - size, one]))
    first = jnp.concatenate([high, middle], 0).astype(jnp.bfloat16)
    last = jnp.concatenate([low, high], 0).astype(jnp.bfloat16)
    return jnp.concatenate([first, first, last, jnp.zeros((HALF - 6 * SUB, size.shape[1]), jnp.bfloat16)], 0)


GROUP = 4


def flat_tiles(count, runs, most, table, sides, middles, weights, other_at, buffers, tiles, rows_ref, cols_ref):
    share, width = rows_ref.shape[0] - 1, rows_ref.shape[2]
    chunks = pieces_of(width)

    def steps(state):
        found = []
        for _ in range(GROUP):
            run, t = state
            a, start, size = (runs[3 * run + k] for k in range(3))
            found.append((a, a + table[start + t]))
            over = t + 1 >= size
            state = jnp.minimum(run + over.astype(jnp.int32), most), jnp.where(over, 0, t + 1)
        return state, found

    def other_of(a, n):
        here = pl.ds(a, 1)
        return other_side([wide(other_at(c, n)) - wide(middles[c, here, :]) for c in range(3)])

    def products(found, ahead):
        none = jnp.zeros((HALF, width), jnp.bfloat16)
        for k in range(0, GROUP, 2):
            (a, n), (b, m) = ((jnp.minimum(a, share - 1), n) for a, n in found[k : k + 2])
            left = jnp.concatenate([other_of(a, n), none], 0)
            right = jnp.concatenate([none, other_of(b, m)], 0)
            both = jnp.dot(
                sides[0, a] + sides[1, b], jnp.concatenate([left, right], 1), preferred_element_type=jnp.float32
            )
            ahead[k] = both[:, :width]
            ahead[k + 1] = both[:, width:]

    def weigh(at, found, ahead):
        for k, (a, n) in enumerate(found):
            alone = a == n
            row = jnp.where(alone, share, a)
            own = jnp.minimum(a, share - 1)
            other = wide(other_at(3, n))
            down = [None] * 2
            for c, here in enumerate(chunks):
                left = ahead[k, here, :]
                rest = jnp.maximum(left, 0.0)
                inverse = pltpu.reciprocal((1.01 - left) * (weights[own, here, :] + other), approx=True)
                tile = rest * rest * inverse
                tiles[at + k, here, :] = tile
                rows_ref[row, here, :] = rows_ref[row, here, :] + tile
                if cols_ref is not None:
                    gather(down, c, tile)
            if cols_ref is not None:
                there = pl.ds(pl.multiple_of(jnp.where(alone, share, n) * SUB, SUB), SUB)
                cols_ref[there, :] = cols_ref[there, :] + tree(down)

    def turn(i, carry):
        state, found = carry
        at = i * (2 * GROUP)
        state, later = steps(state)
        products(later, buffers[1])
        weigh(at, found, buffers[0])
        state, last = steps(state)
        products(last, buffers[0])
        weigh(at + GROUP, later, buffers[1])
        return state, last

    state, found = steps((jnp.int32(0), jnp.int32(0)))
    products(found, buffers[0])
    lax.fori_loop(0, lax.div(count + (2 * GROUP - 1), 2 * GROUP), turn, (state, found))


def spread_columns(out, index, rows):
    count, width = rows.shape
    turned = rows.T
    for a in range(count):
        out[index(a)] = jnp.broadcast_to(turned[:, a : a + 1], (width, width))


def lane_sums(parts, count, width):
    lanes = lax.broadcasted_iota(jnp.int32, (width, width), 1)
    turned = jnp.zeros((width, width), jnp.float32)
    for a in range(count):
        turned = jnp.where(lanes == a, jnp.sum(parts[a], axis=1, keepdims=True), turned)
    return turned.T[:count]


def sub_sums(cols):
    return jnp.sum(cols[...].reshape(-1, SUB, cols.shape[1]), axis=1)


def alive_rows(meta, share, width):
    return lax.broadcasted_iota(jnp.int32, (share, width), 0) < meta[0]


def prepare(
    counts, densities, position_in, phase_in, right_side_in, table_in,
    meta, table, hood, near, density, source, first_swap, second_swap, phase, right_side, sems
):
    share, width = source.shape
    capacity = phase.shape[0]
    body_rows = pl.ds(share, capacity)
    copies = [
        pltpu.make_async_copy(phase_in, phase, sems.at[0]),
        pltpu.make_async_copy(position_in, hood.at[pl.ds(0, 3), body_rows, :], sems.at[1]),
        pltpu.make_async_copy(right_side_in, right_side, sems.at[2]),
        pltpu.make_async_copy(table_in, table, sems.at[3]),
    ]
    for copy in copies:
        copy.start()
    piece, column = lax.axis_index("piece"), lax.axis_index("col")
    filled = counts[piece]
    filled_before = counts[jnp.maximum(piece - 1, 0)]
    before = jnp.int32(0)
    total = jnp.int32(0)
    for p in range(counts.shape[0]):
        before = before + jnp.where(p < piece, counts[p], 0)
        total = total + counts[p]
    meta[0] = jnp.clip(filled - column * share, 0, share)
    meta[1] = before + column * share
    meta[2] = total
    meta[3] = column * share
    meta[4] = filled
    meta[5] = filled_before
    own_rows = pl.ds(pl.multiple_of(share + column * share, SUB), share)
    copies[0].wait()
    labels = phase[...]
    whole = sum(jnp.where(labels == k, densities[k], 0.0) for k in range(densities.shape[0]))
    hood[3, body_rows, :] = whole * (width / 2.0)
    density[...] = hood[3, own_rows, :] * (2.0 / width)
    copies[1].wait()
    even = lax.rem(piece, 2) == 0
    for k in range(4):
        tail, head = hood[k, pl.ds(filled, share), :], hood[k, share : 2 * share, :]
        first_swap[k] = jnp.where(even, tail, head)
        second_swap[k] = jnp.where(even, head, tail)
        near[k, 0:share, :] = hood[k, own_rows, :]
    for copy in copies[2:]:
        copy.wait()
    source[...] = jnp.where(alive_rows(meta, share, width), right_side[...], 0.0)


def finish_tiles(tiles, end):
    for t in range(TURN):
        tiles[end + t] = jnp.zeros(tiles.shape[1:], jnp.float32)


def build_inner(
    meta, table, near, plan, outer_runs, tiles, sides, middles, weights, rows_out, cols_out, self_ref,
    inner_runs, rows_ref, cols_ref, *buffers,
):
    share, width = rows_out.shape[0], rows_out.shape[2]
    chunks = pieces_of(width)
    write_runs(meta, table, plan, inner_runs, outer_runs, share)
    for k in range(3):
        first = near[k, 0:share, 0:1]
        middles[k] = jnp.broadcast_to(jnp.floor(first) + 0.5, (share, width))
    low = lax.broadcasted_iota(jnp.int32, (width, width), 1) < HALF
    for a in range(0, share, 2):
        pair = []
        for b in (a, a + 1):
            here = slice(b, b + 1)
            pair.append(own_side([wide(near[k, here, :] - middles[k, here, :]) for k in range(3)]))
        turned = jnp.concatenate(pair, 0).T
        moved = pltpu.roll(turned, HALF, 1)
        for at, b, half, side in ((0, a, low, turned), (1, a, ~low, moved), (0, a + 1, low, moved), (1, a + 1, ~low, turned)):
            sides[at, b] = jnp.where(half, side, 0.0).astype(jnp.bfloat16)
    spread_columns(weights, lambda a: a, near[3, 0:share, :])
    cols_ref[...] = jnp.zeros_like(cols_ref)
    rows_ref[...] = jnp.zeros_like(rows_ref)
    count = plan[share * FIELDS]
    flat_tiles(
        count, inner_runs, plan[share * FIELDS + 2], table, sides, middles, weights,
        lambda k, n: near[k, pl.ds(n, 1), :], buffers, tiles, rows_ref, cols_ref,
    )
    finish_tiles(tiles, count)
    lane = lax.broadcasted_iota(jnp.int32, (SUB, width), 1)
    sublane = lax.broadcasted_iota(jnp.int32, (SUB, width), 0)

    def block(a, at):
        at = at + plan[a * FIELDS]
        down = [None] * 4
        for c, here in enumerate(chunks):
            tile = jnp.where(lane == sublane + c * SUB, 0.0, tiles[at, here, :])
            tiles[at, here, :] = tile
            gather(down, c, tile)
        self_ref[pl.ds(pl.multiple_of(a * SUB, SUB), SUB), :] = tree(down)
        return at + 1

    lax.fori_loop(0, meta[0], block, 0)
    rows_out[...] = rows_ref[0:share]
    cols_out[...] = cols_ref[0 : share * SUB, :]


def count_listed(meta, lists, width):
    capacity = lists[0].shape[1]
    filled, filled_before = meta[4], meta[5]
    start = lax.axis_index("piece") * capacity
    steps = lax.broadcasted_iota(jnp.int32, (2 * REACH, capacity), 0)
    partial = [None] * 4
    row = 0
    for ref in lists:
        ids = ref[...]
        slot = ids - start
        gap = jnp.where(slot < 0, capacity - filled_before, jnp.where(slot >= capacity, filled - capacity, 0))
        away = slot - lax.broadcasted_iota(jnp.int32, ids.shape, 1) + gap
        away = jnp.where(ids < 0, -REACH, away) + REACH
        for k in range(ids.shape[0]):
            gather(partial, row, jnp.where(steps == away[k : k + 1], 1.0, 0.0))
            row += 1
    return jnp.concatenate([tree(partial), jnp.zeros((width - 2 * REACH, capacity), jnp.float32)], 0).T


def factor(times, a, n):
    lane = lax.broadcasted_iota(jnp.int32, (1, times.shape[1]), 1)
    return jnp.sum(jnp.where(lane == n - a + REACH, times[pl.ds(a, 1), :], 0.0), axis=1, keepdims=True)


def either(flag, run):
    @pl.when(flag == 0)
    def _():
        run(False)

    @pl.when(flag != 0)
    def _():
        run(True)


TAIL = 13


def build_outer(
    meta, table, plan, runs, around, first, second, density, source, tiles_in, sides, middles, weights,
    rows_ref, cols_ref, self_ref, *rest
):
    lists, rest = rest[:-TAIL], rest[-TAIL:]
    again_ref, tiles, diagonal_ref, precond_ref, times, alone_ref, hood, work, sums_ref, extra, all_times, *buffers = rest
    share, width = diagonal_ref.shape
    base, filled = meta[3], meta[4]
    even = lax.rem(lax.axis_index("piece"), 2) == 0
    for k in range(4):
        hood[k, 0:share, :] = jnp.where(even, second[k], first[k])
        hood[k, share:, :] = around[k, share:, :]
        hood[k, pl.ds(share + filled, share), :] = jnp.where(even, first[k], second[k])
    alive = alive_rows(meta, share, width)
    all_times[...] = count_listed(meta, lists, width)
    often = jnp.where(alive, all_times[pl.ds(pl.multiple_of(base, SUB), share), :], 0.0)
    times[...] = often
    lane = lax.broadcasted_iota(jnp.int32, (share, width), 1)
    again = jnp.max(jnp.where((lane == REACH) | (lane == 0), 0.0, often)) > 1.5
    again_ref[0] = again.astype(jnp.int32)


    work[...] = jnp.zeros_like(work)
    count = plan[share * FIELDS + 1]
    flat_tiles(
        count, runs, plan[share * FIELDS + 3], table, sides, middles, weights,
        lambda k, n: hood[k, pl.ds(base + share + n, 1), :], buffers, tiles, work, None,
    )
    finish_tiles(tiles, count)
    sums_ref[...] = lane_sums([rows_ref[a] + work[a] for a in range(share)], share, width) + sub_sums(cols_ref)

    @pl.when(again)
    def _():
        extra[...] = jnp.zeros_like(extra)
        work[...] = jnp.zeros_like(work)

        def block(a, state):
            count, place_of = inner_range(plan, table, a)

            def inner(t, at):
                n = place_of(t)
                tile = tiles_in[at]
                work[a] = work[a] + tile * factor(times, a, n)
                there = pl.ds(n, 1)
                down = jnp.sum(tile, axis=0, keepdims=True)
                extra[there, :] = extra[there, :] + down * factor(times, n, a)
                return at + 1

            at = lax.fori_loop(0, count, inner, state[0]) + 1
            count, place_far = outer_range(plan, table, a)

            def outer(t, at):
                work[a] = work[a] + tiles[at] * factor(times, a, place_far(t))
                return at + 1

            return at, lax.fori_loop(0, count, outer, state[1])

        lax.fori_loop(0, meta[0], block, (0, 0))
        sums_ref[...] = lane_sums(work, share, width) + extra[...]

    alone = jnp.sum(jnp.where(lane == REACH, often, 0.0), axis=1, keepdims=True)
    alone_ref[...] = jnp.broadcast_to(alone, (share, width))
    pairs = jnp.where(alive, sums_ref[...] + sub_sums(self_ref) * alone, 0.0)
    diagonal = 1.0 / density[...] + pairs
    diagonal_ref[...] = diagonal
    precond_ref[...] = source[...] / diagonal


def apply_inner(meta, table, plan, again, field, alone, times, tiles, rows_ref, cols_ref, spread, near, lone, cols):
    share, width = field.shape
    chunks = pieces_of(width)
    near[0:share, :] = field[...]
    near[share:, :] = jnp.zeros((SUB, width), jnp.float32)
    lone[...] = field[...] * alone[...]
    spread_columns(spread, lambda a: a, field[...])
    cols[...] = jnp.zeros_like(cols)

    def run(weighted):
        def block(a, at):
            count, place_of = inner_range(plan, table, a)

            def fetch(t):
                n = jnp.where(t < count, place_of(t), share)
                return n, wide(near[pl.ds(n, 1), :])

            def pairs(fetched, carry):
                at, sums = carry
                if weighted:
                    fetched = [(n, value * factor(times, a, jnp.minimum(n, share - 1))) for n, value in fetched]
                down = [[None] * 2 for _ in fetched]
                result = []
                for c, (here, total) in enumerate(zip(chunks, sums)):
                    own = spread[a, here, :]
                    found = []
                    for t, (_, value) in enumerate(fetched):
                        tile = tiles[at + t, here, :]
                        gather(down[t], c, tile * own)
                        found.append(tile * value)
                    result.append(total + tree(found))
                for (n, _), partial in zip(fetched, down):
                    there = pl.ds(pl.multiple_of(n * SUB, SUB), SUB)
                    partial = tree(partial)
                    if weighted:
                        partial = partial * factor(times, jnp.minimum(n, share - 1), a)
                    cols[there, :] = cols[there, :] + partial
                return at + len(fetched), result

            zero = jnp.zeros((SUB, width), jnp.float32)
            _, sums = padded_sweep(count, fetch, pairs, (at, [zero] * len(chunks)))
            at = at + count
            value = wide(lone[pl.ds(a, 1), :])
            for here, old in zip(chunks, sums):
                rows_ref[a, here, :] = old + tiles[at, here, :] * value
            return at + 1

        lax.fori_loop(0, meta[0], block, 0)

    either(again[0], run)
    cols_ref[...] = cols[0 : share * SUB, :]


def apply_outer(meta, table, plan, again, received, times, tiles, rows_ref, cols_ref, work, hood):
    first, second, *ends = received
    columns = len(received)
    share, width = first.shape
    chunks = pieces_of(width)
    base, filled = meta[3], meta[4]
    column = lax.div(base, share)
    odd = lax.rem(column, 2) == 1
    before = jnp.where(odd, first[...], second[...])
    after = jnp.where(odd, second[...], first[...])
    own = 3 * share
    for c, end in enumerate(ends, 1):
        hood[pl.ds(own - meta[5] + c * share, share), :] = end[...]
    from_last = own - meta[5] + (columns - 1) * share
    hood[pl.ds(jnp.where(column == 0, from_last, own - share), share), :] = before
    hood[own + share : own + 2 * share, :] = after
    head = after
    for c, end in enumerate(ends, 1):
        head = jnp.where(column == c, end[...], head)
    hood[pl.ds(own + jnp.clip(filled - base, 0, 2 * share), share), :] = head
    nothing = hood.shape[0] - SUB
    hood[nothing:, :] = jnp.zeros((SUB, width), jnp.float32)

    def run(weighted):
        def block(a, at):
            count, place_of = outer_range(plan, table, a)

            def fetch(t):
                place = place_of(t)
                value = hood[pl.ds(jnp.where(t < count, own + place, nothing), 1), :]
                if weighted:
                    value = value * factor(times, a, place)
                return wide(value)

            def pairs(values, carry):
                at, sums = carry
                result = []
                for here, total in zip(chunks, sums):
                    result.append(total + tree([tiles[at + t, here, :] * value for t, value in enumerate(values)]))
                return at + len(values), result

            _, sums = padded_sweep(count, fetch, pairs, (at, [rows_ref[a, here, :] for here in chunks]))
            for here, values in zip(chunks, sums):
                work[a, here, :] = values
            return at + count

        lax.fori_loop(0, meta[0], block, 0)

    either(again[0], run)
    return jnp.where(alive_rows(meta, share, width), lane_sums(work, share, width) + sub_sums(cols_ref), 0.0)


def apply_first(meta, table, plan, again, diagonal, times, *rest):
    *received, tiles, rows_ref, cols_ref, spill_ref, scaled_ref, work, hood = rest
    spill = apply_outer(meta, table, plan, again, received, times, tiles, rows_ref, cols_ref, work, hood)
    spill_ref[...] = spill
    scaled_ref[...] = spill / diagonal[...]


def apply_second(meta, table, plan, again, source, precond, spill, scaled, times, *rest):
    *received, tiles, rows_ref, cols_ref, twice_ref, sums_ref, work, hood = rest
    twice = apply_outer(meta, table, plan, again, received, times, tiles, rows_ref, cols_ref, work, hood)
    twice_ref[...] = twice
    share, width = twice.shape
    lane = lax.broadcasted_iota(jnp.int32, (1, width), 1)
    sums = jnp.zeros((1, width), jnp.float32)
    pairs = ((source[...], precond[...]), (spill[...], precond[...]), (spill[...], scaled[...]), (scaled[...], twice))
    for k, (first, second) in enumerate(pairs):
        along = jnp.sum(first * second, axis=0, keepdims=True)
        sums = jnp.where(lane == k, jnp.sum(along, axis=1, keepdims=True), sums)
    sums_ref[...] = wide(sums)


def finish(source, precond, spill, scaled, twice, *rest):
    *parts, solution_ref, residual_ref = rest
    sums = tree([ref[...] for ref in parts])

    def pick(k):
        return sums[0:1, k : k + 1]

    weighted, cross, square, last = pick(0), pick(1), pick(2), pick(3)
    part = cross / weighted
    advance = 1.0 / (1.0 - part)
    keep = -part * advance
    weighted_next = advance * advance * (square - cross * part)
    bent = keep * keep * cross + 2.0 * keep * advance * square + advance * advance * last
    blend = weighted_next / weighted
    advance_next = weighted_next / (weighted_next - bent - blend * weighted_next / advance)
    residual = keep * source[...] + advance * spill[...]
    next_precond = keep * precond[...] + advance * scaled[...]
    direction = next_precond + blend * precond[...]
    image = residual - keep * spill[...] - advance * twice[...] + blend * (source[...] - spill[...])
    solution_ref[...] = advance * precond[...] + advance_next * direction
    residual_ref[...] = residual - advance_next * image


def held(array):
    return pltpu.with_memory_space_constraint(array, pltpu.VMEM)


def body(positions, phase, neighbours, counts, phase_density, right_side):
    capacity, width = phase.shape
    columns = lax.axis_size("col")
    pieces = lax.axis_size("piece")
    share = capacity // columns
    f32 = jnp.float32
    vector = jax.ShapeDtypeStruct((share, width), f32)
    few = jax.ShapeDtypeStruct((SUB, width), f32)
    message = jax.ShapeDtypeStruct((4, share, width), f32)
    most_inner, most_outer = tile_bounds(share)
    inner_tiles = pltpu.VMEM((most_inner + 2 * GROUP, width, width), f32)
    outer_tiles = pltpu.VMEM((most_outer + 2 * GROUP, width, width), f32)
    ahead = pltpu.VMEM((GROUP, width, width), f32)
    square_more = pltpu.VMEM((share + 1, width, width), f32)
    square = pltpu.VMEM((share, width, width), f32)
    narrow = pltpu.VMEM((share * SUB, width), f32)
    table = jnp.asarray(FLAT)

    def call(kernel, args, outs, scratch=(), work=0, scalars=2, far=0, **more):
        return pl.pallas_call(
            kernel,
            out_shape=outs,
            in_specs=[SMEM] * scalars + [HBM] * far + [VMEM] * (len(args) - scalars - far),
            out_specs=[SMEM if getattr(o, "memory_space", None) == pltpu.SMEM else VMEM for o in outs],
            scratch_shapes=scratch,
            compiler_params=LIMIT,
            cost_estimate=pl.CostEstimate(flops=work * width * width, bytes_accessed=0, transcendentals=0),
            name=kernel.__name__,
            **more,
        )(*args)

    def swap(values, axis, step):
        return lax.ppermute(values, axis, [(i, i ^ step) for i in range(lax.axis_size(axis))])

    col_steps = [(1 << k) | 1 for k in range(columns.bit_length() - 1)]
    lists = [neighbours.T]
    for step in col_steps:
        known = lists[0] if len(lists) == 1 else jnp.concatenate(lists, 0)
        lists = [known, swap(known, "col", step)]

    def away(array):
        return pltpu.with_memory_space_constraint(array, pltpu.HBM)

    around = jax.ShapeDtypeStruct((4, capacity + 2 * share, width), f32)
    near = jax.ShapeDtypeStruct((4, 2 * share, width), f32)
    far = [away(array) for array in (positions, phase, right_side, table)]
    meta, table, around, near, density, source, first, second = call(
        prepare,
        (away(counts), away(phase_density), *far),
        [pltpu.SMEM((8,), jnp.int32), pltpu.SMEM(table.shape, jnp.int32), around, near, vector, vector, message, message],
        [pltpu.VMEM(phase.shape, jnp.int32), pltpu.VMEM((share, width), f32), pltpu.SemaphoreType.DMA((4,))],
        far=len(far),
    )
    meta, table = (pltpu.with_memory_space_constraint(array, pltpu.SMEM) for array in (meta, table))
    first = lax.ppermute(first, "piece", [(i, i ^ 1) for i in range(pieces)])
    axes = ("piece", "col")
    device = [(p, c) for p in range(pieces) for c in range(columns)]
    partner = [(p + (1 if p % 2 else -1), c) for p, c in device]
    partner = [(q, d) if 0 <= q < pieces else (p, c) for (q, d), (p, c) in zip(partner, device)]
    second = lax.ppermute(second, axes, [(i, q * columns + d) for i, (q, d) in enumerate(partner)])

    plan, runs, tiles_in, sides, middles, weights, rows, cols, selfs = call(
        build_inner,
        (meta, table, near),
        [pltpu.SMEM((share * FIELDS + 4,), jnp.int32), pltpu.SMEM((6 * share + 3,), jnp.int32), inner_tiles,
         pltpu.VMEM((2, share, width, width), jnp.bfloat16), pltpu.VMEM((3, share, width), f32), square, square, narrow, narrow],
        [pltpu.SMEM((3 * share + 3,), jnp.int32), square_more, pltpu.VMEM(((share + 1) * SUB, width), f32), ahead, ahead],
        16 * most_inner,
    )
    plan, runs = (pltpu.with_memory_space_constraint(array, pltpu.SMEM) for array in (plan, runs))
    again, tiles_out, diagonal, precond, times, alone = call(
        build_outer,
        (meta, table, plan, runs, around, first, second, density, source,
         held(tiles_in), held(sides), held(middles), held(weights), held(rows), held(cols), held(selfs), *lists),
        [pltpu.SMEM((1,), jnp.int32), outer_tiles, vector, vector, vector, vector],
        [pltpu.VMEM((4, capacity + 2 * share, width), f32), square_more]
        + [pltpu.VMEM((share, width), f32)] * 2 + [pltpu.VMEM((capacity, width), f32), ahead, ahead],
        16 * most_outer,
        scalars=4,
    )
    again = pltpu.with_memory_space_constraint(again, pltpu.SMEM)

    def inner(field):
        return call(
            apply_inner,
            (meta, table, plan, again, field, alone, times, held(tiles_in)),
            [square, narrow],
            [pltpu.VMEM((share, width, width), f32), pltpu.VMEM((share + SUB, width), f32), pltpu.VMEM((share, width), f32),
             pltpu.VMEM(((share + 1) * SUB, width), f32)],
            4 * most_inner,
            scalars=4,
        )

    def exchange(field):
        count = pieces * columns
        swaps = [[i ^ 1 for i in range(count)], [i - 1 if i % 2 == 0 else i + 1 for i in range(count)]]
        swaps[1][0], swaps[1][-1] = 0, count - 1
        for c in range(1, columns - 1):
            to = {}
            for p in range(pieces - 1):
                low, high = p * columns + c, (p + 1) * columns
                to[low], to[high] = high, low
            swaps.append([to.get(i, i) for i in range(count)])
        return [lax.ppermute(field, axes, list(enumerate(to))) for to in swaps]

    scratch = [pltpu.VMEM((share, width, width), f32), pltpu.VMEM((8 * share, width), f32)]

    received = exchange(precond)
    rows, cols = inner(precond)
    spill, scaled = call(
        apply_first,
        (meta, table, plan, again, diagonal, times, *received, held(tiles_out), held(rows), held(cols)),
        [vector, vector],
        scratch,
        2 * most_outer,
        scalars=4,
    )

    received = exchange(scaled)
    rows, cols = inner(scaled)
    twice, sums = call(
        apply_second,
        (meta, table, plan, again, source, precond, spill, scaled, times, *received, held(tiles_out), held(rows), held(cols)),
        [vector, few],
        scratch,
        2 * most_outer,
        scalars=4,
    )

    def together(values, axis, low, size):
        return tree([values] + [swap(values, axis, low * k) for k in range(1, size)])

    sums = together(sums, "piece", 1, 2)
    for step in col_steps:
        sums = sums + swap(sums, "col", step)
    step = 2
    while pieces // step > 4:
        sums = together(sums, "piece", step, 4)
        step *= 4
    others = [swap(sums, "piece", step * k) for k in range(1, pieces // step)]

    return tuple(call(
        finish,
        (source, precond, spill, scaled, twice, sums, *others),
        [vector, vector],
        scalars=0,
    ))


def solution(mesh):
    placed = (
        P(None, "piece", None),
        P("piece", None),
        P("piece", "col"),
        P(),
        P(),
        P(("piece", "col"), None),
    )
    return jax.shard_map(
        body,
        mesh=mesh,
        in_specs=placed,
        out_specs=(P(("piece", "col"), None), P(("piece", "col"), None)),
        check_vma=False,
    )
```

```python
import jax
import jax.numpy as jnp
import numpy as np
from jax import lax
from jax.experimental import pallas as pl
from jax.experimental.pallas import tpu as pltpu
from jax.sharding import PartitionSpec as P

ITERS = 2
SIDE = 4
LAYER = SIDE * SIDE
REACH = 2 * LAYER
SUB = 8
VMEM = pl.BlockSpec(memory_space=pltpu.VMEM)
SMEM = pl.BlockSpec(memory_space=pltpu.SMEM)
HBM = pl.BlockSpec(memory_space=pltpu.HBM)


def stencil_tables():
    levels = SIDE.bit_length() - 1

    def cell(code):
        across = sum((code >> (2 * level) & 1) << level for level in range(levels))
        along = sum((code >> (2 * level + 1) & 1) << level for level in range(levels))
        return across, along

    place = {cell(code): code for code in range(LAYER)}
    rows = []
    for code in range(LAYER):
        across, along = cell(code)
        rows.append(
            sorted(
                step_z * LAYER + place[across + step_x, along + step_y] - code
                for step_z in (-1, 0, 1)
                for step_y in (-1, 0, 1)
                for step_x in (-1, 0, 1)
                if (across + step_x, along + step_y) in place
            )
        )
    longest = max(len(row) for row in rows)
    offsets = np.zeros((LAYER, longest), np.int32)
    below = np.zeros((LAYER, 2 * REACH + 1), np.int32)
    for code, row in enumerate(rows):
        offsets[code, : len(row)] = row
        for t in range(-REACH, REACH + 1):
            below[code, t + REACH] = sum(offset < t for offset in row)
    return offsets, below


OFFSETS, BELOW = stencil_tables()
WIDEST = OFFSETS.shape[1]
TABLE = np.concatenate([OFFSETS, BELOW], 1)
STRIDE = TABLE.shape[1]
FLAT = np.concatenate([TABLE.reshape(-1), np.zeros(8, np.int32)])
LIMIT = pltpu.CompilerParams(vmem_limit_bytes=8 * 1024 * 1024)


def tile_bounds(share):
    inner = outer = 0
    for first in range(LAYER):
        for live in range(1, share + 1):
            near = far = 0
            for a in range(live):
                code = (first + a) % LAYER
                row = [int(o) for o in OFFSETS[code][: BELOW[code, -1]]]
                near += sum(0 <= a + o and o <= 0 for o in row)
                far += sum(a + o < 0 or a + o >= live for o in row)
            inner, outer = max(inner, near), max(outer, far)
    return inner, outer


def rank(table, code, t):
    return table[code * STRIDE + jnp.clip(t, -REACH, REACH) + REACH + WIDEST]


FIELDS = 6


def write_plan(meta, table, plan, a):
    code = lax.bitwise_and(meta[1] + a, LAYER - 1)
    place = meta[1] + a
    low, split, middle = rank(table, code, -place), rank(table, code, -a), rank(table, code, 0)
    resume, high = rank(table, code, meta[0] - a), rank(table, code, meta[2] - place)
    row = code * STRIDE
    ahead = split - low
    plan[a * FIELDS] = middle - split
    plan[a * FIELDS + 1] = row + split
    plan[a * FIELDS + 2] = ahead + jnp.maximum(high - resume, 0)
    plan[a * FIELDS + 3] = ahead
    plan[a * FIELDS + 4] = row + low
    plan[a * FIELDS + 5] = row + resume - ahead


def write_run(runs, at, a, start, count):
    runs[3 * at], runs[3 * at + 1], runs[3 * at + 2] = a, start, count
    return at + (count > 0).astype(jnp.int32)


def write_runs(meta, table, plan, inner_runs, outer_runs, share):
    inner = outer = total = far = jnp.int32(0)
    for a in range(share):
        write_plan(meta, table, plan, a)
        alive = a < meta[0]
        count, start, count_far, ahead, start_far, start_after = (plan[a * FIELDS + k] for k in range(FIELDS))
        inner = write_run(inner_runs, inner, a, start, jnp.where(alive, count + 1, 0))
        outer = write_run(outer_runs, outer, a, start_far, jnp.where(alive, ahead, 0))
        outer = write_run(outer_runs, outer, a, start_after + ahead, jnp.where(alive, count_far - ahead, 0))
        total = total + jnp.where(alive, count + 1, 0)
        far = far + jnp.where(alive, count_far, 0)
    for runs, at in ((inner_runs, inner), (outer_runs, outer)):
        write_run(runs, at, share, len(FLAT) - 8, jnp.int32(1))
    plan[share * FIELDS] = total
    plan[share * FIELDS + 1] = far
    plan[share * FIELDS + 2] = inner
    plan[share * FIELDS + 3] = outer


def inner_range(plan, table, a):
    start = plan[a * FIELDS + 1]
    return plan[a * FIELDS], lambda t: a + table[start + t]


def outer_range(plan, table, a):
    ahead, start, start_after = (plan[a * FIELDS + k] for k in (3, 4, 5))
    return plan[a * FIELDS + 2], lambda t: a + table[t + jnp.where(t < ahead, start, start_after)]


TURN = 3


def padded_sweep(count, fetch, step, carry):
    def turn(i, state):
        carry, *now = state
        later = [fetch(TURN * (i + 1) + k) for k in range(TURN)]
        return step(now, carry), *later

    state = (carry, *(fetch(k) for k in range(TURN)))
    return lax.fori_loop(0, lax.div(count + (TURN - 1), TURN), turn, state)[0]


def tree(terms):
    while len(terms) > 1:
        terms = [a + b for a, b in zip(terms[::2], terms[1::2])] + terms[len(terms) // 2 * 2 :]
    return terms[0]


def gather(partial, c, term):
    if c < len(partial):
        partial[c] = term
    else:
        partial[c % len(partial)] = partial[c % len(partial)] + term


def pieces_of(width):
    return [slice(c * SUB, (c + 1) * SUB) for c in range(width // SUB)]


def wide(row):
    return jnp.broadcast_to(row, (SUB, row.shape[1]))


def three_parts(values):
    high = values.astype(jnp.bfloat16).astype(jnp.float32)
    rest = values - high
    middle = rest.astype(jnp.bfloat16).astype(jnp.float32)
    return high, middle, rest - middle


def stacked(rows):
    sublane = lax.broadcasted_iota(jnp.int32, rows[0].shape, 0)
    result = jnp.zeros(rows[0].shape, jnp.float32)
    for k, row in enumerate(rows):
        result = jnp.where(sublane == k, row, result)
    return result


def half_size(x):
    return 0.5 - (x[0] * x[0] + x[1] * x[1] + x[2] * x[2])


def own_side(x, which):
    nothing = [jnp.zeros_like(x[0])] * 4
    rows = [2.0 * x[0], 2.0 * x[1], 2.0 * x[2], jnp.ones_like(x[0])]
    high, middle, low = three_parts(stacked(nothing + rows if which else rows))
    sizes = stacked(list(three_parts(half_size(x))))
    width = sizes.shape[1]
    rest = jnp.zeros((width - 7 * SUB, width), jnp.float32)
    return jnp.concatenate([high, high, middle, middle, high, low, sizes, rest], 0)


def other_sides(first, second):
    rows = [*first, half_size(first), *second, half_size(second)]
    high, middle, low = three_parts(stacked(rows))
    width = high.shape[1]
    ones = jnp.where(lax.broadcasted_iota(jnp.int32, (2 * SUB, width), 0) < 3, 1.0, 0.0).astype(jnp.bfloat16)
    front = jnp.concatenate([high, middle], 0).astype(jnp.bfloat16)
    back = jnp.concatenate([low, high], 0).astype(jnp.bfloat16)
    rest = jnp.zeros((width - 8 * SUB, width), jnp.bfloat16)
    return jnp.concatenate([front, front, back, ones, rest], 0)


GROUP = 4


def flat_tiles(count, runs, most, table, sides, middles, weights, other_at, buffers, tiles, rows_ref, cols_ref):
    share, width = rows_ref.shape[0] - 1, rows_ref.shape[2]
    chunks = pieces_of(width)

    def steps(state):
        found = []
        for _ in range(GROUP):
            run, t = state
            a, start, size = (runs[3 * run + k] for k in range(3))
            found.append((a, a + table[start + t]))
            over = t + 1 >= size
            state = jnp.minimum(run + over.astype(jnp.int32), most), jnp.where(over, 0, t + 1)
        return state, found

    def other_of(a, n):
        here = pl.ds(a, 1)
        return [wide(other_at(c, n)) - wide(middles[c, here, :]) for c in range(3)]

    def products(found, ahead):
        for k in range(0, GROUP, 2):
            (a, n), (b, m) = ((jnp.minimum(a, share - 1), n) for a, n in found[k : k + 2])
            own = jnp.concatenate([sides[0, a], sides[1, b]], 0)
            both = jnp.dot(own, other_sides(other_of(a, n), other_of(b, m)), preferred_element_type=jnp.float32)
            ahead[k] = both[:width]
            ahead[k + 1] = both[width:]

    def weigh(at, found, ahead):
        for k, (a, n) in enumerate(found):
            alone = a == n
            row = jnp.where(alone, share, a)
            own = jnp.minimum(a, share - 1)
            other = wide(other_at(3, n))
            down = [None] * 2
            for c, here in enumerate(chunks):
                left = ahead[k, here, :]
                rest = jnp.maximum(left, 0.0)
                inverse = pltpu.reciprocal((1.01 - left) * (weights[own, here, :] + other), approx=True)
                tile = rest * rest * inverse
                tiles[at + k, here, :] = tile
                rows_ref[row, here, :] = rows_ref[row, here, :] + tile
                if cols_ref is not None:
                    gather(down, c, tile)
            if cols_ref is not None:
                there = pl.ds(pl.multiple_of(jnp.where(alone, share, n) * SUB, SUB), SUB)
                cols_ref[there, :] = cols_ref[there, :] + tree(down)

    def turn(i, carry):
        state, found = carry
        at = i * (2 * GROUP)
        state, later = steps(state)
        products(later, buffers[1])
        weigh(at, found, buffers[0])
        state, last = steps(state)
        products(last, buffers[0])
        weigh(at + GROUP, later, buffers[1])
        return state, last

    state, found = steps((jnp.int32(0), jnp.int32(0)))
    products(found, buffers[0])
    lax.fori_loop(0, lax.div(count + (2 * GROUP - 1), 2 * GROUP), turn, (state, found))


def spread_columns(out, index, rows):
    count, width = rows.shape
    turned = rows.T
    for a in range(count):
        out[index(a)] = jnp.broadcast_to(turned[:, a : a + 1], (width, width))


def lane_sums(parts, count, width):
    lanes = lax.broadcasted_iota(jnp.int32, (width, width), 1)
    turned = jnp.zeros((width, width), jnp.float32)
    for a in range(count):
        turned = jnp.where(lanes == a, jnp.sum(parts[a], axis=1, keepdims=True), turned)
    return turned.T[:count]


def sub_sums(cols):
    return jnp.sum(cols[...].reshape(-1, SUB, cols.shape[1]), axis=1)


def alive_rows(meta, share, width):
    return lax.broadcasted_iota(jnp.int32, (share, width), 0) < meta[0]


def prepare(
    counts, densities, position_in, phase_in, right_side_in, table_in,
    meta, table, hood, near, density, source, first_swap, second_swap, phase, right_side, sems
):
    share, width = source.shape
    capacity = phase.shape[0]
    body_rows = pl.ds(share, capacity)
    copies = [
        pltpu.make_async_copy(phase_in, phase, sems.at[0]),
        pltpu.make_async_copy(position_in, hood.at[pl.ds(0, 3), body_rows, :], sems.at[1]),
        pltpu.make_async_copy(right_side_in, right_side, sems.at[2]),
        pltpu.make_async_copy(table_in, table, sems.at[3]),
    ]
    for copy in copies:
        copy.start()
    piece, column = lax.axis_index("piece"), lax.axis_index("col")
    filled = counts[piece]
    filled_before = counts[jnp.maximum(piece - 1, 0)]
    before = jnp.int32(0)
    total = jnp.int32(0)
    for p in range(counts.shape[0]):
        before = before + jnp.where(p < piece, counts[p], 0)
        total = total + counts[p]
    meta[0] = jnp.clip(filled - column * share, 0, share)
    meta[1] = before + column * share
    meta[2] = total
    meta[3] = column * share
    meta[4] = filled
    meta[5] = filled_before
    own_rows = pl.ds(pl.multiple_of(share + column * share, SUB), share)
    copies[0].wait()
    labels = phase[...]
    whole = sum(jnp.where(labels == k, densities[k], 0.0) for k in range(densities.shape[0]))
    hood[3, body_rows, :] = whole * (width / 2.0)
    density[...] = hood[3, own_rows, :] * (2.0 / width)
    copies[1].wait()
    even = lax.rem(piece, 2) == 0
    for k in range(4):
        tail, head = hood[k, pl.ds(filled, share), :], hood[k, share : 2 * share, :]
        first_swap[k] = jnp.where(even, tail, head)
        second_swap[k] = jnp.where(even, head, tail)
        near[k, 0:share, :] = hood[k, own_rows, :]
    for copy in copies[2:]:
        copy.wait()
    source[...] = jnp.where(alive_rows(meta, share, width), right_side[...], 0.0)


def finish_tiles(tiles, end):
    for t in range(TURN):
        tiles[end + t] = jnp.zeros(tiles.shape[1:], jnp.float32)


def build_inner(
    meta, table, near, plan, outer_runs, tiles, sides, middles, weights, rows_out, cols_out, self_ref,
    inner_runs, rows_ref, cols_ref, *buffers,
):
    share, width = rows_out.shape[0], rows_out.shape[2]
    chunks = pieces_of(width)
    write_runs(meta, table, plan, inner_runs, outer_runs, share)
    for k in range(3):
        first = near[k, 0:share, 0:1]
        middles[k] = jnp.broadcast_to(jnp.floor(first) + 0.5, (share, width))
    for a in range(share):
        here = slice(a, a + 1)
        centred = [wide(near[k, here, :] - middles[k, here, :]) for k in range(3)]
        for which in range(2):
            sides[which, a] = own_side(centred, which).T.astype(jnp.bfloat16)
    spread_columns(weights, lambda a: a, near[3, 0:share, :])
    cols_ref[...] = jnp.zeros_like(cols_ref)
    rows_ref[...] = jnp.zeros_like(rows_ref)
    count = plan[share * FIELDS]
    flat_tiles(
        count, inner_runs, plan[share * FIELDS + 2], table, sides, middles, weights,
        lambda k, n: near[k, pl.ds(n, 1), :], buffers, tiles, rows_ref, cols_ref,
    )
    finish_tiles(tiles, count)
    lane = lax.broadcasted_iota(jnp.int32, (SUB, width), 1)
    sublane = lax.broadcasted_iota(jnp.int32, (SUB, width), 0)

    def block(a, at):
        at = at + plan[a * FIELDS]
        down = [None] * 4
        for c, here in enumerate(chunks):
            tile = jnp.where(lane == sublane + c * SUB, 0.0, tiles[at, here, :])
            tiles[at, here, :] = tile
            gather(down, c, tile)
        self_ref[pl.ds(pl.multiple_of(a * SUB, SUB), SUB), :] = tree(down)
        return at + 1

    lax.fori_loop(0, meta[0], block, 0)
    rows_out[...] = rows_ref[0:share]
    cols_out[...] = cols_ref[0 : share * SUB, :]


def count_listed(meta, lists, width):
    capacity = lists[0].shape[1]
    filled, filled_before = meta[4], meta[5]
    start = lax.axis_index("piece") * capacity
    steps = lax.broadcasted_iota(jnp.int32, (2 * REACH, capacity), 0)
    partial = [None] * 4
    row = 0
    for ref in lists:
        ids = ref[...]
        slot = ids - start
        gap = jnp.where(slot < 0, capacity - filled_before, jnp.where(slot >= capacity, filled - capacity, 0))
        away = slot - lax.broadcasted_iota(jnp.int32, ids.shape, 1) + gap
        away = jnp.where(ids < 0, -REACH, away) + REACH
        for k in range(ids.shape[0]):
            gather(partial, row, jnp.where(steps == away[k : k + 1], 1.0, 0.0))
            row += 1
    return jnp.concatenate([tree(partial), jnp.zeros((width - 2 * REACH, capacity), jnp.float32)], 0).T


def factor(times, a, n):
    lane = lax.broadcasted_iota(jnp.int32, (1, times.shape[1]), 1)
    return jnp.sum(jnp.where(lane == n - a + REACH, times[pl.ds(a, 1), :], 0.0), axis=1, keepdims=True)


def either(flag, run):
    @pl.when(flag == 0)
    def _():
        run(False)

    @pl.when(flag != 0)
    def _():
        run(True)


TAIL = 13


def build_outer(
    meta, table, plan, runs, around, first, second, density, source, tiles_in, sides, middles, weights,
    rows_ref, cols_ref, self_ref, *rest
):
    lists, rest = rest[:-TAIL], rest[-TAIL:]
    again_ref, tiles, diagonal_ref, precond_ref, times, alone_ref, hood, work, sums_ref, extra, all_times, *buffers = rest
    share, width = diagonal_ref.shape
    base, filled = meta[3], meta[4]
    even = lax.rem(lax.axis_index("piece"), 2) == 0
    for k in range(4):
        hood[k, 0:share, :] = jnp.where(even, second[k], first[k])
        hood[k, share:, :] = around[k, share:, :]
        hood[k, pl.ds(share + filled, share), :] = jnp.where(even, first[k], second[k])
    alive = alive_rows(meta, share, width)
    all_times[...] = count_listed(meta, lists, width)
    often = jnp.where(alive, all_times[pl.ds(pl.multiple_of(base, SUB), share), :], 0.0)
    times[...] = often
    lane = lax.broadcasted_iota(jnp.int32, (share, width), 1)
    again = jnp.max(jnp.where((lane == REACH) | (lane == 0), 0.0, often)) > 1.5
    again_ref[0] = again.astype(jnp.int32)


    work[...] = jnp.zeros_like(work)
    count = plan[share * FIELDS + 1]
    flat_tiles(
        count, runs, plan[share * FIELDS + 3], table, sides, middles, weights,
        lambda k, n: hood[k, pl.ds(base + share + n, 1), :], buffers, tiles, work, None,
    )
    finish_tiles(tiles, count)
    sums_ref[...] = lane_sums([rows_ref[a] + work[a] for a in range(share)], share, width) + sub_sums(cols_ref)

    @pl.when(again)
    def _():
        extra[...] = jnp.zeros_like(extra)
        work[...] = jnp.zeros_like(work)

        def block(a, state):
            count, place_of = inner_range(plan, table, a)

            def inner(t, at):
                n = place_of(t)
                tile = tiles_in[at]
                work[a] = work[a] + tile * factor(times, a, n)
                there = pl.ds(n, 1)
                down = jnp.sum(tile, axis=0, keepdims=True)
                extra[there, :] = extra[there, :] + down * factor(times, n, a)
                return at + 1

            at = lax.fori_loop(0, count, inner, state[0]) + 1
            count, place_far = outer_range(plan, table, a)

            def outer(t, at):
                work[a] = work[a] + tiles[at] * factor(times, a, place_far(t))
                return at + 1

            return at, lax.fori_loop(0, count, outer, state[1])

        lax.fori_loop(0, meta[0], block, (0, 0))
        sums_ref[...] = lane_sums(work, share, width) + extra[...]

    alone = jnp.sum(jnp.where(lane == REACH, often, 0.0), axis=1, keepdims=True)
    alone_ref[...] = jnp.broadcast_to(alone, (share, width))
    pairs = jnp.where(alive, sums_ref[...] + sub_sums(self_ref) * alone, 0.0)
    diagonal = 1.0 / density[...] + pairs
    diagonal_ref[...] = diagonal
    precond_ref[...] = source[...] / diagonal


def apply_inner(meta, table, plan, again, field, alone, times, tiles, rows_ref, cols_ref, spread, near, lone, cols):
    share, width = field.shape
    chunks = pieces_of(width)
    near[0:share, :] = field[...]
    near[share:, :] = jnp.zeros((SUB, width), jnp.float32)
    lone[...] = field[...] * alone[...]
    spread_columns(spread, lambda a: a, field[...])
    cols[...] = jnp.zeros_like(cols)

    def run(weighted):
        def block(a, at):
            count, place_of = inner_range(plan, table, a)

            def fetch(t):
                n = jnp.where(t < count, place_of(t), share)
                return n, wide(near[pl.ds(n, 1), :])

            def pairs(fetched, carry):
                at, sums = carry
                if weighted:
                    fetched = [(n, value * factor(times, a, jnp.minimum(n, share - 1))) for n, value in fetched]
                down = [[None] * 2 for _ in fetched]
                result = []
                for c, (here, total) in enumerate(zip(chunks, sums)):
                    own = spread[a, here, :]
                    found = []
                    for t, (_, value) in enumerate(fetched):
                        tile = tiles[at + t, here, :]
                        gather(down[t], c, tile * own)
                        found.append(tile * value)
                    result.append(total + tree(found))
                for (n, _), partial in zip(fetched, down):
                    there = pl.ds(pl.multiple_of(n * SUB, SUB), SUB)
                    partial = tree(partial)
                    if weighted:
                        partial = partial * factor(times, jnp.minimum(n, share - 1), a)
                    cols[there, :] = cols[there, :] + partial
                return at + len(fetched), result

            zero = jnp.zeros((SUB, width), jnp.float32)
            _, sums = padded_sweep(count, fetch, pairs, (at, [zero] * len(chunks)))
            at = at + count
            value = wide(lone[pl.ds(a, 1), :])
            for here, old in zip(chunks, sums):
                rows_ref[a, here, :] = old + tiles[at, here, :] * value
            return at + 1

        lax.fori_loop(0, meta[0], block, 0)

    either(again[0], run)
    cols_ref[...] = cols[0 : share * SUB, :]


def apply_outer(meta, table, plan, again, received, times, tiles, rows_ref, cols_ref, work, hood):
    first, second, *ends = received
    columns = len(received)
    share, width = first.shape
    chunks = pieces_of(width)
    base, filled = meta[3], meta[4]
    column = lax.div(base, share)
    odd = lax.rem(column, 2) == 1
    before = jnp.where(odd, first[...], second[...])
    after = jnp.where(odd, second[...], first[...])
    own = 3 * share
    for c, end in enumerate(ends, 1):
        hood[pl.ds(own - meta[5] + c * share, share), :] = end[...]
    from_last = own - meta[5] + (columns - 1) * share
    hood[pl.ds(jnp.where(column == 0, from_last, own - share), share), :] = before
    hood[own + share : own + 2 * share, :] = after
    head = after
    for c, end in enumerate(ends, 1):
        head = jnp.where(column == c, end[...], head)
    hood[pl.ds(own + jnp.clip(filled - base, 0, 2 * share), share), :] = head
    nothing = hood.shape[0] - SUB
    hood[nothing:, :] = jnp.zeros((SUB, width), jnp.float32)

    def run(weighted):
        def block(a, at):
            count, place_of = outer_range(plan, table, a)

            def fetch(t):
                place = place_of(t)
                value = hood[pl.ds(jnp.where(t < count, own + place, nothing), 1), :]
                if weighted:
                    value = value * factor(times, a, place)
                return wide(value)

            def pairs(values, carry):
                at, sums = carry
                result = []
                for here, total in zip(chunks, sums):
                    result.append(total + tree([tiles[at + t, here, :] * value for t, value in enumerate(values)]))
                return at + len(values), result

            _, sums = padded_sweep(count, fetch, pairs, (at, [rows_ref[a, here, :] for here in chunks]))
            for here, values in zip(chunks, sums):
                work[a, here, :] = values
            return at + count

        lax.fori_loop(0, meta[0], block, 0)

    either(again[0], run)
    return jnp.where(alive_rows(meta, share, width), lane_sums(work, share, width) + sub_sums(cols_ref), 0.0)


def apply_first(meta, table, plan, again, diagonal, times, *rest):
    *received, tiles, rows_ref, cols_ref, spill_ref, scaled_ref, work, hood = rest
    spill = apply_outer(meta, table, plan, again, received, times, tiles, rows_ref, cols_ref, work, hood)
    spill_ref[...] = spill
    scaled_ref[...] = spill / diagonal[...]


def apply_second(meta, table, plan, again, source, precond, spill, scaled, times, *rest):
    *received, tiles, rows_ref, cols_ref, twice_ref, sums_ref, work, hood = rest
    twice = apply_outer(meta, table, plan, again, received, times, tiles, rows_ref, cols_ref, work, hood)
    twice_ref[...] = twice
    share, width = twice.shape
    lane = lax.broadcasted_iota(jnp.int32, (1, width), 1)
    sums = jnp.zeros((1, width), jnp.float32)
    pairs = ((source[...], precond[...]), (spill[...], precond[...]), (spill[...], scaled[...]), (scaled[...], twice))
    for k, (first, second) in enumerate(pairs):
        along = jnp.sum(first * second, axis=0, keepdims=True)
        sums = jnp.where(lane == k, jnp.sum(along, axis=1, keepdims=True), sums)
    sums_ref[...] = wide(sums)


def finish(source, precond, spill, scaled, twice, *rest):
    *parts, solution_ref, residual_ref = rest
    sums = tree([ref[...] for ref in parts])

    def pick(k):
        return sums[0:1, k : k + 1]

    weighted, cross, square, last = pick(0), pick(1), pick(2), pick(3)
    part = cross / weighted
    advance = 1.0 / (1.0 - part)
    keep = -part * advance
    weighted_next = advance * advance * (square - cross * part)
    bent = keep * keep * cross + 2.0 * keep * advance * square + advance * advance * last
    blend = weighted_next / weighted
    advance_next = weighted_next / (weighted_next - bent - blend * weighted_next / advance)
    residual = keep * source[...] + advance * spill[...]
    next_precond = keep * precond[...] + advance * scaled[...]
    direction = next_precond + blend * precond[...]
    image = residual - keep * spill[...] - advance * twice[...] + blend * (source[...] - spill[...])
    solution_ref[...] = advance * precond[...] + advance_next * direction
    residual_ref[...] = residual - advance_next * image


def held(array):
    return pltpu.with_memory_space_constraint(array, pltpu.VMEM)


def body(positions, phase, neighbours, counts, phase_density, right_side):
    capacity, width = phase.shape
    columns = lax.axis_size("col")
    pieces = lax.axis_size("piece")
    share = capacity // columns
    f32 = jnp.float32
    vector = jax.ShapeDtypeStruct((share, width), f32)
    few = jax.ShapeDtypeStruct((SUB, width), f32)
    message = jax.ShapeDtypeStruct((4, share, width), f32)
    most_inner, most_outer = tile_bounds(share)
    inner_tiles = pltpu.VMEM((most_inner + 2 * GROUP, width, width), f32)
    outer_tiles = pltpu.VMEM((most_outer + 2 * GROUP, width, width), f32)
    ahead = pltpu.VMEM((GROUP, width, width), f32)
    square_more = pltpu.VMEM((share + 1, width, width), f32)
    square = pltpu.VMEM((share, width, width), f32)
    narrow = pltpu.VMEM((share * SUB, width), f32)
    table = jnp.asarray(FLAT)

    def call(kernel, args, outs, scratch=(), work=0, scalars=2, far=0, **more):
        return pl.pallas_call(
            kernel,
            out_shape=outs,
            in_specs=[SMEM] * scalars + [HBM] * far + [VMEM] * (len(args) - scalars - far),
            out_specs=[SMEM if getattr(o, "memory_space", None) == pltpu.SMEM else VMEM for o in outs],
            scratch_shapes=scratch,
            compiler_params=LIMIT,
            cost_estimate=pl.CostEstimate(flops=work * width * width, bytes_accessed=0, transcendentals=0),
            name=kernel.__name__,
            **more,
        )(*args)

    def swap(values, axis, step):
        return lax.ppermute(values, axis, [(i, i ^ step) for i in range(lax.axis_size(axis))])

    col_steps = [(1 << k) | 1 for k in range(columns.bit_length() - 1)]
    lists = [neighbours.T]
    for step in col_steps:
        known = lists[0] if len(lists) == 1 else jnp.concatenate(lists, 0)
        lists = [known, swap(known, "col", step)]

    def away(array):
        return pltpu.with_memory_space_constraint(array, pltpu.HBM)

    around = jax.ShapeDtypeStruct((4, capacity + 2 * share, width), f32)
    near = jax.ShapeDtypeStruct((4, 2 * share, width), f32)
    far = [away(array) for array in (positions, phase, right_side, table)]
    meta, table, around, near, density, source, first, second = call(
        prepare,
        (away(counts), away(phase_density), *far),
        [pltpu.SMEM((8,), jnp.int32), pltpu.SMEM(table.shape, jnp.int32), around, near, vector, vector, message, message],
        [pltpu.VMEM(phase.shape, jnp.int32), pltpu.VMEM((share, width), f32), pltpu.SemaphoreType.DMA((4,))],
        far=len(far),
    )
    meta, table = (pltpu.with_memory_space_constraint(array, pltpu.SMEM) for array in (meta, table))
    first = lax.ppermute(first, "piece", [(i, i ^ 1) for i in range(pieces)])
    axes = ("piece", "col")
    device = [(p, c) for p in range(pieces) for c in range(columns)]
    partner = [(p + (1 if p % 2 else -1), c) for p, c in device]
    partner = [(q, d) if 0 <= q < pieces else (p, c ^ 1) for (q, d), (p, c) in zip(partner, device)]
    second = lax.ppermute(second, axes, [(i, q * columns + d) for i, (q, d) in enumerate(partner)])

    plan, runs, tiles_in, sides, middles, weights, rows, cols, selfs = call(
        build_inner,
        (meta, table, near),
        [pltpu.SMEM((share * FIELDS + 4,), jnp.int32), pltpu.SMEM((6 * share + 3,), jnp.int32), inner_tiles,
         pltpu.VMEM((2, share, width, width), jnp.bfloat16), pltpu.VMEM((3, share, width), f32), square, square, narrow, narrow],
        [pltpu.SMEM((3 * share + 3,), jnp.int32), square_more, pltpu.VMEM(((share + 1) * SUB, width), f32), ahead, ahead],
        16 * most_inner,
    )
    plan, runs = (pltpu.with_memory_space_constraint(array, pltpu.SMEM) for array in (plan, runs))
    again, tiles_out, diagonal, precond, times, alone = call(
        build_outer,
        (meta, table, plan, runs, around, first, second, density, source,
         held(tiles_in), held(sides), held(middles), held(weights), held(rows), held(cols), held(selfs), *lists),
        [pltpu.SMEM((1,), jnp.int32), outer_tiles, vector, vector, vector, vector],
        [pltpu.VMEM((4, capacity + 2 * share, width), f32), square_more]
        + [pltpu.VMEM((share, width), f32)] * 2 + [pltpu.VMEM((capacity, width), f32), ahead, ahead],
        16 * most_outer,
        scalars=4,
    )
    again = pltpu.with_memory_space_constraint(again, pltpu.SMEM)

    def inner(field):
        return call(
            apply_inner,
            (meta, table, plan, again, field, alone, times, held(tiles_in)),
            [square, narrow],
            [pltpu.VMEM((share, width, width), f32), pltpu.VMEM((share + SUB, width), f32), pltpu.VMEM((share, width), f32),
             pltpu.VMEM(((share + 1) * SUB, width), f32)],
            4 * most_inner,
            scalars=4,
        )

    def exchange(field):
        count = pieces * columns
        swaps = [[i ^ 1 for i in range(count)], [i - 1 if i % 2 == 0 else i + 1 for i in range(count)]]
        swaps[1][0], swaps[1][-1] = count - 1, 0
        for c in range(1, columns - 1):
            to = {}
            for p in range(pieces - 1):
                low, high = p * columns + c, (p + 1) * columns
                to[low], to[high] = high, low
            for p in range(pieces):
                rest = [i for i in range(p * columns, (p + 1) * columns) if i not in to]
                to.update(zip(rest, rest[1:] + rest[:1]))
            swaps.append([to[i] for i in range(count)])
        return [lax.ppermute(field, axes, list(enumerate(to))) for to in swaps]

    scratch = [pltpu.VMEM((share, width, width), f32), pltpu.VMEM((8 * share, width), f32)]

    received = exchange(precond)
    rows, cols = inner(precond)
    spill, scaled = call(
        apply_first,
        (meta, table, plan, again, diagonal, times, *received, held(tiles_out), held(rows), held(cols)),
        [vector, vector],
        scratch,
        2 * most_outer,
        scalars=4,
    )

    received = exchange(scaled)
    rows, cols = inner(scaled)
    twice, sums = call(
        apply_second,
        (meta, table, plan, again, source, precond, spill, scaled, times, *received, held(tiles_out), held(rows), held(cols)),
        [vector, few],
        scratch,
        2 * most_outer,
        scalars=4,
    )

    def together(values, axis, low, size):
        return tree([values] + [swap(values, axis, low * k) for k in range(1, size)])

    sums = together(sums, "piece", 1, 2)
    sums = together(sums, "col", 1, columns)
    step = 2
    while pieces // step > 4:
        sums = together(sums, "piece", step, 4)
        step *= 4
    others = [swap(sums, "piece", step * k) for k in range(1, pieces // step)]

    return tuple(call(
        finish,
        (source, precond, spill, scaled, twice, sums, *others),
        [vector, vector],
        scalars=0,
    ))


def solution(mesh):
    placed = (
        P(None, "piece", None),
        P("piece", None),
        P("piece", "col"),
        P(),
        P(),
        P(("piece", "col"), None),
    )
    return jax.shard_map(
        body,
        mesh=mesh,
        in_specs=placed,
        out_specs=(P(("piece", "col"), None), P(("piece", "col"), None)),
        check_vma=False,
    )
```

```python
import jax
import jax.numpy as jnp
import numpy as np
from jax import lax
from jax.experimental import pallas as pl
from jax.experimental.pallas import tpu as pltpu
from jax.sharding import PartitionSpec as P

ITERS = 2
SIDE = 4
LAYER = SIDE * SIDE
REACH = 2 * LAYER
SUB = 8
VMEM = pl.BlockSpec(memory_space=pltpu.VMEM)
SMEM = pl.BlockSpec(memory_space=pltpu.SMEM)
HBM = pl.BlockSpec(memory_space=pltpu.HBM)


def stencil_tables():
    levels = SIDE.bit_length() - 1

    def cell(code):
        across = sum((code >> (2 * level) & 1) << level for level in range(levels))
        along = sum((code >> (2 * level + 1) & 1) << level for level in range(levels))
        return across, along

    place = {cell(code): code for code in range(LAYER)}
    rows = []
    for code in range(LAYER):
        across, along = cell(code)
        rows.append(
            sorted(
                step_z * LAYER + place[across + step_x, along + step_y] - code
                for step_z in (-1, 0, 1)
                for step_y in (-1, 0, 1)
                for step_x in (-1, 0, 1)
                if (across + step_x, along + step_y) in place
            )
        )
    longest = max(len(row) for row in rows)
    offsets = np.zeros((LAYER, longest), np.int32)
    below = np.zeros((LAYER, 2 * REACH + 1), np.int32)
    for code, row in enumerate(rows):
        offsets[code, : len(row)] = row
        for t in range(-REACH, REACH + 1):
            below[code, t + REACH] = sum(offset < t for offset in row)
    return offsets, below


OFFSETS, BELOW = stencil_tables()
WIDEST = OFFSETS.shape[1]
TABLE = np.concatenate([OFFSETS, BELOW], 1)
STRIDE = TABLE.shape[1]
FLAT = np.concatenate([TABLE.reshape(-1), np.zeros(8, np.int32)])
LIMIT = pltpu.CompilerParams(vmem_limit_bytes=8 * 1024 * 1024)


def tile_bounds(share):
    inner = outer = 0
    for first in range(LAYER):
        for live in range(1, share + 1):
            near = far = 0
            for a in range(live):
                code = (first + a) % LAYER
                row = [int(o) for o in OFFSETS[code][: BELOW[code, -1]]]
                near += sum(0 <= a + o and o <= 0 for o in row)
                far += sum(a + o < 0 or a + o >= live for o in row)
            inner, outer = max(inner, near), max(outer, far)
    return inner, outer


def rank(table, code, t):
    return table[code * STRIDE + jnp.clip(t, -REACH, REACH) + REACH + WIDEST]


FIELDS = 6


def write_plan(meta, table, plan, a):
    code = lax.bitwise_and(meta[1] + a, LAYER - 1)
    place = meta[1] + a
    low, split, middle = rank(table, code, -place), rank(table, code, -a), rank(table, code, 0)
    resume, high = rank(table, code, meta[0] - a), rank(table, code, meta[2] - place)
    row = code * STRIDE
    ahead = split - low
    plan[a * FIELDS] = middle - split
    plan[a * FIELDS + 1] = row + split
    plan[a * FIELDS + 2] = ahead + jnp.maximum(high - resume, 0)
    plan[a * FIELDS + 3] = ahead
    plan[a * FIELDS + 4] = row + low
    plan[a * FIELDS + 5] = row + resume - ahead


def write_run(runs, at, a, start, count):
    runs[3 * at], runs[3 * at + 1], runs[3 * at + 2] = a, start, count
    return at + (count > 0).astype(jnp.int32)


def write_runs(meta, table, plan, inner_runs, outer_runs, share):
    inner = outer = total = far = jnp.int32(0)
    for a in range(share):
        write_plan(meta, table, plan, a)
        alive = a < meta[0]
        count, start, count_far, ahead, start_far, start_after = (plan[a * FIELDS + k] for k in range(FIELDS))
        inner = write_run(inner_runs, inner, a, start, jnp.where(alive, count + 1, 0))
        outer = write_run(outer_runs, outer, a, start_far, jnp.where(alive, ahead, 0))
        outer = write_run(outer_runs, outer, a, start_after + ahead, jnp.where(alive, count_far - ahead, 0))
        total = total + jnp.where(alive, count + 1, 0)
        far = far + jnp.where(alive, count_far, 0)
    for runs, at in ((inner_runs, inner), (outer_runs, outer)):
        write_run(runs, at, share, len(FLAT) - 8, jnp.int32(1))
    plan[share * FIELDS] = total
    plan[share * FIELDS + 1] = far
    plan[share * FIELDS + 2] = inner
    plan[share * FIELDS + 3] = outer


def inner_range(plan, table, a):
    start = plan[a * FIELDS + 1]
    return plan[a * FIELDS], lambda t: a + table[start + t]


def outer_range(plan, table, a):
    ahead, start, start_after = (plan[a * FIELDS + k] for k in (3, 4, 5))
    return plan[a * FIELDS + 2], lambda t: a + table[t + jnp.where(t < ahead, start, start_after)]


TURN = 3


def padded_sweep(count, fetch, step, carry):
    def turn(i, state):
        carry, *now = state
        later = [fetch(TURN * (i + 1) + k) for k in range(TURN)]
        return step(now, carry), *later

    state = (carry, *(fetch(k) for k in range(TURN)))
    return lax.fori_loop(0, lax.div(count + (TURN - 1), TURN), turn, state)[0]


def tree(terms):
    while len(terms) > 1:
        terms = [a + b for a, b in zip(terms[::2], terms[1::2])] + terms[len(terms) // 2 * 2 :]
    return terms[0]


def gather(partial, c, term):
    if c < len(partial):
        partial[c] = term
    else:
        partial[c % len(partial)] = partial[c % len(partial)] + term


def pieces_of(width):
    return [slice(c * SUB, (c + 1) * SUB) for c in range(width // SUB)]


def wide(row):
    return jnp.broadcast_to(row, (SUB, row.shape[1]))


def three_parts(values):
    high = values.astype(jnp.bfloat16).astype(jnp.float32)
    rest = values - high
    middle = rest.astype(jnp.bfloat16).astype(jnp.float32)
    return high, middle, rest - middle


def stacked(rows):
    sublane = lax.broadcasted_iota(jnp.int32, rows[0].shape, 0)
    result = jnp.zeros(rows[0].shape, jnp.float32)
    for k, row in enumerate(rows):
        result = jnp.where(sublane == k, row, result)
    return result


def half_size(x):
    return 0.5 - (x[0] * x[0] + x[1] * x[1] + x[2] * x[2])


def own_side(x, which):
    nothing = [jnp.zeros_like(x[0])] * 4
    rows = [2.0 * x[0], 2.0 * x[1], 2.0 * x[2], jnp.ones_like(x[0])]
    high, middle, low = three_parts(stacked(nothing + rows if which else rows))
    sizes = stacked(list(three_parts(half_size(x))))
    width = sizes.shape[1]
    rest = jnp.zeros((width - 7 * SUB, width), jnp.float32)
    return jnp.concatenate([high, high, middle, middle, high, low, sizes, rest], 0)


def other_sides(first, second):
    rows = [*first, half_size(first), *second, half_size(second)]
    high, middle, low = three_parts(stacked(rows))
    width = high.shape[1]
    ones = jnp.where(lax.broadcasted_iota(jnp.int32, (2 * SUB, width), 0) < 3, 1.0, 0.0).astype(jnp.bfloat16)
    front = jnp.concatenate([high, middle], 0).astype(jnp.bfloat16)
    back = jnp.concatenate([low, high], 0).astype(jnp.bfloat16)
    rest = jnp.zeros((width - 8 * SUB, width), jnp.bfloat16)
    return jnp.concatenate([front, front, back, ones, rest], 0)


GROUP = 4


def flat_tiles(count, runs, most, table, sides, middles, weights, other_at, buffers, tiles, sums_ref, both_ways):
    share, width = weights.shape[:2]
    chunks = pieces_of(width)
    lane = lax.broadcasted_iota(jnp.int32, (SUB, width), 1)
    diagonal = lane - lax.broadcasted_iota(jnp.int32, (SUB, width), 0)

    def add_to(block, term):
        here = pl.ds(pl.multiple_of(block * SUB, SUB), SUB)
        sums_ref[here, :] = sums_ref[here, :] + term

    def steps(state):
        found = []
        for _ in range(GROUP):
            run, t = state
            a, start, size = (runs[3 * run + k] for k in range(3))
            found.append((a, a + table[start + t]))
            over = t + 1 >= size
            state = jnp.minimum(run + over.astype(jnp.int32), most), jnp.where(over, 0, t + 1)
        return state, found

    def other_of(a, n):
        here = pl.ds(a, 1)
        return [wide(other_at(c, n)) - wide(middles[c, here, :]) for c in range(3)]

    def products(found, ahead):
        for k in range(0, GROUP, 2):
            (a, n), (b, m) = ((jnp.minimum(a, share - 1), n) for a, n in found[k : k + 2])
            own = jnp.concatenate([sides[0, a], sides[1, b]], 0)
            both = jnp.dot(own, other_sides(other_of(a, n), other_of(b, m)), preferred_element_type=jnp.float32)
            ahead[k] = both[:width]
            ahead[k + 1] = both[width:]

    def weigh(at, found, ahead):
        for k, (a, n) in enumerate(found):
            own = jnp.minimum(a, share - 1)
            other = wide(other_at(3, n))
            down = [None] * 2
            along = jnp.zeros((SUB, width), jnp.float32)
            for c, here in enumerate(chunks):
                left = ahead[k, here, :]
                rest = jnp.maximum(left, 0.0)
                inverse = pltpu.reciprocal((1.01 - left) * (weights[own, here, :] + other), approx=True)
                tile = rest * rest * inverse
                tiles[at + k, here, :] = tile
                along = jnp.where(diagonal == c * SUB, jnp.sum(tile, axis=1, keepdims=True), along)
                if both_ways:
                    gather(down, c, tile)
            if both_ways:
                alone = a == n
                add_to(jnp.where(alone, share, a), along)
                add_to(jnp.where(alone, share, n), tree(down))
            else:
                add_to(a, along)

    def turn(i, carry):
        state, found = carry
        at = i * (2 * GROUP)
        state, later = steps(state)
        products(later, buffers[1])
        weigh(at, found, buffers[0])
        state, last = steps(state)
        products(last, buffers[0])
        weigh(at + GROUP, later, buffers[1])
        return state, last

    state, found = steps((jnp.int32(0), jnp.int32(0)))
    products(found, buffers[0])
    lax.fori_loop(0, lax.div(count + (2 * GROUP - 1), 2 * GROUP), turn, (state, found))


def spread_columns(out, index, rows):
    count, width = rows.shape
    turned = rows.T
    for a in range(count):
        out[index(a)] = jnp.broadcast_to(turned[:, a : a + 1], (width, width))


def lane_sums(parts, count, width):
    lanes = lax.broadcasted_iota(jnp.int32, (width, width), 1)
    turned = jnp.zeros((width, width), jnp.float32)
    for a in range(count):
        turned = jnp.where(lanes == a, jnp.sum(parts[a], axis=1, keepdims=True), turned)
    return turned.T[:count]


def sub_sums(cols):
    return jnp.sum(cols[...].reshape(-1, SUB, cols.shape[1]), axis=1)


def alive_rows(meta, share, width):
    return lax.broadcasted_iota(jnp.int32, (share, width), 0) < meta[0]


def prepare(
    counts, densities, position_in, phase_in, right_side_in, table_in,
    meta, table, hood, near, density, source, first_swap, second_swap, phase, right_side, sems
):
    share, width = source.shape
    capacity = phase.shape[0]
    body_rows = pl.ds(share, capacity)
    copies = [
        pltpu.make_async_copy(phase_in, phase, sems.at[0]),
        pltpu.make_async_copy(position_in, hood.at[pl.ds(0, 3), body_rows, :], sems.at[1]),
        pltpu.make_async_copy(right_side_in, right_side, sems.at[2]),
        pltpu.make_async_copy(table_in, table, sems.at[3]),
    ]
    for copy in copies:
        copy.start()
    piece, column = lax.axis_index("piece"), lax.axis_index("col")
    filled = counts[piece]
    filled_before = counts[jnp.maximum(piece - 1, 0)]
    before = jnp.int32(0)
    total = jnp.int32(0)
    for p in range(counts.shape[0]):
        before = before + jnp.where(p < piece, counts[p], 0)
        total = total + counts[p]
    meta[0] = jnp.clip(filled - column * share, 0, share)
    meta[1] = before + column * share
    meta[2] = total
    meta[3] = column * share
    meta[4] = filled
    meta[5] = filled_before
    own_rows = pl.ds(pl.multiple_of(share + column * share, SUB), share)
    copies[0].wait()
    labels = phase[...]
    whole = sum(jnp.where(labels == k, densities[k], 0.0) for k in range(densities.shape[0]))
    hood[3, body_rows, :] = whole * (width / 2.0)
    density[...] = hood[3, own_rows, :] * (2.0 / width)
    copies[1].wait()
    even = lax.rem(piece, 2) == 0
    for k in range(4):
        tail, head = hood[k, pl.ds(filled, share), :], hood[k, share : 2 * share, :]
        first_swap[k] = jnp.where(even, tail, head)
        second_swap[k] = jnp.where(even, head, tail)
        near[k, 0:share, :] = hood[k, own_rows, :]
    for copy in copies[2:]:
        copy.wait()
    source[...] = jnp.where(alive_rows(meta, share, width), right_side[...], 0.0)


def finish_tiles(tiles, end):
    for t in range(TURN):
        tiles[end + t] = jnp.zeros(tiles.shape[1:], jnp.float32)


def build_inner(
    meta, table, near, plan, outer_runs, tiles, sides, middles, weights, sums_out, self_ref,
    inner_runs, sums_ref, *buffers,
):
    share, width = weights.shape[:2]
    chunks = pieces_of(width)
    write_runs(meta, table, plan, inner_runs, outer_runs, share)
    for k in range(3):
        first = near[k, 0:share, 0:1]
        middles[k] = jnp.broadcast_to(jnp.floor(first) + 0.5, (share, width))
    for a in range(share):
        here = slice(a, a + 1)
        centred = [wide(near[k, here, :] - middles[k, here, :]) for k in range(3)]
        for which in range(2):
            sides[which, a] = own_side(centred, which).T.astype(jnp.bfloat16)
    spread_columns(weights, lambda a: a, near[3, 0:share, :])
    sums_ref[...] = jnp.zeros_like(sums_ref)
    count = plan[share * FIELDS]
    flat_tiles(
        count, inner_runs, plan[share * FIELDS + 2], table, sides, middles, weights,
        lambda k, n: near[k, pl.ds(n, 1), :], buffers, tiles, sums_ref, True,
    )
    finish_tiles(tiles, count)
    lane = lax.broadcasted_iota(jnp.int32, (SUB, width), 1)
    sublane = lax.broadcasted_iota(jnp.int32, (SUB, width), 0)

    def block(a, at):
        at = at + plan[a * FIELDS]
        down = [None] * 4
        for c, here in enumerate(chunks):
            tile = jnp.where(lane == sublane + c * SUB, 0.0, tiles[at, here, :])
            tiles[at, here, :] = tile
            gather(down, c, tile)
        self_ref[pl.ds(pl.multiple_of(a * SUB, SUB), SUB), :] = tree(down)
        return at + 1

    lax.fori_loop(0, meta[0], block, 0)
    sums_out[...] = sums_ref[0 : share * SUB, :]


def count_listed(meta, lists, width):
    capacity = lists[0].shape[1]
    filled, filled_before = meta[4], meta[5]
    start = lax.axis_index("piece") * capacity
    steps = lax.broadcasted_iota(jnp.int32, (2 * REACH, capacity), 0)
    partial = [None] * 4
    row = 0
    for ref in lists:
        ids = ref[...]
        slot = ids - start
        gap = jnp.where(slot < 0, capacity - filled_before, jnp.where(slot >= capacity, filled - capacity, 0))
        away = slot - lax.broadcasted_iota(jnp.int32, ids.shape, 1) + gap
        away = jnp.where(ids < 0, -REACH, away) + REACH
        for k in range(ids.shape[0]):
            gather(partial, row, jnp.where(steps == away[k : k + 1], 1.0, 0.0))
            row += 1
    return jnp.concatenate([tree(partial), jnp.zeros((width - 2 * REACH, capacity), jnp.float32)], 0).T


def factor(times, a, n):
    lane = lax.broadcasted_iota(jnp.int32, (1, times.shape[1]), 1)
    return jnp.sum(jnp.where(lane == n - a + REACH, times[pl.ds(a, 1), :], 0.0), axis=1, keepdims=True)


def either(flag, run):
    @pl.when(flag == 0)
    def _():
        run(False)

    @pl.when(flag != 0)
    def _():
        run(True)


TAIL = 14


def build_outer(
    meta, table, plan, runs, around, first, second, density, source, tiles_in, sides, middles, weights,
    inner_sums, self_ref, *rest
):
    lists, rest = rest[:-TAIL], rest[-TAIL:]
    again_ref, tiles, diagonal_ref, precond_ref, times, alone_ref, hood, work, outer_sums, sums_ref, extra, all_times, *buffers = rest
    share, width = diagonal_ref.shape
    base, filled = meta[3], meta[4]
    even = lax.rem(lax.axis_index("piece"), 2) == 0
    for k in range(4):
        hood[k, 0:share, :] = jnp.where(even, second[k], first[k])
        hood[k, share:, :] = around[k, share:, :]
        hood[k, pl.ds(share + filled, share), :] = jnp.where(even, first[k], second[k])
    alive = alive_rows(meta, share, width)
    all_times[...] = count_listed(meta, lists, width)
    often = jnp.where(alive, all_times[pl.ds(pl.multiple_of(base, SUB), share), :], 0.0)
    times[...] = often
    lane = lax.broadcasted_iota(jnp.int32, (share, width), 1)
    again = jnp.max(jnp.where((lane == REACH) | (lane == 0), 0.0, often)) > 1.5
    again_ref[0] = again.astype(jnp.int32)


    outer_sums[...] = jnp.zeros_like(outer_sums)
    count = plan[share * FIELDS + 1]
    flat_tiles(
        count, runs, plan[share * FIELDS + 3], table, sides, middles, weights,
        lambda k, n: hood[k, pl.ds(base + share + n, 1), :], buffers, tiles, outer_sums, False,
    )
    finish_tiles(tiles, count)
    sums_ref[...] = sub_sums(inner_sums) + sub_sums(outer_sums)[0:share]

    @pl.when(again)
    def _():
        extra[...] = jnp.zeros_like(extra)
        work[...] = jnp.zeros_like(work)

        def block(a, state):
            count, place_of = inner_range(plan, table, a)

            def inner(t, at):
                n = place_of(t)
                tile = tiles_in[at]
                work[a] = work[a] + tile * factor(times, a, n)
                there = pl.ds(n, 1)
                down = jnp.sum(tile, axis=0, keepdims=True)
                extra[there, :] = extra[there, :] + down * factor(times, n, a)
                return at + 1

            at = lax.fori_loop(0, count, inner, state[0]) + 1
            count, place_far = outer_range(plan, table, a)

            def outer(t, at):
                work[a] = work[a] + tiles[at] * factor(times, a, place_far(t))
                return at + 1

            return at, lax.fori_loop(0, count, outer, state[1])

        lax.fori_loop(0, meta[0], block, (0, 0))
        sums_ref[...] = lane_sums(work, share, width) + extra[...]

    alone = jnp.sum(jnp.where(lane == REACH, often, 0.0), axis=1, keepdims=True)
    alone_ref[...] = jnp.broadcast_to(alone, (share, width))
    pairs = jnp.where(alive, sums_ref[...] + sub_sums(self_ref) * alone, 0.0)
    diagonal = 1.0 / density[...] + pairs
    diagonal_ref[...] = diagonal
    precond_ref[...] = source[...] / diagonal


def apply_inner(meta, table, plan, again, field, alone, times, tiles, rows_ref, cols_ref, spread, near, lone, cols):
    share, width = field.shape
    chunks = pieces_of(width)
    near[0:share, :] = field[...]
    near[share:, :] = jnp.zeros((SUB, width), jnp.float32)
    lone[...] = field[...] * alone[...]
    spread_columns(spread, lambda a: a, field[...])
    cols[...] = jnp.zeros_like(cols)

    def run(weighted):
        def block(a, at):
            count, place_of = inner_range(plan, table, a)

            def fetch(t):
                n = jnp.where(t < count, place_of(t), share)
                return n, wide(near[pl.ds(n, 1), :])

            def pairs(fetched, carry):
                at, sums = carry
                if weighted:
                    fetched = [(n, value * factor(times, a, jnp.minimum(n, share - 1))) for n, value in fetched]
                down = [[None] * 2 for _ in fetched]
                result = []
                for c, (here, total) in enumerate(zip(chunks, sums)):
                    own = spread[a, here, :]
                    found = []
                    for t, (_, value) in enumerate(fetched):
                        tile = tiles[at + t, here, :]
                        gather(down[t], c, tile * own)
                        found.append(tile * value)
                    result.append(total + tree(found))
                for (n, _), partial in zip(fetched, down):
                    there = pl.ds(pl.multiple_of(n * SUB, SUB), SUB)
                    partial = tree(partial)
                    if weighted:
                        partial = partial * factor(times, jnp.minimum(n, share - 1), a)
                    cols[there, :] = cols[there, :] + partial
                return at + len(fetched), result

            zero = jnp.zeros((SUB, width), jnp.float32)
            _, sums = padded_sweep(count, fetch, pairs, (at, [zero] * len(chunks)))
            at = at + count
            value = wide(lone[pl.ds(a, 1), :])
            for here, old in zip(chunks, sums):
                rows_ref[a, here, :] = old + tiles[at, here, :] * value
            return at + 1

        lax.fori_loop(0, meta[0], block, 0)

    either(again[0], run)
    cols_ref[...] = cols[0 : share * SUB, :]


def apply_outer(meta, table, plan, again, received, times, tiles, rows_ref, cols_ref, work, hood):
    first, second, *ends = received
    columns = len(received)
    share, width = first.shape
    chunks = pieces_of(width)
    base, filled = meta[3], meta[4]
    column = lax.div(base, share)
    odd = lax.rem(column, 2) == 1
    before = jnp.where(odd, first[...], second[...])
    after = jnp.where(odd, second[...], first[...])
    own = 3 * share
    for c, end in enumerate(ends, 1):
        hood[pl.ds(own - meta[5] + c * share, share), :] = end[...]
    from_last = own - meta[5] + (columns - 1) * share
    hood[pl.ds(jnp.where(column == 0, from_last, own - share), share), :] = before
    hood[own + share : own + 2 * share, :] = after
    head = after
    for c, end in enumerate(ends, 1):
        head = jnp.where(column == c, end[...], head)
    hood[pl.ds(own + jnp.clip(filled - base, 0, 2 * share), share), :] = head
    nothing = hood.shape[0] - SUB
    hood[nothing:, :] = jnp.zeros((SUB, width), jnp.float32)

    def run(weighted):
        def block(a, at):
            count, place_of = outer_range(plan, table, a)

            def fetch(t):
                place = place_of(t)
                value = hood[pl.ds(jnp.where(t < count, own + place, nothing), 1), :]
                if weighted:
                    value = value * factor(times, a, place)
                return wide(value)

            def pairs(values, carry):
                at, sums = carry
                result = []
                for here, total in zip(chunks, sums):
                    result.append(total + tree([tiles[at + t, here, :] * value for t, value in enumerate(values)]))
                return at + len(values), result

            _, sums = padded_sweep(count, fetch, pairs, (at, [rows_ref[a, here, :] for here in chunks]))
            for here, values in zip(chunks, sums):
                work[a, here, :] = values
            return at + count

        lax.fori_loop(0, meta[0], block, 0)

    either(again[0], run)
    return jnp.where(alive_rows(meta, share, width), lane_sums(work, share, width) + sub_sums(cols_ref), 0.0)


def apply_first(meta, table, plan, again, diagonal, times, *rest):
    *received, tiles, rows_ref, cols_ref, spill_ref, scaled_ref, work, hood = rest
    spill = apply_outer(meta, table, plan, again, received, times, tiles, rows_ref, cols_ref, work, hood)
    spill_ref[...] = spill
    scaled_ref[...] = spill / diagonal[...]


def apply_second(meta, table, plan, again, source, precond, spill, scaled, times, *rest):
    *received, tiles, rows_ref, cols_ref, twice_ref, sums_ref, work, hood = rest
    twice = apply_outer(meta, table, plan, again, received, times, tiles, rows_ref, cols_ref, work, hood)
    twice_ref[...] = twice
    share, width = twice.shape
    lane = lax.broadcasted_iota(jnp.int32, (1, width), 1)
    sums = jnp.zeros((1, width), jnp.float32)
    pairs = ((source[...], precond[...]), (spill[...], precond[...]), (spill[...], scaled[...]), (scaled[...], twice))
    for k, (first, second) in enumerate(pairs):
        along = jnp.sum(first * second, axis=0, keepdims=True)
        sums = jnp.where(lane == k, jnp.sum(along, axis=1, keepdims=True), sums)
    sums_ref[...] = wide(sums)


def finish(source, precond, spill, scaled, twice, *rest):
    *parts, solution_ref, residual_ref = rest
    sums = tree([ref[...] for ref in parts])

    def pick(k):
        return sums[0:1, k : k + 1]

    weighted, cross, square, last = pick(0), pick(1), pick(2), pick(3)
    part = cross / weighted
    advance = 1.0 / (1.0 - part)
    keep = -part * advance
    weighted_next = advance * advance * (square - cross * part)
    bent = keep * keep * cross + 2.0 * keep * advance * square + advance * advance * last
    blend = weighted_next / weighted
    advance_next = weighted_next / (weighted_next - bent - blend * weighted_next / advance)
    residual = keep * source[...] + advance * spill[...]
    next_precond = keep * precond[...] + advance * scaled[...]
    direction = next_precond + blend * precond[...]
    image = residual - keep * spill[...] - advance * twice[...] + blend * (source[...] - spill[...])
    solution_ref[...] = advance * precond[...] + advance_next * direction
    residual_ref[...] = residual - advance_next * image


def held(array):
    return pltpu.with_memory_space_constraint(array, pltpu.VMEM)


def body(positions, phase, neighbours, counts, phase_density, right_side):
    capacity, width = phase.shape
    columns = lax.axis_size("col")
    pieces = lax.axis_size("piece")
    share = capacity // columns
    f32 = jnp.float32
    vector = jax.ShapeDtypeStruct((share, width), f32)
    few = jax.ShapeDtypeStruct((SUB, width), f32)
    message = jax.ShapeDtypeStruct((4, share, width), f32)
    most_inner, most_outer = tile_bounds(share)
    inner_tiles = pltpu.VMEM((most_inner + 2 * GROUP, width, width), f32)
    outer_tiles = pltpu.VMEM((most_outer + 2 * GROUP, width, width), f32)
    ahead = pltpu.VMEM((GROUP, width, width), f32)
    narrow_more = pltpu.VMEM(((share + 1) * SUB, width), f32)
    square = pltpu.VMEM((share, width, width), f32)
    narrow = pltpu.VMEM((share * SUB, width), f32)
    table = jnp.asarray(FLAT)

    def call(kernel, args, outs, scratch=(), work=0, scalars=2, far=0, **more):
        return pl.pallas_call(
            kernel,
            out_shape=outs,
            in_specs=[SMEM] * scalars + [HBM] * far + [VMEM] * (len(args) - scalars - far),
            out_specs=[SMEM if getattr(o, "memory_space", None) == pltpu.SMEM else VMEM for o in outs],
            scratch_shapes=scratch,
            compiler_params=LIMIT,
            cost_estimate=pl.CostEstimate(flops=work * width * width, bytes_accessed=0, transcendentals=0),
            name=kernel.__name__,
            **more,
        )(*args)

    def swap(values, axis, step):
        return lax.ppermute(values, axis, [(i, i ^ step) for i in range(lax.axis_size(axis))])

    col_steps = [(1 << k) | 1 for k in range(columns.bit_length() - 1)]
    lists = [neighbours.T]
    for step in col_steps:
        known = lists[0] if len(lists) == 1 else jnp.concatenate(lists, 0)
        lists = [known, swap(known, "col", step)]

    def away(array):
        return pltpu.with_memory_space_constraint(array, pltpu.HBM)

    around = jax.ShapeDtypeStruct((4, capacity + 2 * share, width), f32)
    near = jax.ShapeDtypeStruct((4, 2 * share, width), f32)
    far = [away(array) for array in (positions, phase, right_side, table)]
    meta, table, around, near, density, source, first, second = call(
        prepare,
        (away(counts), away(phase_density), *far),
        [pltpu.SMEM((8,), jnp.int32), pltpu.SMEM(table.shape, jnp.int32), around, near, vector, vector, message, message],
        [pltpu.VMEM(phase.shape, jnp.int32), pltpu.VMEM((share, width), f32), pltpu.SemaphoreType.DMA((4,))],
        far=len(far),
    )
    meta, table = (pltpu.with_memory_space_constraint(array, pltpu.SMEM) for array in (meta, table))
    first = lax.ppermute(first, "piece", [(i, i ^ 1) for i in range(pieces)])
    axes = ("piece", "col")
    device = [(p, c) for p in range(pieces) for c in range(columns)]
    partner = [(p + (1 if p % 2 else -1), c) for p, c in device]
    partner = [(q, d) if 0 <= q < pieces else (p, c ^ 1) for (q, d), (p, c) in zip(partner, device)]
    second = lax.ppermute(second, axes, [(i, q * columns + d) for i, (q, d) in enumerate(partner)])

    plan, runs, tiles_in, sides, middles, weights, inner_sums, selfs = call(
        build_inner,
        (meta, table, near),
        [pltpu.SMEM((share * FIELDS + 4,), jnp.int32), pltpu.SMEM((6 * share + 3,), jnp.int32), inner_tiles,
         pltpu.VMEM((2, share, width, width), jnp.bfloat16), pltpu.VMEM((3, share, width), f32), square, narrow, narrow],
        [pltpu.SMEM((3 * share + 3,), jnp.int32), narrow_more, ahead, ahead],
        16 * most_inner,
    )
    plan, runs = (pltpu.with_memory_space_constraint(array, pltpu.SMEM) for array in (plan, runs))
    again, tiles_out, diagonal, precond, times, alone = call(
        build_outer,
        (meta, table, plan, runs, around, first, second, density, source,
         held(tiles_in), held(sides), held(middles), held(weights), held(inner_sums), held(selfs), *lists),
        [pltpu.SMEM((1,), jnp.int32), outer_tiles, vector, vector, vector, vector],
        [pltpu.VMEM((4, capacity + 2 * share, width), f32), square, narrow_more]
        + [pltpu.VMEM((share, width), f32)] * 2 + [pltpu.VMEM((capacity, width), f32), ahead, ahead],
        16 * most_outer,
        scalars=4,
    )
    again = pltpu.with_memory_space_constraint(again, pltpu.SMEM)

    def inner(field):
        return call(
            apply_inner,
            (meta, table, plan, again, field, alone, times, held(tiles_in)),
            [square, narrow],
            [pltpu.VMEM((share, width, width), f32), pltpu.VMEM((share + SUB, width), f32), pltpu.VMEM((share, width), f32),
             pltpu.VMEM(((share + 1) * SUB, width), f32)],
            4 * most_inner,
            scalars=4,
        )

    def exchange(field):
        count = pieces * columns
        swaps = [[i ^ 1 for i in range(count)], [i - 1 if i % 2 == 0 else i + 1 for i in range(count)]]
        swaps[1][0], swaps[1][-1] = count - 1, 0
        for c in range(1, columns - 1):
            to = {}
            for p in range(pieces - 1):
                low, high = p * columns + c, (p + 1) * columns
                to[low], to[high] = high, low
            for p in range(pieces):
                rest = [i for i in range(p * columns, (p + 1) * columns) if i not in to]
                to.update(zip(rest, rest[1:] + rest[:1]))
            swaps.append([to[i] for i in range(count)])
        return [lax.ppermute(field, axes, list(enumerate(to))) for to in swaps]

    scratch = [pltpu.VMEM((share, width, width), f32), pltpu.VMEM((8 * share, width), f32)]

    received = exchange(precond)
    rows, cols = inner(precond)
    spill, scaled = call(
        apply_first,
        (meta, table, plan, again, diagonal, times, *received, held(tiles_out), held(rows), held(cols)),
        [vector, vector],
        scratch,
        2 * most_outer,
        scalars=4,
    )

    received = exchange(scaled)
    rows, cols = inner(scaled)
    twice, sums = call(
        apply_second,
        (meta, table, plan, again, source, precond, spill, scaled, times, *received, held(tiles_out), held(rows), held(cols)),
        [vector, few],
        scratch,
        2 * most_outer,
        scalars=4,
    )

    def together(values, axis, low, size):
        return tree([values] + [swap(values, axis, low * k) for k in range(1, size)])

    sums = together(sums, "piece", 1, 2)
    sums = together(sums, "col", 1, columns)
    step = 2
    while pieces // step > 4:
        sums = together(sums, "piece", step, 4)
        step *= 4
    others = [swap(sums, "piece", step * k) for k in range(1, pieces // step)]

    return tuple(call(
        finish,
        (source, precond, spill, scaled, twice, sums, *others),
        [vector, vector],
        scalars=0,
    ))


def solution(mesh):
    placed = (
        P(None, "piece", None),
        P("piece", None),
        P("piece", "col"),
        P(),
        P(),
        P(("piece", "col"), None),
    )
    return jax.shard_map(
        body,
        mesh=mesh,
        in_specs=placed,
        out_specs=(P(("piece", "col"), None), P(("piece", "col"), None)),
        check_vma=False,
    )
```

```python
import jax
import jax.numpy as jnp
import numpy as np
from jax import lax
from jax.experimental import pallas as pl
from jax.experimental.pallas import tpu as pltpu
from jax.sharding import PartitionSpec as P

ITERS = 2
SIDE = 4
LAYER = SIDE * SIDE
REACH = 2 * LAYER
SUB = 8
VMEM = pl.BlockSpec(memory_space=pltpu.VMEM)
SMEM = pl.BlockSpec(memory_space=pltpu.SMEM)
HBM = pl.BlockSpec(memory_space=pltpu.HBM)


def stencil_tables():
    levels = SIDE.bit_length() - 1

    def cell(code):
        across = sum((code >> (2 * level) & 1) << level for level in range(levels))
        along = sum((code >> (2 * level + 1) & 1) << level for level in range(levels))
        return across, along

    place = {cell(code): code for code in range(LAYER)}
    rows = []
    for code in range(LAYER):
        across, along = cell(code)
        rows.append(
            sorted(
                step_z * LAYER + place[across + step_x, along + step_y] - code
                for step_z in (-1, 0, 1)
                for step_y in (-1, 0, 1)
                for step_x in (-1, 0, 1)
                if (across + step_x, along + step_y) in place
            )
        )
    longest = max(len(row) for row in rows)
    offsets = np.zeros((LAYER, longest), np.int32)
    below = np.zeros((LAYER, 2 * REACH + 1), np.int32)
    for code, row in enumerate(rows):
        offsets[code, : len(row)] = row
        for t in range(-REACH, REACH + 1):
            below[code, t + REACH] = sum(offset < t for offset in row)
    return offsets, below


OFFSETS, BELOW = stencil_tables()
WIDEST = OFFSETS.shape[1]
TABLE = np.concatenate([OFFSETS, BELOW], 1)
STRIDE = TABLE.shape[1]
LIMIT = pltpu.CompilerParams(vmem_limit_bytes=8 * 1024 * 1024)


def evened(count):
    return (count + 1) // 2 * 2 if isinstance(count, int) else lax.bitwise_and(count + 1, -2)


def tile_bounds(share):
    inner = outer = 0
    for first in range(LAYER):
        for live in range(1, share + 1):
            near = far = 0
            for a in range(live):
                code = (first + a) % LAYER
                row = [int(o) for o in OFFSETS[code][: BELOW[code, -1]]]
                near += evened(sum(0 <= a + o and o <= 0 for o in row))
                far += evened(sum(a + o < 0 or a + o >= live for o in row))
            inner, outer = max(inner, near), max(outer, far)
    return inner, outer


def rank(table, code, t):
    return table[code * STRIDE + jnp.clip(t, -REACH, REACH) + REACH + WIDEST]


FIELDS = 6


def write_plan(meta, table, plan, a):
    code = lax.bitwise_and(meta[1] + a, LAYER - 1)
    place = meta[1] + a
    low, split, middle = rank(table, code, -place), rank(table, code, -a), rank(table, code, 0)
    resume, high = rank(table, code, meta[0] - a), rank(table, code, meta[2] - place)
    row = code * STRIDE
    ahead = split - low
    plan[a * FIELDS] = middle - split
    plan[a * FIELDS + 1] = row + split
    plan[a * FIELDS + 2] = ahead + jnp.maximum(high - resume, 0)
    plan[a * FIELDS + 3] = ahead
    plan[a * FIELDS + 4] = row + low
    plan[a * FIELDS + 5] = row + resume - ahead


RUN = 5


def write_run(runs, at, a, count, ahead, start, start_after):
    for k, value in enumerate((a, count, ahead, start, start_after)):
        runs[RUN * at + k] = value
    return at + (count > 0).astype(jnp.int32)


def write_runs(meta, table, plan, inner_runs, outer_runs, share):
    inner = outer = total = far = jnp.int32(0)
    for a in range(share):
        write_plan(meta, table, plan, a)
        alive = a < meta[0]
        count, start, count_far, ahead, start_far, start_after = (plan[a * FIELDS + k] for k in range(FIELDS))
        count, count_far = jnp.where(alive, count + 1, 0), jnp.where(alive, count_far, 0)
        inner = write_run(inner_runs, inner, a, count, count, start, start)
        outer = write_run(outer_runs, outer, a, count_far, ahead, start_far, start_after)
        total, far = total + evened(count), far + evened(count_far)
    for runs, at in ((inner_runs, inner), (outer_runs, outer)):
        runs[RUN * at], runs[RUN * at + 1] = share, 0
        for k in range(2, RUN):
            runs[RUN * at + k] = 0
    plan[share * FIELDS] = total
    plan[share * FIELDS + 1] = far
    plan[share * FIELDS + 2] = inner
    plan[share * FIELDS + 3] = outer


def inner_range(plan, table, a):
    start = plan[a * FIELDS + 1]
    return plan[a * FIELDS], lambda t: a + table[start + t]


def outer_range(plan, table, a):
    ahead, start, start_after = (plan[a * FIELDS + k] for k in (3, 4, 5))
    return plan[a * FIELDS + 2], lambda t: a + table[t + jnp.where(t < ahead, start, start_after)]


TURN = 3


def padded_sweep(count, fetch, step, carry):
    def turn(i, state):
        carry, *now = state
        later = [fetch(TURN * (i + 1) + k) for k in range(TURN)]
        return step(now, carry), *later

    state = (carry, *(fetch(k) for k in range(TURN)))
    return lax.fori_loop(0, lax.div(count + (TURN - 1), TURN), turn, state)[0]


def tree(terms):
    while len(terms) > 1:
        terms = [a + b for a, b in zip(terms[::2], terms[1::2])] + terms[len(terms) // 2 * 2 :]
    return terms[0]


def gather(partial, c, term):
    if c < len(partial):
        partial[c] = term
    else:
        partial[c % len(partial)] = partial[c % len(partial)] + term


def pieces_of(width):
    return [slice(c * SUB, (c + 1) * SUB) for c in range(width // SUB)]


def wide(row):
    return jnp.broadcast_to(row, (SUB, row.shape[1]))


def three_parts(values):
    high = values.astype(jnp.bfloat16).astype(jnp.float32)
    rest = values - high
    middle = rest.astype(jnp.bfloat16).astype(jnp.float32)
    return high, middle, rest - middle


def stacked(rows):
    sublane = lax.broadcasted_iota(jnp.int32, rows[0].shape, 0)
    result = jnp.zeros(rows[0].shape, jnp.float32)
    for k, row in enumerate(rows):
        result = jnp.where(sublane == k, row, result)
    return result


def half_size(x):
    return 0.5 - (x[0] * x[0] + x[1] * x[1] + x[2] * x[2])


def own_side(x, which):
    nothing = [jnp.zeros_like(x[0])] * 4
    rows = [2.0 * x[0], 2.0 * x[1], 2.0 * x[2], jnp.ones_like(x[0])]
    high, middle, low = three_parts(stacked(nothing + rows if which else rows))
    sizes = stacked(list(three_parts(half_size(x))))
    width = sizes.shape[1]
    rest = jnp.zeros((width - 7 * SUB, width), jnp.float32)
    return jnp.concatenate([high, high, middle, middle, high, low, sizes, rest], 0)


def other_sides(first, second):
    rows = [*first, half_size(first), *second, half_size(second)]
    high, middle, low = three_parts(stacked(rows))
    width = high.shape[1]
    ones = jnp.where(lax.broadcasted_iota(jnp.int32, (2 * SUB, width), 0) < 3, 1.0, 0.0).astype(jnp.bfloat16)
    front = jnp.concatenate([high, middle], 0).astype(jnp.bfloat16)
    back = jnp.concatenate([low, high], 0).astype(jnp.bfloat16)
    rest = jnp.zeros((width - 8 * SUB, width), jnp.bfloat16)
    return jnp.concatenate([front, front, back, ones, rest], 0)


GROUP = 4


FAR = 1024.0


def flat_tiles(count, runs, most, empty, table, sides, middles, weights, other_at, buffers, tiles, sums_ref, both_ways):
    share, width = weights.shape[:2]
    chunks = pieces_of(width)
    lane = lax.broadcasted_iota(jnp.int32, (SUB, width), 1)
    diagonal = lane - lax.broadcasted_iota(jnp.int32, (SUB, width), 0)

    def add_to(block, term):
        here = pl.ds(pl.multiple_of(block * SUB, SUB), SUB)
        sums_ref[here, :] = sums_ref[here, :] + term

    def steps(state):
        found = []
        for _ in range(GROUP // 2):
            run, t = state
            a, size, ahead, start, start_after = (runs[RUN * run + k] for k in range(RUN))
            places = []
            for u in (t, t + 1):
                offset = table[u + jnp.where(u < ahead, start, start_after)]
                places.append(jnp.where(u < size, a + offset, empty))
            found.append((a, places))
            over = t + 2 >= size
            state = jnp.minimum(run + over.astype(jnp.int32), most), jnp.where(over, 0, t + 2)
        return state, found

    def products(found, ahead):
        for k, (a, places) in enumerate(found):
            own = jnp.minimum(a, share - 1)
            here = pl.ds(own, 1)
            middle = [wide(middles[c, here, :]) for c in range(3)]
            others = [[wide(other_at(c, n)) - middle[c] for c in range(3)] for n in places]
            both = jnp.dot(
                jnp.concatenate([sides[0, own], sides[1, own]], 0), other_sides(*others),
                preferred_element_type=jnp.float32,
            )
            ahead[2 * k] = both[:width]
            ahead[2 * k + 1] = both[width:]

    def weigh(at, found, ahead):
        for k, (a, places) in enumerate(found):
            own = jnp.minimum(a, share - 1)
            others = [wide(other_at(3, n)) for n in places]
            down = [[None] * 2 for _ in places]
            along = jnp.zeros((SUB, width), jnp.float32)
            for c, here in enumerate(chunks):
                weight = weights[own, here, :]
                pair = []
                for u in range(2):
                    left = ahead[2 * k + u, here, :]
                    rest = jnp.maximum(left, 0.0)
                    inverse = pltpu.reciprocal((1.01 - left) * (weight + others[u]), approx=True)
                    tile = rest * rest * inverse
                    tiles[at + 2 * k + u, here, :] = tile
                    pair.append(tile)
                    if both_ways:
                        gather(down[u], c, tile)
                along = jnp.where(diagonal == c * SUB, jnp.sum(pair[0] + pair[1], axis=1, keepdims=True), along)
            add_to(a, along)
            if both_ways:
                for n, partial in zip(places, down):
                    add_to(jnp.where(n == a, share, n), tree(partial))

    def turn(i, carry):
        state, found = carry
        at = i * (2 * GROUP)
        state, later = steps(state)
        products(later, buffers[1])
        weigh(at, found, buffers[0])
        state, last = steps(state)
        products(last, buffers[0])
        weigh(at + GROUP, later, buffers[1])
        return state, last

    state, found = steps((jnp.int32(0), jnp.int32(0)))
    products(found, buffers[0])
    lax.fori_loop(0, lax.div(count + (2 * GROUP - 1), 2 * GROUP), turn, (state, found))


def spread_columns(out, index, rows):
    count, width = rows.shape
    turned = rows.T
    for a in range(count):
        out[index(a)] = jnp.broadcast_to(turned[:, a : a + 1], (width, width))


def lane_sums(parts, count, width):
    lanes = lax.broadcasted_iota(jnp.int32, (width, width), 1)
    turned = jnp.zeros((width, width), jnp.float32)
    for a in range(count):
        turned = jnp.where(lanes == a, jnp.sum(parts[a], axis=1, keepdims=True), turned)
    return turned.T[:count]


def sub_sums(cols):
    return jnp.sum(cols[...].reshape(-1, SUB, cols.shape[1]), axis=1)


def alive_rows(meta, share, width):
    return lax.broadcasted_iota(jnp.int32, (share, width), 0) < meta[0]


def prepare(
    counts, densities, position_in, phase_in, right_side_in, table_in,
    meta, table, hood, near, density, source, first_swap, second_swap, phase, right_side, sems
):
    share, width = source.shape
    capacity = phase.shape[0]
    body_rows = pl.ds(share, capacity)
    copies = [
        pltpu.make_async_copy(phase_in, phase, sems.at[0]),
        pltpu.make_async_copy(position_in, hood.at[pl.ds(0, 3), body_rows, :], sems.at[1]),
        pltpu.make_async_copy(right_side_in, right_side, sems.at[2]),
        pltpu.make_async_copy(table_in, table, sems.at[3]),
    ]
    for copy in copies:
        copy.start()
    piece, column = lax.axis_index("piece"), lax.axis_index("col")
    filled = counts[piece]
    filled_before = counts[jnp.maximum(piece - 1, 0)]
    before = jnp.int32(0)
    total = jnp.int32(0)
    for p in range(counts.shape[0]):
        before = before + jnp.where(p < piece, counts[p], 0)
        total = total + counts[p]
    meta[0] = jnp.clip(filled - column * share, 0, share)
    meta[1] = before + column * share
    meta[2] = total
    meta[3] = column * share
    meta[4] = filled
    meta[5] = filled_before
    own_rows = pl.ds(pl.multiple_of(share + column * share, SUB), share)
    copies[0].wait()
    labels = phase[...]
    whole = sum(jnp.where(labels == k, densities[k], 0.0) for k in range(densities.shape[0]))
    hood[3, body_rows, :] = whole * (width / 2.0)
    density[...] = hood[3, own_rows, :] * (2.0 / width)
    copies[1].wait()
    even = lax.rem(piece, 2) == 0
    for k in range(4):
        tail, head = hood[k, pl.ds(filled, share), :], hood[k, share : 2 * share, :]
        first_swap[k] = jnp.where(even, tail, head)
        second_swap[k] = jnp.where(even, head, tail)
        near[k, 0:share, :] = hood[k, own_rows, :]
    for copy in copies[2:]:
        copy.wait()
    source[...] = jnp.where(alive_rows(meta, share, width), right_side[...], 0.0)


def finish_tiles(tiles, end):
    for t in range(TURN):
        tiles[end + t] = jnp.zeros(tiles.shape[1:], jnp.float32)


def build_inner(
    meta, table, near, plan, outer_runs, tiles, sides, middles, weights, sums_out, self_ref,
    inner_runs, sums_ref, far_near, *buffers,
):
    share, width = weights.shape[:2]
    chunks = pieces_of(width)
    write_runs(meta, table, plan, inner_runs, outer_runs, share)
    for k in range(3):
        first = near[k, 0:share, 0:1]
        middles[k] = jnp.broadcast_to(jnp.floor(first) + 0.5, (share, width))
    for a in range(share):
        here = slice(a, a + 1)
        centred = [wide(near[k, here, :] - middles[k, here, :]) for k in range(3)]
        for which in range(2):
            sides[which, a] = own_side(centred, which).T.astype(jnp.bfloat16)
    spread_columns(weights, lambda a: a, near[3, 0:share, :])
    sums_ref[...] = jnp.zeros_like(sums_ref)
    for k in range(4):
        far_near[k, 0 : 2 * share, :] = near[k]
        far_near[k, share : share + SUB, :] = jnp.full((SUB, width), FAR, jnp.float32)
    count = plan[share * FIELDS]
    flat_tiles(
        count, inner_runs, plan[share * FIELDS + 2], share, table, sides, middles, weights,
        lambda k, n: far_near[k, pl.ds(n, 1), :], buffers, tiles, sums_ref, True,
    )
    finish_tiles(tiles, count)
    lane = lax.broadcasted_iota(jnp.int32, (SUB, width), 1)
    sublane = lax.broadcasted_iota(jnp.int32, (SUB, width), 0)

    def block(a, at):
        count = plan[a * FIELDS]
        at = at + count
        down = [None] * 4
        apart = [None] * 4
        for c, here in enumerate(chunks):
            same = lane == sublane + c * SUB
            whole = tiles[at, here, :]
            tile = jnp.where(same, 0.0, whole)
            tiles[at, here, :] = tile
            gather(down, c, tile)
            gather(apart, c, jnp.where(same, whole, 0.0))
        there = pl.ds(pl.multiple_of(a * SUB, SUB), SUB)
        self_ref[there, :] = tree(down)
        sums_ref[there, :] = sums_ref[there, :] - tree(apart)
        return at - count + evened(count + 1)

    lax.fori_loop(0, meta[0], block, 0)
    sums_out[...] = sums_ref[0 : share * SUB, :]


def count_listed(meta, lists, width):
    capacity = lists[0].shape[1]
    filled, filled_before = meta[4], meta[5]
    start = lax.axis_index("piece") * capacity
    steps = lax.broadcasted_iota(jnp.int32, (2 * REACH, capacity), 0)
    partial = [None] * 4
    row = 0
    for ref in lists:
        ids = ref[...]
        slot = ids - start
        gap = jnp.where(slot < 0, capacity - filled_before, jnp.where(slot >= capacity, filled - capacity, 0))
        away = slot - lax.broadcasted_iota(jnp.int32, ids.shape, 1) + gap
        away = jnp.where(ids < 0, -REACH, away) + REACH
        for k in range(ids.shape[0]):
            gather(partial, row, jnp.where(steps == away[k : k + 1], 1.0, 0.0))
            row += 1
    return jnp.concatenate([tree(partial), jnp.zeros((width - 2 * REACH, capacity), jnp.float32)], 0).T


def factor(times, a, n):
    lane = lax.broadcasted_iota(jnp.int32, (1, times.shape[1]), 1)
    return jnp.sum(jnp.where(lane == n - a + REACH, times[pl.ds(a, 1), :], 0.0), axis=1, keepdims=True)


def either(flag, run):
    @pl.when(flag == 0)
    def _():
        run(False)

    @pl.when(flag != 0)
    def _():
        run(True)


TAIL = 14


def build_outer(
    meta, table, plan, runs, around, first, second, density, source, tiles_in, sides, middles, weights,
    inner_sums, self_ref, *rest
):
    lists, rest = rest[:-TAIL], rest[-TAIL:]
    again_ref, tiles, diagonal_ref, precond_ref, times, alone_ref, hood, work, outer_sums, sums_ref, extra, all_times, *buffers = rest
    share, width = diagonal_ref.shape
    base, filled = meta[3], meta[4]
    even = lax.rem(lax.axis_index("piece"), 2) == 0
    for k in range(4):
        hood[k, 0:share, :] = jnp.where(even, second[k], first[k])
        hood[k, share : around.shape[1], :] = around[k, share:, :]
        hood[k, pl.ds(share + filled, share), :] = jnp.where(even, first[k], second[k])
    hood[:, around.shape[1] :, :] = jnp.full((4, SUB, width), FAR, jnp.float32)
    alive = alive_rows(meta, share, width)
    all_times[...] = count_listed(meta, lists, width)
    often = jnp.where(alive, all_times[pl.ds(pl.multiple_of(base, SUB), share), :], 0.0)
    times[...] = often
    lane = lax.broadcasted_iota(jnp.int32, (share, width), 1)
    again = jnp.max(jnp.where((lane == REACH) | (lane == 0), 0.0, often)) > 1.5
    again_ref[0] = again.astype(jnp.int32)


    outer_sums[...] = jnp.zeros_like(outer_sums)
    count = plan[share * FIELDS + 1]
    flat_tiles(
        count, runs, plan[share * FIELDS + 3], hood.shape[1] - SUB - base - share, table, sides, middles, weights,
        lambda k, n: hood[k, pl.ds(base + share + n, 1), :], buffers, tiles, outer_sums, False,
    )
    finish_tiles(tiles, count)
    sums_ref[...] = sub_sums(inner_sums) + sub_sums(outer_sums)[0:share]

    @pl.when(again)
    def _():
        extra[...] = jnp.zeros_like(extra)
        work[...] = jnp.zeros_like(work)

        def block(a, state):
            count, place_of = inner_range(plan, table, a)

            def inner(t, at):
                n = place_of(t)
                tile = tiles_in[at]
                work[a] = work[a] + tile * factor(times, a, n)
                there = pl.ds(n, 1)
                down = jnp.sum(tile, axis=0, keepdims=True)
                extra[there, :] = extra[there, :] + down * factor(times, n, a)
                return at + 1

            at = lax.fori_loop(0, count, inner, state[0])
            work[a] = work[a] + tiles_in[at]
            at = at - count + evened(count + 1)
            count, place_far = outer_range(plan, table, a)

            def outer(t, at):
                work[a] = work[a] + tiles[at] * factor(times, a, place_far(t))
                return at + 1

            lax.fori_loop(0, count, outer, state[1])
            return at, state[1] + evened(count)

        lax.fori_loop(0, meta[0], block, (0, 0))
        sums_ref[...] = lane_sums(work, share, width) + extra[...]

    alone = jnp.sum(jnp.where(lane == REACH, often, 0.0), axis=1, keepdims=True)
    alone_ref[...] = jnp.broadcast_to(alone, (share, width))
    pairs = jnp.where(alive, sums_ref[...] + sub_sums(self_ref) * (alone - 1.0), 0.0)
    diagonal = 1.0 / density[...] + pairs
    diagonal_ref[...] = diagonal
    precond_ref[...] = source[...] / diagonal


def apply_inner(meta, table, plan, again, field, alone, times, tiles, rows_ref, cols_ref, spread, near, lone, cols):
    share, width = field.shape
    chunks = pieces_of(width)
    near[0:share, :] = field[...]
    near[share:, :] = jnp.zeros((SUB, width), jnp.float32)
    lone[...] = field[...] * alone[...]
    spread_columns(spread, lambda a: a, field[...])
    cols[...] = jnp.zeros_like(cols)

    def run(weighted):
        def block(a, at):
            count, place_of = inner_range(plan, table, a)

            def fetch(t):
                n = jnp.where(t < count, place_of(t), share)
                return n, wide(near[pl.ds(n, 1), :])

            def pairs(fetched, carry):
                at, sums = carry
                if weighted:
                    fetched = [(n, value * factor(times, a, jnp.minimum(n, share - 1))) for n, value in fetched]
                down = [[None] * 2 for _ in fetched]
                result = []
                for c, (here, total) in enumerate(zip(chunks, sums)):
                    own = spread[a, here, :]
                    found = []
                    for t, (_, value) in enumerate(fetched):
                        tile = tiles[at + t, here, :]
                        gather(down[t], c, tile * own)
                        found.append(tile * value)
                    result.append(total + tree(found))
                for (n, _), partial in zip(fetched, down):
                    there = pl.ds(pl.multiple_of(n * SUB, SUB), SUB)
                    partial = tree(partial)
                    if weighted:
                        partial = partial * factor(times, jnp.minimum(n, share - 1), a)
                    cols[there, :] = cols[there, :] + partial
                return at + len(fetched), result

            zero = jnp.zeros((SUB, width), jnp.float32)
            _, sums = padded_sweep(count, fetch, pairs, (at, [zero] * len(chunks)))
            value = wide(lone[pl.ds(a, 1), :])
            for here, old in zip(chunks, sums):
                rows_ref[a, here, :] = old + tiles[at + count, here, :] * value
            return at + evened(count + 1)

        lax.fori_loop(0, meta[0], block, 0)

    either(again[0], run)
    cols_ref[...] = cols[0 : share * SUB, :]


def apply_outer(meta, table, plan, again, received, times, tiles, rows_ref, cols_ref, work, hood):
    first, second, *ends = received
    columns = len(received)
    share, width = first.shape
    chunks = pieces_of(width)
    base, filled = meta[3], meta[4]
    column = lax.div(base, share)
    odd = lax.rem(column, 2) == 1
    before = jnp.where(odd, first[...], second[...])
    after = jnp.where(odd, second[...], first[...])
    own = 3 * share
    for c, end in enumerate(ends, 1):
        hood[pl.ds(own - meta[5] + c * share, share), :] = end[...]
    from_last = own - meta[5] + (columns - 1) * share
    hood[pl.ds(jnp.where(column == 0, from_last, own - share), share), :] = before
    hood[own + share : own + 2 * share, :] = after
    head = after
    for c, end in enumerate(ends, 1):
        head = jnp.where(column == c, end[...], head)
    hood[pl.ds(own + jnp.clip(filled - base, 0, 2 * share), share), :] = head
    nothing = hood.shape[0] - SUB
    hood[nothing:, :] = jnp.zeros((SUB, width), jnp.float32)

    def run(weighted):
        def block(a, at):
            count, place_of = outer_range(plan, table, a)

            def fetch(t):
                place = place_of(t)
                value = hood[pl.ds(jnp.where(t < count, own + place, nothing), 1), :]
                if weighted:
                    value = value * factor(times, a, place)
                return wide(value)

            def pairs(values, carry):
                at, sums = carry
                result = []
                for here, total in zip(chunks, sums):
                    result.append(total + tree([tiles[at + t, here, :] * value for t, value in enumerate(values)]))
                return at + len(values), result

            _, sums = padded_sweep(count, fetch, pairs, (at, [rows_ref[a, here, :] for here in chunks]))
            for here, values in zip(chunks, sums):
                work[a, here, :] = values
            return at + evened(count)

        lax.fori_loop(0, meta[0], block, 0)

    either(again[0], run)
    return jnp.where(alive_rows(meta, share, width), lane_sums(work, share, width) + sub_sums(cols_ref), 0.0)


def apply_first(meta, table, plan, again, diagonal, times, *rest):
    *received, tiles, rows_ref, cols_ref, spill_ref, scaled_ref, work, hood = rest
    spill = apply_outer(meta, table, plan, again, received, times, tiles, rows_ref, cols_ref, work, hood)
    spill_ref[...] = spill
    scaled_ref[...] = spill / diagonal[...]


def apply_second(meta, table, plan, again, source, precond, spill, scaled, times, *rest):
    *received, tiles, rows_ref, cols_ref, twice_ref, sums_ref, work, hood = rest
    twice = apply_outer(meta, table, plan, again, received, times, tiles, rows_ref, cols_ref, work, hood)
    twice_ref[...] = twice
    share, width = twice.shape
    lane = lax.broadcasted_iota(jnp.int32, (1, width), 1)
    sums = jnp.zeros((1, width), jnp.float32)
    pairs = ((source[...], precond[...]), (spill[...], precond[...]), (spill[...], scaled[...]), (scaled[...], twice))
    for k, (first, second) in enumerate(pairs):
        along = jnp.sum(first * second, axis=0, keepdims=True)
        sums = jnp.where(lane == k, jnp.sum(along, axis=1, keepdims=True), sums)
    sums_ref[...] = wide(sums)


def finish(source, precond, spill, scaled, twice, *rest):
    *parts, solution_ref, residual_ref = rest
    sums = tree([ref[...] for ref in parts])

    def pick(k):
        return sums[0:1, k : k + 1]

    weighted, cross, square, last = pick(0), pick(1), pick(2), pick(3)
    part = cross / weighted
    advance = 1.0 / (1.0 - part)
    keep = -part * advance
    weighted_next = advance * advance * (square - cross * part)
    bent = keep * keep * cross + 2.0 * keep * advance * square + advance * advance * last
    blend = weighted_next / weighted
    advance_next = weighted_next / (weighted_next - bent - blend * weighted_next / advance)
    residual = keep * source[...] + advance * spill[...]
    next_precond = keep * precond[...] + advance * scaled[...]
    direction = next_precond + blend * precond[...]
    image = residual - keep * spill[...] - advance * twice[...] + blend * (source[...] - spill[...])
    solution_ref[...] = advance * precond[...] + advance_next * direction
    residual_ref[...] = residual - advance_next * image


def held(array):
    return pltpu.with_memory_space_constraint(array, pltpu.VMEM)


def body(positions, phase, neighbours, counts, phase_density, right_side):
    capacity, width = phase.shape
    columns = lax.axis_size("col")
    pieces = lax.axis_size("piece")
    share = capacity // columns
    f32 = jnp.float32
    vector = jax.ShapeDtypeStruct((share, width), f32)
    few = jax.ShapeDtypeStruct((SUB, width), f32)
    message = jax.ShapeDtypeStruct((4, share, width), f32)
    most_inner, most_outer = tile_bounds(share)
    inner_tiles = pltpu.VMEM((most_inner + 2 * GROUP, width, width), f32)
    outer_tiles = pltpu.VMEM((most_outer + 2 * GROUP, width, width), f32)
    ahead = pltpu.VMEM((GROUP, width, width), f32)
    narrow_more = pltpu.VMEM(((share + 1) * SUB, width), f32)
    square = pltpu.VMEM((share, width, width), f32)
    narrow = pltpu.VMEM((share * SUB, width), f32)
    table = jnp.asarray(TABLE.reshape(-1))

    def call(kernel, args, outs, scratch=(), work=0, scalars=2, far=0, **more):
        return pl.pallas_call(
            kernel,
            out_shape=outs,
            in_specs=[SMEM] * scalars + [HBM] * far + [VMEM] * (len(args) - scalars - far),
            out_specs=[SMEM if getattr(o, "memory_space", None) == pltpu.SMEM else VMEM for o in outs],
            scratch_shapes=scratch,
            compiler_params=LIMIT,
            cost_estimate=pl.CostEstimate(flops=work * width * width, bytes_accessed=0, transcendentals=0),
            name=kernel.__name__,
            **more,
        )(*args)

    def swap(values, axis, step):
        return lax.ppermute(values, axis, [(i, i ^ step) for i in range(lax.axis_size(axis))])

    col_steps = [(1 << k) | 1 for k in range(columns.bit_length() - 1)]
    lists = [neighbours.T]
    for step in col_steps:
        known = lists[0] if len(lists) == 1 else jnp.concatenate(lists, 0)
        lists = [known, swap(known, "col", step)]

    def away(array):
        return pltpu.with_memory_space_constraint(array, pltpu.HBM)

    around = jax.ShapeDtypeStruct((4, capacity + 2 * share, width), f32)
    near = jax.ShapeDtypeStruct((4, 2 * share, width), f32)
    far = [away(array) for array in (positions, phase, right_side, table)]
    meta, table, around, near, density, source, first, second = call(
        prepare,
        (away(counts), away(phase_density), *far),
        [pltpu.SMEM((8,), jnp.int32), pltpu.SMEM(table.shape, jnp.int32), around, near, vector, vector, message, message],
        [pltpu.VMEM(phase.shape, jnp.int32), pltpu.VMEM((share, width), f32), pltpu.SemaphoreType.DMA((4,))],
        far=len(far),
    )
    meta, table = (pltpu.with_memory_space_constraint(array, pltpu.SMEM) for array in (meta, table))
    first = lax.ppermute(first, "piece", [(i, i ^ 1) for i in range(pieces)])
    axes = ("piece", "col")
    device = [(p, c) for p in range(pieces) for c in range(columns)]
    partner = [(p + (1 if p % 2 else -1), c) for p, c in device]
    partner = [(q, d) if 0 <= q < pieces else (p, c ^ 1) for (q, d), (p, c) in zip(partner, device)]
    second = lax.ppermute(second, axes, [(i, q * columns + d) for i, (q, d) in enumerate(partner)])

    plan, runs, tiles_in, sides, middles, weights, inner_sums, selfs = call(
        build_inner,
        (meta, table, near),
        [pltpu.SMEM((share * FIELDS + 4,), jnp.int32), pltpu.SMEM((RUN * (share + 1),), jnp.int32), inner_tiles,
         pltpu.VMEM((2, share, width, width), jnp.bfloat16), pltpu.VMEM((3, share, width), f32), square, narrow, narrow],
        [pltpu.SMEM((RUN * (share + 1),), jnp.int32), narrow_more, pltpu.VMEM((4, 2 * share, width), f32), ahead, ahead],
        16 * most_inner,
    )
    plan, runs = (pltpu.with_memory_space_constraint(array, pltpu.SMEM) for array in (plan, runs))
    again, tiles_out, diagonal, precond, times, alone = call(
        build_outer,
        (meta, table, plan, runs, around, first, second, density, source,
         held(tiles_in), held(sides), held(middles), held(weights), held(inner_sums), held(selfs), *lists),
        [pltpu.SMEM((1,), jnp.int32), outer_tiles, vector, vector, vector, vector],
        [pltpu.VMEM((4, capacity + 2 * share + SUB, width), f32), square, narrow_more]
        + [pltpu.VMEM((share, width), f32)] * 2 + [pltpu.VMEM((capacity, width), f32), ahead, ahead],
        16 * most_outer,
        scalars=4,
    )
    again = pltpu.with_memory_space_constraint(again, pltpu.SMEM)

    def inner(field):
        return call(
            apply_inner,
            (meta, table, plan, again, field, alone, times, held(tiles_in)),
            [square, narrow],
            [pltpu.VMEM((share, width, width), f32), pltpu.VMEM((share + SUB, width), f32), pltpu.VMEM((share, width), f32),
             pltpu.VMEM(((share + 1) * SUB, width), f32)],
            4 * most_inner,
            scalars=4,
        )

    def exchange(field):
        count = pieces * columns
        swaps = [[i ^ 1 for i in range(count)], [i - 1 if i % 2 == 0 else i + 1 for i in range(count)]]
        swaps[1][0], swaps[1][-1] = count - 1, 0
        for c in range(1, columns - 1):
            to = {}
            for p in range(pieces - 1):
                low, high = p * columns + c, (p + 1) * columns
                to[low], to[high] = high, low
            for p in range(pieces):
                rest = [i for i in range(p * columns, (p + 1) * columns) if i not in to]
                to.update(zip(rest, rest[1:] + rest[:1]))
            swaps.append([to[i] for i in range(count)])
        return [lax.ppermute(field, axes, list(enumerate(to))) for to in swaps]

    scratch = [pltpu.VMEM((share, width, width), f32), pltpu.VMEM((8 * share, width), f32)]

    received = exchange(precond)
    rows, cols = inner(precond)
    spill, scaled = call(
        apply_first,
        (meta, table, plan, again, diagonal, times, *received, held(tiles_out), held(rows), held(cols)),
        [vector, vector],
        scratch,
        2 * most_outer,
        scalars=4,
    )

    received = exchange(scaled)
    rows, cols = inner(scaled)
    twice, sums = call(
        apply_second,
        (meta, table, plan, again, source, precond, spill, scaled, times, *received, held(tiles_out), held(rows), held(cols)),
        [vector, few],
        scratch,
        2 * most_outer,
        scalars=4,
    )

    def together(values, axis, low, size):
        return tree([values] + [swap(values, axis, low * k) for k in range(1, size)])

    sums = together(sums, "piece", 1, 2)
    sums = together(sums, "col", 1, columns)
    step = 2
    while pieces // step > 4:
        sums = together(sums, "piece", step, 4)
        step *= 4
    others = [swap(sums, "piece", step * k) for k in range(1, pieces // step)]

    return tuple(call(
        finish,
        (source, precond, spill, scaled, twice, sums, *others),
        [vector, vector],
        scalars=0,
    ))


def solution(mesh):
    placed = (
        P(None, "piece", None),
        P("piece", None),
        P("piece", "col"),
        P(),
        P(),
        P(("piece", "col"), None),
    )
    return jax.shard_map(
        body,
        mesh=mesh,
        in_specs=placed,
        out_specs=(P(("piece", "col"), None), P(("piece", "col"), None)),
        check_vma=False,
    )
```

```python
import jax
import jax.numpy as jnp
import numpy as np
from jax import lax
from jax.experimental import pallas as pl
from jax.experimental.pallas import tpu as pltpu
from jax.sharding import PartitionSpec as P

ITERS = 2
SIDE = 4
LAYER = SIDE * SIDE
REACH = 2 * LAYER
SUB = 8
VMEM = pl.BlockSpec(memory_space=pltpu.VMEM)
SMEM = pl.BlockSpec(memory_space=pltpu.SMEM)
HBM = pl.BlockSpec(memory_space=pltpu.HBM)


def stencil_tables():
    levels = SIDE.bit_length() - 1

    def cell(code):
        across = sum((code >> (2 * level) & 1) << level for level in range(levels))
        along = sum((code >> (2 * level + 1) & 1) << level for level in range(levels))
        return across, along

    place = {cell(code): code for code in range(LAYER)}
    rows = []
    for code in range(LAYER):
        across, along = cell(code)
        rows.append(
            sorted(
                step_z * LAYER + place[across + step_x, along + step_y] - code
                for step_z in (-1, 0, 1)
                for step_y in (-1, 0, 1)
                for step_x in (-1, 0, 1)
                if (across + step_x, along + step_y) in place
            )
        )
    longest = max(len(row) for row in rows)
    offsets = np.zeros((LAYER, longest), np.int32)
    below = np.zeros((LAYER, 2 * REACH + 1), np.int32)
    for code, row in enumerate(rows):
        offsets[code, : len(row)] = row
        for t in range(-REACH, REACH + 1):
            below[code, t + REACH] = sum(offset < t for offset in row)
    return offsets, below


OFFSETS, BELOW = stencil_tables()
WIDEST = OFFSETS.shape[1]
TABLE = np.concatenate([OFFSETS, BELOW], 1)
STRIDE = TABLE.shape[1]
FLAT = np.concatenate([TABLE.reshape(-1), np.zeros(8, np.int32)])
LIMIT = pltpu.CompilerParams(vmem_limit_bytes=8 * 1024 * 1024)


def tile_bounds(share):
    inner = outer = 0
    for first in range(LAYER):
        for live in range(1, share + 1):
            near = far = 0
            for a in range(live):
                code = (first + a) % LAYER
                row = [int(o) for o in OFFSETS[code][: BELOW[code, -1]]]
                near += sum(0 <= a + o and o <= 0 for o in row)
                far += sum(a + o < 0 or a + o >= live for o in row)
            inner, outer = max(inner, near), max(outer, far)
    return inner, outer


def rank(table, code, t):
    return table[code * STRIDE + jnp.clip(t, -REACH, REACH) + REACH + WIDEST]


FIELDS = 6


def write_plan(meta, table, plan, a):
    code = lax.bitwise_and(meta[1] + a, LAYER - 1)
    place = meta[1] + a
    low, split, middle = rank(table, code, -place), rank(table, code, -a), rank(table, code, 0)
    resume, high = rank(table, code, meta[0] - a), rank(table, code, meta[2] - place)
    row = code * STRIDE
    ahead = split - low
    plan[a * FIELDS] = middle - split
    plan[a * FIELDS + 1] = row + split
    plan[a * FIELDS + 2] = ahead + jnp.maximum(high - resume, 0)
    plan[a * FIELDS + 3] = ahead
    plan[a * FIELDS + 4] = row + low
    plan[a * FIELDS + 5] = row + resume - ahead


def write_run(runs, at, a, start, count):
    runs[3 * at], runs[3 * at + 1], runs[3 * at + 2] = a, start, count
    return at + (count > 0).astype(jnp.int32)


def write_runs(meta, table, plan, inner_runs, outer_runs, share):
    inner = outer = total = far = jnp.int32(0)
    for a in range(share):
        write_plan(meta, table, plan, a)
        alive = a < meta[0]
        count, start, count_far, ahead, start_far, start_after = (plan[a * FIELDS + k] for k in range(FIELDS))
        inner = write_run(inner_runs, inner, a, start, jnp.where(alive, count + 1, 0))
        outer = write_run(outer_runs, outer, a, start_far, jnp.where(alive, ahead, 0))
        outer = write_run(outer_runs, outer, a, start_after + ahead, jnp.where(alive, count_far - ahead, 0))
        total = total + jnp.where(alive, count + 1, 0)
        far = far + jnp.where(alive, count_far, 0)
    for runs, at in ((inner_runs, inner), (outer_runs, outer)):
        write_run(runs, at, share, len(FLAT) - 8, jnp.int32(1))
    plan[share * FIELDS] = total
    plan[share * FIELDS + 1] = far
    plan[share * FIELDS + 2] = inner
    plan[share * FIELDS + 3] = outer


def inner_range(plan, table, a):
    start = plan[a * FIELDS + 1]
    return plan[a * FIELDS], lambda t: a + table[start + t]


def outer_range(plan, table, a):
    ahead, start, start_after = (plan[a * FIELDS + k] for k in (3, 4, 5))
    return plan[a * FIELDS + 2], lambda t: a + table[t + jnp.where(t < ahead, start, start_after)]


TURN = 3


def padded_sweep(count, fetch, step, carry):
    def turn(i, state):
        carry, *now = state
        later = [fetch(TURN * (i + 1) + k) for k in range(TURN)]
        return step(now, carry), *later

    state = (carry, *(fetch(k) for k in range(TURN)))
    return lax.fori_loop(0, lax.div(count + (TURN - 1), TURN), turn, state)[0]


def tree(terms):
    while len(terms) > 1:
        terms = [a + b for a, b in zip(terms[::2], terms[1::2])] + terms[len(terms) // 2 * 2 :]
    return terms[0]


def gather(partial, c, term):
    if c < len(partial):
        partial[c] = term
    else:
        partial[c % len(partial)] = partial[c % len(partial)] + term


def pieces_of(width):
    return [slice(c * SUB, (c + 1) * SUB) for c in range(width // SUB)]


def wide(row):
    return jnp.broadcast_to(row, (SUB, row.shape[1]))


def three_parts(values):
    high = values.astype(jnp.bfloat16).astype(jnp.float32)
    rest = values - high
    middle = rest.astype(jnp.bfloat16).astype(jnp.float32)
    return high, middle, rest - middle


def stacked(rows):
    sublane = lax.broadcasted_iota(jnp.int32, rows[0].shape, 0)
    result = jnp.zeros(rows[0].shape, jnp.float32)
    for k, row in enumerate(rows):
        result = jnp.where(sublane == k, row, result)
    return result


def half_size(x):
    return 0.5 - (x[0] * x[0] + x[1] * x[1] + x[2] * x[2])


def own_side(x, which):
    nothing = [jnp.zeros_like(x[0])] * 4
    rows = [2.0 * x[0], 2.0 * x[1], 2.0 * x[2], jnp.ones_like(x[0])]
    high, middle, low = three_parts(stacked(nothing + rows if which else rows))
    sizes = stacked(list(three_parts(half_size(x))))
    width = sizes.shape[1]
    rest = jnp.zeros((width - 7 * SUB, width), jnp.float32)
    return jnp.concatenate([high, high, middle, middle, high, low, sizes, rest], 0)


def other_sides(first, second):
    rows = [*first, half_size(first), *second, half_size(second)]
    high, middle, low = three_parts(stacked(rows))
    width = high.shape[1]
    ones = jnp.where(lax.broadcasted_iota(jnp.int32, (2 * SUB, width), 0) < 3, 1.0, 0.0).astype(jnp.bfloat16)
    front = jnp.concatenate([high, middle], 0).astype(jnp.bfloat16)
    back = jnp.concatenate([low, high], 0).astype(jnp.bfloat16)
    rest = jnp.zeros((width - 8 * SUB, width), jnp.bfloat16)
    return jnp.concatenate([front, front, back, ones, rest], 0)


GROUP = 4


def flat_tiles(count, runs, most, table, sides, middles, weights, other_at, buffers, tiles, rows_ref, cols_ref):
    share, width = rows_ref.shape[0] - 1, rows_ref.shape[2]
    chunks = pieces_of(width)

    def steps(state):
        found = []
        for _ in range(GROUP):
            run, t = state
            a, start, size = (runs[3 * run + k] for k in range(3))
            found.append((a, a + table[start + t]))
            over = t + 1 >= size
            state = jnp.minimum(run + over.astype(jnp.int32), most), jnp.where(over, 0, t + 1)
        return state, found

    def other_of(a, n):
        here = pl.ds(a, 1)
        return [wide(other_at(c, n)) - wide(middles[c, here, :]) for c in range(3)]

    def products(found, ahead):
        for k in range(0, GROUP, 2):
            (a, n), (b, m) = ((jnp.minimum(a, share - 1), n) for a, n in found[k : k + 2])
            own = jnp.concatenate([sides[0, a], sides[1, b]], 0)
            both = jnp.dot(own, other_sides(other_of(a, n), other_of(b, m)), preferred_element_type=jnp.float32)
            ahead[k] = both[:width]
            ahead[k + 1] = both[width:]

    def weigh(at, found, ahead):
        for k, (a, n) in enumerate(found):
            alone = a == n
            row = jnp.where(alone, share, a)
            own = jnp.minimum(a, share - 1)
            other = wide(other_at(3, n))
            down = [None] * 2
            for c, here in enumerate(chunks):
                left = ahead[k, here, :]
                rest = jnp.maximum(left, 0.0)
                inverse = pltpu.reciprocal((1.01 - left) * (weights[own, here, :] + other), approx=True)
                tile = rest * rest * inverse
                tiles[at + k, here, :] = tile
                rows_ref[row, here, :] = rows_ref[row, here, :] + tile
                if cols_ref is not None:
                    gather(down, c, tile)
            if cols_ref is not None:
                there = pl.ds(pl.multiple_of(jnp.where(alone, share, n) * SUB, SUB), SUB)
                cols_ref[there, :] = cols_ref[there, :] + tree(down)

    def turn(i, carry):
        state, found = carry
        at = i * (2 * GROUP)
        state, later = steps(state)
        products(later, buffers[1])
        weigh(at, found, buffers[0])
        state, last = steps(state)
        products(last, buffers[0])
        weigh(at + GROUP, later, buffers[1])
        return state, last

    state, found = steps((jnp.int32(0), jnp.int32(0)))
    products(found, buffers[0])
    lax.fori_loop(0, lax.div(count + (2 * GROUP - 1), 2 * GROUP), turn, (state, found))


def spread_columns(out, index, rows):
    count, width = rows.shape
    turned = rows.T
    for a in range(count):
        out[index(a)] = jnp.broadcast_to(turned[:, a : a + 1], (width, width))


def lane_sums(parts, count, width):
    lanes = lax.broadcasted_iota(jnp.int32, (width, width), 1)
    turned = jnp.zeros((width, width), jnp.float32)
    for a in range(count):
        turned = jnp.where(lanes == a, jnp.sum(parts[a], axis=1, keepdims=True), turned)
    return turned.T[:count]


def sub_sums(cols):
    return jnp.sum(cols[...].reshape(-1, SUB, cols.shape[1]), axis=1)


def alive_rows(meta, share, width):
    return lax.broadcasted_iota(jnp.int32, (share, width), 0) < meta[0]


def prepare(
    counts, densities, position_in, phase_in, right_side_in, table_in,
    meta, table, hood, near, density, source, first_swap, second_swap, phase, right_side, sems
):
    share, width = source.shape
    capacity = phase.shape[0]
    body_rows = pl.ds(share, capacity)
    copies = [
        pltpu.make_async_copy(phase_in, phase, sems.at[0]),
        pltpu.make_async_copy(position_in, hood.at[pl.ds(0, 3), body_rows, :], sems.at[1]),
        pltpu.make_async_copy(right_side_in, right_side, sems.at[2]),
        pltpu.make_async_copy(table_in, table, sems.at[3]),
    ]
    for copy in copies:
        copy.start()
    piece, column = lax.axis_index("piece"), lax.axis_index("col")
    filled = counts[piece]
    filled_before = counts[jnp.maximum(piece - 1, 0)]
    before = jnp.int32(0)
    total = jnp.int32(0)
    for p in range(counts.shape[0]):
        before = before + jnp.where(p < piece, counts[p], 0)
        total = total + counts[p]
    meta[0] = jnp.clip(filled - column * share, 0, share)
    meta[1] = before + column * share
    meta[2] = total
    meta[3] = column * share
    meta[4] = filled
    meta[5] = filled_before
    own_rows = pl.ds(pl.multiple_of(share + column * share, SUB), share)
    copies[0].wait()
    labels = phase[...]
    whole = sum(jnp.where(labels == k, densities[k], 0.0) for k in range(densities.shape[0]))
    hood[3, body_rows, :] = whole * (width / 2.0)
    density[...] = hood[3, own_rows, :] * (2.0 / width)
    copies[1].wait()
    even = lax.rem(piece, 2) == 0
    for k in range(4):
        tail, head = hood[k, pl.ds(filled, share), :], hood[k, share : 2 * share, :]
        first_swap[k] = jnp.where(even, tail, head)
        second_swap[k] = jnp.where(even, head, tail)
        near[k, 0:share, :] = hood[k, own_rows, :]
    for copy in copies[2:]:
        copy.wait()
    source[...] = jnp.where(alive_rows(meta, share, width), right_side[...], 0.0)


def finish_tiles(tiles, end):
    for t in range(TURN):
        tiles[end + t] = jnp.zeros(tiles.shape[1:], jnp.float32)


def build_inner(
    meta, table, near, plan, outer_runs, tiles, sides, middles, weights, rows_out, cols_out, self_ref,
    inner_runs, rows_ref, cols_ref, *buffers,
):
    share, width = rows_out.shape[0], rows_out.shape[2]
    chunks = pieces_of(width)
    write_runs(meta, table, plan, inner_runs, outer_runs, share)
    for k in range(3):
        first = near[k, 0:share, 0:1]
        middles[k] = jnp.broadcast_to(jnp.floor(first) + 0.5, (share, width))
    for a in range(share):
        here = slice(a, a + 1)
        centred = [wide(near[k, here, :] - middles[k, here, :]) for k in range(3)]
        for which in range(2):
            sides[which, a] = own_side(centred, which).T.astype(jnp.bfloat16)
    spread_columns(weights, lambda a: a, near[3, 0:share, :])
    cols_ref[...] = jnp.zeros_like(cols_ref)
    rows_ref[...] = jnp.zeros_like(rows_ref)
    count = plan[share * FIELDS]
    flat_tiles(
        count, inner_runs, plan[share * FIELDS + 2], table, sides, middles, weights,
        lambda k, n: near[k, pl.ds(n, 1), :], buffers, tiles, rows_ref, cols_ref,
    )
    finish_tiles(tiles, count)
    lane = lax.broadcasted_iota(jnp.int32, (SUB, width), 1)
    sublane = lax.broadcasted_iota(jnp.int32, (SUB, width), 0)

    def block(a, at):
        at = at + plan[a * FIELDS]
        down = [None] * 4
        for c, here in enumerate(chunks):
            tile = jnp.where(lane == sublane + c * SUB, 0.0, tiles[at, here, :])
            tiles[at, here, :] = tile
            gather(down, c, tile)
        self_ref[pl.ds(pl.multiple_of(a * SUB, SUB), SUB), :] = tree(down)
        return at + 1

    lax.fori_loop(0, meta[0], block, 0)
    rows_out[...] = rows_ref[0:share]
    cols_out[...] = cols_ref[0 : share * SUB, :]


def count_listed(meta, lists, width):
    capacity = lists[0].shape[1]
    filled, filled_before = meta[4], meta[5]
    start = lax.axis_index("piece") * capacity
    steps = lax.broadcasted_iota(jnp.int32, (2 * REACH, capacity), 0)
    partial = [None] * 4
    row = 0
    for ref in lists:
        ids = ref[...]
        slot = ids - start
        gap = jnp.where(slot < 0, capacity - filled_before, jnp.where(slot >= capacity, filled - capacity, 0))
        away = slot - lax.broadcasted_iota(jnp.int32, ids.shape, 1) + gap
        away = jnp.where(ids < 0, -REACH, away) + REACH
        for k in range(ids.shape[0]):
            gather(partial, row, jnp.where(steps == away[k : k + 1], 1.0, 0.0))
            row += 1
    return jnp.concatenate([tree(partial), jnp.zeros((width - 2 * REACH, capacity), jnp.float32)], 0).T


def factor(times, a, n):
    lane = lax.broadcasted_iota(jnp.int32, (1, times.shape[1]), 1)
    return jnp.sum(jnp.where(lane == n - a + REACH, times[pl.ds(a, 1), :], 0.0), axis=1, keepdims=True)


def either(flag, run):
    @pl.when(flag == 0)
    def _():
        run(False)

    @pl.when(flag != 0)
    def _():
        run(True)


TAIL = 13


def build_outer(
    meta, table, plan, runs, around, first, second, density, source, tiles_in, sides, middles, weights,
    rows_ref, cols_ref, self_ref, *rest
):
    lists, rest = rest[:-TAIL], rest[-TAIL:]
    again_ref, tiles, diagonal_ref, precond_ref, times, alone_ref, hood, work, sums_ref, extra, all_times, *buffers = rest
    share, width = diagonal_ref.shape
    base, filled = meta[3], meta[4]
    even = lax.rem(lax.axis_index("piece"), 2) == 0
    for k in range(4):
        hood[k, 0:share, :] = jnp.where(even, second[k], first[k])
        hood[k, share:, :] = around[k, share:, :]
        hood[k, pl.ds(share + filled, share), :] = jnp.where(even, first[k], second[k])
    alive = alive_rows(meta, share, width)
    all_times[...] = count_listed(meta, lists, width)
    often = jnp.where(alive, all_times[pl.ds(pl.multiple_of(base, SUB), share), :], 0.0)
    times[...] = often
    lane = lax.broadcasted_iota(jnp.int32, (share, width), 1)
    again = jnp.max(jnp.where((lane == REACH) | (lane == 0), 0.0, often)) > 1.5
    again_ref[0] = again.astype(jnp.int32)


    work[...] = jnp.zeros_like(work)
    count = plan[share * FIELDS + 1]
    flat_tiles(
        count, runs, plan[share * FIELDS + 3], table, sides, middles, weights,
        lambda k, n: hood[k, pl.ds(base + share + n, 1), :], buffers, tiles, work, None,
    )
    finish_tiles(tiles, count)
    sums_ref[...] = lane_sums([rows_ref[a] + work[a] for a in range(share)], share, width) + sub_sums(cols_ref)

    @pl.when(again)
    def _():
        extra[...] = jnp.zeros_like(extra)
        work[...] = jnp.zeros_like(work)

        def block(a, state):
            count, place_of = inner_range(plan, table, a)

            def inner(t, at):
                n = place_of(t)
                tile = tiles_in[at]
                work[a] = work[a] + tile * factor(times, a, n)
                there = pl.ds(n, 1)
                down = jnp.sum(tile, axis=0, keepdims=True)
                extra[there, :] = extra[there, :] + down * factor(times, n, a)
                return at + 1

            at = lax.fori_loop(0, count, inner, state[0]) + 1
            count, place_far = outer_range(plan, table, a)

            def outer(t, at):
                work[a] = work[a] + tiles[at] * factor(times, a, place_far(t))
                return at + 1

            return at, lax.fori_loop(0, count, outer, state[1])

        lax.fori_loop(0, meta[0], block, (0, 0))
        sums_ref[...] = lane_sums(work, share, width) + extra[...]

    alone = jnp.sum(jnp.where(lane == REACH, often, 0.0), axis=1, keepdims=True)
    alone_ref[...] = jnp.broadcast_to(alone, (share, width))
    pairs = jnp.where(alive, sums_ref[...] + sub_sums(self_ref) * alone, 0.0)
    diagonal = 1.0 / density[...] + pairs
    diagonal_ref[...] = diagonal
    precond_ref[...] = source[...] / diagonal


def apply_inner(meta, table, plan, again, field, alone, times, tiles, rows_ref, cols_ref, spread, near, lone, cols):
    share, width = field.shape
    chunks = pieces_of(width)
    near[0:share, :] = field[...]
    near[share:, :] = jnp.zeros((SUB, width), jnp.float32)
    lone[...] = field[...] * alone[...]
    spread_columns(spread, lambda a: a, field[...])
    cols[...] = jnp.zeros_like(cols)

    def run(weighted):
        def block(a, at):
            count, place_of = inner_range(plan, table, a)

            def fetch(t):
                n = jnp.where(t < count, place_of(t), share)
                return n, wide(near[pl.ds(n, 1), :])

            def pairs(fetched, carry):
                at, sums = carry
                if weighted:
                    fetched = [(n, value * factor(times, a, jnp.minimum(n, share - 1))) for n, value in fetched]
                down = [[None] * 2 for _ in fetched]
                result = []
                for c, (here, total) in enumerate(zip(chunks, sums)):
                    own = spread[a, here, :]
                    found = []
                    for t, (_, value) in enumerate(fetched):
                        tile = tiles[at + t, here, :]
                        gather(down[t], c, tile * own)
                        found.append(tile * value)
                    result.append(total + tree(found))
                for (n, _), partial in zip(fetched, down):
                    there = pl.ds(pl.multiple_of(n * SUB, SUB), SUB)
                    partial = tree(partial)
                    if weighted:
                        partial = partial * factor(times, jnp.minimum(n, share - 1), a)
                    cols[there, :] = cols[there, :] + partial
                return at + len(fetched), result

            zero = jnp.zeros((SUB, width), jnp.float32)
            _, sums = padded_sweep(count, fetch, pairs, (at, [zero] * len(chunks)))
            at = at + count
            value = wide(lone[pl.ds(a, 1), :])
            for here, old in zip(chunks, sums):
                rows_ref[a, here, :] = old + tiles[at, here, :] * value
            return at + 1

        lax.fori_loop(0, meta[0], block, 0)

    either(again[0], run)
    cols_ref[...] = cols[0 : share * SUB, :]


def apply_outer(meta, table, plan, again, received, times, tiles, rows_ref, cols_ref, work, hood):
    first, second, *ends = received
    columns = len(received)
    share, width = first.shape
    chunks = pieces_of(width)
    base, filled = meta[3], meta[4]
    column = lax.div(base, share)
    odd = lax.rem(column, 2) == 1
    before = jnp.where(odd, first[...], second[...])
    after = jnp.where(odd, second[...], first[...])
    own = 3 * share
    for c, end in enumerate(ends, 1):
        hood[pl.ds(own - meta[5] + c * share, share), :] = end[...]
    from_last = own - meta[5] + (columns - 1) * share
    hood[pl.ds(jnp.where(column == 0, from_last, own - share), share), :] = before
    hood[own + share : own + 2 * share, :] = after
    head = after
    for c, end in enumerate(ends, 1):
        head = jnp.where(column == c, end[...], head)
    hood[pl.ds(own + jnp.clip(filled - base, 0, 2 * share), share), :] = head
    nothing = hood.shape[0] - SUB
    hood[nothing:, :] = jnp.zeros((SUB, width), jnp.float32)

    def run(weighted):
        def block(a, at):
            count, place_of = outer_range(plan, table, a)

            def fetch(t):
                place = place_of(t)
                value = hood[pl.ds(jnp.where(t < count, own + place, nothing), 1), :]
                if weighted:
                    value = value * factor(times, a, place)
                return wide(value)

            def pairs(values, carry):
                at, sums = carry
                result = []
                for here, total in zip(chunks, sums):
                    result.append(total + tree([tiles[at + t, here, :] * value for t, value in enumerate(values)]))
                return at + len(values), result

            _, sums = padded_sweep(count, fetch, pairs, (at, [rows_ref[a, here, :] for here in chunks]))
            for here, values in zip(chunks, sums):
                work[a, here, :] = values
            return at + count

        lax.fori_loop(0, meta[0], block, 0)

    either(again[0], run)
    return jnp.where(alive_rows(meta, share, width), lane_sums(work, share, width) + sub_sums(cols_ref), 0.0)


def apply_first(meta, table, plan, again, diagonal, times, *rest):
    *received, tiles, rows_ref, cols_ref, spill_ref, scaled_ref, work, hood = rest
    spill = apply_outer(meta, table, plan, again, received, times, tiles, rows_ref, cols_ref, work, hood)
    spill_ref[...] = spill
    scaled_ref[...] = spill / diagonal[...]


def apply_second(meta, table, plan, again, source, precond, spill, scaled, times, *rest):
    *received, tiles, rows_ref, cols_ref, twice_ref, sums_ref, work, hood = rest
    twice = apply_outer(meta, table, plan, again, received, times, tiles, rows_ref, cols_ref, work, hood)
    twice_ref[...] = twice
    share, width = twice.shape
    lane = lax.broadcasted_iota(jnp.int32, (1, width), 1)
    sums = jnp.zeros((1, width), jnp.float32)
    pairs = ((source[...], precond[...]), (spill[...], precond[...]), (spill[...], scaled[...]), (scaled[...], twice))
    for k, (first, second) in enumerate(pairs):
        along = jnp.sum(first * second, axis=0, keepdims=True)
        sums = jnp.where(lane == k, jnp.sum(along, axis=1, keepdims=True), sums)
    sums_ref[...] = wide(sums)


def finish(source, precond, spill, scaled, twice, *rest):
    *parts, solution_ref, residual_ref = rest
    sums = tree([ref[...] for ref in parts])

    def pick(k):
        return sums[0:1, k : k + 1]

    weighted, cross, square, last = pick(0), pick(1), pick(2), pick(3)
    part = cross / weighted
    advance = 1.0 / (1.0 - part)
    keep = -part * advance
    weighted_next = advance * advance * (square - cross * part)
    bent = keep * keep * cross + 2.0 * keep * advance * square + advance * advance * last
    blend = weighted_next / weighted
    advance_next = weighted_next / (weighted_next - bent - blend * weighted_next / advance)
    residual = keep * source[...] + advance * spill[...]
    next_precond = keep * precond[...] + advance * scaled[...]
    direction = next_precond + blend * precond[...]
    image = residual - keep * spill[...] - advance * twice[...] + blend * (source[...] - spill[...])
    solution_ref[...] = advance * precond[...] + advance_next * direction
    residual_ref[...] = residual - advance_next * image


def held(array):
    return pltpu.with_memory_space_constraint(array, pltpu.VMEM)


def body(positions, phase, neighbours, counts, phase_density, right_side):
    capacity, width = phase.shape
    columns = lax.axis_size("col")
    pieces = lax.axis_size("piece")
    share = capacity // columns
    f32 = jnp.float32
    vector = jax.ShapeDtypeStruct((share, width), f32)
    few = jax.ShapeDtypeStruct((SUB, width), f32)
    message = jax.ShapeDtypeStruct((4, share, width), f32)
    most_inner, most_outer = tile_bounds(share)
    inner_tiles = pltpu.VMEM((most_inner + 2 * GROUP, width, width), f32)
    outer_tiles = pltpu.VMEM((most_outer + 2 * GROUP, width, width), f32)
    ahead = pltpu.VMEM((GROUP, width, width), f32)
    square_more = pltpu.VMEM((share + 1, width, width), f32)
    square = pltpu.VMEM((share, width, width), f32)
    narrow = pltpu.VMEM((share * SUB, width), f32)
    table = jnp.asarray(FLAT)

    def call(kernel, args, outs, scratch=(), work=0, scalars=2, far=0, **more):
        return pl.pallas_call(
            kernel,
            out_shape=outs,
            in_specs=[SMEM] * scalars + [HBM] * far + [VMEM] * (len(args) - scalars - far),
            out_specs=[SMEM if getattr(o, "memory_space", None) == pltpu.SMEM else VMEM for o in outs],
            scratch_shapes=scratch,
            compiler_params=LIMIT,
            cost_estimate=pl.CostEstimate(flops=work * width * width, bytes_accessed=0, transcendentals=0),
            name=kernel.__name__,
            **more,
        )(*args)

    def swap(values, axis, step):
        return lax.ppermute(values, axis, [(i, i ^ step) for i in range(lax.axis_size(axis))])

    col_steps = [(1 << k) | 1 for k in range(columns.bit_length() - 1)]
    lists = [neighbours.T]
    for step in col_steps:
        known = lists[0] if len(lists) == 1 else jnp.concatenate(lists, 0)
        lists = [known, swap(known, "col", step)]

    def away(array):
        return pltpu.with_memory_space_constraint(array, pltpu.HBM)

    around = jax.ShapeDtypeStruct((4, capacity + 2 * share, width), f32)
    near = jax.ShapeDtypeStruct((4, 2 * share, width), f32)
    far = [away(array) for array in (positions, phase, right_side, table)]
    meta, table, around, near, density, source, first, second = call(
        prepare,
        (away(counts), away(phase_density), *far),
        [pltpu.SMEM((8,), jnp.int32), pltpu.SMEM(table.shape, jnp.int32), around, near, vector, vector, message, message],
        [pltpu.VMEM(phase.shape, jnp.int32), pltpu.VMEM((share, width), f32), pltpu.SemaphoreType.DMA((4,))],
        far=len(far),
    )
    meta, table = (pltpu.with_memory_space_constraint(array, pltpu.SMEM) for array in (meta, table))
    first = lax.ppermute(first, "piece", [(i, i ^ 1) for i in range(pieces)])
    axes = ("piece", "col")
    device = [(p, c) for p in range(pieces) for c in range(columns)]
    partner = [(p + (1 if p % 2 else -1), c) for p, c in device]
    partner = [(q, d) if 0 <= q < pieces else (p, c ^ 1) for (q, d), (p, c) in zip(partner, device)]
    second = lax.ppermute(second, axes, [(i, q * columns + d) for i, (q, d) in enumerate(partner)])

    plan, runs, tiles_in, sides, middles, weights, rows, cols, selfs = call(
        build_inner,
        (meta, table, near),
        [pltpu.SMEM((share * FIELDS + 4,), jnp.int32), pltpu.SMEM((6 * share + 3,), jnp.int32), inner_tiles,
         pltpu.VMEM((2, share, width, width), jnp.bfloat16), pltpu.VMEM((3, share, width), f32), square, square, narrow, narrow],
        [pltpu.SMEM((3 * share + 3,), jnp.int32), square_more, pltpu.VMEM(((share + 1) * SUB, width), f32), ahead, ahead],
        16 * most_inner,
    )
    plan, runs = (pltpu.with_memory_space_constraint(array, pltpu.SMEM) for array in (plan, runs))
    again, tiles_out, diagonal, precond, times, alone = call(
        build_outer,
        (meta, table, plan, runs, around, first, second, density, source,
         held(tiles_in), held(sides), held(middles), held(weights), held(rows), held(cols), held(selfs), *lists),
        [pltpu.SMEM((1,), jnp.int32), outer_tiles, vector, vector, vector, vector],
        [pltpu.VMEM((4, capacity + 2 * share, width), f32), square_more]
        + [pltpu.VMEM((share, width), f32)] * 2 + [pltpu.VMEM((capacity, width), f32), ahead, ahead],
        16 * most_outer,
        scalars=4,
    )
    again = pltpu.with_memory_space_constraint(again, pltpu.SMEM)

    def inner(field):
        return call(
            apply_inner,
            (meta, table, plan, again, field, alone, times, held(tiles_in)),
            [square, narrow],
            [pltpu.VMEM((share, width, width), f32), pltpu.VMEM((share + SUB, width), f32), pltpu.VMEM((share, width), f32),
             pltpu.VMEM(((share + 1) * SUB, width), f32)],
            4 * most_inner,
            scalars=4,
        )

    def exchange(field):
        count = pieces * columns
        swaps = [[i ^ 1 for i in range(count)], [i - 1 if i % 2 == 0 else i + 1 for i in range(count)]]
        swaps[1][0], swaps[1][-1] = count - 1, 0
        for c in range(1, columns - 1):
            to = {}
            for p in range(pieces - 1):
                low, high = p * columns + c, (p + 1) * columns
                to[low], to[high] = high, low
            for p in range(pieces):
                rest = [i for i in range(p * columns, (p + 1) * columns) if i not in to]
                to.update(zip(rest, rest[1:] + rest[:1]))
            swaps.append([to[i] for i in range(count)])
        received = [lax.ppermute(field, axes, list(enumerate(to))) for to in swaps[::-1]]
        return received[::-1]

    scratch = [pltpu.VMEM((share, width, width), f32), pltpu.VMEM((8 * share, width), f32)]

    received = exchange(precond)
    rows, cols = inner(precond)
    spill, scaled = call(
        apply_first,
        (meta, table, plan, again, diagonal, times, *received, held(tiles_out), held(rows), held(cols)),
        [vector, vector],
        scratch,
        2 * most_outer,
        scalars=4,
    )

    received = exchange(scaled)
    rows, cols = inner(scaled)
    twice, sums = call(
        apply_second,
        (meta, table, plan, again, source, precond, spill, scaled, times, *received, held(tiles_out), held(rows), held(cols)),
        [vector, few],
        scratch,
        2 * most_outer,
        scalars=4,
    )

    def together(values, axis, low, size):
        return tree([values] + [swap(values, axis, low * k) for k in range(size - 1, 0, -1)][::-1])

    sums = together(sums, "piece", 1, 2)
    sums = together(sums, "col", 1, columns)
    step = 2
    while pieces // step > 4:
        sums = together(sums, "piece", step, 4)
        step *= 4
    others = [swap(sums, "piece", step * k) for k in range(pieces // step - 1, 0, -1)][::-1]

    return tuple(call(
        finish,
        (source, precond, spill, scaled, twice, sums, *others),
        [vector, vector],
        scalars=0,
    ))


def solution(mesh):
    placed = (
        P(None, "piece", None),
        P("piece", None),
        P("piece", "col"),
        P(),
        P(),
        P(("piece", "col"), None),
    )
    return jax.shard_map(
        body,
        mesh=mesh,
        in_specs=placed,
        out_specs=(P(("piece", "col"), None), P(("piece", "col"), None)),
        check_vma=False,
    )
```

```python
import jax
import jax.numpy as jnp
import numpy as np
from jax import lax
from jax.experimental import pallas as pl
from jax.experimental.pallas import tpu as pltpu
from jax.sharding import PartitionSpec as P

ITERS = 2
SIDE = 4
LAYER = SIDE * SIDE
REACH = 2 * LAYER
SUB = 8
VMEM = pl.BlockSpec(memory_space=pltpu.VMEM)
SMEM = pl.BlockSpec(memory_space=pltpu.SMEM)
HBM = pl.BlockSpec(memory_space=pltpu.HBM)


def stencil_tables():
    levels = SIDE.bit_length() - 1

    def cell(code):
        across = sum((code >> (2 * level) & 1) << level for level in range(levels))
        along = sum((code >> (2 * level + 1) & 1) << level for level in range(levels))
        return across, along

    place = {cell(code): code for code in range(LAYER)}
    rows = []
    for code in range(LAYER):
        across, along = cell(code)
        rows.append(
            sorted(
                step_z * LAYER + place[across + step_x, along + step_y] - code
                for step_z in (-1, 0, 1)
                for step_y in (-1, 0, 1)
                for step_x in (-1, 0, 1)
                if (across + step_x, along + step_y) in place
            )
        )
    longest = max(len(row) for row in rows)
    offsets = np.zeros((LAYER, longest), np.int32)
    below = np.zeros((LAYER, 2 * REACH + 1), np.int32)
    for code, row in enumerate(rows):
        offsets[code, : len(row)] = row
        for t in range(-REACH, REACH + 1):
            below[code, t + REACH] = sum(offset < t for offset in row)
    return offsets, below


OFFSETS, BELOW = stencil_tables()
WIDEST = OFFSETS.shape[1]
TABLE = np.concatenate([OFFSETS, BELOW], 1)
STRIDE = TABLE.shape[1]
FLAT = np.concatenate([TABLE.reshape(-1), np.zeros(8, np.int32)])
LIMIT = pltpu.CompilerParams(vmem_limit_bytes=8 * 1024 * 1024)


def tile_bounds(share):
    inner = outer = 0
    for first in range(LAYER):
        for live in range(1, share + 1):
            near = far = 0
            for a in range(live):
                code = (first + a) % LAYER
                row = [int(o) for o in OFFSETS[code][: BELOW[code, -1]]]
                near += sum(0 <= a + o and o <= 0 for o in row)
                far += sum(a + o < 0 or a + o >= live for o in row)
            inner, outer = max(inner, near), max(outer, far)
    return inner, outer


def rank(table, code, t):
    return table[code * STRIDE + jnp.clip(t, -REACH, REACH) + REACH + WIDEST]


FIELDS = 6


def write_plan(meta, table, plan, a):
    code = lax.bitwise_and(meta[1] + a, LAYER - 1)
    place = meta[1] + a
    low, split, middle = rank(table, code, -place), rank(table, code, -a), rank(table, code, 0)
    resume, high = rank(table, code, meta[0] - a), rank(table, code, meta[2] - place)
    row = code * STRIDE
    ahead = split - low
    plan[a * FIELDS] = middle - split
    plan[a * FIELDS + 1] = row + split
    plan[a * FIELDS + 2] = ahead + jnp.maximum(high - resume, 0)
    plan[a * FIELDS + 3] = ahead
    plan[a * FIELDS + 4] = row + low
    plan[a * FIELDS + 5] = row + resume - ahead


def write_run(runs, at, a, start, count):
    runs[3 * at], runs[3 * at + 1], runs[3 * at + 2] = a, start, count
    return at + (count > 0).astype(jnp.int32)


def write_runs(meta, table, plan, inner_runs, outer_runs, share):
    inner = outer = total = far = jnp.int32(0)
    for a in range(share):
        write_plan(meta, table, plan, a)
        alive = a < meta[0]
        count, start, count_far, ahead, start_far, start_after = (plan[a * FIELDS + k] for k in range(FIELDS))
        inner = write_run(inner_runs, inner, a, start, jnp.where(alive, count + 1, 0))
        outer = write_run(outer_runs, outer, a, start_far, jnp.where(alive, ahead, 0))
        outer = write_run(outer_runs, outer, a, start_after + ahead, jnp.where(alive, count_far - ahead, 0))
        total = total + jnp.where(alive, count + 1, 0)
        far = far + jnp.where(alive, count_far, 0)
    for runs, at in ((inner_runs, inner), (outer_runs, outer)):
        write_run(runs, at, share, len(FLAT) - 8, jnp.int32(1))
    plan[share * FIELDS] = total
    plan[share * FIELDS + 1] = far
    plan[share * FIELDS + 2] = inner
    plan[share * FIELDS + 3] = outer


def inner_range(plan, table, a):
    start = plan[a * FIELDS + 1]
    return plan[a * FIELDS], lambda t: a + table[start + t]


def outer_range(plan, table, a):
    ahead, start, start_after = (plan[a * FIELDS + k] for k in (3, 4, 5))
    return plan[a * FIELDS + 2], lambda t: a + table[t + jnp.where(t < ahead, start, start_after)]


TURN = 3


def padded_sweep(count, fetch, step, carry):
    def turn(i, state):
        carry, *now = state
        later = [fetch(TURN * (i + 1) + k) for k in range(TURN)]
        return step(now, carry), *later

    state = (carry, *(fetch(k) for k in range(TURN)))
    return lax.fori_loop(0, lax.div(count + (TURN - 1), TURN), turn, state)[0]


def tree(terms):
    while len(terms) > 1:
        terms = [a + b for a, b in zip(terms[::2], terms[1::2])] + terms[len(terms) // 2 * 2 :]
    return terms[0]


def gather(partial, c, term):
    if c < len(partial):
        partial[c] = term
    else:
        partial[c % len(partial)] = partial[c % len(partial)] + term


def pieces_of(width):
    return [slice(c * SUB, (c + 1) * SUB) for c in range(width // SUB)]


def wide(row):
    return jnp.broadcast_to(row, (SUB, row.shape[1]))


def three_parts(values):
    high = values.astype(jnp.bfloat16).astype(jnp.float32)
    rest = values - high
    middle = rest.astype(jnp.bfloat16).astype(jnp.float32)
    return high, middle, rest - middle


def stacked(rows):
    sublane = lax.broadcasted_iota(jnp.int32, rows[0].shape, 0)
    result = jnp.zeros(rows[0].shape, jnp.float32)
    for k, row in enumerate(rows):
        result = jnp.where(sublane == k, row, result)
    return result


def half_size(x):
    return 0.5 - (x[0] * x[0] + x[1] * x[1] + x[2] * x[2])


def own_side(x, which):
    nothing = [jnp.zeros_like(x[0])] * 4
    rows = [2.0 * x[0], 2.0 * x[1], 2.0 * x[2], jnp.ones_like(x[0])]
    high, middle, low = three_parts(stacked(nothing + rows if which else rows))
    sizes = stacked(list(three_parts(half_size(x))))
    width = sizes.shape[1]
    rest = jnp.zeros((width - 7 * SUB, width), jnp.float32)
    return jnp.concatenate([high, high, middle, middle, high, low, sizes, rest], 0)


def other_sides(first, second):
    rows = [*first, half_size(first), *second, half_size(second)]
    high, middle, low = three_parts(stacked(rows))
    width = high.shape[1]
    ones = jnp.where(lax.broadcasted_iota(jnp.int32, (2 * SUB, width), 0) < 3, 1.0, 0.0).astype(jnp.bfloat16)
    front = jnp.concatenate([high, middle], 0).astype(jnp.bfloat16)
    back = jnp.concatenate([low, high], 0).astype(jnp.bfloat16)
    rest = jnp.zeros((width - 8 * SUB, width), jnp.bfloat16)
    return jnp.concatenate([front, front, back, ones, rest], 0)


GROUP = 4


def flat_tiles(count, runs, most, table, sides, middles, weights, other_at, buffers, tiles, rows_ref, cols_ref):
    share, width = rows_ref.shape[0] - 1, rows_ref.shape[2]
    chunks = pieces_of(width)

    def steps(state):
        found = []
        for _ in range(GROUP):
            run, t = state
            a, start, size = (runs[3 * run + k] for k in range(3))
            found.append((a, a + table[start + t]))
            over = t + 1 >= size
            state = jnp.minimum(run + over.astype(jnp.int32), most), jnp.where(over, 0, t + 1)
        return state, found

    def other_of(a, n):
        here = pl.ds(a, 1)
        return [wide(other_at(c, n)) - wide(middles[c, here, :]) for c in range(3)]

    def products(found, ahead):
        for k in range(0, GROUP, 2):
            (a, n), (b, m) = ((jnp.minimum(a, share - 1), n) for a, n in found[k : k + 2])
            own = jnp.concatenate([sides[0, a], sides[1, b]], 0)
            both = jnp.dot(own, other_sides(other_of(a, n), other_of(b, m)), preferred_element_type=jnp.float32)
            ahead[k] = both[:width]
            ahead[k + 1] = both[width:]

    def weigh(at, found, ahead):
        for k, (a, n) in enumerate(found):
            alone = a == n
            row = jnp.where(alone, share, a)
            own = jnp.minimum(a, share - 1)
            other = wide(other_at(3, n))
            down = [None] * 2
            for c in range(0, len(chunks), 2):
                above, below = [], []
                for here in chunks[c : c + 2]:
                    left = ahead[k, here, :]
                    rest = jnp.maximum(left, 0.0)
                    above.append(rest * rest)
                    below.append((1.01 - left) * (weights[own, here, :] + other))
                inverse = pltpu.reciprocal(below[0] * below[1], approx=True)
                pair = above[0] * (inverse * below[1]), above[1] * (inverse * below[0])
                for b, (here, tile) in enumerate(zip(chunks[c : c + 2], pair)):
                    tiles[at + k, here, :] = tile
                    rows_ref[row, here, :] = rows_ref[row, here, :] + tile
                    if cols_ref is not None:
                        gather(down, c + b, tile)
            if cols_ref is not None:
                there = pl.ds(pl.multiple_of(jnp.where(alone, share, n) * SUB, SUB), SUB)
                cols_ref[there, :] = cols_ref[there, :] + tree(down)

    def turn(i, carry):
        state, found = carry
        at = i * (2 * GROUP)
        state, later = steps(state)
        products(later, buffers[1])
        weigh(at, found, buffers[0])
        state, last = steps(state)
        products(last, buffers[0])
        weigh(at + GROUP, later, buffers[1])
        return state, last

    state, found = steps((jnp.int32(0), jnp.int32(0)))
    products(found, buffers[0])
    lax.fori_loop(0, lax.div(count + (2 * GROUP - 1), 2 * GROUP), turn, (state, found))


def spread_columns(out, index, rows):
    count, width = rows.shape
    turned = rows.T
    for a in range(count):
        out[index(a)] = jnp.broadcast_to(turned[:, a : a + 1], (width, width))


def lane_sums(parts, count, width):
    lanes = lax.broadcasted_iota(jnp.int32, (width, width), 1)
    turned = jnp.zeros((width, width), jnp.float32)
    for a in range(count):
        turned = jnp.where(lanes == a, jnp.sum(parts[a], axis=1, keepdims=True), turned)
    return turned.T[:count]


def sub_sums(cols):
    return jnp.sum(cols[...].reshape(-1, SUB, cols.shape[1]), axis=1)


def alive_rows(meta, share, width):
    return lax.broadcasted_iota(jnp.int32, (share, width), 0) < meta[0]


def prepare(
    counts, densities, position_in, phase_in, right_side_in, table_in,
    meta, table, hood, near, density, source, first_swap, second_swap, phase, right_side, sems
):
    share, width = source.shape
    capacity = phase.shape[0]
    body_rows = pl.ds(share, capacity)
    copies = [
        pltpu.make_async_copy(phase_in, phase, sems.at[0]),
        pltpu.make_async_copy(position_in, hood.at[pl.ds(0, 3), body_rows, :], sems.at[1]),
        pltpu.make_async_copy(right_side_in, right_side, sems.at[2]),
        pltpu.make_async_copy(table_in, table, sems.at[3]),
    ]
    for copy in copies:
        copy.start()
    piece, column = lax.axis_index("piece"), lax.axis_index("col")
    filled = counts[piece]
    filled_before = counts[jnp.maximum(piece - 1, 0)]
    before = jnp.int32(0)
    total = jnp.int32(0)
    for p in range(counts.shape[0]):
        before = before + jnp.where(p < piece, counts[p], 0)
        total = total + counts[p]
    meta[0] = jnp.clip(filled - column * share, 0, share)
    meta[1] = before + column * share
    meta[2] = total
    meta[3] = column * share
    meta[4] = filled
    meta[5] = filled_before
    own_rows = pl.ds(pl.multiple_of(share + column * share, SUB), share)
    copies[0].wait()
    labels = phase[...]
    whole = sum(jnp.where(labels == k, densities[k], 0.0) for k in range(densities.shape[0]))
    hood[3, body_rows, :] = whole * (width / 2.0)
    density[...] = hood[3, own_rows, :] * (2.0 / width)
    copies[1].wait()
    even = lax.rem(piece, 2) == 0
    for k in range(4):
        tail, head = hood[k, pl.ds(filled, share), :], hood[k, share : 2 * share, :]
        first_swap[k] = jnp.where(even, tail, head)
        second_swap[k] = jnp.where(even, head, tail)
        near[k, 0:share, :] = hood[k, own_rows, :]
    for copy in copies[2:]:
        copy.wait()
    source[...] = jnp.where(alive_rows(meta, share, width), right_side[...], 0.0)


def finish_tiles(tiles, end):
    for t in range(TURN):
        tiles[end + t] = jnp.zeros(tiles.shape[1:], jnp.float32)


def build_inner(
    meta, table, near, plan, outer_runs, tiles, sides, middles, weights, rows_out, cols_out, self_ref,
    inner_runs, rows_ref, cols_ref, *buffers,
):
    share, width = rows_out.shape[0], rows_out.shape[2]
    chunks = pieces_of(width)
    write_runs(meta, table, plan, inner_runs, outer_runs, share)
    for k in range(3):
        first = near[k, 0:share, 0:1]
        middles[k] = jnp.broadcast_to(jnp.floor(first) + 0.5, (share, width))
    for a in range(share):
        here = slice(a, a + 1)
        centred = [wide(near[k, here, :] - middles[k, here, :]) for k in range(3)]
        for which in range(2):
            sides[which, a] = own_side(centred, which).T.astype(jnp.bfloat16)
    spread_columns(weights, lambda a: a, near[3, 0:share, :])
    cols_ref[...] = jnp.zeros_like(cols_ref)
    rows_ref[...] = jnp.zeros_like(rows_ref)
    count = plan[share * FIELDS]
    flat_tiles(
        count, inner_runs, plan[share * FIELDS + 2], table, sides, middles, weights,
        lambda k, n: near[k, pl.ds(n, 1), :], buffers, tiles, rows_ref, cols_ref,
    )
    finish_tiles(tiles, count)
    lane = lax.broadcasted_iota(jnp.int32, (SUB, width), 1)
    sublane = lax.broadcasted_iota(jnp.int32, (SUB, width), 0)

    def block(a, at):
        at = at + plan[a * FIELDS]
        down = [None] * 4
        for c, here in enumerate(chunks):
            tile = jnp.where(lane == sublane + c * SUB, 0.0, tiles[at, here, :])
            tiles[at, here, :] = tile
            gather(down, c, tile)
        self_ref[pl.ds(pl.multiple_of(a * SUB, SUB), SUB), :] = tree(down)
        return at + 1

    lax.fori_loop(0, meta[0], block, 0)
    rows_out[...] = rows_ref[0:share]
    cols_out[...] = cols_ref[0 : share * SUB, :]


def count_listed(meta, lists, width):
    capacity = lists[0].shape[1]
    filled, filled_before = meta[4], meta[5]
    start = lax.axis_index("piece") * capacity
    steps = lax.broadcasted_iota(jnp.int32, (2 * REACH, capacity), 0)
    partial = [None] * 4
    row = 0
    for ref in lists:
        ids = ref[...]
        slot = ids - start
        gap = jnp.where(slot < 0, capacity - filled_before, jnp.where(slot >= capacity, filled - capacity, 0))
        away = slot - lax.broadcasted_iota(jnp.int32, ids.shape, 1) + gap
        away = jnp.where(ids < 0, -REACH, away) + REACH
        for k in range(ids.shape[0]):
            gather(partial, row, jnp.where(steps == away[k : k + 1], 1.0, 0.0))
            row += 1
    return jnp.concatenate([tree(partial), jnp.zeros((width - 2 * REACH, capacity), jnp.float32)], 0).T


def factor(times, a, n):
    lane = lax.broadcasted_iota(jnp.int32, (1, times.shape[1]), 1)
    return jnp.sum(jnp.where(lane == n - a + REACH, times[pl.ds(a, 1), :], 0.0), axis=1, keepdims=True)


def either(flag, run):
    @pl.when(flag == 0)
    def _():
        run(False)

    @pl.when(flag != 0)
    def _():
        run(True)


TAIL = 13


def build_outer(
    meta, table, plan, runs, around, first, second, density, source, tiles_in, sides, middles, weights,
    rows_ref, cols_ref, self_ref, *rest
):
    lists, rest = rest[:-TAIL], rest[-TAIL:]
    again_ref, tiles, diagonal_ref, precond_ref, times, alone_ref, hood, work, sums_ref, extra, all_times, *buffers = rest
    share, width = diagonal_ref.shape
    base, filled = meta[3], meta[4]
    even = lax.rem(lax.axis_index("piece"), 2) == 0
    for k in range(4):
        hood[k, 0:share, :] = jnp.where(even, second[k], first[k])
        hood[k, share:, :] = around[k, share:, :]
        hood[k, pl.ds(share + filled, share), :] = jnp.where(even, first[k], second[k])
    alive = alive_rows(meta, share, width)
    all_times[...] = count_listed(meta, lists, width)
    often = jnp.where(alive, all_times[pl.ds(pl.multiple_of(base, SUB), share), :], 0.0)
    times[...] = often
    lane = lax.broadcasted_iota(jnp.int32, (share, width), 1)
    again = jnp.max(jnp.where((lane == REACH) | (lane == 0), 0.0, often)) > 1.5
    again_ref[0] = again.astype(jnp.int32)


    work[...] = jnp.zeros_like(work)
    count = plan[share * FIELDS + 1]
    flat_tiles(
        count, runs, plan[share * FIELDS + 3], table, sides, middles, weights,
        lambda k, n: hood[k, pl.ds(base + share + n, 1), :], buffers, tiles, work, None,
    )
    finish_tiles(tiles, count)
    sums_ref[...] = lane_sums([rows_ref[a] + work[a] for a in range(share)], share, width) + sub_sums(cols_ref)

    @pl.when(again)
    def _():
        extra[...] = jnp.zeros_like(extra)
        work[...] = jnp.zeros_like(work)

        def block(a, state):
            count, place_of = inner_range(plan, table, a)

            def inner(t, at):
                n = place_of(t)
                tile = tiles_in[at]
                work[a] = work[a] + tile * factor(times, a, n)
                there = pl.ds(n, 1)
                down = jnp.sum(tile, axis=0, keepdims=True)
                extra[there, :] = extra[there, :] + down * factor(times, n, a)
                return at + 1

            at = lax.fori_loop(0, count, inner, state[0]) + 1
            count, place_far = outer_range(plan, table, a)

            def outer(t, at):
                work[a] = work[a] + tiles[at] * factor(times, a, place_far(t))
                return at + 1

            return at, lax.fori_loop(0, count, outer, state[1])

        lax.fori_loop(0, meta[0], block, (0, 0))
        sums_ref[...] = lane_sums(work, share, width) + extra[...]

    alone = jnp.sum(jnp.where(lane == REACH, often, 0.0), axis=1, keepdims=True)
    alone_ref[...] = jnp.broadcast_to(alone, (share, width))
    pairs = jnp.where(alive, sums_ref[...] + sub_sums(self_ref) * alone, 0.0)
    diagonal = 1.0 / density[...] + pairs
    diagonal_ref[...] = diagonal
    precond_ref[...] = source[...] / diagonal


def apply_inner(meta, table, plan, again, field, alone, times, tiles, rows_ref, cols_ref, spread, near, lone, cols):
    share, width = field.shape
    chunks = pieces_of(width)
    near[0:share, :] = field[...]
    near[share:, :] = jnp.zeros((SUB, width), jnp.float32)
    lone[...] = field[...] * alone[...]
    spread_columns(spread, lambda a: a, field[...])
    cols[...] = jnp.zeros_like(cols)

    def run(weighted):
        def block(a, at):
            count, place_of = inner_range(plan, table, a)

            def fetch(t):
                n = jnp.where(t < count, place_of(t), share)
                return n, wide(near[pl.ds(n, 1), :])

            def pairs(fetched, carry):
                at, sums = carry
                if weighted:
                    fetched = [(n, value * factor(times, a, jnp.minimum(n, share - 1))) for n, value in fetched]
                down = [[None] * 2 for _ in fetched]
                result = []
                for c, (here, total) in enumerate(zip(chunks, sums)):
                    own = spread[a, here, :]
                    found = []
                    for t, (_, value) in enumerate(fetched):
                        tile = tiles[at + t, here, :]
                        gather(down[t], c, tile * own)
                        found.append(tile * value)
                    result.append(total + tree(found))
                for (n, _), partial in zip(fetched, down):
                    there = pl.ds(pl.multiple_of(n * SUB, SUB), SUB)
                    partial = tree(partial)
                    if weighted:
                        partial = partial * factor(times, jnp.minimum(n, share - 1), a)
                    cols[there, :] = cols[there, :] + partial
                return at + len(fetched), result

            zero = jnp.zeros((SUB, width), jnp.float32)
            _, sums = padded_sweep(count, fetch, pairs, (at, [zero] * len(chunks)))
            at = at + count
            value = wide(lone[pl.ds(a, 1), :])
            for here, old in zip(chunks, sums):
                rows_ref[a, here, :] = old + tiles[at, here, :] * value
            return at + 1

        lax.fori_loop(0, meta[0], block, 0)

    either(again[0], run)
    cols_ref[...] = cols[0 : share * SUB, :]


def apply_outer(meta, table, plan, again, received, times, tiles, rows_ref, cols_ref, work, hood):
    *ends, second, first = received
    ends = ends[::-1]
    columns = len(received)
    share, width = first.shape
    chunks = pieces_of(width)
    base, filled = meta[3], meta[4]
    column = lax.div(base, share)
    odd = lax.rem(column, 2) == 1
    before = jnp.where(odd, first[...], second[...])
    after = jnp.where(odd, second[...], first[...])
    own = 3 * share
    for c, end in enumerate(ends, 1):
        hood[pl.ds(own - meta[5] + c * share, share), :] = end[...]
    from_last = own - meta[5] + (columns - 1) * share
    hood[pl.ds(jnp.where(column == 0, from_last, own - share), share), :] = before
    hood[own + share : own + 2 * share, :] = after
    head = after
    for c, end in enumerate(ends, 1):
        head = jnp.where(column == c, end[...], head)
    hood[pl.ds(own + jnp.clip(filled - base, 0, 2 * share), share), :] = head
    nothing = hood.shape[0] - SUB
    hood[nothing:, :] = jnp.zeros((SUB, width), jnp.float32)

    def run(weighted):
        def block(a, at):
            count, place_of = outer_range(plan, table, a)

            def fetch(t):
                place = place_of(t)
                value = hood[pl.ds(jnp.where(t < count, own + place, nothing), 1), :]
                if weighted:
                    value = value * factor(times, a, place)
                return wide(value)

            def pairs(values, carry):
                at, sums = carry
                result = []
                for here, total in zip(chunks, sums):
                    result.append(total + tree([tiles[at + t, here, :] * value for t, value in enumerate(values)]))
                return at + len(values), result

            _, sums = padded_sweep(count, fetch, pairs, (at, [rows_ref[a, here, :] for here in chunks]))
            for here, values in zip(chunks, sums):
                work[a, here, :] = values
            return at + count

        lax.fori_loop(0, meta[0], block, 0)

    either(again[0], run)
    return jnp.where(alive_rows(meta, share, width), lane_sums(work, share, width) + sub_sums(cols_ref), 0.0)


def apply_first(meta, table, plan, again, diagonal, times, *rest):
    *received, tiles, rows_ref, cols_ref, spill_ref, scaled_ref, work, hood = rest
    spill = apply_outer(meta, table, plan, again, received, times, tiles, rows_ref, cols_ref, work, hood)
    spill_ref[...] = spill
    scaled_ref[...] = spill / diagonal[...]


def apply_second(meta, table, plan, again, source, precond, spill, scaled, times, *rest):
    *received, tiles, rows_ref, cols_ref, twice_ref, sums_ref, work, hood = rest
    twice = apply_outer(meta, table, plan, again, received, times, tiles, rows_ref, cols_ref, work, hood)
    twice_ref[...] = twice
    share, width = twice.shape
    lane = lax.broadcasted_iota(jnp.int32, (1, width), 1)
    sums = jnp.zeros((1, width), jnp.float32)
    pairs = ((source[...], precond[...]), (spill[...], precond[...]), (spill[...], scaled[...]), (scaled[...], twice))
    for k, (first, second) in enumerate(pairs):
        along = jnp.sum(first * second, axis=0, keepdims=True)
        sums = jnp.where(lane == k, jnp.sum(along, axis=1, keepdims=True), sums)
    sums_ref[...] = wide(sums)


def finish(source, precond, spill, scaled, twice, *rest):
    *parts, solution_ref, residual_ref = rest
    sums = tree([ref[...] for ref in parts])

    def pick(k):
        return sums[0:1, k : k + 1]

    weighted, cross, square, last = pick(0), pick(1), pick(2), pick(3)
    part = cross / weighted
    advance = 1.0 / (1.0 - part)
    keep = -part * advance
    weighted_next = advance * advance * (square - cross * part)
    bent = keep * keep * cross + 2.0 * keep * advance * square + advance * advance * last
    blend = weighted_next / weighted
    advance_next = weighted_next / (weighted_next - bent - blend * weighted_next / advance)
    residual = keep * source[...] + advance * spill[...]
    next_precond = keep * precond[...] + advance * scaled[...]
    direction = next_precond + blend * precond[...]
    image = residual - keep * spill[...] - advance * twice[...] + blend * (source[...] - spill[...])
    solution_ref[...] = advance * precond[...] + advance_next * direction
    residual_ref[...] = residual - advance_next * image


def held(array):
    return pltpu.with_memory_space_constraint(array, pltpu.VMEM)


def body(positions, phase, neighbours, counts, phase_density, right_side):
    capacity, width = phase.shape
    columns = lax.axis_size("col")
    pieces = lax.axis_size("piece")
    share = capacity // columns
    f32 = jnp.float32
    vector = jax.ShapeDtypeStruct((share, width), f32)
    few = jax.ShapeDtypeStruct((SUB, width), f32)
    message = jax.ShapeDtypeStruct((4, share, width), f32)
    most_inner, most_outer = tile_bounds(share)
    inner_tiles = pltpu.VMEM((most_inner + 2 * GROUP, width, width), f32)
    outer_tiles = pltpu.VMEM((most_outer + 2 * GROUP, width, width), f32)
    ahead = pltpu.VMEM((GROUP, width, width), f32)
    square_more = pltpu.VMEM((share + 1, width, width), f32)
    square = pltpu.VMEM((share, width, width), f32)
    narrow = pltpu.VMEM((share * SUB, width), f32)
    table = jnp.asarray(FLAT)

    def call(kernel, args, outs, scratch=(), work=0, scalars=2, far=0, **more):
        return pl.pallas_call(
            kernel,
            out_shape=outs,
            in_specs=[SMEM] * scalars + [HBM] * far + [VMEM] * (len(args) - scalars - far),
            out_specs=[SMEM if getattr(o, "memory_space", None) == pltpu.SMEM else VMEM for o in outs],
            scratch_shapes=scratch,
            compiler_params=LIMIT,
            cost_estimate=pl.CostEstimate(flops=work * width * width, bytes_accessed=0, transcendentals=0),
            name=kernel.__name__,
            **more,
        )(*args)

    def swap(values, axis, step):
        return lax.ppermute(values, axis, [(i, i ^ step) for i in range(lax.axis_size(axis))])

    col_steps = [(1 << k) | 1 for k in range(columns.bit_length() - 1)]
    lists = [neighbours.T]
    for step in col_steps:
        known = lists[0] if len(lists) == 1 else jnp.concatenate(lists, 0)
        lists = [known, swap(known, "col", step)]

    def away(array):
        return pltpu.with_memory_space_constraint(array, pltpu.HBM)

    around = jax.ShapeDtypeStruct((4, capacity + 2 * share, width), f32)
    near = jax.ShapeDtypeStruct((4, 2 * share, width), f32)
    far = [away(array) for array in (positions, phase, right_side, table)]
    meta, table, around, near, density, source, first, second = call(
        prepare,
        (away(counts), away(phase_density), *far),
        [pltpu.SMEM((8,), jnp.int32), pltpu.SMEM(table.shape, jnp.int32), around, near, vector, vector, message, message],
        [pltpu.VMEM(phase.shape, jnp.int32), pltpu.VMEM((share, width), f32), pltpu.SemaphoreType.DMA((4,))],
        far=len(far),
    )
    meta, table = (pltpu.with_memory_space_constraint(array, pltpu.SMEM) for array in (meta, table))
    first = lax.ppermute(first, "piece", [(i, i ^ 1) for i in range(pieces)])
    axes = ("piece", "col")
    device = [(p, c) for p in range(pieces) for c in range(columns)]
    partner = [(p + (1 if p % 2 else -1), c) for p, c in device]
    partner = [(q, d) if 0 <= q < pieces else (p, c ^ 1) for (q, d), (p, c) in zip(partner, device)]
    second = lax.ppermute(second, axes, [(i, q * columns + d) for i, (q, d) in enumerate(partner)])

    plan, runs, tiles_in, sides, middles, weights, rows, cols, selfs = call(
        build_inner,
        (meta, table, near),
        [pltpu.SMEM((share * FIELDS + 4,), jnp.int32), pltpu.SMEM((6 * share + 3,), jnp.int32), inner_tiles,
         pltpu.VMEM((2, share, width, width), jnp.bfloat16), pltpu.VMEM((3, share, width), f32), square, square, narrow, narrow],
        [pltpu.SMEM((3 * share + 3,), jnp.int32), square_more, pltpu.VMEM(((share + 1) * SUB, width), f32), ahead, ahead],
        16 * most_inner,
    )
    plan, runs = (pltpu.with_memory_space_constraint(array, pltpu.SMEM) for array in (plan, runs))
    again, tiles_out, diagonal, precond, times, alone = call(
        build_outer,
        (meta, table, plan, runs, around, first, second, density, source,
         held(tiles_in), held(sides), held(middles), held(weights), held(rows), held(cols), held(selfs), *lists),
        [pltpu.SMEM((1,), jnp.int32), outer_tiles, vector, vector, vector, vector],
        [pltpu.VMEM((4, capacity + 2 * share, width), f32), square_more]
        + [pltpu.VMEM((share, width), f32)] * 2 + [pltpu.VMEM((capacity, width), f32), ahead, ahead],
        16 * most_outer,
        scalars=4,
    )
    again = pltpu.with_memory_space_constraint(again, pltpu.SMEM)

    def inner(field):
        return call(
            apply_inner,
            (meta, table, plan, again, field, alone, times, held(tiles_in)),
            [square, narrow],
            [pltpu.VMEM((share, width, width), f32), pltpu.VMEM((share + SUB, width), f32), pltpu.VMEM((share, width), f32),
             pltpu.VMEM(((share + 1) * SUB, width), f32)],
            4 * most_inner,
            scalars=4,
        )

    def exchange(field):
        count = pieces * columns
        swaps = [[i ^ 1 for i in range(count)], [i - 1 if i % 2 == 0 else i + 1 for i in range(count)]]
        swaps[1][0], swaps[1][-1] = count - 1, 0
        for c in range(1, columns - 1):
            to = {}
            for p in range(pieces - 1):
                low, high = p * columns + c, (p + 1) * columns
                to[low], to[high] = high, low
            for p in range(pieces):
                rest = [i for i in range(p * columns, (p + 1) * columns) if i not in to]
                to.update(zip(rest, rest[1:] + rest[:1]))
            swaps.append([to[i] for i in range(count)])
        return [lax.ppermute(field, axes, list(enumerate(to))) for to in swaps[::-1]]

    scratch = [pltpu.VMEM((share, width, width), f32), pltpu.VMEM((8 * share, width), f32)]

    received = exchange(precond)
    rows, cols = inner(precond)
    spill, scaled = call(
        apply_first,
        (meta, table, plan, again, diagonal, times, *received, held(tiles_out), held(rows), held(cols)),
        [vector, vector],
        scratch,
        2 * most_outer,
        scalars=4,
    )

    received = exchange(scaled)
    rows, cols = inner(scaled)
    twice, sums = call(
        apply_second,
        (meta, table, plan, again, source, precond, spill, scaled, times, *received, held(tiles_out), held(rows), held(cols)),
        [vector, few],
        scratch,
        2 * most_outer,
        scalars=4,
    )

    def together(values, axis, low, size):
        return tree([values] + [swap(values, axis, low * k) for k in range(size - 1, 0, -1)][::-1])

    sums = together(sums, "piece", 1, 2)
    sums = together(sums, "col", 1, columns)
    step = 2
    while pieces // step > 4:
        sums = together(sums, "piece", step, 4)
        step *= 4
    others = [swap(sums, "piece", step * k) for k in range(pieces // step - 1, 0, -1)][::-1]

    return tuple(call(
        finish,
        (source, precond, spill, scaled, twice, sums, *others),
        [vector, vector],
        scalars=0,
    ))


def solution(mesh):
    placed = (
        P(None, "piece", None),
        P("piece", None),
        P("piece", "col"),
        P(),
        P(),
        P(("piece", "col"), None),
    )
    return jax.shard_map(
        body,
        mesh=mesh,
        in_specs=placed,
        out_specs=(P(("piece", "col"), None), P(("piece", "col"), None)),
        check_vma=False,
    )
```

```python
import jax
import jax.numpy as jnp
import numpy as np
from jax import lax
from jax.experimental import pallas as pl
from jax.experimental.pallas import tpu as pltpu
from jax.sharding import PartitionSpec as P

ITERS = 2
SIDE = 4
LAYER = SIDE * SIDE
REACH = 2 * LAYER
SUB = 8
VMEM = pl.BlockSpec(memory_space=pltpu.VMEM)
SMEM = pl.BlockSpec(memory_space=pltpu.SMEM)
HBM = pl.BlockSpec(memory_space=pltpu.HBM)


def stencil_tables():
    levels = SIDE.bit_length() - 1

    def cell(code):
        across = sum((code >> (2 * level) & 1) << level for level in range(levels))
        along = sum((code >> (2 * level + 1) & 1) << level for level in range(levels))
        return across, along

    place = {cell(code): code for code in range(LAYER)}
    rows = []
    for code in range(LAYER):
        across, along = cell(code)
        rows.append(
            sorted(
                step_z * LAYER + place[across + step_x, along + step_y] - code
                for step_z in (-1, 0, 1)
                for step_y in (-1, 0, 1)
                for step_x in (-1, 0, 1)
                if (across + step_x, along + step_y) in place
            )
        )
    longest = max(len(row) for row in rows)
    offsets = np.zeros((LAYER, longest), np.int32)
    below = np.zeros((LAYER, 2 * REACH + 1), np.int32)
    for code, row in enumerate(rows):
        offsets[code, : len(row)] = row
        for t in range(-REACH, REACH + 1):
            below[code, t + REACH] = sum(offset < t for offset in row)
    return offsets, below


OFFSETS, BELOW = stencil_tables()
WIDEST = OFFSETS.shape[1]
TABLE = np.concatenate([OFFSETS, BELOW], 1)
STRIDE = TABLE.shape[1]
FLAT = np.concatenate([TABLE.reshape(-1), np.zeros(8, np.int32)])
LIMIT = pltpu.CompilerParams(vmem_limit_bytes=8 * 1024 * 1024)


def tile_bounds(share):
    inner = outer = 0
    for first in range(LAYER):
        for live in range(1, share + 1):
            near = far = 0
            for a in range(live):
                code = (first + a) % LAYER
                row = [int(o) for o in OFFSETS[code][: BELOW[code, -1]]]
                near += sum(0 <= a + o and o <= 0 for o in row)
                far += sum(a + o < 0 or a + o >= live for o in row)
            inner, outer = max(inner, near), max(outer, far)
    return inner, outer


def rank(table, code, t):
    return table[code * STRIDE + jnp.clip(t, -REACH, REACH) + REACH + WIDEST]


FIELDS = 6


def write_plan(meta, table, plan, a):
    code = lax.bitwise_and(meta[1] + a, LAYER - 1)
    place = meta[1] + a
    low, split, middle = rank(table, code, -place), rank(table, code, -a), rank(table, code, 0)
    resume, high = rank(table, code, meta[0] - a), rank(table, code, meta[2] - place)
    row = code * STRIDE
    ahead = split - low
    plan[a * FIELDS] = middle - split
    plan[a * FIELDS + 1] = row + split
    plan[a * FIELDS + 2] = ahead + jnp.maximum(high - resume, 0)
    plan[a * FIELDS + 3] = ahead
    plan[a * FIELDS + 4] = row + low
    plan[a * FIELDS + 5] = row + resume - ahead


def write_run(runs, at, a, start, count):
    runs[3 * at], runs[3 * at + 1], runs[3 * at + 2] = a, start, count
    return at + (count > 0).astype(jnp.int32)


def write_runs(meta, table, plan, inner_runs, outer_runs, share):
    inner = outer = total = far = jnp.int32(0)
    for a in range(share):
        write_plan(meta, table, plan, a)
        alive = a < meta[0]
        count, start, count_far, ahead, start_far, start_after = (plan[a * FIELDS + k] for k in range(FIELDS))
        inner = write_run(inner_runs, inner, a, start, jnp.where(alive, count + 1, 0))
        outer = write_run(outer_runs, outer, a, start_far, jnp.where(alive, ahead, 0))
        outer = write_run(outer_runs, outer, a, start_after + ahead, jnp.where(alive, count_far - ahead, 0))
        total = total + jnp.where(alive, count + 1, 0)
        far = far + jnp.where(alive, count_far, 0)
    for runs, at in ((inner_runs, inner), (outer_runs, outer)):
        write_run(runs, at, share, len(FLAT) - 8, jnp.int32(1))
    plan[share * FIELDS] = total
    plan[share * FIELDS + 1] = far
    plan[share * FIELDS + 2] = inner
    plan[share * FIELDS + 3] = outer


def inner_range(plan, table, a):
    start = plan[a * FIELDS + 1]
    return plan[a * FIELDS], lambda t: a + table[start + t]


def outer_range(plan, table, a):
    ahead, start, start_after = (plan[a * FIELDS + k] for k in (3, 4, 5))
    return plan[a * FIELDS + 2], lambda t: a + table[t + jnp.where(t < ahead, start, start_after)]


TURN = 3


def padded_sweep(count, fetch, step, carry):
    def turn(i, state):
        carry, *now = state
        later = [fetch(TURN * (i + 1) + k) for k in range(TURN)]
        return step(now, carry), *later

    state = (carry, *(fetch(k) for k in range(TURN)))
    return lax.fori_loop(0, lax.div(count + (TURN - 1), TURN), turn, state)[0]


def tree(terms):
    while len(terms) > 1:
        terms = [a + b for a, b in zip(terms[::2], terms[1::2])] + terms[len(terms) // 2 * 2 :]
    return terms[0]


def gather(partial, c, term):
    if c < len(partial):
        partial[c] = term
    else:
        partial[c % len(partial)] = partial[c % len(partial)] + term


def pieces_of(width):
    return [slice(c * SUB, (c + 1) * SUB) for c in range(width // SUB)]


def wide(row):
    return jnp.broadcast_to(row, (SUB, row.shape[1]))


def three_parts(values):
    high = values.astype(jnp.bfloat16).astype(jnp.float32)
    rest = values - high
    middle = rest.astype(jnp.bfloat16).astype(jnp.float32)
    return high, middle, rest - middle


def stacked(rows):
    sublane = lax.broadcasted_iota(jnp.int32, rows[0].shape, 0)
    result = jnp.zeros(rows[0].shape, jnp.float32)
    for k, row in enumerate(rows):
        result = jnp.where(sublane == k, row, result)
    return result


def half_size(x):
    return 0.5 - (x[0] * x[0] + x[1] * x[1] + x[2] * x[2])


def own_side(x, which):
    nothing = [jnp.zeros_like(x[0])] * 4
    rows = [2.0 * x[0], 2.0 * x[1], 2.0 * x[2], jnp.ones_like(x[0])]
    high, middle, low = three_parts(stacked(nothing + rows if which else rows))
    sizes = stacked(list(three_parts(half_size(x))))
    width = sizes.shape[1]
    rest = jnp.zeros((width - 7 * SUB, width), jnp.float32)
    return jnp.concatenate([high, high, middle, middle, high, low, sizes, rest], 0)


def other_sides(first, second):
    rows = [*first, half_size(first), *second, half_size(second)]
    high, middle, low = three_parts(stacked(rows))
    width = high.shape[1]
    ones = jnp.where(lax.broadcasted_iota(jnp.int32, (2 * SUB, width), 0) < 3, 1.0, 0.0).astype(jnp.bfloat16)
    front = jnp.concatenate([high, middle], 0).astype(jnp.bfloat16)
    back = jnp.concatenate([low, high], 0).astype(jnp.bfloat16)
    rest = jnp.zeros((width - 8 * SUB, width), jnp.bfloat16)
    return jnp.concatenate([front, front, back, ones, rest], 0)


GROUP = 4


def flat_tiles(count, runs, most, table, sides, middles, weights, other_at, buffers, tiles, rows_ref, cols_ref):
    share, width = rows_ref.shape[0] - 1, rows_ref.shape[2]
    chunks = pieces_of(width)

    def steps(state):
        found = []
        for _ in range(GROUP):
            run, t = state
            a, start, size = (runs[3 * run + k] for k in range(3))
            found.append((a, a + table[start + t]))
            over = t + 1 >= size
            state = jnp.minimum(run + over.astype(jnp.int32), most), jnp.where(over, 0, t + 1)
        return state, found

    def other_of(a, n):
        here = pl.ds(a, 1)
        return [wide(other_at(c, n)) - wide(middles[c, here, :]) for c in range(3)]

    def products(found, ahead):
        for k in range(0, GROUP, 2):
            (a, n), (b, m) = ((jnp.minimum(a, share - 1), n) for a, n in found[k : k + 2])
            own = jnp.concatenate([sides[0, a], sides[1, b]], 0)
            both = jnp.dot(own, other_sides(other_of(a, n), other_of(b, m)), preferred_element_type=jnp.float32)
            ahead[k] = both[:width]
            ahead[k + 1] = both[width:]

    def weigh(at, found, ahead):
        for k, (a, n) in enumerate(found):
            alone = a == n
            row = jnp.where(alone, share, a)
            own = jnp.minimum(a, share - 1)
            other = wide(other_at(3, n))
            down = [None] * 2
            for c, here in enumerate(chunks):
                left = ahead[k, here, :]
                rest = jnp.maximum(left, 0.0)
                inverse = pltpu.reciprocal((1.01 - left) * (weights[own, here, :] + other), approx=True)
                tile = rest * rest * inverse
                tiles[at + k, here, :] = tile
                rows_ref[row, here, :] = rows_ref[row, here, :] + tile
                if cols_ref is not None:
                    gather(down, c, tile)
            if cols_ref is not None:
                there = pl.ds(pl.multiple_of(jnp.where(alone, share, n) * SUB, SUB), SUB)
                cols_ref[there, :] = cols_ref[there, :] + tree(down)

    def turn(i, carry):
        state, found = carry
        at = i * (2 * GROUP)
        state, later = steps(state)
        products(later, buffers[1])
        weigh(at, found, buffers[0])
        state, last = steps(state)
        products(last, buffers[0])
        weigh(at + GROUP, later, buffers[1])
        return state, last

    state, found = steps((jnp.int32(0), jnp.int32(0)))
    products(found, buffers[0])
    lax.fori_loop(0, lax.div(count + (2 * GROUP - 1), 2 * GROUP), turn, (state, found))


def spread_columns(out, index, rows):
    count, width = rows.shape
    turned = rows.T
    for a in range(count):
        out[index(a)] = jnp.broadcast_to(turned[:, a : a + 1], (width, width))


def lane_sums(parts, count, width):
    lanes = lax.broadcasted_iota(jnp.int32, (width, width), 1)
    turned = jnp.zeros((width, width), jnp.float32)
    for a in range(count):
        turned = jnp.where(lanes == a, jnp.sum(parts[a], axis=1, keepdims=True), turned)
    return turned.T[:count]


def sub_sums(cols):
    return jnp.sum(cols[...].reshape(-1, SUB, cols.shape[1]), axis=1)


def alive_rows(meta, share, width):
    return lax.broadcasted_iota(jnp.int32, (share, width), 0) < meta[0]


def prepare(
    counts, densities, position_in, phase_in, right_side_in, table_in, lists_in,
    meta, table, hood, near, density, source, first_swap, second_swap, lists, phase, right_side, sems
):
    share, width = source.shape
    capacity = phase.shape[0]
    body_rows = pl.ds(share, capacity)
    copies = [
        pltpu.make_async_copy(phase_in, phase, sems.at[0]),
        pltpu.make_async_copy(position_in, hood.at[pl.ds(0, 3), body_rows, :], sems.at[1]),
        pltpu.make_async_copy(right_side_in, right_side, sems.at[2]),
        pltpu.make_async_copy(table_in, table, sems.at[3]),
        pltpu.make_async_copy(lists_in, lists, sems.at[4]),
    ]
    for copy in copies:
        copy.start()
    piece, column = lax.axis_index("piece"), lax.axis_index("col")
    filled = counts[piece]
    filled_before = counts[jnp.maximum(piece - 1, 0)]
    before = jnp.int32(0)
    total = jnp.int32(0)
    for p in range(counts.shape[0]):
        before = before + jnp.where(p < piece, counts[p], 0)
        total = total + counts[p]
    meta[0] = jnp.clip(filled - column * share, 0, share)
    meta[1] = before + column * share
    meta[2] = total
    meta[3] = column * share
    meta[4] = filled
    meta[5] = filled_before
    own_rows = pl.ds(pl.multiple_of(share + column * share, SUB), share)
    copies[0].wait()
    labels = phase[...]
    whole = sum(jnp.where(labels == k, densities[k], 0.0) for k in range(densities.shape[0]))
    hood[3, body_rows, :] = whole * (width / 2.0)
    density[...] = hood[3, own_rows, :] * (2.0 / width)
    copies[1].wait()
    even = lax.rem(piece, 2) == 0
    for k in range(4):
        tail, head = hood[k, pl.ds(filled, share), :], hood[k, share : 2 * share, :]
        first_swap[k] = jnp.where(even, tail, head)
        second_swap[k] = jnp.where(even, head, tail)
        near[k, 0:share, :] = hood[k, own_rows, :]
    for copy in copies[2:]:
        copy.wait()
    source[...] = jnp.where(alive_rows(meta, share, width), right_side[...], 0.0)


def finish_tiles(tiles, end):
    for t in range(TURN):
        tiles[end + t] = jnp.zeros(tiles.shape[1:], jnp.float32)


def build_inner(
    meta, table, near, plan, outer_runs, tiles, sides, middles, weights, rows_out, cols_out, self_ref,
    inner_runs, rows_ref, cols_ref, *buffers,
):
    share, width = rows_out.shape[0], rows_out.shape[2]
    chunks = pieces_of(width)
    write_runs(meta, table, plan, inner_runs, outer_runs, share)
    for k in range(3):
        first = near[k, 0:share, 0:1]
        middles[k] = jnp.broadcast_to(jnp.floor(first) + 0.5, (share, width))
    for a in range(share):
        here = slice(a, a + 1)
        centred = [wide(near[k, here, :] - middles[k, here, :]) for k in range(3)]
        for which in range(2):
            sides[which, a] = own_side(centred, which).T.astype(jnp.bfloat16)
    spread_columns(weights, lambda a: a, near[3, 0:share, :])
    cols_ref[...] = jnp.zeros_like(cols_ref)
    rows_ref[...] = jnp.zeros_like(rows_ref)
    count = plan[share * FIELDS]
    flat_tiles(
        count, inner_runs, plan[share * FIELDS + 2], table, sides, middles, weights,
        lambda k, n: near[k, pl.ds(n, 1), :], buffers, tiles, rows_ref, cols_ref,
    )
    finish_tiles(tiles, count)
    lane = lax.broadcasted_iota(jnp.int32, (SUB, width), 1)
    sublane = lax.broadcasted_iota(jnp.int32, (SUB, width), 0)

    def block(a, at):
        at = at + plan[a * FIELDS]
        down = [None] * 4
        for c, here in enumerate(chunks):
            tile = jnp.where(lane == sublane + c * SUB, 0.0, tiles[at, here, :])
            tiles[at, here, :] = tile
            gather(down, c, tile)
        self_ref[pl.ds(pl.multiple_of(a * SUB, SUB), SUB), :] = tree(down)
        return at + 1

    lax.fori_loop(0, meta[0], block, 0)
    rows_out[...] = rows_ref[0:share]
    cols_out[...] = cols_ref[0 : share * SUB, :]


def count_listed(meta, lists, width):
    capacity = lists[0].shape[1]
    filled, filled_before = meta[4], meta[5]
    start = lax.axis_index("piece") * capacity
    steps = lax.broadcasted_iota(jnp.int32, (2 * REACH, capacity), 0)
    partial = [None] * 4
    row = 0
    for ref in lists:
        ids = ref[...]
        slot = ids - start
        gap = jnp.where(slot < 0, capacity - filled_before, jnp.where(slot >= capacity, filled - capacity, 0))
        away = slot - lax.broadcasted_iota(jnp.int32, ids.shape, 1) + gap
        away = jnp.where(ids < 0, -REACH, away) + REACH
        for k in range(ids.shape[0]):
            gather(partial, row, jnp.where(steps == away[k : k + 1], 1.0, 0.0))
            row += 1
    return jnp.concatenate([tree(partial), jnp.zeros((width - 2 * REACH, capacity), jnp.float32)], 0).T


def factor(times, a, n):
    lane = lax.broadcasted_iota(jnp.int32, (1, times.shape[1]), 1)
    return jnp.sum(jnp.where(lane == n - a + REACH, times[pl.ds(a, 1), :], 0.0), axis=1, keepdims=True)


def either(flag, run):
    @pl.when(flag == 0)
    def _():
        run(False)

    @pl.when(flag != 0)
    def _():
        run(True)


TAIL = 13


def build_outer(
    meta, table, plan, runs, around, first, second, density, source, tiles_in, sides, middles, weights,
    rows_ref, cols_ref, self_ref, *rest
):
    lists, rest = rest[:-TAIL], rest[-TAIL:]
    again_ref, tiles, diagonal_ref, precond_ref, times, alone_ref, hood, work, sums_ref, extra, all_times, *buffers = rest
    share, width = diagonal_ref.shape
    base, filled = meta[3], meta[4]
    even = lax.rem(lax.axis_index("piece"), 2) == 0
    for k in range(4):
        hood[k, 0:share, :] = jnp.where(even, second[k], first[k])
        hood[k, share:, :] = around[k, share:, :]
        hood[k, pl.ds(share + filled, share), :] = jnp.where(even, first[k], second[k])
    alive = alive_rows(meta, share, width)
    all_times[...] = count_listed(meta, lists, width)
    often = jnp.where(alive, all_times[pl.ds(pl.multiple_of(base, SUB), share), :], 0.0)
    times[...] = often
    lane = lax.broadcasted_iota(jnp.int32, (share, width), 1)
    again = jnp.max(jnp.where((lane == REACH) | (lane == 0), 0.0, often)) > 1.5
    again_ref[0] = again.astype(jnp.int32)


    work[...] = jnp.zeros_like(work)
    count = plan[share * FIELDS + 1]
    flat_tiles(
        count, runs, plan[share * FIELDS + 3], table, sides, middles, weights,
        lambda k, n: hood[k, pl.ds(base + share + n, 1), :], buffers, tiles, work, None,
    )
    finish_tiles(tiles, count)
    sums_ref[...] = lane_sums([rows_ref[a] + work[a] for a in range(share)], share, width) + sub_sums(cols_ref)

    @pl.when(again)
    def _():
        extra[...] = jnp.zeros_like(extra)
        work[...] = jnp.zeros_like(work)

        def block(a, state):
            count, place_of = inner_range(plan, table, a)

            def inner(t, at):
                n = place_of(t)
                tile = tiles_in[at]
                work[a] = work[a] + tile * factor(times, a, n)
                there = pl.ds(n, 1)
                down = jnp.sum(tile, axis=0, keepdims=True)
                extra[there, :] = extra[there, :] + down * factor(times, n, a)
                return at + 1

            at = lax.fori_loop(0, count, inner, state[0]) + 1
            count, place_far = outer_range(plan, table, a)

            def outer(t, at):
                work[a] = work[a] + tiles[at] * factor(times, a, place_far(t))
                return at + 1

            return at, lax.fori_loop(0, count, outer, state[1])

        lax.fori_loop(0, meta[0], block, (0, 0))
        sums_ref[...] = lane_sums(work, share, width) + extra[...]

    alone = jnp.sum(jnp.where(lane == REACH, often, 0.0), axis=1, keepdims=True)
    alone_ref[...] = jnp.broadcast_to(alone, (share, width))
    pairs = jnp.where(alive, sums_ref[...] + sub_sums(self_ref) * alone, 0.0)
    diagonal = 1.0 / density[...] + pairs
    diagonal_ref[...] = diagonal
    precond_ref[...] = source[...] / diagonal


def apply_inner(meta, table, plan, again, field, alone, times, tiles, rows_ref, cols_ref, spread, near, lone, cols):
    share, width = field.shape
    chunks = pieces_of(width)
    near[0:share, :] = field[...]
    near[share:, :] = jnp.zeros((SUB, width), jnp.float32)
    lone[...] = field[...] * alone[...]
    spread_columns(spread, lambda a: a, field[...])
    cols[...] = jnp.zeros_like(cols)

    def run(weighted):
        def block(a, at):
            count, place_of = inner_range(plan, table, a)

            def fetch(t):
                n = jnp.where(t < count, place_of(t), share)
                return n, wide(near[pl.ds(n, 1), :])

            def pairs(fetched, carry):
                at, sums = carry
                if weighted:
                    fetched = [(n, value * factor(times, a, jnp.minimum(n, share - 1))) for n, value in fetched]
                down = [[None] * 2 for _ in fetched]
                result = []
                for c, (here, total) in enumerate(zip(chunks, sums)):
                    own = spread[a, here, :]
                    found = []
                    for t, (_, value) in enumerate(fetched):
                        tile = tiles[at + t, here, :]
                        gather(down[t], c, tile * own)
                        found.append(tile * value)
                    result.append(total + tree(found))
                for (n, _), partial in zip(fetched, down):
                    there = pl.ds(pl.multiple_of(n * SUB, SUB), SUB)
                    partial = tree(partial)
                    if weighted:
                        partial = partial * factor(times, jnp.minimum(n, share - 1), a)
                    cols[there, :] = cols[there, :] + partial
                return at + len(fetched), result

            zero = jnp.zeros((SUB, width), jnp.float32)
            _, sums = padded_sweep(count, fetch, pairs, (at, [zero] * len(chunks)))
            at = at + count
            value = wide(lone[pl.ds(a, 1), :])
            for here, old in zip(chunks, sums):
                rows_ref[a, here, :] = old + tiles[at, here, :] * value
            return at + 1

        lax.fori_loop(0, meta[0], block, 0)

    either(again[0], run)
    cols_ref[...] = cols[0 : share * SUB, :]


def apply_outer(meta, table, plan, again, received, times, tiles, rows_ref, cols_ref, work, hood):
    first, second, *ends = received
    columns = len(received)
    share, width = first.shape
    chunks = pieces_of(width)
    base, filled = meta[3], meta[4]
    column = lax.div(base, share)
    odd = lax.rem(column, 2) == 1
    before = jnp.where(odd, first[...], second[...])
    after = jnp.where(odd, second[...], first[...])
    own = 3 * share
    for c, end in enumerate(ends, 1):
        hood[pl.ds(own - meta[5] + c * share, share), :] = end[...]
    from_last = own - meta[5] + (columns - 1) * share
    hood[pl.ds(jnp.where(column == 0, from_last, own - share), share), :] = before
    hood[own + share : own + 2 * share, :] = after
    head = after
    for c, end in enumerate(ends, 1):
        head = jnp.where(column == c, end[...], head)
    hood[pl.ds(own + jnp.clip(filled - base, 0, 2 * share), share), :] = head
    nothing = hood.shape[0] - SUB
    hood[nothing:, :] = jnp.zeros((SUB, width), jnp.float32)

    def run(weighted):
        def block(a, at):
            count, place_of = outer_range(plan, table, a)

            def fetch(t):
                place = place_of(t)
                value = hood[pl.ds(jnp.where(t < count, own + place, nothing), 1), :]
                if weighted:
                    value = value * factor(times, a, place)
                return wide(value)

            def pairs(values, carry):
                at, sums = carry
                result = []
                for here, total in zip(chunks, sums):
                    result.append(total + tree([tiles[at + t, here, :] * value for t, value in enumerate(values)]))
                return at + len(values), result

            _, sums = padded_sweep(count, fetch, pairs, (at, [rows_ref[a, here, :] for here in chunks]))
            for here, values in zip(chunks, sums):
                work[a, here, :] = values
            return at + count

        lax.fori_loop(0, meta[0], block, 0)

    either(again[0], run)
    return jnp.where(alive_rows(meta, share, width), lane_sums(work, share, width) + sub_sums(cols_ref), 0.0)


def apply_first(meta, table, plan, again, diagonal, times, *rest):
    *received, tiles, rows_ref, cols_ref, spill_ref, scaled_ref, work, hood = rest
    spill = apply_outer(meta, table, plan, again, received, times, tiles, rows_ref, cols_ref, work, hood)
    spill_ref[...] = spill
    scaled_ref[...] = spill / diagonal[...]


def apply_second(meta, table, plan, again, source, precond, spill, scaled, times, *rest):
    *received, tiles, rows_ref, cols_ref, twice_ref, sums_ref, work, hood = rest
    twice = apply_outer(meta, table, plan, again, received, times, tiles, rows_ref, cols_ref, work, hood)
    twice_ref[...] = twice
    share, width = twice.shape
    lane = lax.broadcasted_iota(jnp.int32, (1, width), 1)
    sums = jnp.zeros((1, width), jnp.float32)
    pairs = ((source[...], precond[...]), (spill[...], precond[...]), (spill[...], scaled[...]), (scaled[...], twice))
    for k, (first, second) in enumerate(pairs):
        along = jnp.sum(first * second, axis=0, keepdims=True)
        sums = jnp.where(lane == k, jnp.sum(along, axis=1, keepdims=True), sums)
    sums_ref[...] = wide(sums)


def finish(source, precond, spill, scaled, twice, *rest):
    *parts, solution_ref, residual_ref = rest
    sums = tree([ref[...] for ref in parts])

    def pick(k):
        return sums[0:1, k : k + 1]

    weighted, cross, square, last = pick(0), pick(1), pick(2), pick(3)
    part = cross / weighted
    advance = 1.0 / (1.0 - part)
    keep = -part * advance
    weighted_next = advance * advance * (square - cross * part)
    bent = keep * keep * cross + 2.0 * keep * advance * square + advance * advance * last
    blend = weighted_next / weighted
    advance_next = weighted_next / (weighted_next - bent - blend * weighted_next / advance)
    residual = keep * source[...] + advance * spill[...]
    next_precond = keep * precond[...] + advance * scaled[...]
    direction = next_precond + blend * precond[...]
    image = residual - keep * spill[...] - advance * twice[...] + blend * (source[...] - spill[...])
    solution_ref[...] = advance * precond[...] + advance_next * direction
    residual_ref[...] = residual - advance_next * image


def held(array):
    return pltpu.with_memory_space_constraint(array, pltpu.VMEM)


def body(positions, phase, neighbours, counts, phase_density, right_side):
    capacity, width = phase.shape
    columns = lax.axis_size("col")
    pieces = lax.axis_size("piece")
    share = capacity // columns
    f32 = jnp.float32
    vector = jax.ShapeDtypeStruct((share, width), f32)
    few = jax.ShapeDtypeStruct((SUB, width), f32)
    message = jax.ShapeDtypeStruct((4, share, width), f32)
    most_inner, most_outer = tile_bounds(share)
    inner_tiles = pltpu.VMEM((most_inner + 2 * GROUP, width, width), f32)
    outer_tiles = pltpu.VMEM((most_outer + 2 * GROUP, width, width), f32)
    ahead = pltpu.VMEM((GROUP, width, width), f32)
    square_more = pltpu.VMEM((share + 1, width, width), f32)
    square = pltpu.VMEM((share, width, width), f32)
    narrow = pltpu.VMEM((share * SUB, width), f32)
    table = jnp.asarray(FLAT)

    def call(kernel, args, outs, scratch=(), work=0, scalars=2, far=0, **more):
        return pl.pallas_call(
            kernel,
            out_shape=outs,
            in_specs=[SMEM] * scalars + [HBM] * far + [VMEM] * (len(args) - scalars - far),
            out_specs=[SMEM if getattr(o, "memory_space", None) == pltpu.SMEM else VMEM for o in outs],
            scratch_shapes=scratch,
            compiler_params=LIMIT,
            cost_estimate=pl.CostEstimate(flops=work * width * width, bytes_accessed=0, transcendentals=0),
            name=kernel.__name__,
            **more,
        )(*args)

    def swap(values, axis, step):
        return lax.ppermute(values, axis, [(i, i ^ step) for i in range(lax.axis_size(axis))])

    def away(array):
        return pltpu.with_memory_space_constraint(array, pltpu.HBM)

    around = jax.ShapeDtypeStruct((4, capacity + 2 * share, width), f32)
    near = jax.ShapeDtypeStruct((4, 2 * share, width), f32)
    far = [away(array) for array in (positions, phase, right_side, table, neighbours.T)]
    meta, table, around, near, density, source, first, second, own_lists = call(
        prepare,
        (away(counts), away(phase_density), *far),
        [pltpu.SMEM((8,), jnp.int32), pltpu.SMEM(table.shape, jnp.int32), around, near, vector, vector, message, message,
         jax.ShapeDtypeStruct(far[-1].shape, jnp.int32)],
        [pltpu.VMEM(phase.shape, jnp.int32), pltpu.VMEM((share, width), f32), pltpu.SemaphoreType.DMA((5,))],
        far=len(far),
    )
    meta, table = (pltpu.with_memory_space_constraint(array, pltpu.SMEM) for array in (meta, table))
    first = lax.ppermute(first, "piece", [(i, i ^ 1) for i in range(pieces)])
    axes = ("piece", "col")
    device = [(p, c) for p in range(pieces) for c in range(columns)]
    partner = [(p + (1 if p % 2 else -1), c) for p, c in device]
    partner = [(q, d) if 0 <= q < pieces else (p, c ^ 1) for (q, d), (p, c) in zip(partner, device)]
    second = lax.ppermute(second, axes, [(i, q * columns + d) for i, (q, d) in enumerate(partner)])

    col_steps = [(1 << k) | 1 for k in range(columns.bit_length() - 1)]
    lists = [own_lists]
    for step in col_steps:
        known = lists[0] if len(lists) == 1 else jnp.concatenate(lists, 0)
        lists = [known, swap(known, "col", step)]

    plan, runs, tiles_in, sides, middles, weights, rows, cols, selfs = call(
        build_inner,
        (meta, table, near),
        [pltpu.SMEM((share * FIELDS + 4,), jnp.int32), pltpu.SMEM((6 * share + 3,), jnp.int32), inner_tiles,
         pltpu.VMEM((2, share, width, width), jnp.bfloat16), pltpu.VMEM((3, share, width), f32), square, square, narrow, narrow],
        [pltpu.SMEM((3 * share + 3,), jnp.int32), square_more, pltpu.VMEM(((share + 1) * SUB, width), f32), ahead, ahead],
        16 * most_inner,
    )
    plan, runs = (pltpu.with_memory_space_constraint(array, pltpu.SMEM) for array in (plan, runs))
    again, tiles_out, diagonal, precond, times, alone = call(
        build_outer,
        (meta, table, plan, runs, around, first, second, density, source,
         held(tiles_in), held(sides), held(middles), held(weights), held(rows), held(cols), held(selfs), *lists),
        [pltpu.SMEM((1,), jnp.int32), outer_tiles, vector, vector, vector, vector],
        [pltpu.VMEM((4, capacity + 2 * share, width), f32), square_more]
        + [pltpu.VMEM((share, width), f32)] * 2 + [pltpu.VMEM((capacity, width), f32), ahead, ahead],
        16 * most_outer,
        scalars=4,
    )
    again = pltpu.with_memory_space_constraint(again, pltpu.SMEM)

    def inner(field):
        return call(
            apply_inner,
            (meta, table, plan, again, field, alone, times, held(tiles_in)),
            [square, narrow],
            [pltpu.VMEM((share, width, width), f32), pltpu.VMEM((share + SUB, width), f32), pltpu.VMEM((share, width), f32),
             pltpu.VMEM(((share + 1) * SUB, width), f32)],
            4 * most_inner,
            scalars=4,
        )

    def exchange(field):
        count = pieces * columns
        swaps = [[i ^ 1 for i in range(count)], [i - 1 if i % 2 == 0 else i + 1 for i in range(count)]]
        swaps[1][0], swaps[1][-1] = count - 1, 0
        for c in range(1, columns - 1):
            to = {}
            for p in range(pieces - 1):
                low, high = p * columns + c, (p + 1) * columns
                to[low], to[high] = high, low
            spare = {c % (columns - 1) + 1: [0], (c + 1) % (columns - 1) + 1: [(pieces - 1) * columns + c]}
            for p in range(0, pieces, 2):
                for d in range(1, columns):
                    if d != c:
                        ring = [p * columns + d, (p + 1) * columns + d]
                        ring += spare.get(d, []) if p == (0 if spare.get(d) == [0] else pieces - 2) else []
                        to.update(zip(ring, ring[1:] + ring[:1]))
            swaps.append([to[i] for i in range(count)])
        return [lax.ppermute(field, axes, list(enumerate(to))) for to in swaps]

    scratch = [pltpu.VMEM((share, width, width), f32), pltpu.VMEM((8 * share, width), f32)]

    received = exchange(precond)
    rows, cols = inner(precond)
    spill, scaled = call(
        apply_first,
        (meta, table, plan, again, diagonal, times, *received, held(tiles_out), held(rows), held(cols)),
        [vector, vector],
        scratch,
        2 * most_outer,
        scalars=4,
    )

    received = exchange(scaled)
    rows, cols = inner(scaled)
    twice, sums = call(
        apply_second,
        (meta, table, plan, again, source, precond, spill, scaled, times, *received, held(tiles_out), held(rows), held(cols)),
        [vector, few],
        scratch,
        2 * most_outer,
        scalars=4,
    )

    def together(values, axis, low, size):
        return tree([values] + [swap(values, axis, low * k) for k in range(1, size)])

    sums = together(sums, "piece", 1, 2)
    sums = together(sums, "col", 1, columns)
    step = 2
    while pieces // step > 4:
        sums = together(sums, "piece", step, 4)
        step *= 4
    others = [swap(sums, "piece", step * k) for k in range(1, pieces // step)]

    return tuple(call(
        finish,
        (source, precond, spill, scaled, twice, sums, *others),
        [vector, vector],
        scalars=0,
    ))


def solution(mesh):
    placed = (
        P(None, "piece", None),
        P("piece", None),
        P("piece", "col"),
        P(),
        P(),
        P(("piece", "col"), None),
    )
    return jax.shard_map(
        body,
        mesh=mesh,
        in_specs=placed,
        out_specs=(P(("piece", "col"), None), P(("piece", "col"), None)),
        check_vma=False,
    )
```

```python
import jax
import jax.numpy as jnp
import numpy as np
from jax import lax
from jax.experimental import pallas as pl
from jax.experimental.pallas import tpu as pltpu
from jax.sharding import PartitionSpec as P

ITERS = 2
SIDE = 4
LAYER = SIDE * SIDE
REACH = 2 * LAYER
SUB = 8
VMEM = pl.BlockSpec(memory_space=pltpu.VMEM)
SMEM = pl.BlockSpec(memory_space=pltpu.SMEM)
HBM = pl.BlockSpec(memory_space=pltpu.HBM)


def stencil_tables():
    levels = SIDE.bit_length() - 1

    def cell(code):
        across = sum((code >> (2 * level) & 1) << level for level in range(levels))
        along = sum((code >> (2 * level + 1) & 1) << level for level in range(levels))
        return across, along

    place = {cell(code): code for code in range(LAYER)}
    rows = []
    for code in range(LAYER):
        across, along = cell(code)
        rows.append(
            sorted(
                step_z * LAYER + place[across + step_x, along + step_y] - code
                for step_z in (-1, 0, 1)
                for step_y in (-1, 0, 1)
                for step_x in (-1, 0, 1)
                if (across + step_x, along + step_y) in place
            )
        )
    longest = max(len(row) for row in rows)
    offsets = np.zeros((LAYER, longest), np.int32)
    below = np.zeros((LAYER, 2 * REACH + 1), np.int32)
    for code, row in enumerate(rows):
        offsets[code, : len(row)] = row
        for t in range(-REACH, REACH + 1):
            below[code, t + REACH] = sum(offset < t for offset in row)
    return offsets, below


OFFSETS, BELOW = stencil_tables()
WIDEST = OFFSETS.shape[1]
TABLE = np.concatenate([OFFSETS, BELOW], 1)
STRIDE = TABLE.shape[1]
FLAT = np.concatenate([TABLE.reshape(-1), np.zeros(8, np.int32)])
LIMIT = pltpu.CompilerParams(vmem_limit_bytes=8 * 1024 * 1024)


def tile_bounds(share):
    inner = outer = 0
    for first in range(LAYER):
        for live in range(1, share + 1):
            near = far = 0
            for a in range(live):
                code = (first + a) % LAYER
                row = [int(o) for o in OFFSETS[code][: BELOW[code, -1]]]
                near += sum(0 <= a + o and o <= 0 for o in row)
                far += sum(a + o < 0 or a + o >= live for o in row)
            inner, outer = max(inner, near), max(outer, far)
    return inner, outer


def rank(table, code, t):
    return table[code * STRIDE + jnp.clip(t, -REACH, REACH) + REACH + WIDEST]


FIELDS = 6


def write_plan(meta, table, plan, a):
    code = lax.bitwise_and(meta[1] + a, LAYER - 1)
    place = meta[1] + a
    low, split, middle = rank(table, code, -place), rank(table, code, -a), rank(table, code, 0)
    resume, high = rank(table, code, meta[0] - a), rank(table, code, meta[2] - place)
    row = code * STRIDE
    ahead = split - low
    plan[a * FIELDS] = middle - split
    plan[a * FIELDS + 1] = row + split
    plan[a * FIELDS + 2] = ahead + jnp.maximum(high - resume, 0)
    plan[a * FIELDS + 3] = ahead
    plan[a * FIELDS + 4] = row + low
    plan[a * FIELDS + 5] = row + resume - ahead


def write_run(runs, at, a, start, count):
    runs[3 * at], runs[3 * at + 1], runs[3 * at + 2] = a, start, count
    return at + (count > 0).astype(jnp.int32)


def write_runs(meta, table, plan, inner_runs, outer_runs, share):
    inner = outer = total = far = jnp.int32(0)
    for a in range(share):
        write_plan(meta, table, plan, a)
        alive = a < meta[0]
        count, start, count_far, ahead, start_far, start_after = (plan[a * FIELDS + k] for k in range(FIELDS))
        inner = write_run(inner_runs, inner, a, start, jnp.where(alive, count + 1, 0))
        outer = write_run(outer_runs, outer, a, start_far, jnp.where(alive, ahead, 0))
        outer = write_run(outer_runs, outer, a, start_after + ahead, jnp.where(alive, count_far - ahead, 0))
        total = total + jnp.where(alive, count + 1, 0)
        far = far + jnp.where(alive, count_far, 0)
    for runs, at in ((inner_runs, inner), (outer_runs, outer)):
        write_run(runs, at, share, len(FLAT) - 8, jnp.int32(1))
    plan[share * FIELDS] = total
    plan[share * FIELDS + 1] = far
    plan[share * FIELDS + 2] = inner
    plan[share * FIELDS + 3] = outer


def inner_range(plan, table, a):
    start = plan[a * FIELDS + 1]
    return plan[a * FIELDS], lambda t: a + table[start + t]


def outer_range(plan, table, a):
    ahead, start, start_after = (plan[a * FIELDS + k] for k in (3, 4, 5))
    return plan[a * FIELDS + 2], lambda t: a + table[t + jnp.where(t < ahead, start, start_after)]


TURN = 3


def padded_sweep(count, fetch, step, carry):
    def turn(i, state):
        carry, *now = state
        later = [fetch(TURN * (i + 1) + k) for k in range(TURN)]
        return step(now, carry), *later

    state = (carry, *(fetch(k) for k in range(TURN)))
    return lax.fori_loop(0, lax.div(count + (TURN - 1), TURN), turn, state)[0]


def tree(terms):
    while len(terms) > 1:
        terms = [a + b for a, b in zip(terms[::2], terms[1::2])] + terms[len(terms) // 2 * 2 :]
    return terms[0]


def gather(partial, c, term):
    if c < len(partial):
        partial[c] = term
    else:
        partial[c % len(partial)] = partial[c % len(partial)] + term


def pieces_of(width):
    return [slice(c * SUB, (c + 1) * SUB) for c in range(width // SUB)]


def wide(row):
    return jnp.broadcast_to(row, (SUB, row.shape[1]))


def three_parts(values):
    high = values.astype(jnp.bfloat16).astype(jnp.float32)
    rest = values - high
    middle = rest.astype(jnp.bfloat16).astype(jnp.float32)
    return high, middle, rest - middle


def stacked(rows):
    sublane = lax.broadcasted_iota(jnp.int32, rows[0].shape, 0)
    result = jnp.zeros(rows[0].shape, jnp.float32)
    for k, row in enumerate(rows):
        result = jnp.where(sublane == k, row, result)
    return result


def half_size(x):
    return 0.5 - (x[0] * x[0] + x[1] * x[1] + x[2] * x[2])


def own_side(x, which):
    nothing = [jnp.zeros_like(x[0])] * 4
    rows = [2.0 * x[0], 2.0 * x[1], 2.0 * x[2], jnp.ones_like(x[0])]
    high, middle, low = three_parts(stacked(nothing + rows if which else rows))
    sizes = stacked(list(three_parts(half_size(x))))
    width = sizes.shape[1]
    rest = jnp.zeros((width - 7 * SUB, width), jnp.float32)
    return jnp.concatenate([high, high, middle, middle, high, low, sizes, rest], 0)


def other_sides(first, second):
    rows = [*first, half_size(first), *second, half_size(second)]
    high, middle, low = three_parts(stacked(rows))
    width = high.shape[1]
    ones = jnp.where(lax.broadcasted_iota(jnp.int32, (2 * SUB, width), 0) < 3, 1.0, 0.0).astype(jnp.bfloat16)
    front = jnp.concatenate([high, middle], 0).astype(jnp.bfloat16)
    back = jnp.concatenate([low, high], 0).astype(jnp.bfloat16)
    rest = jnp.zeros((width - 8 * SUB, width), jnp.bfloat16)
    return jnp.concatenate([front, front, back, ones, rest], 0)


GROUP = 4


def flat_tiles(count, runs, most, table, sides, middles, weights, other_at, buffers, tiles, rows_ref, cols_ref):
    share, width = rows_ref.shape[0] - 1, rows_ref.shape[2]
    chunks = pieces_of(width)

    def steps(state):
        found = []
        for _ in range(GROUP):
            run, t = state
            a, start, size = (runs[3 * run + k] for k in range(3))
            found.append((a, a + table[start + t]))
            over = t + 1 >= size
            state = jnp.minimum(run + over.astype(jnp.int32), most), jnp.where(over, 0, t + 1)
        return state, found

    def other_of(a, n):
        here = pl.ds(a, 1)
        return [wide(other_at(c, n)) - wide(middles[c, here, :]) for c in range(3)]

    def products(found, ahead):
        for k in range(0, GROUP, 2):
            (a, n), (b, m) = ((jnp.minimum(a, share - 1), n) for a, n in found[k : k + 2])
            own = jnp.concatenate([sides[0, a], sides[1, b]], 0)
            both = jnp.dot(own, other_sides(other_of(a, n), other_of(b, m)), preferred_element_type=jnp.float32)
            ahead[k] = both[:width]
            ahead[k + 1] = both[width:]

    def weigh(at, found, ahead):
        for k, (a, n) in enumerate(found):
            alone = a == n
            row = jnp.where(alone, share, a)
            own = jnp.minimum(a, share - 1)
            other = wide(other_at(3, n))
            down = [None] * 2
            for c, here in enumerate(chunks):
                left = ahead[k, here, :]
                rest = jnp.maximum(left, 0.0)
                inverse = pltpu.reciprocal((1.01 - left) * (weights[own, here, :] + other), approx=True)
                tile = rest * rest * inverse
                tiles[at + k, here, :] = tile
                rows_ref[row, here, :] = rows_ref[row, here, :] + tile
                if cols_ref is not None:
                    gather(down, c, tile)
            if cols_ref is not None:
                there = pl.ds(pl.multiple_of(jnp.where(alone, share, n) * SUB, SUB), SUB)
                cols_ref[there, :] = cols_ref[there, :] + tree(down)

    def turn(i, carry):
        state, found = carry
        at = i * (2 * GROUP)
        state, later = steps(state)
        products(later, buffers[1])
        weigh(at, found, buffers[0])
        state, last = steps(state)
        products(last, buffers[0])
        weigh(at + GROUP, later, buffers[1])
        return state, last

    state, found = steps((jnp.int32(0), jnp.int32(0)))
    products(found, buffers[0])
    lax.fori_loop(0, lax.div(count + (2 * GROUP - 1), 2 * GROUP), turn, (state, found))


def spread_columns(out, index, rows):
    count, width = rows.shape
    turned = rows.T
    for a in range(count):
        out[index(a)] = jnp.broadcast_to(turned[:, a : a + 1], (width, width))


def lane_sums(parts, count, width):
    lanes = lax.broadcasted_iota(jnp.int32, (width, width), 1)
    turned = jnp.zeros((width, width), jnp.float32)
    for a in range(count):
        turned = jnp.where(lanes == a, jnp.sum(parts[a], axis=1, keepdims=True), turned)
    return turned.T[:count]


def sub_sums(cols):
    return jnp.sum(cols[...].reshape(-1, SUB, cols.shape[1]), axis=1)


def alive_rows(meta, share, width):
    return lax.broadcasted_iota(jnp.int32, (share, width), 0) < meta[0]


def prepare(
    counts, densities, position_in, phase_in, right_side_in, table_in, lists_in,
    meta, table, hood, near, density, source, first_swap, second_swap, lists, phase, right_side, sems
):
    share, width = source.shape
    capacity = phase.shape[0]
    body_rows = pl.ds(share, capacity)
    copies = [
        pltpu.make_async_copy(phase_in, phase, sems.at[0]),
        pltpu.make_async_copy(position_in, hood.at[pl.ds(0, 3), body_rows, :], sems.at[1]),
        pltpu.make_async_copy(right_side_in, right_side, sems.at[2]),
        pltpu.make_async_copy(table_in, table, sems.at[3]),
        pltpu.make_async_copy(lists_in, lists, sems.at[4]),
    ]
    for copy in copies:
        copy.start()
    piece, column = lax.axis_index("piece"), lax.axis_index("col")
    filled = counts[piece]
    filled_before = counts[jnp.maximum(piece - 1, 0)]
    before = jnp.int32(0)
    total = jnp.int32(0)
    for p in range(counts.shape[0]):
        before = before + jnp.where(p < piece, counts[p], 0)
        total = total + counts[p]
    meta[0] = jnp.clip(filled - column * share, 0, share)
    meta[1] = before + column * share
    meta[2] = total
    meta[3] = column * share
    meta[4] = filled
    meta[5] = filled_before
    own_rows = pl.ds(pl.multiple_of(share + column * share, SUB), share)
    copies[0].wait()
    labels = phase[...]
    whole = sum(jnp.where(labels == k, densities[k], 0.0) for k in range(densities.shape[0]))
    hood[3, body_rows, :] = whole * (width / 2.0)
    density[...] = hood[3, own_rows, :] * (2.0 / width)
    copies[1].wait()
    even = lax.rem(piece, 2) == 0
    for k in range(4):
        tail, head = hood[k, pl.ds(filled, share), :], hood[k, share : 2 * share, :]
        first_swap[k] = jnp.where(even, tail, head)
        second_swap[k] = jnp.where(even, head, tail)
        near[k, 0:share, :] = hood[k, own_rows, :]
    for copy in copies[2:]:
        copy.wait()
    source[...] = jnp.where(alive_rows(meta, share, width), right_side[...], 0.0)


def finish_tiles(tiles, end):
    for t in range(TURN):
        tiles[end + t] = jnp.zeros(tiles.shape[1:], jnp.float32)


def build_inner(
    meta, table, near, plan, outer_runs, tiles, sides, middles, weights, rows_ref, cols_ref, self_ref,
    inner_runs, *buffers,
):
    share, width = weights.shape[:2]
    chunks = pieces_of(width)
    write_runs(meta, table, plan, inner_runs, outer_runs, share)
    for k in range(3):
        first = near[k, 0:share, 0:1]
        middles[k] = jnp.broadcast_to(jnp.floor(first) + 0.5, (share, width))
    for a in range(share):
        here = slice(a, a + 1)
        centred = [wide(near[k, here, :] - middles[k, here, :]) for k in range(3)]
        for which in range(2):
            sides[which, a] = own_side(centred, which).T.astype(jnp.bfloat16)
    spread_columns(weights, lambda a: a, near[3, 0:share, :])
    cols_ref[...] = jnp.zeros_like(cols_ref)
    rows_ref[...] = jnp.zeros_like(rows_ref)
    count = plan[share * FIELDS]
    flat_tiles(
        count, inner_runs, plan[share * FIELDS + 2], table, sides, middles, weights,
        lambda k, n: near[k, pl.ds(n, 1), :], buffers, tiles, rows_ref, cols_ref,
    )
    finish_tiles(tiles, count)
    lane = lax.broadcasted_iota(jnp.int32, (SUB, width), 1)
    sublane = lax.broadcasted_iota(jnp.int32, (SUB, width), 0)

    def block(a, at):
        at = at + plan[a * FIELDS]
        down = [None] * 4
        for c, here in enumerate(chunks):
            tile = jnp.where(lane == sublane + c * SUB, 0.0, tiles[at, here, :])
            tiles[at, here, :] = tile
            gather(down, c, tile)
        self_ref[pl.ds(pl.multiple_of(a * SUB, SUB), SUB), :] = tree(down)
        return at + 1

    lax.fori_loop(0, meta[0], block, 0)


def count_listed(meta, lists, width):
    capacity = lists[0].shape[1]
    filled, filled_before = meta[4], meta[5]
    start = lax.axis_index("piece") * capacity
    steps = lax.broadcasted_iota(jnp.int32, (2 * REACH, capacity), 0)
    partial = [None] * 4
    row = 0
    for ref in lists:
        ids = ref[...]
        slot = ids - start
        gap = jnp.where(slot < 0, capacity - filled_before, jnp.where(slot >= capacity, filled - capacity, 0))
        away = slot - lax.broadcasted_iota(jnp.int32, ids.shape, 1) + gap
        away = jnp.where(ids < 0, -REACH, away) + REACH
        for k in range(ids.shape[0]):
            gather(partial, row, jnp.where(steps == away[k : k + 1], 1.0, 0.0))
            row += 1
    return jnp.concatenate([tree(partial), jnp.zeros((width - 2 * REACH, capacity), jnp.float32)], 0).T


def factor(times, a, n):
    lane = lax.broadcasted_iota(jnp.int32, (1, times.shape[1]), 1)
    return jnp.sum(jnp.where(lane == n - a + REACH, times[pl.ds(a, 1), :], 0.0), axis=1, keepdims=True)


def either(flag, run):
    @pl.when(flag == 0)
    def _():
        run(False)

    @pl.when(flag != 0)
    def _():
        run(True)


TAIL = 13


def build_outer(
    meta, table, plan, runs, around, first, second, density, source, tiles_in, sides, middles, weights,
    rows_ref, cols_ref, self_ref, *rest
):
    lists, rest = rest[:-TAIL], rest[-TAIL:]
    again_ref, tiles, diagonal_ref, precond_ref, times, alone_ref, hood, work, sums_ref, extra, all_times, *buffers = rest
    share, width = diagonal_ref.shape
    base, filled = meta[3], meta[4]
    even = lax.rem(lax.axis_index("piece"), 2) == 0
    for k in range(4):
        hood[k, 0:share, :] = jnp.where(even, second[k], first[k])
        hood[k, share:, :] = around[k, share:, :]
        hood[k, pl.ds(share + filled, share), :] = jnp.where(even, first[k], second[k])
    alive = alive_rows(meta, share, width)
    all_times[...] = count_listed(meta, lists, width)
    often = jnp.where(alive, all_times[pl.ds(pl.multiple_of(base, SUB), share), :], 0.0)
    times[...] = often
    lane = lax.broadcasted_iota(jnp.int32, (share, width), 1)
    again = jnp.max(jnp.where((lane == REACH) | (lane == 0), 0.0, often)) > 1.5
    again_ref[0] = again.astype(jnp.int32)


    work[...] = jnp.zeros_like(work)
    count = plan[share * FIELDS + 1]
    flat_tiles(
        count, runs, plan[share * FIELDS + 3], table, sides, middles, weights,
        lambda k, n: hood[k, pl.ds(base + share + n, 1), :], buffers, tiles, work, None,
    )
    finish_tiles(tiles, count)
    sums_ref[...] = lane_sums([rows_ref[a] + work[a] for a in range(share)], share, width) + sub_sums(cols_ref)[0:share]

    @pl.when(again)
    def _():
        extra[...] = jnp.zeros_like(extra)
        work[...] = jnp.zeros_like(work)

        def block(a, state):
            count, place_of = inner_range(plan, table, a)

            def inner(t, at):
                n = place_of(t)
                tile = tiles_in[at]
                work[a] = work[a] + tile * factor(times, a, n)
                there = pl.ds(n, 1)
                down = jnp.sum(tile, axis=0, keepdims=True)
                extra[there, :] = extra[there, :] + down * factor(times, n, a)
                return at + 1

            at = lax.fori_loop(0, count, inner, state[0]) + 1
            count, place_far = outer_range(plan, table, a)

            def outer(t, at):
                work[a] = work[a] + tiles[at] * factor(times, a, place_far(t))
                return at + 1

            return at, lax.fori_loop(0, count, outer, state[1])

        lax.fori_loop(0, meta[0], block, (0, 0))
        sums_ref[...] = lane_sums(work, share, width) + extra[...]

    alone = jnp.sum(jnp.where(lane == REACH, often, 0.0), axis=1, keepdims=True)
    alone_ref[...] = jnp.broadcast_to(alone, (share, width))
    pairs = jnp.where(alive, sums_ref[...] + sub_sums(self_ref) * alone, 0.0)
    diagonal = 1.0 / density[...] + pairs
    diagonal_ref[...] = diagonal
    precond_ref[...] = source[...] / diagonal


def apply_inner(meta, table, plan, again, field, alone, times, tiles, rows_ref, cols_ref, spread, near, lone, cols):
    share, width = field.shape
    chunks = pieces_of(width)
    near[0:share, :] = field[...]
    near[share:, :] = jnp.zeros((SUB, width), jnp.float32)
    lone[...] = field[...] * alone[...]
    spread_columns(spread, lambda a: a, field[...])
    cols[...] = jnp.zeros_like(cols)

    def run(weighted):
        def block(a, at):
            count, place_of = inner_range(plan, table, a)

            def fetch(t):
                n = jnp.where(t < count, place_of(t), share)
                return n, wide(near[pl.ds(n, 1), :])

            def pairs(fetched, carry):
                at, sums = carry
                if weighted:
                    fetched = [(n, value * factor(times, a, jnp.minimum(n, share - 1))) for n, value in fetched]
                down = [[None] * 2 for _ in fetched]
                result = []
                for c, (here, total) in enumerate(zip(chunks, sums)):
                    own = spread[a, here, :]
                    found = []
                    for t, (_, value) in enumerate(fetched):
                        tile = tiles[at + t, here, :]
                        gather(down[t], c, tile * own)
                        found.append(tile * value)
                    result.append(total + tree(found))
                for (n, _), partial in zip(fetched, down):
                    there = pl.ds(pl.multiple_of(n * SUB, SUB), SUB)
                    partial = tree(partial)
                    if weighted:
                        partial = partial * factor(times, jnp.minimum(n, share - 1), a)
                    cols[there, :] = cols[there, :] + partial
                return at + len(fetched), result

            zero = jnp.zeros((SUB, width), jnp.float32)
            _, sums = padded_sweep(count, fetch, pairs, (at, [zero] * len(chunks)))
            at = at + count
            value = wide(lone[pl.ds(a, 1), :])
            for here, old in zip(chunks, sums):
                rows_ref[a, here, :] = old + tiles[at, here, :] * value
            return at + 1

        lax.fori_loop(0, meta[0], block, 0)

    either(again[0], run)
    cols_ref[...] = cols[0 : share * SUB, :]


def apply_outer(meta, table, plan, again, received, times, tiles, rows_ref, cols_ref, work, hood):
    first, second, *ends = received
    columns = len(received)
    share, width = first.shape
    chunks = pieces_of(width)
    base, filled = meta[3], meta[4]
    column = lax.div(base, share)
    odd = lax.rem(column, 2) == 1
    before = jnp.where(odd, first[...], second[...])
    after = jnp.where(odd, second[...], first[...])
    own = 3 * share
    for c, end in enumerate(ends, 1):
        hood[pl.ds(own - meta[5] + c * share, share), :] = end[...]
    from_last = own - meta[5] + (columns - 1) * share
    hood[pl.ds(jnp.where(column == 0, from_last, own - share), share), :] = before
    hood[own + share : own + 2 * share, :] = after
    head = after
    for c, end in enumerate(ends, 1):
        head = jnp.where(column == c, end[...], head)
    hood[pl.ds(own + jnp.clip(filled - base, 0, 2 * share), share), :] = head
    nothing = hood.shape[0] - SUB
    hood[nothing:, :] = jnp.zeros((SUB, width), jnp.float32)

    def run(weighted):
        def block(a, at):
            count, place_of = outer_range(plan, table, a)

            def fetch(t):
                place = place_of(t)
                value = hood[pl.ds(jnp.where(t < count, own + place, nothing), 1), :]
                if weighted:
                    value = value * factor(times, a, place)
                return wide(value)

            def pairs(values, carry):
                at, sums = carry
                result = []
                for here, total in zip(chunks, sums):
                    result.append(total + tree([tiles[at + t, here, :] * value for t, value in enumerate(values)]))
                return at + len(values), result

            _, sums = padded_sweep(count, fetch, pairs, (at, [rows_ref[a, here, :] for here in chunks]))
            for here, values in zip(chunks, sums):
                work[a, here, :] = values
            return at + count

        lax.fori_loop(0, meta[0], block, 0)

    either(again[0], run)
    return jnp.where(alive_rows(meta, share, width), lane_sums(work, share, width) + sub_sums(cols_ref), 0.0)


def apply_first(meta, table, plan, again, diagonal, times, *rest):
    *received, tiles, rows_ref, cols_ref, spill_ref, scaled_ref, work, hood = rest
    spill = apply_outer(meta, table, plan, again, received, times, tiles, rows_ref, cols_ref, work, hood)
    spill_ref[...] = spill
    scaled_ref[...] = spill / diagonal[...]


def apply_second(meta, table, plan, again, source, precond, spill, scaled, times, *rest):
    *received, tiles, rows_ref, cols_ref, twice_ref, sums_ref, work, hood = rest
    twice = apply_outer(meta, table, plan, again, received, times, tiles, rows_ref, cols_ref, work, hood)
    twice_ref[...] = twice
    share, width = twice.shape
    lane = lax.broadcasted_iota(jnp.int32, (1, width), 1)
    sums = jnp.zeros((1, width), jnp.float32)
    pairs = ((source[...], precond[...]), (spill[...], precond[...]), (spill[...], scaled[...]), (scaled[...], twice))
    for k, (first, second) in enumerate(pairs):
        along = jnp.sum(first * second, axis=0, keepdims=True)
        sums = jnp.where(lane == k, jnp.sum(along, axis=1, keepdims=True), sums)
    sums_ref[...] = sums


def finish(source, precond, spill, scaled, twice, *rest):
    *parts, solution_ref, residual_ref = rest
    sums = tree([ref[...] for ref in parts])

    def pick(k):
        return sums[0:1, k : k + 1]

    weighted, cross, square, last = pick(0), pick(1), pick(2), pick(3)
    part = cross / weighted
    advance = 1.0 / (1.0 - part)
    keep = -part * advance
    weighted_next = advance * advance * (square - cross * part)
    bent = keep * keep * cross + 2.0 * keep * advance * square + advance * advance * last
    blend = weighted_next / weighted
    advance_next = weighted_next / (weighted_next - bent - blend * weighted_next / advance)
    residual = keep * source[...] + advance * spill[...]
    next_precond = keep * precond[...] + advance * scaled[...]
    direction = next_precond + blend * precond[...]
    image = residual - keep * spill[...] - advance * twice[...] + blend * (source[...] - spill[...])
    solution_ref[...] = advance * precond[...] + advance_next * direction
    residual_ref[...] = residual - advance_next * image


def held(array):
    return pltpu.with_memory_space_constraint(array, pltpu.VMEM)


def body(positions, phase, neighbours, counts, phase_density, right_side):
    capacity, width = phase.shape
    columns = lax.axis_size("col")
    pieces = lax.axis_size("piece")
    share = capacity // columns
    f32 = jnp.float32
    vector = jax.ShapeDtypeStruct((share, width), f32)
    few = jax.ShapeDtypeStruct((1, width), f32)
    message = jax.ShapeDtypeStruct((4, share, width), f32)
    most_inner, most_outer = tile_bounds(share)
    inner_tiles = pltpu.VMEM((most_inner + 2 * GROUP, width, width), f32)
    outer_tiles = pltpu.VMEM((most_outer + 2 * GROUP, width, width), f32)
    ahead = pltpu.VMEM((GROUP, width, width), f32)
    square_more = pltpu.VMEM((share + 1, width, width), f32)
    narrow_more = pltpu.VMEM(((share + 1) * SUB, width), f32)
    square = pltpu.VMEM((share, width, width), f32)
    narrow = pltpu.VMEM((share * SUB, width), f32)
    table = jnp.asarray(FLAT)

    def call(kernel, args, outs, scratch=(), work=0, scalars=2, far=0, **more):
        return pl.pallas_call(
            kernel,
            out_shape=outs,
            in_specs=[SMEM] * scalars + [HBM] * far + [VMEM] * (len(args) - scalars - far),
            out_specs=[SMEM if getattr(o, "memory_space", None) == pltpu.SMEM else VMEM for o in outs],
            scratch_shapes=scratch,
            compiler_params=LIMIT,
            cost_estimate=pl.CostEstimate(flops=work * width * width, bytes_accessed=0, transcendentals=0),
            name=kernel.__name__,
            **more,
        )(*args)

    def swap(values, axis, step):
        return lax.ppermute(values, axis, [(i, i ^ step) for i in range(lax.axis_size(axis))])

    def away(array):
        return pltpu.with_memory_space_constraint(array, pltpu.HBM)

    around = jax.ShapeDtypeStruct((4, capacity + 2 * share, width), f32)
    near = jax.ShapeDtypeStruct((4, 2 * share, width), f32)
    far = [away(array) for array in (positions, phase, right_side, table, neighbours.T)]
    meta, table, around, near, density, source, first, second, own_lists = call(
        prepare,
        (away(counts), away(phase_density), *far),
        [pltpu.SMEM((8,), jnp.int32), pltpu.SMEM(table.shape, jnp.int32), around, near, vector, vector, message, message,
         jax.ShapeDtypeStruct(far[-1].shape, jnp.int32)],
        [pltpu.VMEM(phase.shape, jnp.int32), pltpu.VMEM((share, width), f32), pltpu.SemaphoreType.DMA((5,))],
        far=len(far),
    )
    meta, table = (pltpu.with_memory_space_constraint(array, pltpu.SMEM) for array in (meta, table))
    first = lax.ppermute(first, "piece", [(i, i ^ 1) for i in range(pieces)])
    axes = ("piece", "col")
    device = [(p, c) for p in range(pieces) for c in range(columns)]
    partner = [(p + (1 if p % 2 else -1), c) for p, c in device]
    partner = [(q, d) if 0 <= q < pieces else (p, c ^ 1) for (q, d), (p, c) in zip(partner, device)]
    second = lax.ppermute(second, axes, [(i, q * columns + d) for i, (q, d) in enumerate(partner)])

    col_steps = [(1 << k) | 1 for k in range(columns.bit_length() - 1)]
    lists = [own_lists]
    for step in col_steps:
        known = lists[0] if len(lists) == 1 else jnp.concatenate(lists, 0)
        lists = [known, swap(known, "col", step)]

    plan, runs, tiles_in, sides, middles, weights, rows, cols, selfs = call(
        build_inner,
        (meta, table, near),
        [pltpu.SMEM((share * FIELDS + 4,), jnp.int32), pltpu.SMEM((6 * share + 3,), jnp.int32), inner_tiles,
         pltpu.VMEM((2, share, width, width), jnp.bfloat16), pltpu.VMEM((3, share, width), f32), square,
         square_more, narrow_more, narrow],
        [pltpu.SMEM((3 * share + 3,), jnp.int32), ahead, ahead],
        16 * most_inner,
    )
    plan, runs = (pltpu.with_memory_space_constraint(array, pltpu.SMEM) for array in (plan, runs))
    again, tiles_out, diagonal, precond, times, alone = call(
        build_outer,
        (meta, table, plan, runs, around, first, second, density, source,
         held(tiles_in), held(sides), held(middles), held(weights), held(rows), held(cols), held(selfs), *lists),
        [pltpu.SMEM((1,), jnp.int32), outer_tiles, vector, vector, vector, vector],
        [pltpu.VMEM((4, capacity + 2 * share, width), f32), square_more]
        + [pltpu.VMEM((share, width), f32)] * 2 + [pltpu.VMEM((capacity, width), f32), ahead, ahead],
        16 * most_outer,
        scalars=4,
    )
    again = pltpu.with_memory_space_constraint(again, pltpu.SMEM)

    def inner(field):
        return call(
            apply_inner,
            (meta, table, plan, again, field, alone, times, held(tiles_in)),
            [square, narrow],
            [pltpu.VMEM((share, width, width), f32), pltpu.VMEM((share + SUB, width), f32), pltpu.VMEM((share, width), f32),
             pltpu.VMEM(((share + 1) * SUB, width), f32)],
            4 * most_inner,
            scalars=4,
        )

    def exchange(field):
        count = pieces * columns
        swaps = [[i ^ 1 for i in range(count)], [i - 1 if i % 2 == 0 else i + 1 for i in range(count)]]
        swaps[1][0], swaps[1][-1] = count - 1, 0
        for c in range(1, columns - 1):
            to = {}
            for p in range(pieces - 1):
                low, high = p * columns + c, (p + 1) * columns
                to[low], to[high] = high, low
            spare = {c % (columns - 1) + 1: [0], (c + 1) % (columns - 1) + 1: [(pieces - 1) * columns + c]}
            for p in range(0, pieces, 2):
                for d in range(1, columns):
                    if d != c:
                        ring = [p * columns + d, (p + 1) * columns + d]
                        ring += spare.get(d, []) if p == (0 if spare.get(d) == [0] else pieces - 2) else []
                        to.update(zip(ring, ring[1:] + ring[:1]))
            swaps.append([to[i] for i in range(count)])
        received = [lax.ppermute(field, axes, list(enumerate(to))) for to in swaps[1:]]
        rows, cols = inner(field)
        late, cols = lax.optimization_barrier((field, cols))
        return [lax.ppermute(late, axes, list(enumerate(swaps[0]))), *received], rows, cols

    scratch = [pltpu.VMEM((share, width, width), f32), pltpu.VMEM((8 * share, width), f32)]

    received, rows, cols = exchange(precond)
    spill, scaled = call(
        apply_first,
        (meta, table, plan, again, diagonal, times, *received, held(tiles_out), held(rows), held(cols)),
        [vector, vector],
        scratch,
        2 * most_outer,
        scalars=4,
    )

    received, rows, cols = exchange(scaled)
    twice, sums = call(
        apply_second,
        (meta, table, plan, again, source, precond, spill, scaled, times, *received, held(tiles_out), held(rows), held(cols)),
        [vector, few],
        scratch,
        2 * most_outer,
        scalars=4,
    )

    def together(values, axis, low, size):
        return tree([values] + [swap(values, axis, low * k) for k in range(1, size)])

    sums = together(sums, "piece", 1, 2)
    sums = together(sums, "col", 1, columns)
    step = 2
    while pieces // step > 4:
        sums = together(sums, "piece", step, 4)
        step *= 4
    others = [swap(sums, "piece", step * k) for k in range(1, pieces // step)]

    return tuple(call(
        finish,
        (source, precond, spill, scaled, twice, sums, *others),
        [vector, vector],
        scalars=0,
    ))


def solution(mesh):
    placed = (
        P(None, "piece", None),
        P("piece", None),
        P("piece", "col"),
        P(),
        P(),
        P(("piece", "col"), None),
    )
    return jax.shard_map(
        body,
        mesh=mesh,
        in_specs=placed,
        out_specs=(P(("piece", "col"), None), P(("piece", "col"), None)),
        check_vma=False,
    )
```

```python
import jax
import jax.numpy as jnp
import numpy as np
from jax import lax
from jax.experimental import pallas as pl
from jax.experimental.pallas import tpu as pltpu
from jax.sharding import PartitionSpec as P

ITERS = 2
SIDE = 4
LAYER = SIDE * SIDE
REACH = 2 * LAYER
SUB = 8
VMEM = pl.BlockSpec(memory_space=pltpu.VMEM)
SMEM = pl.BlockSpec(memory_space=pltpu.SMEM)
HBM = pl.BlockSpec(memory_space=pltpu.HBM)


def stencil_tables():
    levels = SIDE.bit_length() - 1

    def cell(code):
        across = sum((code >> (2 * level) & 1) << level for level in range(levels))
        along = sum((code >> (2 * level + 1) & 1) << level for level in range(levels))
        return across, along

    place = {cell(code): code for code in range(LAYER)}
    rows = []
    for code in range(LAYER):
        across, along = cell(code)
        rows.append(
            sorted(
                step_z * LAYER + place[across + step_x, along + step_y] - code
                for step_z in (-1, 0, 1)
                for step_y in (-1, 0, 1)
                for step_x in (-1, 0, 1)
                if (across + step_x, along + step_y) in place
            )
        )
    longest = max(len(row) for row in rows)
    offsets = np.zeros((LAYER, longest), np.int32)
    below = np.zeros((LAYER, 2 * REACH + 1), np.int32)
    for code, row in enumerate(rows):
        offsets[code, : len(row)] = row
        for t in range(-REACH, REACH + 1):
            below[code, t + REACH] = sum(offset < t for offset in row)
    return offsets, below


OFFSETS, BELOW = stencil_tables()
WIDEST = OFFSETS.shape[1]
TABLE = np.concatenate([OFFSETS, BELOW], 1)
STRIDE = TABLE.shape[1]
FLAT = np.concatenate([TABLE.reshape(-1), np.zeros(8, np.int32)])
LIMIT = pltpu.CompilerParams(vmem_limit_bytes=8 * 1024 * 1024)


def tile_bounds(share):
    inner = outer = 0
    for first in range(LAYER):
        for live in range(1, share + 1):
            near = far = 0
            for a in range(live):
                code = (first + a) % LAYER
                row = [int(o) for o in OFFSETS[code][: BELOW[code, -1]]]
                near += sum(0 <= a + o and o <= 0 for o in row)
                far += sum(a + o < 0 or a + o >= live for o in row)
            inner, outer = max(inner, near), max(outer, far)
    return inner, outer


def rank(table, code, t):
    return table[code * STRIDE + jnp.clip(t, -REACH, REACH) + REACH + WIDEST]


FIELDS = 6


def write_plan(meta, table, plan, a):
    code = lax.bitwise_and(meta[1] + a, LAYER - 1)
    place = meta[1] + a
    low, split, middle = rank(table, code, -place), rank(table, code, -a), rank(table, code, 0)
    resume, high = rank(table, code, meta[0] - a), rank(table, code, meta[2] - place)
    row = code * STRIDE
    ahead = split - low
    plan[a * FIELDS] = middle - split
    plan[a * FIELDS + 1] = row + split
    plan[a * FIELDS + 2] = ahead + jnp.maximum(high - resume, 0)
    plan[a * FIELDS + 3] = ahead
    plan[a * FIELDS + 4] = row + low
    plan[a * FIELDS + 5] = row + resume - ahead


def write_run(runs, at, a, start, count):
    runs[3 * at], runs[3 * at + 1], runs[3 * at + 2] = a, start, count
    return at + (count > 0).astype(jnp.int32)


def write_runs(meta, table, plan, inner_runs, outer_runs, share):
    inner = outer = total = far = jnp.int32(0)
    for a in range(share):
        write_plan(meta, table, plan, a)
        alive = a < meta[0]
        count, start, count_far, ahead, start_far, start_after = (plan[a * FIELDS + k] for k in range(FIELDS))
        inner = write_run(inner_runs, inner, a, start, jnp.where(alive, count + 1, 0))
        outer = write_run(outer_runs, outer, a, start_far, jnp.where(alive, ahead, 0))
        outer = write_run(outer_runs, outer, a, start_after + ahead, jnp.where(alive, count_far - ahead, 0))
        total = total + jnp.where(alive, count + 1, 0)
        far = far + jnp.where(alive, count_far, 0)
    for runs, at in ((inner_runs, inner), (outer_runs, outer)):
        write_run(runs, at, share, len(FLAT) - 8, jnp.int32(1))
    plan[share * FIELDS] = total
    plan[share * FIELDS + 1] = far
    plan[share * FIELDS + 2] = inner
    plan[share * FIELDS + 3] = outer


def inner_range(plan, table, a):
    start = plan[a * FIELDS + 1]
    return plan[a * FIELDS], lambda t: a + table[start + t]


def outer_range(plan, table, a):
    ahead, start, start_after = (plan[a * FIELDS + k] for k in (3, 4, 5))
    return plan[a * FIELDS + 2], lambda t: a + table[t + jnp.where(t < ahead, start, start_after)]


TURN = 3


def padded_sweep(count, fetch, step, carry):
    def turn(i, state):
        carry, *now = state
        later = [fetch(TURN * (i + 1) + k) for k in range(TURN)]
        return step(now, carry), *later

    state = (carry, *(fetch(k) for k in range(TURN)))
    return lax.fori_loop(0, lax.div(count + (TURN - 1), TURN), turn, state)[0]


def tree(terms):
    while len(terms) > 1:
        terms = [a + b for a, b in zip(terms[::2], terms[1::2])] + terms[len(terms) // 2 * 2 :]
    return terms[0]


def gather(partial, c, term):
    if c < len(partial):
        partial[c] = term
    else:
        partial[c % len(partial)] = partial[c % len(partial)] + term


def pieces_of(width):
    return [slice(c * SUB, (c + 1) * SUB) for c in range(width // SUB)]


def wide(row):
    return jnp.broadcast_to(row, (SUB, row.shape[1]))


def three_parts(values):
    high = values.astype(jnp.bfloat16).astype(jnp.float32)
    rest = values - high
    middle = rest.astype(jnp.bfloat16).astype(jnp.float32)
    return high, middle, rest - middle


def stacked(rows):
    sublane = lax.broadcasted_iota(jnp.int32, rows[0].shape, 0)
    result = jnp.zeros(rows[0].shape, jnp.float32)
    for k, row in enumerate(rows):
        result = jnp.where(sublane == k, row, result)
    return result


def half_size(x):
    return 0.5 - (x[0] * x[0] + x[1] * x[1] + x[2] * x[2])


def own_side(x):
    high, middle, low = three_parts(stacked([2.0 * x[0], 2.0 * x[1], 2.0 * x[2], jnp.ones_like(x[0])]))
    sizes = stacked(list(three_parts(half_size(x))))
    width = sizes.shape[1]
    rest = jnp.zeros((width - 7 * SUB, width), jnp.float32)
    return jnp.concatenate([high, high, middle, middle, high, low, sizes, rest], 0)


def other_sides(first, second):
    rows = [*first, half_size(first), *second, half_size(second)]
    high, middle, low = three_parts(stacked(rows))
    width = high.shape[1]
    ones = jnp.where(lax.broadcasted_iota(jnp.int32, (2 * SUB, width), 0) < 3, 1.0, 0.0).astype(jnp.bfloat16)
    front = jnp.concatenate([high, middle], 0).astype(jnp.bfloat16)
    back = jnp.concatenate([low, high], 0).astype(jnp.bfloat16)
    rest = jnp.zeros((width - 8 * SUB, width), jnp.bfloat16)
    return jnp.concatenate([front, front, back, ones, rest], 0)


GROUP = 6


def flat_tiles(count, runs, most, table, sides, middles, weights, other_at, buffers, tiles, rows_ref, cols_ref):
    share, width = rows_ref.shape[0] - 1, rows_ref.shape[2]
    chunks = pieces_of(width)

    def steps(state):
        found = []
        for _ in range(GROUP):
            run, t = state
            a, start, size = (runs[3 * run + k] for k in range(3))
            found.append((a, a + table[start + t]))
            over = t + 1 >= size
            state = jnp.minimum(run + over.astype(jnp.int32), most), jnp.where(over, 0, t + 1)
        return state, found

    def other_of(a, n):
        here = pl.ds(a, 1)
        return [wide(other_at(c, n)) - wide(middles[c, here, :]) for c in range(3)]

    def products(found, ahead):
        for k in range(0, GROUP, 2):
            (a, n), (b, m) = ((jnp.minimum(a, share - 1), n) for a, n in found[k : k + 2])
            own = jnp.concatenate([sides[0, a], sides[1, b]], 0)
            both = jnp.dot(own, other_sides(other_of(a, n), other_of(b, m)), preferred_element_type=jnp.float32)
            ahead[k] = both[:width]
            ahead[k + 1] = both[width:]

    def weigh(at, found, ahead):
        for k, (a, n) in enumerate(found):
            alone = a == n
            row = jnp.where(alone, share, a)
            own = jnp.minimum(a, share - 1)
            other = wide(other_at(3, n))
            down = [None] * 2
            for c, here in enumerate(chunks):
                left = ahead[k, here, :]
                rest = jnp.maximum(left, 0.0)
                inverse = pltpu.reciprocal((1.01 - left) * (weights[own, here, :] + other), approx=True)
                tile = rest * rest * inverse
                tiles[at + k, here, :] = tile
                rows_ref[row, here, :] = rows_ref[row, here, :] + tile
                if cols_ref is not None:
                    gather(down, c, tile)
            if cols_ref is not None:
                there = pl.ds(pl.multiple_of(jnp.where(alone, share, n) * SUB, SUB), SUB)
                cols_ref[there, :] = cols_ref[there, :] + tree(down)

    def turn(i, carry):
        state, found = carry
        at = i * (2 * GROUP)
        state, later = steps(state)
        products(later, buffers[1])
        weigh(at, found, buffers[0])
        state, last = steps(state)
        products(last, buffers[0])
        weigh(at + GROUP, later, buffers[1])
        return state, last

    state, found = steps((jnp.int32(0), jnp.int32(0)))
    products(found, buffers[0])
    lax.fori_loop(0, lax.div(count + (2 * GROUP - 1), 2 * GROUP), turn, (state, found))


def spread_columns(out, index, rows):
    count, width = rows.shape
    turned = rows.T
    for a in range(count):
        out[index(a)] = jnp.broadcast_to(turned[:, a : a + 1], (width, width))


def lane_sums(parts, count, width):
    lanes = lax.broadcasted_iota(jnp.int32, (width, width), 1)
    turned = jnp.zeros((width, width), jnp.float32)
    for a in range(count):
        turned = jnp.where(lanes == a, jnp.sum(parts[a], axis=1, keepdims=True), turned)
    return turned.T[:count]


def sub_sums(cols):
    return jnp.sum(cols[...].reshape(-1, SUB, cols.shape[1]), axis=1)


def alive_rows(meta, share, width):
    return lax.broadcasted_iota(jnp.int32, (share, width), 0) < meta[0]


def prepare(
    counts, densities, position_in, phase_in, right_side_in, table_in, lists_in,
    meta, table, hood, near, density, source, first_swap, second_swap, lists, phase, right_side, sems
):
    share, width = source.shape
    capacity = phase.shape[0]
    body_rows = pl.ds(share, capacity)
    copies = [
        pltpu.make_async_copy(phase_in, phase, sems.at[0]),
        pltpu.make_async_copy(position_in, hood.at[pl.ds(0, 3), body_rows, :], sems.at[1]),
        pltpu.make_async_copy(right_side_in, right_side, sems.at[2]),
        pltpu.make_async_copy(table_in, table, sems.at[3]),
        pltpu.make_async_copy(lists_in, lists, sems.at[4]),
    ]
    for copy in copies:
        copy.start()
    piece, column = lax.axis_index("piece"), lax.axis_index("col")
    filled = counts[piece]
    filled_before = counts[jnp.maximum(piece - 1, 0)]
    before = jnp.int32(0)
    total = jnp.int32(0)
    for p in range(counts.shape[0]):
        before = before + jnp.where(p < piece, counts[p], 0)
        total = total + counts[p]
    meta[0] = jnp.clip(filled - column * share, 0, share)
    meta[1] = before + column * share
    meta[2] = total
    meta[3] = column * share
    meta[4] = filled
    meta[5] = filled_before
    own_rows = pl.ds(pl.multiple_of(share + column * share, SUB), share)
    copies[0].wait()
    labels = phase[...]
    whole = sum(jnp.where(labels == k, densities[k], 0.0) for k in range(densities.shape[0]))
    hood[3, body_rows, :] = whole * (width / 2.0)
    density[...] = hood[3, own_rows, :] * (2.0 / width)
    copies[1].wait()
    even = lax.rem(piece, 2) == 0
    for k in range(4):
        tail, head = hood[k, pl.ds(filled, share), :], hood[k, share : 2 * share, :]
        first_swap[k] = jnp.where(even, tail, head)
        second_swap[k] = jnp.where(even, head, tail)
        near[k, 0:share, :] = hood[k, own_rows, :]
    for copy in copies[2:]:
        copy.wait()
    source[...] = jnp.where(alive_rows(meta, share, width), right_side[...], 0.0)


def finish_tiles(tiles, end):
    for t in range(TURN):
        tiles[end + t] = jnp.zeros(tiles.shape[1:], jnp.float32)


def build_inner(
    meta, table, near, plan, outer_runs, tiles, sides, middles, weights, rows_ref, cols_ref, self_ref,
    inner_runs, *buffers,
):
    share, width = weights.shape[:2]
    chunks = pieces_of(width)
    write_runs(meta, table, plan, inner_runs, outer_runs, share)
    for k in range(3):
        first = near[k, 0:share, 0:1]
        middles[k] = jnp.broadcast_to(jnp.floor(first) + 0.5, (share, width))
    parts = lax.broadcasted_iota(jnp.int32, (width, width), 1) < 6 * SUB
    for a in range(share):
        here = slice(a, a + 1)
        centred = [wide(near[k, here, :] - middles[k, here, :]) for k in range(3)]
        turned = own_side(centred).T
        sides[0, a] = turned.astype(jnp.bfloat16)
        sides[1, a] = jnp.where(parts, pltpu.roll(turned, SUB // 2, 1), turned).astype(jnp.bfloat16)
    spread_columns(weights, lambda a: a, near[3, 0:share, :])
    cols_ref[...] = jnp.zeros_like(cols_ref)
    rows_ref[...] = jnp.zeros_like(rows_ref)
    count = plan[share * FIELDS]
    flat_tiles(
        count, inner_runs, plan[share * FIELDS + 2], table, sides, middles, weights,
        lambda k, n: near[k, pl.ds(n, 1), :], buffers, tiles, rows_ref, cols_ref,
    )
    finish_tiles(tiles, count)
    lane = lax.broadcasted_iota(jnp.int32, (SUB, width), 1)
    sublane = lax.broadcasted_iota(jnp.int32, (SUB, width), 0)

    def block(a, at):
        at = at + plan[a * FIELDS]
        down = [None] * 4
        for c, here in enumerate(chunks):
            tile = jnp.where(lane == sublane + c * SUB, 0.0, tiles[at, here, :])
            tiles[at, here, :] = tile
            gather(down, c, tile)
        self_ref[pl.ds(pl.multiple_of(a * SUB, SUB), SUB), :] = tree(down)
        return at + 1

    lax.fori_loop(0, meta[0], block, 0)


def count_listed(meta, lists, width):
    capacity = lists[0].shape[1]
    filled, filled_before = meta[4], meta[5]
    start = lax.axis_index("piece") * capacity
    steps = lax.broadcasted_iota(jnp.int32, (2 * REACH, capacity), 0)
    partial = [None] * 4
    row = 0
    for ref in lists:
        ids = ref[...]
        slot = ids - start
        gap = jnp.where(slot < 0, capacity - filled_before, jnp.where(slot >= capacity, filled - capacity, 0))
        away = slot - lax.broadcasted_iota(jnp.int32, ids.shape, 1) + gap
        away = jnp.where(ids < 0, -REACH, away) + REACH
        for k in range(ids.shape[0]):
            gather(partial, row, jnp.where(steps == away[k : k + 1], 1.0, 0.0))
            row += 1
    return jnp.concatenate([tree(partial), jnp.zeros((width - 2 * REACH, capacity), jnp.float32)], 0).T


def factor(times, a, n):
    lane = lax.broadcasted_iota(jnp.int32, (1, times.shape[1]), 1)
    return jnp.sum(jnp.where(lane == n - a + REACH, times[pl.ds(a, 1), :], 0.0), axis=1, keepdims=True)


def either(flag, run):
    @pl.when(flag == 0)
    def _():
        run(False)

    @pl.when(flag != 0)
    def _():
        run(True)


TAIL = 13


def build_outer(
    meta, table, plan, runs, around, first, second, density, source, tiles_in, sides, middles, weights,
    rows_ref, cols_ref, self_ref, *rest
):
    lists, rest = rest[:-TAIL], rest[-TAIL:]
    again_ref, tiles, diagonal_ref, precond_ref, times, alone_ref, hood, work, sums_ref, extra, all_times, *buffers = rest
    share, width = diagonal_ref.shape
    base, filled = meta[3], meta[4]
    even = lax.rem(lax.axis_index("piece"), 2) == 0
    for k in range(4):
        hood[k, 0:share, :] = jnp.where(even, second[k], first[k])
        hood[k, share:, :] = around[k, share:, :]
        hood[k, pl.ds(share + filled, share), :] = jnp.where(even, first[k], second[k])
    alive = alive_rows(meta, share, width)
    all_times[...] = count_listed(meta, lists, width)
    often = jnp.where(alive, all_times[pl.ds(pl.multiple_of(base, SUB), share), :], 0.0)
    times[...] = often
    lane = lax.broadcasted_iota(jnp.int32, (share, width), 1)
    again = jnp.max(jnp.where((lane == REACH) | (lane == 0), 0.0, often)) > 1.5
    again_ref[0] = again.astype(jnp.int32)


    work[...] = jnp.zeros_like(work)
    count = plan[share * FIELDS + 1]
    flat_tiles(
        count, runs, plan[share * FIELDS + 3], table, sides, middles, weights,
        lambda k, n: hood[k, pl.ds(base + share + n, 1), :], buffers, tiles, work, None,
    )
    finish_tiles(tiles, count)
    sums_ref[...] = lane_sums([rows_ref[a] + work[a] for a in range(share)], share, width) + sub_sums(cols_ref)[0:share]

    @pl.when(again)
    def _():
        extra[...] = jnp.zeros_like(extra)
        work[...] = jnp.zeros_like(work)

        def block(a, state):
            count, place_of = inner_range(plan, table, a)

            def inner(t, at):
                n = place_of(t)
                tile = tiles_in[at]
                work[a] = work[a] + tile * factor(times, a, n)
                there = pl.ds(n, 1)
                down = jnp.sum(tile, axis=0, keepdims=True)
                extra[there, :] = extra[there, :] + down * factor(times, n, a)
                return at + 1

            at = lax.fori_loop(0, count, inner, state[0]) + 1
            count, place_far = outer_range(plan, table, a)

            def outer(t, at):
                work[a] = work[a] + tiles[at] * factor(times, a, place_far(t))
                return at + 1

            return at, lax.fori_loop(0, count, outer, state[1])

        lax.fori_loop(0, meta[0], block, (0, 0))
        sums_ref[...] = lane_sums(work, share, width) + extra[...]

    alone = jnp.sum(jnp.where(lane == REACH, often, 0.0), axis=1, keepdims=True)
    alone_ref[...] = jnp.broadcast_to(alone, (share, width))
    pairs = jnp.where(alive, sums_ref[...] + sub_sums(self_ref) * alone, 0.0)
    diagonal = 1.0 / density[...] + pairs
    diagonal_ref[...] = diagonal
    precond_ref[...] = source[...] / diagonal


def apply_inner(meta, table, plan, again, field, alone, times, tiles, rows_ref, cols_ref, spread, near, lone, cols):
    share, width = field.shape
    chunks = pieces_of(width)
    near[0:share, :] = field[...]
    near[share:, :] = jnp.zeros((SUB, width), jnp.float32)
    lone[...] = field[...] * alone[...]
    spread_columns(spread, lambda a: a, field[...])
    cols[...] = jnp.zeros_like(cols)

    def run(weighted):
        def block(a, at):
            count, place_of = inner_range(plan, table, a)

            def fetch(t):
                n = jnp.where(t < count, place_of(t), share)
                return n, wide(near[pl.ds(n, 1), :])

            def pairs(fetched, carry):
                at, sums = carry
                if weighted:
                    fetched = [(n, value * factor(times, a, jnp.minimum(n, share - 1))) for n, value in fetched]
                down = [[None] * 2 for _ in fetched]
                result = []
                for c, (here, total) in enumerate(zip(chunks, sums)):
                    own = spread[a, here, :]
                    found = []
                    for t, (_, value) in enumerate(fetched):
                        tile = tiles[at + t, here, :]
                        gather(down[t], c, tile * own)
                        found.append(tile * value)
                    result.append(total + tree(found))
                for (n, _), partial in zip(fetched, down):
                    there = pl.ds(pl.multiple_of(n * SUB, SUB), SUB)
                    partial = tree(partial)
                    if weighted:
                        partial = partial * factor(times, jnp.minimum(n, share - 1), a)
                    cols[there, :] = cols[there, :] + partial
                return at + len(fetched), result

            zero = jnp.zeros((SUB, width), jnp.float32)
            _, sums = padded_sweep(count, fetch, pairs, (at, [zero] * len(chunks)))
            at = at + count
            value = wide(lone[pl.ds(a, 1), :])
            for here, old in zip(chunks, sums):
                rows_ref[a, here, :] = old + tiles[at, here, :] * value
            return at + 1

        lax.fori_loop(0, meta[0], block, 0)

    either(again[0], run)
    cols_ref[...] = cols[0 : share * SUB, :]


def apply_outer(meta, table, plan, again, received, times, tiles, rows_ref, cols_ref, work, hood):
    first, second, *ends = received
    columns = len(received)
    share, width = first.shape
    chunks = pieces_of(width)
    base, filled = meta[3], meta[4]
    column = lax.div(base, share)
    odd = lax.rem(column, 2) == 1
    before = jnp.where(odd, first[...], second[...])
    after = jnp.where(odd, second[...], first[...])
    own = 3 * share
    for c, end in enumerate(ends, 1):
        hood[pl.ds(own - meta[5] + c * share, share), :] = end[...]
    from_last = own - meta[5] + (columns - 1) * share
    hood[pl.ds(jnp.where(column == 0, from_last, own - share), share), :] = before
    hood[own + share : own + 2 * share, :] = after
    head = after
    for c, end in enumerate(ends, 1):
        head = jnp.where(column == c, end[...], head)
    hood[pl.ds(own + jnp.clip(filled - base, 0, 2 * share), share), :] = head
    nothing = hood.shape[0] - SUB
    hood[nothing:, :] = jnp.zeros((SUB, width), jnp.float32)

    def run(weighted):
        def block(a, at):
            count, place_of = outer_range(plan, table, a)

            def fetch(t):
                place = place_of(t)
                value = hood[pl.ds(jnp.where(t < count, own + place, nothing), 1), :]
                if weighted:
                    value = value * factor(times, a, place)
                return wide(value)

            def pairs(values, carry):
                at, sums = carry
                result = []
                for here, total in zip(chunks, sums):
                    result.append(total + tree([tiles[at + t, here, :] * value for t, value in enumerate(values)]))
                return at + len(values), result

            _, sums = padded_sweep(count, fetch, pairs, (at, [rows_ref[a, here, :] for here in chunks]))
            for here, values in zip(chunks, sums):
                work[a, here, :] = values
            return at + count

        lax.fori_loop(0, meta[0], block, 0)

    either(again[0], run)
    return jnp.where(alive_rows(meta, share, width), lane_sums(work, share, width) + sub_sums(cols_ref), 0.0)


def apply_first(meta, table, plan, again, diagonal, times, *rest):
    *received, tiles, rows_ref, cols_ref, spill_ref, scaled_ref, work, hood = rest
    spill = apply_outer(meta, table, plan, again, received, times, tiles, rows_ref, cols_ref, work, hood)
    spill_ref[...] = spill
    scaled_ref[...] = spill / diagonal[...]


def apply_second(meta, table, plan, again, source, precond, spill, scaled, times, *rest):
    *received, tiles, rows_ref, cols_ref, twice_ref, sums_ref, work, hood = rest
    twice = apply_outer(meta, table, plan, again, received, times, tiles, rows_ref, cols_ref, work, hood)
    twice_ref[...] = twice
    share, width = twice.shape
    lane = lax.broadcasted_iota(jnp.int32, (1, width), 1)
    sums = jnp.zeros((1, width), jnp.float32)
    pairs = ((source[...], precond[...]), (spill[...], precond[...]), (spill[...], scaled[...]), (scaled[...], twice))
    for k, (first, second) in enumerate(pairs):
        along = jnp.sum(first * second, axis=0, keepdims=True)
        sums = jnp.where(lane == k, jnp.sum(along, axis=1, keepdims=True), sums)
    sums_ref[...] = wide(sums)


def finish(source, precond, spill, scaled, twice, *rest):
    *parts, solution_ref, residual_ref = rest
    sums = tree([ref[...] for ref in parts])

    def pick(k):
        return sums[0:1, k : k + 1]

    weighted, cross, square, last = pick(0), pick(1), pick(2), pick(3)
    part = cross / weighted
    advance = 1.0 / (1.0 - part)
    keep = -part * advance
    weighted_next = advance * advance * (square - cross * part)
    bent = keep * keep * cross + 2.0 * keep * advance * square + advance * advance * last
    blend = weighted_next / weighted
    advance_next = weighted_next / (weighted_next - bent - blend * weighted_next / advance)
    residual = keep * source[...] + advance * spill[...]
    next_precond = keep * precond[...] + advance * scaled[...]
    direction = next_precond + blend * precond[...]
    image = residual - keep * spill[...] - advance * twice[...] + blend * (source[...] - spill[...])
    solution_ref[...] = advance * precond[...] + advance_next * direction
    residual_ref[...] = residual - advance_next * image


def held(array):
    return pltpu.with_memory_space_constraint(array, pltpu.VMEM)


def body(positions, phase, neighbours, counts, phase_density, right_side):
    capacity, width = phase.shape
    columns = lax.axis_size("col")
    pieces = lax.axis_size("piece")
    share = capacity // columns
    f32 = jnp.float32
    vector = jax.ShapeDtypeStruct((share, width), f32)
    few = jax.ShapeDtypeStruct((SUB, width), f32)
    message = jax.ShapeDtypeStruct((4, share, width), f32)
    most_inner, most_outer = tile_bounds(share)
    inner_tiles = pltpu.VMEM((most_inner + 2 * GROUP, width, width), f32)
    outer_tiles = pltpu.VMEM((most_outer + 2 * GROUP, width, width), f32)
    ahead = pltpu.VMEM((GROUP, width, width), f32)
    square_more = pltpu.VMEM((share + 1, width, width), f32)
    narrow_more = pltpu.VMEM(((share + 1) * SUB, width), f32)
    square = pltpu.VMEM((share, width, width), f32)
    narrow = pltpu.VMEM((share * SUB, width), f32)
    table = jnp.asarray(FLAT)

    def call(kernel, args, outs, scratch=(), work=0, scalars=2, far=0, **more):
        return pl.pallas_call(
            kernel,
            out_shape=outs,
            in_specs=[SMEM] * scalars + [HBM] * far + [VMEM] * (len(args) - scalars - far),
            out_specs=[SMEM if getattr(o, "memory_space", None) == pltpu.SMEM else VMEM for o in outs],
            scratch_shapes=scratch,
            compiler_params=LIMIT,
            cost_estimate=pl.CostEstimate(flops=work * width * width, bytes_accessed=0, transcendentals=0),
            name=kernel.__name__,
            **more,
        )(*args)

    def swap(values, axis, step):
        return lax.ppermute(values, axis, [(i, i ^ step) for i in range(lax.axis_size(axis))])

    def away(array):
        return pltpu.with_memory_space_constraint(array, pltpu.HBM)

    around = jax.ShapeDtypeStruct((4, capacity + 2 * share, width), f32)
    near = jax.ShapeDtypeStruct((4, 2 * share, width), f32)
    far = [away(array) for array in (positions, phase, right_side, table, neighbours.T)]
    meta, table, around, near, density, source, first, second, own_lists = call(
        prepare,
        (away(counts), away(phase_density), *far),
        [pltpu.SMEM((8,), jnp.int32), pltpu.SMEM(table.shape, jnp.int32), around, near, vector, vector, message, message,
         jax.ShapeDtypeStruct(far[-1].shape, jnp.int32)],
        [pltpu.VMEM(phase.shape, jnp.int32), pltpu.VMEM((share, width), f32), pltpu.SemaphoreType.DMA((5,))],
        far=len(far),
    )
    meta, table = (pltpu.with_memory_space_constraint(array, pltpu.SMEM) for array in (meta, table))
    first = lax.ppermute(first, "piece", [(i, i ^ 1) for i in range(pieces)])
    axes = ("piece", "col")
    device = [(p, c) for p in range(pieces) for c in range(columns)]
    partner = [(p + (1 if p % 2 else -1), c) for p, c in device]
    partner = [(q, d) if 0 <= q < pieces else (p, c ^ 1) for (q, d), (p, c) in zip(partner, device)]
    second = lax.ppermute(second, axes, [(i, q * columns + d) for i, (q, d) in enumerate(partner)])

    col_steps = [(1 << k) | 1 for k in range(columns.bit_length() - 1)]
    lists = [own_lists]
    for step in col_steps:
        known = lists[0] if len(lists) == 1 else jnp.concatenate(lists, 0)
        lists = [known, swap(known, "col", step)]

    plan, runs, tiles_in, sides, middles, weights, rows, cols, selfs = call(
        build_inner,
        (meta, table, near),
        [pltpu.SMEM((share * FIELDS + 4,), jnp.int32), pltpu.SMEM((6 * share + 3,), jnp.int32), inner_tiles,
         pltpu.VMEM((2, share, width, width), jnp.bfloat16), pltpu.VMEM((3, share, width), f32), square,
         square_more, narrow_more, narrow],
        [pltpu.SMEM((3 * share + 3,), jnp.int32), ahead, ahead],
        16 * most_inner,
    )
    plan, runs = (pltpu.with_memory_space_constraint(array, pltpu.SMEM) for array in (plan, runs))
    again, tiles_out, diagonal, precond, times, alone = call(
        build_outer,
        (meta, table, plan, runs, around, first, second, density, source,
         held(tiles_in), held(sides), held(middles), held(weights), held(rows), held(cols), held(selfs), *lists),
        [pltpu.SMEM((1,), jnp.int32), outer_tiles, vector, vector, vector, vector],
        [pltpu.VMEM((4, capacity + 2 * share, width), f32), square_more]
        + [pltpu.VMEM((share, width), f32)] * 2 + [pltpu.VMEM((capacity, width), f32), ahead, ahead],
        16 * most_outer,
        scalars=4,
    )
    again = pltpu.with_memory_space_constraint(again, pltpu.SMEM)

    def inner(field):
        return call(
            apply_inner,
            (meta, table, plan, again, field, alone, times, held(tiles_in)),
            [square, narrow],
            [pltpu.VMEM((share, width, width), f32), pltpu.VMEM((share + SUB, width), f32), pltpu.VMEM((share, width), f32),
             pltpu.VMEM(((share + 1) * SUB, width), f32)],
            4 * most_inner,
            scalars=4,
        )

    def exchange(field):
        count = pieces * columns
        swaps = [[i ^ 1 for i in range(count)], [i - 1 if i % 2 == 0 else i + 1 for i in range(count)]]
        swaps[1][0], swaps[1][-1] = count - 1, 0
        for c in range(1, columns - 1):
            to = {}
            for p in range(pieces - 1):
                low, high = p * columns + c, (p + 1) * columns
                to[low], to[high] = high, low
            spare = {c % (columns - 1) + 1: [0], (c + 1) % (columns - 1) + 1: [(pieces - 1) * columns + c]}
            for p in range(0, pieces, 2):
                for d in range(1, columns):
                    if d != c:
                        ring = [p * columns + d, (p + 1) * columns + d]
                        ring += spare.get(d, []) if p == (0 if spare.get(d) == [0] else pieces - 2) else []
                        to.update(zip(ring, ring[1:] + ring[:1]))
            swaps.append([to[i] for i in range(count)])
        return [lax.ppermute(field, axes, list(enumerate(to))) for to in swaps]

    scratch = [pltpu.VMEM((share, width, width), f32), pltpu.VMEM((8 * share, width), f32)]

    received = exchange(precond)
    rows, cols = inner(precond)
    spill, scaled = call(
        apply_first,
        (meta, table, plan, again, diagonal, times, *received, held(tiles_out), held(rows), held(cols)),
        [vector, vector],
        scratch,
        2 * most_outer,
        scalars=4,
    )

    received = exchange(scaled)
    rows, cols = inner(scaled)
    twice, sums = call(
        apply_second,
        (meta, table, plan, again, source, precond, spill, scaled, times, *received, held(tiles_out), held(rows), held(cols)),
        [vector, few],
        scratch,
        2 * most_outer,
        scalars=4,
    )

    def together(values, axis, low, size):
        return tree([values] + [swap(values, axis, low * k) for k in range(1, size)])

    sums = together(sums, "piece", 1, 2)
    sums = together(sums, "col", 1, columns)
    step = 2
    while pieces // step > 4:
        sums = together(sums, "piece", step, 4)
        step *= 4
    others = [swap(sums, "piece", step * k) for k in range(1, pieces // step)]

    return tuple(call(
        finish,
        (source, precond, spill, scaled, twice, sums, *others),
        [vector, vector],
        scalars=0,
    ))


def solution(mesh):
    placed = (
        P(None, "piece", None),
        P("piece", None),
        P("piece", "col"),
        P(),
        P(),
        P(("piece", "col"), None),
    )
    return jax.shard_map(
        body,
        mesh=mesh,
        in_specs=placed,
        out_specs=(P(("piece", "col"), None), P(("piece", "col"), None)),
        check_vma=False,
    )
```

```python
import jax
import jax.numpy as jnp
import numpy as np
from jax import lax
from jax.experimental import pallas as pl
from jax.experimental.pallas import tpu as pltpu
from jax.sharding import PartitionSpec as P

ITERS = 2
SIDE = 4
LAYER = SIDE * SIDE
REACH = 2 * LAYER
SUB = 8
VMEM = pl.BlockSpec(memory_space=pltpu.VMEM)
SMEM = pl.BlockSpec(memory_space=pltpu.SMEM)
HBM = pl.BlockSpec(memory_space=pltpu.HBM)


def stencil_tables():
    levels = SIDE.bit_length() - 1

    def cell(code):
        across = sum((code >> (2 * level) & 1) << level for level in range(levels))
        along = sum((code >> (2 * level + 1) & 1) << level for level in range(levels))
        return across, along

    place = {cell(code): code for code in range(LAYER)}
    rows = []
    for code in range(LAYER):
        across, along = cell(code)
        rows.append(
            sorted(
                step_z * LAYER + place[across + step_x, along + step_y] - code
                for step_z in (-1, 0, 1)
                for step_y in (-1, 0, 1)
                for step_x in (-1, 0, 1)
                if (across + step_x, along + step_y) in place
            )
        )
    longest = max(len(row) for row in rows)
    offsets = np.zeros((LAYER, longest), np.int32)
    below = np.zeros((LAYER, 2 * REACH + 1), np.int32)
    for code, row in enumerate(rows):
        offsets[code, : len(row)] = row
        for t in range(-REACH, REACH + 1):
            below[code, t + REACH] = sum(offset < t for offset in row)
    return offsets, below


OFFSETS, BELOW = stencil_tables()
WIDEST = OFFSETS.shape[1]
TABLE = np.concatenate([OFFSETS, BELOW], 1)
STRIDE = TABLE.shape[1]
FLAT = np.concatenate([TABLE.reshape(-1), np.zeros(8, np.int32)])
LIMIT = pltpu.CompilerParams(vmem_limit_bytes=8 * 1024 * 1024)


def tile_bounds(share):
    inner = outer = 0
    for first in range(LAYER):
        for live in range(1, share + 1):
            near = far = 0
            for a in range(live):
                code = (first + a) % LAYER
                row = [int(o) for o in OFFSETS[code][: BELOW[code, -1]]]
                near += sum(0 <= a + o and o <= 0 for o in row)
                far += sum(a + o < 0 or a + o >= live for o in row)
            inner, outer = max(inner, near), max(outer, far)
    return inner, outer


def rank(table, code, t):
    return table[code * STRIDE + jnp.clip(t, -REACH, REACH) + REACH + WIDEST]


FIELDS = 6


def write_plan(meta, table, plan, a):
    code = lax.bitwise_and(meta[1] + a, LAYER - 1)
    place = meta[1] + a
    low, split, middle = rank(table, code, -place), rank(table, code, -a), rank(table, code, 0)
    resume, high = rank(table, code, meta[0] - a), rank(table, code, meta[2] - place)
    row = code * STRIDE
    ahead = split - low
    plan[a * FIELDS] = middle - split
    plan[a * FIELDS + 1] = row + split
    plan[a * FIELDS + 2] = ahead + jnp.maximum(high - resume, 0)
    plan[a * FIELDS + 3] = ahead
    plan[a * FIELDS + 4] = row + low
    plan[a * FIELDS + 5] = row + resume - ahead


def write_run(runs, at, a, start, count):
    runs[3 * at], runs[3 * at + 1], runs[3 * at + 2] = a, start, count
    return at + (count > 0).astype(jnp.int32)


def write_runs(meta, table, plan, inner_runs, outer_runs, share):
    inner = outer = total = far = jnp.int32(0)
    for a in range(share):
        write_plan(meta, table, plan, a)
        alive = a < meta[0]
        count, start, count_far, ahead, start_far, start_after = (plan[a * FIELDS + k] for k in range(FIELDS))
        inner = write_run(inner_runs, inner, a, start, jnp.where(alive, count + 1, 0))
        outer = write_run(outer_runs, outer, a, start_far, jnp.where(alive, ahead, 0))
        outer = write_run(outer_runs, outer, a, start_after + ahead, jnp.where(alive, count_far - ahead, 0))
        total = total + jnp.where(alive, count + 1, 0)
        far = far + jnp.where(alive, count_far, 0)
    for runs, at in ((inner_runs, inner), (outer_runs, outer)):
        write_run(runs, at, share, len(FLAT) - 8, jnp.int32(1))
    plan[share * FIELDS] = total
    plan[share * FIELDS + 1] = far
    plan[share * FIELDS + 2] = inner
    plan[share * FIELDS + 3] = outer


def inner_range(plan, table, a):
    start = plan[a * FIELDS + 1]
    return plan[a * FIELDS], lambda t: a + table[start + t]


def outer_range(plan, table, a):
    ahead, start, start_after = (plan[a * FIELDS + k] for k in (3, 4, 5))
    return plan[a * FIELDS + 2], lambda t: a + table[t + jnp.where(t < ahead, start, start_after)]


TURN = 3


def padded_sweep(count, fetch, step, carry):
    def turn(i, state):
        carry, *now = state
        later = [fetch(TURN * (i + 1) + k) for k in range(TURN)]
        return step(now, carry), *later

    state = (carry, *(fetch(k) for k in range(TURN)))
    return lax.fori_loop(0, lax.div(count + (TURN - 1), TURN), turn, state)[0]


def tree(terms):
    while len(terms) > 1:
        terms = [a + b for a, b in zip(terms[::2], terms[1::2])] + terms[len(terms) // 2 * 2 :]
    return terms[0]


def gather(partial, c, term):
    if c < len(partial):
        partial[c] = term
    else:
        partial[c % len(partial)] = partial[c % len(partial)] + term


def pieces_of(width):
    return [slice(c * SUB, (c + 1) * SUB) for c in range(width // SUB)]


def wide(row):
    return jnp.broadcast_to(row, (SUB, row.shape[1]))


def three_parts(values):
    high = values.astype(jnp.bfloat16).astype(jnp.float32)
    rest = values - high
    middle = rest.astype(jnp.bfloat16).astype(jnp.float32)
    return high, middle, rest - middle


def stacked(rows):
    sublane = lax.broadcasted_iota(jnp.int32, rows[0].shape, 0)
    result = jnp.zeros(rows[0].shape, jnp.float32)
    for k, row in enumerate(rows):
        result = jnp.where(sublane == k, row, result)
    return result


def half_size(x):
    return 0.5 - (x[0] * x[0] + x[1] * x[1] + x[2] * x[2])


def own_side(x):
    high, middle, low = three_parts(stacked([2.0 * x[0], 2.0 * x[1], 2.0 * x[2], jnp.ones_like(x[0])]))
    sizes = stacked(list(three_parts(half_size(x))))
    width = sizes.shape[1]
    rest = jnp.zeros((width - 7 * SUB, width), jnp.float32)
    return jnp.concatenate([high, high, middle, middle, high, low, sizes, rest], 0)


def other_sides(first, second):
    rows = [*first, half_size(first), *second, half_size(second)]
    high, middle, low = three_parts(stacked(rows))
    width = high.shape[1]
    ones = jnp.where(lax.broadcasted_iota(jnp.int32, (2 * SUB, width), 0) < 3, 1.0, 0.0).astype(jnp.bfloat16)
    front = jnp.concatenate([high, middle], 0).astype(jnp.bfloat16)
    back = jnp.concatenate([low, high], 0).astype(jnp.bfloat16)
    rest = jnp.zeros((width - 8 * SUB, width), jnp.bfloat16)
    return jnp.concatenate([front, front, back, ones, rest], 0)


GROUP = 8


def flat_tiles(count, runs, most, table, sides, middles, weights, other_at, buffers, tiles, rows_ref, cols_ref):
    share, width = rows_ref.shape[0] - 1, rows_ref.shape[2]
    chunks = pieces_of(width)

    def steps(state):
        found = []
        for _ in range(GROUP):
            run, t = state
            a, start, size = (runs[3 * run + k] for k in range(3))
            found.append((a, a + table[start + t]))
            over = t + 1 >= size
            state = jnp.minimum(run + over.astype(jnp.int32), most), jnp.where(over, 0, t + 1)
        return state, found

    def other_of(a, n):
        here = pl.ds(a, 1)
        return [wide(other_at(c, n)) - wide(middles[c, here, :]) for c in range(3)]

    def products(found, ahead):
        for k in range(0, GROUP, 2):
            (a, n), (b, m) = ((jnp.minimum(a, share - 1), n) for a, n in found[k : k + 2])
            own = jnp.concatenate([sides[0, a], sides[1, b]], 0)
            both = jnp.dot(own, other_sides(other_of(a, n), other_of(b, m)), preferred_element_type=jnp.float32)
            ahead[k] = both[:width]
            ahead[k + 1] = both[width:]

    def weigh(at, found, ahead):
        for k, (a, n) in enumerate(found):
            alone = a == n
            row = jnp.where(alone, share, a)
            own = jnp.minimum(a, share - 1)
            other = wide(other_at(3, n))
            down = [None] * 4
            for c, here in enumerate(chunks):
                left = ahead[k, here, :]
                rest = jnp.maximum(left, 0.0)
                inverse = pltpu.reciprocal((1.01 - left) * (weights[own, here, :] + other), approx=True)
                tile = rest * rest * inverse
                tiles[at + k, here, :] = tile
                rows_ref[row, here, :] = rows_ref[row, here, :] + tile
                if cols_ref is not None:
                    gather(down, c, tile)
            if cols_ref is not None:
                there = pl.ds(pl.multiple_of(jnp.where(alone, share, n) * SUB, SUB), SUB)
                cols_ref[there, :] = cols_ref[there, :] + tree(down)

    def turn(i, carry):
        state, found = carry
        at = i * (2 * GROUP)
        state, later = steps(state)
        products(later, buffers[1])
        weigh(at, found, buffers[0])
        state, last = steps(state)
        products(last, buffers[0])
        weigh(at + GROUP, later, buffers[1])
        return state, last

    state, found = steps((jnp.int32(0), jnp.int32(0)))
    products(found, buffers[0])
    lax.fori_loop(0, lax.div(count + (2 * GROUP - 1), 2 * GROUP), turn, (state, found))


def spread_columns(out, index, rows):
    count, width = rows.shape
    turned = rows.T
    for a in range(count):
        out[index(a)] = jnp.broadcast_to(turned[:, a : a + 1], (width, width))


def lane_sums(parts, count, width):
    lanes = lax.broadcasted_iota(jnp.int32, (width, width), 1)
    turned = jnp.zeros((width, width), jnp.float32)
    for a in range(count):
        turned = jnp.where(lanes == a, jnp.sum(parts[a], axis=1, keepdims=True), turned)
    return turned.T[:count]


def sub_sums(cols):
    return jnp.sum(cols[...].reshape(-1, SUB, cols.shape[1]), axis=1)


def alive_rows(meta, share, width):
    return lax.broadcasted_iota(jnp.int32, (share, width), 0) < meta[0]


def prepare(
    counts, densities, position_in, phase_in, right_side_in, table_in, lists_in,
    meta, table, hood, near, density, source, first_swap, second_swap, lists, phase, right_side, sems
):
    share, width = source.shape
    capacity = phase.shape[0]
    body_rows = pl.ds(share, capacity)
    copies = [
        pltpu.make_async_copy(phase_in, phase, sems.at[0]),
        pltpu.make_async_copy(position_in, hood.at[pl.ds(0, 3), body_rows, :], sems.at[1]),
        pltpu.make_async_copy(right_side_in, right_side, sems.at[2]),
        pltpu.make_async_copy(table_in, table, sems.at[3]),
        pltpu.make_async_copy(lists_in, lists, sems.at[4]),
    ]
    for copy in copies:
        copy.start()
    piece, column = lax.axis_index("piece"), lax.axis_index("col")
    filled = counts[piece]
    filled_before = counts[jnp.maximum(piece - 1, 0)]
    before = jnp.int32(0)
    total = jnp.int32(0)
    for p in range(counts.shape[0]):
        before = before + jnp.where(p < piece, counts[p], 0)
        total = total + counts[p]
    meta[0] = jnp.clip(filled - column * share, 0, share)
    meta[1] = before + column * share
    meta[2] = total
    meta[3] = column * share
    meta[4] = filled
    meta[5] = filled_before
    own_rows = pl.ds(pl.multiple_of(share + column * share, SUB), share)
    copies[0].wait()
    labels = phase[...]
    whole = sum(jnp.where(labels == k, densities[k], 0.0) for k in range(densities.shape[0]))
    hood[3, body_rows, :] = whole * (width / 2.0)
    density[...] = hood[3, own_rows, :] * (2.0 / width)
    copies[1].wait()
    even = lax.rem(piece, 2) == 0
    for k in range(4):
        tail, head = hood[k, pl.ds(filled, share), :], hood[k, share : 2 * share, :]
        first_swap[k] = jnp.where(even, tail, head)
        second_swap[k] = jnp.where(even, head, tail)
        near[k, 0:share, :] = hood[k, own_rows, :]
    for copy in copies[2:]:
        copy.wait()
    source[...] = jnp.where(alive_rows(meta, share, width), right_side[...], 0.0)


def finish_tiles(tiles, end):
    for t in range(TURN):
        tiles[end + t] = jnp.zeros(tiles.shape[1:], jnp.float32)


def build_inner(
    meta, table, near, plan, outer_runs, tiles, sides, middles, weights, rows_ref, cols_ref, self_ref,
    inner_runs, *buffers,
):
    share, width = weights.shape[:2]
    chunks = pieces_of(width)
    write_runs(meta, table, plan, inner_runs, outer_runs, share)
    for k in range(3):
        first = near[k, 0:share, 0:1]
        middles[k] = jnp.broadcast_to(jnp.floor(first) + 0.5, (share, width))
    parts = lax.broadcasted_iota(jnp.int32, (width, width), 1) < 6 * SUB
    for a in range(share):
        here = slice(a, a + 1)
        centred = [wide(near[k, here, :] - middles[k, here, :]) for k in range(3)]
        turned = own_side(centred).T
        sides[0, a] = turned.astype(jnp.bfloat16)
        sides[1, a] = jnp.where(parts, pltpu.roll(turned, SUB // 2, 1), turned).astype(jnp.bfloat16)
    spread_columns(weights, lambda a: a, near[3, 0:share, :])
    cols_ref[...] = jnp.zeros_like(cols_ref)
    rows_ref[...] = jnp.zeros_like(rows_ref)
    count = plan[share * FIELDS]
    flat_tiles(
        count, inner_runs, plan[share * FIELDS + 2], table, sides, middles, weights,
        lambda k, n: near[k, pl.ds(n, 1), :], buffers, tiles, rows_ref, cols_ref,
    )
    finish_tiles(tiles, count)
    lane = lax.broadcasted_iota(jnp.int32, (SUB, width), 1)
    sublane = lax.broadcasted_iota(jnp.int32, (SUB, width), 0)

    def block(a, at):
        at = at + plan[a * FIELDS]
        down = [None] * 4
        for c, here in enumerate(chunks):
            tile = jnp.where(lane == sublane + c * SUB, 0.0, tiles[at, here, :])
            tiles[at, here, :] = tile
            gather(down, c, tile)
        self_ref[pl.ds(pl.multiple_of(a * SUB, SUB), SUB), :] = tree(down)
        return at + 1

    lax.fori_loop(0, meta[0], block, 0)


def count_listed(meta, lists, width):
    capacity = lists[0].shape[1]
    filled, filled_before = meta[4], meta[5]
    start = lax.axis_index("piece") * capacity
    steps = lax.broadcasted_iota(jnp.int32, (2 * REACH, capacity), 0)
    partial = [None] * 4
    row = 0
    for ref in lists:
        ids = ref[...]
        slot = ids - start
        gap = jnp.where(slot < 0, capacity - filled_before, jnp.where(slot >= capacity, filled - capacity, 0))
        away = slot - lax.broadcasted_iota(jnp.int32, ids.shape, 1) + gap
        away = jnp.where(ids < 0, -REACH, away) + REACH
        for k in range(ids.shape[0]):
            gather(partial, row, jnp.where(steps == away[k : k + 1], 1.0, 0.0))
            row += 1
    return jnp.concatenate([tree(partial), jnp.zeros((width - 2 * REACH, capacity), jnp.float32)], 0).T


def factor(times, a, n):
    lane = lax.broadcasted_iota(jnp.int32, (1, times.shape[1]), 1)
    return jnp.sum(jnp.where(lane == n - a + REACH, times[pl.ds(a, 1), :], 0.0), axis=1, keepdims=True)


def either(flag, run):
    @pl.when(flag == 0)
    def _():
        run(False)

    @pl.when(flag != 0)
    def _():
        run(True)


TAIL = 13


def build_outer(
    meta, table, plan, runs, around, first, second, density, source, tiles_in, sides, middles, weights,
    rows_ref, cols_ref, self_ref, *rest
):
    lists, rest = rest[:-TAIL], rest[-TAIL:]
    again_ref, tiles, diagonal_ref, precond_ref, times, alone_ref, hood, work, sums_ref, extra, all_times, *buffers = rest
    share, width = diagonal_ref.shape
    base, filled = meta[3], meta[4]
    even = lax.rem(lax.axis_index("piece"), 2) == 0
    for k in range(4):
        hood[k, 0:share, :] = jnp.where(even, second[k], first[k])
        hood[k, share:, :] = around[k, share:, :]
        hood[k, pl.ds(share + filled, share), :] = jnp.where(even, first[k], second[k])
    alive = alive_rows(meta, share, width)
    all_times[...] = count_listed(meta, lists, width)
    often = jnp.where(alive, all_times[pl.ds(pl.multiple_of(base, SUB), share), :], 0.0)
    times[...] = often
    lane = lax.broadcasted_iota(jnp.int32, (share, width), 1)
    again = jnp.max(jnp.where((lane == REACH) | (lane == 0), 0.0, often)) > 1.5
    again_ref[0] = again.astype(jnp.int32)


    work[...] = jnp.zeros_like(work)
    count = plan[share * FIELDS + 1]
    flat_tiles(
        count, runs, plan[share * FIELDS + 3], table, sides, middles, weights,
        lambda k, n: hood[k, pl.ds(base + share + n, 1), :], buffers, tiles, work, None,
    )
    finish_tiles(tiles, count)
    sums_ref[...] = lane_sums([rows_ref[a] + work[a] for a in range(share)], share, width) + sub_sums(cols_ref)[0:share]

    @pl.when(again)
    def _():
        extra[...] = jnp.zeros_like(extra)
        work[...] = jnp.zeros_like(work)

        def block(a, state):
            count, place_of = inner_range(plan, table, a)

            def inner(t, at):
                n = place_of(t)
                tile = tiles_in[at]
                work[a] = work[a] + tile * factor(times, a, n)
                there = pl.ds(n, 1)
                down = jnp.sum(tile, axis=0, keepdims=True)
                extra[there, :] = extra[there, :] + down * factor(times, n, a)
                return at + 1

            at = lax.fori_loop(0, count, inner, state[0]) + 1
            count, place_far = outer_range(plan, table, a)

            def outer(t, at):
                work[a] = work[a] + tiles[at] * factor(times, a, place_far(t))
                return at + 1

            return at, lax.fori_loop(0, count, outer, state[1])

        lax.fori_loop(0, meta[0], block, (0, 0))
        sums_ref[...] = lane_sums(work, share, width) + extra[...]

    alone = jnp.sum(jnp.where(lane == REACH, often, 0.0), axis=1, keepdims=True)
    alone_ref[...] = jnp.broadcast_to(alone, (share, width))
    pairs = jnp.where(alive, sums_ref[...] + sub_sums(self_ref) * alone, 0.0)
    diagonal = 1.0 / density[...] + pairs
    diagonal_ref[...] = diagonal
    precond_ref[...] = source[...] / diagonal


def apply_inner(meta, table, plan, again, field, alone, times, tiles, rows_ref, cols_ref, spread, near, lone, cols):
    share, width = field.shape
    chunks = pieces_of(width)
    near[0:share, :] = field[...]
    near[share:, :] = jnp.zeros((SUB, width), jnp.float32)
    lone[...] = field[...] * alone[...]
    spread_columns(spread, lambda a: a, field[...])
    cols[...] = jnp.zeros_like(cols)

    def run(weighted):
        def block(a, at):
            count, place_of = inner_range(plan, table, a)

            def fetch(t):
                n = jnp.where(t < count, place_of(t), share)
                return n, wide(near[pl.ds(n, 1), :])

            def pairs(fetched, carry):
                at, sums = carry
                if weighted:
                    fetched = [(n, value * factor(times, a, jnp.minimum(n, share - 1))) for n, value in fetched]
                down = [[None] * 2 for _ in fetched]
                result = []
                for c, (here, total) in enumerate(zip(chunks, sums)):
                    own = spread[a, here, :]
                    found = []
                    for t, (_, value) in enumerate(fetched):
                        tile = tiles[at + t, here, :]
                        gather(down[t], c, tile * own)
                        found.append(tile * value)
                    result.append(total + tree(found))
                for (n, _), partial in zip(fetched, down):
                    there = pl.ds(pl.multiple_of(n * SUB, SUB), SUB)
                    partial = tree(partial)
                    if weighted:
                        partial = partial * factor(times, jnp.minimum(n, share - 1), a)
                    cols[there, :] = cols[there, :] + partial
                return at + len(fetched), result

            zero = jnp.zeros((SUB, width), jnp.float32)
            _, sums = padded_sweep(count, fetch, pairs, (at, [zero] * len(chunks)))
            at = at + count
            value = wide(lone[pl.ds(a, 1), :])
            for here, old in zip(chunks, sums):
                rows_ref[a, here, :] = old + tiles[at, here, :] * value
            return at + 1

        lax.fori_loop(0, meta[0], block, 0)

    either(again[0], run)
    cols_ref[...] = cols[0 : share * SUB, :]


def apply_outer(meta, table, plan, again, received, times, tiles, rows_ref, cols_ref, work, hood):
    first, second, *ends = received
    columns = len(received)
    share, width = first.shape
    chunks = pieces_of(width)
    base, filled = meta[3], meta[4]
    column = lax.div(base, share)
    odd = lax.rem(column, 2) == 1
    before = jnp.where(odd, first[...], second[...])
    after = jnp.where(odd, second[...], first[...])
    own = 3 * share
    for c, end in enumerate(ends, 1):
        hood[pl.ds(own - meta[5] + c * share, share), :] = end[...]
    from_last = own - meta[5] + (columns - 1) * share
    hood[pl.ds(jnp.where(column == 0, from_last, own - share), share), :] = before
    hood[own + share : own + 2 * share, :] = after
    head = after
    for c, end in enumerate(ends, 1):
        head = jnp.where(column == c, end[...], head)
    hood[pl.ds(own + jnp.clip(filled - base, 0, 2 * share), share), :] = head
    nothing = hood.shape[0] - SUB
    hood[nothing:, :] = jnp.zeros((SUB, width), jnp.float32)

    def run(weighted):
        def block(a, at):
            count, place_of = outer_range(plan, table, a)

            def fetch(t):
                place = place_of(t)
                value = hood[pl.ds(jnp.where(t < count, own + place, nothing), 1), :]
                if weighted:
                    value = value * factor(times, a, place)
                return wide(value)

            def pairs(values, carry):
                at, sums = carry
                result = []
                for here, total in zip(chunks, sums):
                    result.append(total + tree([tiles[at + t, here, :] * value for t, value in enumerate(values)]))
                return at + len(values), result

            _, sums = padded_sweep(count, fetch, pairs, (at, [rows_ref[a, here, :] for here in chunks]))
            for here, values in zip(chunks, sums):
                work[a, here, :] = values
            return at + count

        lax.fori_loop(0, meta[0], block, 0)

    either(again[0], run)
    return jnp.where(alive_rows(meta, share, width), lane_sums(work, share, width) + sub_sums(cols_ref), 0.0)


def apply_first(meta, table, plan, again, diagonal, times, *rest):
    *received, tiles, rows_ref, cols_ref, spill_ref, scaled_ref, work, hood = rest
    spill = apply_outer(meta, table, plan, again, received, times, tiles, rows_ref, cols_ref, work, hood)
    spill_ref[...] = spill
    scaled_ref[...] = spill / diagonal[...]


def apply_second(meta, table, plan, again, source, precond, spill, scaled, times, *rest):
    *received, tiles, rows_ref, cols_ref, twice_ref, sums_ref, work, hood = rest
    twice = apply_outer(meta, table, plan, again, received, times, tiles, rows_ref, cols_ref, work, hood)
    twice_ref[...] = twice
    share, width = twice.shape
    lane = lax.broadcasted_iota(jnp.int32, (1, width), 1)
    sums = jnp.zeros((1, width), jnp.float32)
    pairs = ((source[...], precond[...]), (spill[...], precond[...]), (spill[...], scaled[...]), (scaled[...], twice))
    for k, (first, second) in enumerate(pairs):
        along = jnp.sum(first * second, axis=0, keepdims=True)
        sums = jnp.where(lane == k, jnp.sum(along, axis=1, keepdims=True), sums)
    sums_ref[...] = wide(sums)


def finish(source, precond, spill, scaled, twice, *rest):
    *parts, solution_ref, residual_ref = rest
    sums = tree([ref[...] for ref in parts])

    def pick(k):
        return sums[0:1, k : k + 1]

    weighted, cross, square, last = pick(0), pick(1), pick(2), pick(3)
    part = cross / weighted
    advance = 1.0 / (1.0 - part)
    keep = -part * advance
    weighted_next = advance * advance * (square - cross * part)
    bent = keep * keep * cross + 2.0 * keep * advance * square + advance * advance * last
    blend = weighted_next / weighted
    advance_next = weighted_next / (weighted_next - bent - blend * weighted_next / advance)
    residual = keep * source[...] + advance * spill[...]
    next_precond = keep * precond[...] + advance * scaled[...]
    direction = next_precond + blend * precond[...]
    image = residual - keep * spill[...] - advance * twice[...] + blend * (source[...] - spill[...])
    solution_ref[...] = advance * precond[...] + advance_next * direction
    residual_ref[...] = residual - advance_next * image


def held(array):
    return pltpu.with_memory_space_constraint(array, pltpu.VMEM)


def body(positions, phase, neighbours, counts, phase_density, right_side):
    capacity, width = phase.shape
    columns = lax.axis_size("col")
    pieces = lax.axis_size("piece")
    share = capacity // columns
    f32 = jnp.float32
    vector = jax.ShapeDtypeStruct((share, width), f32)
    few = jax.ShapeDtypeStruct((SUB, width), f32)
    message = jax.ShapeDtypeStruct((4, share, width), f32)
    most_inner, most_outer = tile_bounds(share)
    inner_tiles = pltpu.VMEM((most_inner + 2 * GROUP, width, width), f32)
    outer_tiles = pltpu.VMEM((most_outer + 2 * GROUP, width, width), f32)
    ahead = pltpu.VMEM((GROUP, width, width), f32)
    square_more = pltpu.VMEM((share + 1, width, width), f32)
    narrow_more = pltpu.VMEM(((share + 1) * SUB, width), f32)
    square = pltpu.VMEM((share, width, width), f32)
    narrow = pltpu.VMEM((share * SUB, width), f32)
    table = jnp.asarray(FLAT)

    def call(kernel, args, outs, scratch=(), work=0, scalars=2, far=0, **more):
        return pl.pallas_call(
            kernel,
            out_shape=outs,
            in_specs=[SMEM] * scalars + [HBM] * far + [VMEM] * (len(args) - scalars - far),
            out_specs=[SMEM if getattr(o, "memory_space", None) == pltpu.SMEM else VMEM for o in outs],
            scratch_shapes=scratch,
            compiler_params=LIMIT,
            cost_estimate=pl.CostEstimate(flops=work * width * width, bytes_accessed=0, transcendentals=0),
            name=kernel.__name__,
            **more,
        )(*args)

    def swap(values, axis, step):
        return lax.ppermute(values, axis, [(i, i ^ step) for i in range(lax.axis_size(axis))])

    def away(array):
        return pltpu.with_memory_space_constraint(array, pltpu.HBM)

    around = jax.ShapeDtypeStruct((4, capacity + 2 * share, width), f32)
    near = jax.ShapeDtypeStruct((4, 2 * share, width), f32)
    far = [away(array) for array in (positions, phase, right_side, table, neighbours.T)]
    meta, table, around, near, density, source, first, second, own_lists = call(
        prepare,
        (away(counts), away(phase_density), *far),
        [pltpu.SMEM((8,), jnp.int32), pltpu.SMEM(table.shape, jnp.int32), around, near, vector, vector, message, message,
         jax.ShapeDtypeStruct(far[-1].shape, jnp.int32)],
        [pltpu.VMEM(phase.shape, jnp.int32), pltpu.VMEM((share, width), f32), pltpu.SemaphoreType.DMA((5,))],
        far=len(far),
    )
    meta, table = (pltpu.with_memory_space_constraint(array, pltpu.SMEM) for array in (meta, table))
    first = lax.ppermute(first, "piece", [(i, i ^ 1) for i in range(pieces)])
    axes = ("piece", "col")
    device = [(p, c) for p in range(pieces) for c in range(columns)]
    partner = [(p + (1 if p % 2 else -1), c) for p, c in device]
    partner = [(q, d) if 0 <= q < pieces else (p, c ^ 1) for (q, d), (p, c) in zip(partner, device)]
    second = lax.ppermute(second, axes, [(i, q * columns + d) for i, (q, d) in enumerate(partner)])

    col_steps = [(1 << k) | 1 for k in range(columns.bit_length() - 1)]
    lists = [own_lists]
    for step in col_steps:
        known = lists[0] if len(lists) == 1 else jnp.concatenate(lists, 0)
        lists = [known, swap(known, "col", step)]

    plan, runs, tiles_in, sides, middles, weights, rows, cols, selfs = call(
        build_inner,
        (meta, table, near),
        [pltpu.SMEM((share * FIELDS + 4,), jnp.int32), pltpu.SMEM((6 * share + 3,), jnp.int32), inner_tiles,
         pltpu.VMEM((2, share, width, width), jnp.bfloat16), pltpu.VMEM((3, share, width), f32), square,
         square_more, narrow_more, narrow],
        [pltpu.SMEM((3 * share + 3,), jnp.int32), ahead, ahead],
        16 * most_inner,
    )
    plan, runs = (pltpu.with_memory_space_constraint(array, pltpu.SMEM) for array in (plan, runs))
    again, tiles_out, diagonal, precond, times, alone = call(
        build_outer,
        (meta, table, plan, runs, around, first, second, density, source,
         held(tiles_in), held(sides), held(middles), held(weights), held(rows), held(cols), held(selfs), *lists),
        [pltpu.SMEM((1,), jnp.int32), outer_tiles, vector, vector, vector, vector],
        [pltpu.VMEM((4, capacity + 2 * share, width), f32), square_more]
        + [pltpu.VMEM((share, width), f32)] * 2 + [pltpu.VMEM((capacity, width), f32), ahead, ahead],
        16 * most_outer,
        scalars=4,
    )
    again = pltpu.with_memory_space_constraint(again, pltpu.SMEM)

    def inner(field):
        return call(
            apply_inner,
            (meta, table, plan, again, field, alone, times, held(tiles_in)),
            [square, narrow],
            [pltpu.VMEM((share, width, width), f32), pltpu.VMEM((share + SUB, width), f32), pltpu.VMEM((share, width), f32),
             pltpu.VMEM(((share + 1) * SUB, width), f32)],
            4 * most_inner,
            scalars=4,
        )

    def exchange(field):
        count = pieces * columns
        swaps = [[i ^ 1 for i in range(count)], [i - 1 if i % 2 == 0 else i + 1 for i in range(count)]]
        swaps[1][0], swaps[1][-1] = count - 1, 0
        for c in range(1, columns - 1):
            to = {}
            for p in range(pieces - 1):
                low, high = p * columns + c, (p + 1) * columns
                to[low], to[high] = high, low
            spare = {c % (columns - 1) + 1: [0], (c + 1) % (columns - 1) + 1: [(pieces - 1) * columns + c]}
            for p in range(0, pieces, 2):
                for d in range(1, columns):
                    if d != c:
                        ring = [p * columns + d, (p + 1) * columns + d]
                        ring += spare.get(d, []) if p == (0 if spare.get(d) == [0] else pieces - 2) else []
                        to.update(zip(ring, ring[1:] + ring[:1]))
            swaps.append([to[i] for i in range(count)])
        return [lax.ppermute(field, axes, list(enumerate(to))) for to in swaps]

    scratch = [pltpu.VMEM((share, width, width), f32), pltpu.VMEM((8 * share, width), f32)]

    received = exchange(precond)
    rows, cols = inner(precond)
    spill, scaled = call(
        apply_first,
        (meta, table, plan, again, diagonal, times, *received, held(tiles_out), held(rows), held(cols)),
        [vector, vector],
        scratch,
        2 * most_outer,
        scalars=4,
    )

    received = exchange(scaled)
    rows, cols = inner(scaled)
    twice, sums = call(
        apply_second,
        (meta, table, plan, again, source, precond, spill, scaled, times, *received, held(tiles_out), held(rows), held(cols)),
        [vector, few],
        scratch,
        2 * most_outer,
        scalars=4,
    )

    def together(values, axis, low, size):
        return tree([values] + [swap(values, axis, low * k) for k in range(1, size)])

    sums = together(sums, "piece", 1, 2)
    sums = together(sums, "col", 1, columns)
    step = 2
    while pieces // step > 4:
        sums = together(sums, "piece", step, 4)
        step *= 4
    others = [swap(sums, "piece", step * k) for k in range(1, pieces // step)]

    return tuple(call(
        finish,
        (source, precond, spill, scaled, twice, sums, *others),
        [vector, vector],
        scalars=0,
    ))


def solution(mesh):
    placed = (
        P(None, "piece", None),
        P("piece", None),
        P("piece", "col"),
        P(),
        P(),
        P(("piece", "col"), None),
    )
    return jax.shard_map(
        body,
        mesh=mesh,
        in_specs=placed,
        out_specs=(P(("piece", "col"), None), P(("piece", "col"), None)),
        check_vma=False,
    )
```

```python
import jax
import jax.numpy as jnp
import numpy as np
from jax import lax
from jax.experimental import pallas as pl
from jax.experimental.pallas import tpu as pltpu
from jax.sharding import PartitionSpec as P

ITERS = 2
SIDE = 4
LAYER = SIDE * SIDE
REACH = 2 * LAYER
SUB = 8
VMEM = pl.BlockSpec(memory_space=pltpu.VMEM)
SMEM = pl.BlockSpec(memory_space=pltpu.SMEM)
HBM = pl.BlockSpec(memory_space=pltpu.HBM)


def stencil_tables():
    levels = SIDE.bit_length() - 1

    def cell(code):
        across = sum((code >> (2 * level) & 1) << level for level in range(levels))
        along = sum((code >> (2 * level + 1) & 1) << level for level in range(levels))
        return across, along

    place = {cell(code): code for code in range(LAYER)}
    rows = []
    for code in range(LAYER):
        across, along = cell(code)
        rows.append(
            sorted(
                step_z * LAYER + place[across + step_x, along + step_y] - code
                for step_z in (-1, 0, 1)
                for step_y in (-1, 0, 1)
                for step_x in (-1, 0, 1)
                if (across + step_x, along + step_y) in place
            )
        )
    longest = max(len(row) for row in rows)
    offsets = np.zeros((LAYER, longest), np.int32)
    below = np.zeros((LAYER, 2 * REACH + 1), np.int32)
    for code, row in enumerate(rows):
        offsets[code, : len(row)] = row
        for t in range(-REACH, REACH + 1):
            below[code, t + REACH] = sum(offset < t for offset in row)
    return offsets, below


OFFSETS, BELOW = stencil_tables()
WIDEST = OFFSETS.shape[1]
TABLE = np.concatenate([OFFSETS, BELOW], 1)
STRIDE = TABLE.shape[1]
FLAT = np.concatenate([TABLE.reshape(-1), np.zeros(8, np.int32)])
LIMIT = pltpu.CompilerParams(vmem_limit_bytes=8 * 1024 * 1024)


def tile_bounds(share):
    inner = outer = 0
    for first in range(LAYER):
        for live in range(1, share + 1):
            near = far = 0
            for a in range(live):
                code = (first + a) % LAYER
                row = [int(o) for o in OFFSETS[code][: BELOW[code, -1]]]
                near += sum(0 <= a + o and o <= 0 for o in row)
                far += sum(a + o < 0 or a + o >= live for o in row)
            inner, outer = max(inner, near), max(outer, far)
    return inner, outer


def rank(table, code, t):
    return table[code * STRIDE + jnp.clip(t, -REACH, REACH) + REACH + WIDEST]


FIELDS = 6


def write_plan(meta, table, plan, a):
    code = lax.bitwise_and(meta[1] + a, LAYER - 1)
    place = meta[1] + a
    low, split, middle = rank(table, code, -place), rank(table, code, -a), rank(table, code, 0)
    resume, high = rank(table, code, meta[0] - a), rank(table, code, meta[2] - place)
    row = code * STRIDE
    ahead = split - low
    plan[a * FIELDS] = middle - split
    plan[a * FIELDS + 1] = row + split
    plan[a * FIELDS + 2] = ahead + jnp.maximum(high - resume, 0)
    plan[a * FIELDS + 3] = ahead
    plan[a * FIELDS + 4] = row + low
    plan[a * FIELDS + 5] = row + resume - ahead


def write_run(runs, at, a, start, count):
    runs[3 * at], runs[3 * at + 1], runs[3 * at + 2] = a, start, count
    return at + (count > 0).astype(jnp.int32)


def write_runs(meta, table, plan, inner_runs, outer_runs, share):
    inner = outer = total = far = jnp.int32(0)
    for a in range(share):
        write_plan(meta, table, plan, a)
        alive = a < meta[0]
        count, start, count_far, ahead, start_far, start_after = (plan[a * FIELDS + k] for k in range(FIELDS))
        inner = write_run(inner_runs, inner, a, start, jnp.where(alive, count + 1, 0))
        outer = write_run(outer_runs, outer, a, start_far, jnp.where(alive, ahead, 0))
        outer = write_run(outer_runs, outer, a, start_after + ahead, jnp.where(alive, count_far - ahead, 0))
        total = total + jnp.where(alive, count + 1, 0)
        far = far + jnp.where(alive, count_far, 0)
    for runs, at in ((inner_runs, inner), (outer_runs, outer)):
        write_run(runs, at, share, len(FLAT) - 8, jnp.int32(1))
    plan[share * FIELDS] = total
    plan[share * FIELDS + 1] = far
    plan[share * FIELDS + 2] = inner
    plan[share * FIELDS + 3] = outer


def inner_range(plan, table, a):
    start = plan[a * FIELDS + 1]
    return plan[a * FIELDS], lambda t: a + table[start + t]


def outer_range(plan, table, a):
    ahead, start, start_after = (plan[a * FIELDS + k] for k in (3, 4, 5))
    return plan[a * FIELDS + 2], lambda t: a + table[t + jnp.where(t < ahead, start, start_after)]


TURN = 3


def padded_sweep(count, fetch, step, carry):
    def turn(i, state):
        carry, *now = state
        later = [fetch(TURN * (i + 1) + k) for k in range(TURN)]
        return step(now, carry), *later

    state = (carry, *(fetch(k) for k in range(TURN)))
    return lax.fori_loop(0, lax.div(count + (TURN - 1), TURN), turn, state)[0]


def tree(terms):
    while len(terms) > 1:
        terms = [a + b for a, b in zip(terms[::2], terms[1::2])] + terms[len(terms) // 2 * 2 :]
    return terms[0]


def gather(partial, c, term):
    if c < len(partial):
        partial[c] = term
    else:
        partial[c % len(partial)] = partial[c % len(partial)] + term


def pieces_of(width):
    return [slice(c * SUB, (c + 1) * SUB) for c in range(width // SUB)]


def wide(row):
    return jnp.broadcast_to(row, (SUB, row.shape[1]))


def three_parts(values):
    high = values.astype(jnp.bfloat16).astype(jnp.float32)
    rest = values - high
    middle = rest.astype(jnp.bfloat16).astype(jnp.float32)
    return high, middle, rest - middle


def stacked(rows):
    sublane = lax.broadcasted_iota(jnp.int32, rows[0].shape, 0)
    result = jnp.zeros(rows[0].shape, jnp.float32)
    for k, row in enumerate(rows):
        result = jnp.where(sublane == k, row, result)
    return result


def half_size(x):
    return 0.5 - (x[0] * x[0] + x[1] * x[1] + x[2] * x[2])


def own_side(x):
    high, middle, low = three_parts(stacked([2.0 * x[0], 2.0 * x[1], 2.0 * x[2], jnp.ones_like(x[0])]))
    sizes = stacked(list(three_parts(half_size(x))))
    width = sizes.shape[1]
    rest = jnp.zeros((width - 7 * SUB, width), jnp.float32)
    return jnp.concatenate([high, high, middle, middle, high, low, sizes, rest], 0)


def other_sides(first, second):
    rows = [*first, half_size(first), *second, half_size(second)]
    high, middle, low = three_parts(stacked(rows))
    width = high.shape[1]
    ones = jnp.where(lax.broadcasted_iota(jnp.int32, (2 * SUB, width), 0) < 3, 1.0, 0.0).astype(jnp.bfloat16)
    front = jnp.concatenate([high, middle], 0).astype(jnp.bfloat16)
    back = jnp.concatenate([low, high], 0).astype(jnp.bfloat16)
    rest = jnp.zeros((width - 8 * SUB, width), jnp.bfloat16)
    return jnp.concatenate([front, front, back, ones, rest], 0)


GROUP = 8


def flat_tiles(count, runs, most, table, sides, middles, weights, other_at, buffers, tiles, rows_ref, cols_ref):
    share, width = rows_ref.shape[0] - 1, rows_ref.shape[2]
    chunks = pieces_of(width)

    def steps(state):
        found = []
        for _ in range(GROUP):
            run, t = state
            a, start, size = (runs[3 * run + k] for k in range(3))
            found.append((a, a + table[start + t]))
            over = t + 1 >= size
            state = jnp.minimum(run + over.astype(jnp.int32), most), jnp.where(over, 0, t + 1)
        return state, found

    def other_of(a, n):
        here = pl.ds(a, 1)
        return [wide(other_at(c, n)) - wide(middles[c, here, :]) for c in range(3)]

    def products(found, ahead):
        for k in range(0, GROUP, 2):
            (a, n), (b, m) = ((jnp.minimum(a, share - 1), n) for a, n in found[k : k + 2])
            own = jnp.concatenate([sides[0, a], sides[1, b]], 0)
            both = jnp.dot(own, other_sides(other_of(a, n), other_of(b, m)), preferred_element_type=jnp.float32)
            ahead[k] = both[:width]
            ahead[k + 1] = both[width:]

    def weigh(at, found, ahead):
        for k, (a, n) in enumerate(found):
            alone = a == n
            row = jnp.where(alone, share, a)
            own = jnp.minimum(a, share - 1)
            other = wide(other_at(3, n))
            down = [None] * 4
            for c, here in enumerate(chunks):
                left = ahead[k, here, :]
                rest = jnp.maximum(left, 0.0)
                inverse = pltpu.reciprocal((1.01 - left) * (weights[own, here, :] + other), approx=True)
                tile = rest * rest * inverse
                tiles[at + k, here, :] = tile
                rows_ref[row, here, :] = rows_ref[row, here, :] + tile
                if cols_ref is not None:
                    gather(down, c, tile)
            if cols_ref is not None:
                there = pl.ds(pl.multiple_of(jnp.where(alone, share, n) * SUB, SUB), SUB)
                cols_ref[there, :] = cols_ref[there, :] + tree(down)

    def turn(i, carry):
        state, found = carry
        at = i * (2 * GROUP)
        state, later = steps(state)
        products(later, buffers[1])
        weigh(at, found, buffers[0])
        state, last = steps(state)
        products(last, buffers[0])
        weigh(at + GROUP, later, buffers[1])
        return state, last

    state, found = steps((jnp.int32(0), jnp.int32(0)))
    products(found, buffers[0])
    lax.fori_loop(0, lax.div(count + (2 * GROUP - 1), 2 * GROUP), turn, (state, found))


def spread_columns(out, index, rows):
    count, width = rows.shape
    turned = rows.T
    for a in range(count):
        out[index(a)] = jnp.broadcast_to(turned[:, a : a + 1], (width, width))


def lane_sums(parts, count, width):
    lanes = lax.broadcasted_iota(jnp.int32, (width, width), 1)
    turned = jnp.zeros((width, width), jnp.float32)
    for a in range(count):
        turned = jnp.where(lanes == a, jnp.sum(parts[a], axis=1, keepdims=True), turned)
    return turned.T[:count]


def sub_sums(cols):
    return jnp.sum(cols[...].reshape(-1, SUB, cols.shape[1]), axis=1)


def alive_rows(meta, share, width):
    return lax.broadcasted_iota(jnp.int32, (share, width), 0) < meta[0]


def prepare(
    counts, densities, position_in, phase_in, right_side_in, table_in, lists_in,
    meta, table, hood, near, density, source, first_swap, second_swap, lists, phase, right_side, sems
):
    share, width = source.shape
    capacity = phase.shape[0]
    body_rows = pl.ds(share, capacity)
    copies = [
        pltpu.make_async_copy(phase_in, phase, sems.at[0]),
        pltpu.make_async_copy(position_in, hood.at[pl.ds(0, 3), body_rows, :], sems.at[1]),
        pltpu.make_async_copy(right_side_in, right_side, sems.at[2]),
        pltpu.make_async_copy(table_in, table, sems.at[3]),
        pltpu.make_async_copy(lists_in, lists, sems.at[4]),
    ]
    for copy in copies:
        copy.start()
    piece, column = lax.axis_index("piece"), lax.axis_index("col")
    filled = counts[piece]
    filled_before = counts[jnp.maximum(piece - 1, 0)]
    before = jnp.int32(0)
    total = jnp.int32(0)
    for p in range(counts.shape[0]):
        before = before + jnp.where(p < piece, counts[p], 0)
        total = total + counts[p]
    meta[0] = jnp.clip(filled - column * share, 0, share)
    meta[1] = before + column * share
    meta[2] = total
    meta[3] = column * share
    meta[4] = filled
    meta[5] = filled_before
    own_rows = pl.ds(pl.multiple_of(share + column * share, SUB), share)
    copies[0].wait()
    labels = phase[...]
    whole = sum(jnp.where(labels == k, densities[k], 0.0) for k in range(densities.shape[0]))
    hood[3, body_rows, :] = whole * (width / 2.0)
    density[...] = hood[3, own_rows, :] * (2.0 / width)
    copies[1].wait()
    even = lax.rem(piece, 2) == 0
    for k in range(4):
        tail, head = hood[k, pl.ds(filled, share), :], hood[k, share : 2 * share, :]
        first_swap[k] = jnp.where(even, tail, head)
        second_swap[k] = jnp.where(even, head, tail)
        near[k, 0:share, :] = hood[k, own_rows, :]
    for copy in copies[2:]:
        copy.wait()
    source[...] = jnp.where(alive_rows(meta, share, width), right_side[...], 0.0)


def finish_tiles(tiles, end):
    for t in range(TURN):
        tiles[end + t] = jnp.zeros(tiles.shape[1:], jnp.float32)


def build_inner(
    meta, table, near, plan, outer_runs, tiles, sides, middles, weights, rows_ref, cols_ref, self_ref,
    inner_runs, *buffers,
):
    share, width = weights.shape[:2]
    chunks = pieces_of(width)
    write_runs(meta, table, plan, inner_runs, outer_runs, share)
    for k in range(3):
        first = near[k, 0:share, 0:1]
        middles[k] = jnp.broadcast_to(jnp.floor(first) + 0.5, (share, width))
    parts = lax.broadcasted_iota(jnp.int32, (width, width), 1) < 6 * SUB
    for a in range(share):
        here = slice(a, a + 1)
        centred = [wide(near[k, here, :] - middles[k, here, :]) for k in range(3)]
        turned = own_side(centred).T
        sides[0, a] = turned.astype(jnp.bfloat16)
        sides[1, a] = jnp.where(parts, pltpu.roll(turned, SUB // 2, 1), turned).astype(jnp.bfloat16)
    spread_columns(weights, lambda a: a, near[3, 0:share, :])
    cols_ref[...] = jnp.zeros_like(cols_ref)
    rows_ref[...] = jnp.zeros_like(rows_ref)
    count = plan[share * FIELDS]
    flat_tiles(
        count, inner_runs, plan[share * FIELDS + 2], table, sides, middles, weights,
        lambda k, n: near[k, pl.ds(n, 1), :], buffers, tiles, rows_ref, cols_ref,
    )
    finish_tiles(tiles, count)
    lane = lax.broadcasted_iota(jnp.int32, (SUB, width), 1)
    sublane = lax.broadcasted_iota(jnp.int32, (SUB, width), 0)

    def block(a, at):
        at = at + plan[a * FIELDS]
        down = [None] * 4
        for c, here in enumerate(chunks):
            tile = jnp.where(lane == sublane + c * SUB, 0.0, tiles[at, here, :])
            tiles[at, here, :] = tile
            gather(down, c, tile)
        self_ref[pl.ds(pl.multiple_of(a * SUB, SUB), SUB), :] = tree(down)
        return at + 1

    lax.fori_loop(0, meta[0], block, 0)


def count_listed(meta, lists, width):
    capacity = lists[0].shape[1]
    filled, filled_before = meta[4], meta[5]
    start = lax.axis_index("piece") * capacity
    steps = lax.broadcasted_iota(jnp.int32, (2 * REACH, capacity), 0)
    partial = [None] * 4
    row = 0
    for ref in lists:
        ids = ref[...]
        slot = ids - start
        gap = jnp.where(slot < 0, capacity - filled_before, jnp.where(slot >= capacity, filled - capacity, 0))
        away = slot - lax.broadcasted_iota(jnp.int32, ids.shape, 1) + gap
        away = jnp.where(ids < 0, -REACH, away) + REACH
        for k in range(ids.shape[0]):
            gather(partial, row, jnp.where(steps == away[k : k + 1], 1.0, 0.0))
            row += 1
    return jnp.concatenate([tree(partial), jnp.zeros((width - 2 * REACH, capacity), jnp.float32)], 0).T


def factor(times, a, n):
    lane = lax.broadcasted_iota(jnp.int32, (1, times.shape[1]), 1)
    return jnp.sum(jnp.where(lane == n - a + REACH, times[pl.ds(a, 1), :], 0.0), axis=1, keepdims=True)


def either(flag, run):
    @pl.when(flag == 0)
    def _():
        run(False)

    @pl.when(flag != 0)
    def _():
        run(True)


TAIL = 13


def build_outer(
    meta, table, plan, runs, around, first, second, density, source, tiles_in, sides, middles, weights,
    rows_ref, cols_ref, self_ref, *rest
):
    lists, rest = rest[:-TAIL], rest[-TAIL:]
    again_ref, tiles, diagonal_ref, precond_ref, times, alone_ref, hood, work, sums_ref, extra, all_times, *buffers = rest
    share, width = diagonal_ref.shape
    base, filled = meta[3], meta[4]
    even = lax.rem(lax.axis_index("piece"), 2) == 0
    for k in range(4):
        hood[k, 0:share, :] = jnp.where(even, second[k], first[k])
        hood[k, share:, :] = around[k, share:, :]
        hood[k, pl.ds(share + filled, share), :] = jnp.where(even, first[k], second[k])
    alive = alive_rows(meta, share, width)
    all_times[...] = count_listed(meta, lists, width)
    often = jnp.where(alive, all_times[pl.ds(pl.multiple_of(base, SUB), share), :], 0.0)
    times[...] = often
    lane = lax.broadcasted_iota(jnp.int32, (share, width), 1)
    again = jnp.max(jnp.where((lane == REACH) | (lane == 0), 0.0, often)) > 1.5
    again_ref[0] = again.astype(jnp.int32)


    work[...] = jnp.zeros_like(work)
    count = plan[share * FIELDS + 1]
    flat_tiles(
        count, runs, plan[share * FIELDS + 3], table, sides, middles, weights,
        lambda k, n: hood[k, pl.ds(base + share + n, 1), :], buffers, tiles, work, None,
    )
    finish_tiles(tiles, count)
    sums_ref[...] = lane_sums([rows_ref[a] + work[a] for a in range(share)], share, width) + sub_sums(cols_ref)[0:share]

    @pl.when(again)
    def _():
        extra[...] = jnp.zeros_like(extra)
        work[...] = jnp.zeros_like(work)

        def block(a, state):
            count, place_of = inner_range(plan, table, a)

            def inner(t, at):
                n = place_of(t)
                tile = tiles_in[at]
                work[a] = work[a] + tile * factor(times, a, n)
                there = pl.ds(n, 1)
                down = jnp.sum(tile, axis=0, keepdims=True)
                extra[there, :] = extra[there, :] + down * factor(times, n, a)
                return at + 1

            at = lax.fori_loop(0, count, inner, state[0]) + 1
            count, place_far = outer_range(plan, table, a)

            def outer(t, at):
                work[a] = work[a] + tiles[at] * factor(times, a, place_far(t))
                return at + 1

            return at, lax.fori_loop(0, count, outer, state[1])

        lax.fori_loop(0, meta[0], block, (0, 0))
        sums_ref[...] = lane_sums(work, share, width) + extra[...]

    alone = jnp.sum(jnp.where(lane == REACH, often, 0.0), axis=1, keepdims=True)
    alone_ref[...] = jnp.broadcast_to(alone, (share, width))
    pairs = jnp.where(alive, sums_ref[...] + sub_sums(self_ref) * alone, 0.0)
    diagonal = 1.0 / density[...] + pairs
    diagonal_ref[...] = diagonal
    precond_ref[...] = source[...] / diagonal


def apply_inner(meta, table, plan, again, field, alone, times, tiles, rows_ref, cols_ref, spread, near, lone, cols):
    share, width = field.shape
    chunks = pieces_of(width)
    near[0:share, :] = field[...]
    near[share:, :] = jnp.zeros((SUB, width), jnp.float32)
    lone[...] = field[...] * alone[...]
    spread_columns(spread, lambda a: a, field[...])
    cols[...] = jnp.zeros_like(cols)

    def run(weighted):
        def block(a, at):
            count, place_of = inner_range(plan, table, a)

            def fetch(t):
                n = jnp.where(t < count, place_of(t), share)
                return n, wide(near[pl.ds(n, 1), :])

            def pairs(fetched, carry):
                at, sums = carry
                if weighted:
                    fetched = [(n, value * factor(times, a, jnp.minimum(n, share - 1))) for n, value in fetched]
                down = [[None] * 2 for _ in fetched]
                result = []
                for c, (here, total) in enumerate(zip(chunks, sums)):
                    own = spread[a, here, :]
                    found = []
                    for t, (_, value) in enumerate(fetched):
                        tile = tiles[at + t, here, :]
                        gather(down[t], c, tile * own)
                        found.append(tile * value)
                    result.append(total + tree(found))
                for (n, _), partial in zip(fetched, down):
                    there = pl.ds(pl.multiple_of(n * SUB, SUB), SUB)
                    partial = tree(partial)
                    if weighted:
                        partial = partial * factor(times, jnp.minimum(n, share - 1), a)
                    cols[there, :] = cols[there, :] + partial
                return at + len(fetched), result

            zero = jnp.zeros((SUB, width), jnp.float32)
            _, sums = padded_sweep(count, fetch, pairs, (at, [zero] * len(chunks)))
            at = at + count
            value = wide(lone[pl.ds(a, 1), :])
            for here, old in zip(chunks, sums):
                rows_ref[a, here, :] = old + tiles[at, here, :] * value
            return at + 1

        lax.fori_loop(0, meta[0], block, 0)

    either(again[0], run)
    cols_ref[...] = cols[0 : share * SUB, :]


def apply_outer(meta, table, plan, again, received, times, tiles, rows_ref, cols_ref, work, hood):
    first, second, *ends = received
    columns = len(received)
    share, width = first.shape
    chunks = pieces_of(width)
    base, filled = meta[3], meta[4]
    column = lax.div(base, share)
    odd = lax.rem(column, 2) == 1
    before = jnp.where(odd, first[...], second[...])
    after = jnp.where(odd, second[...], first[...])
    own = 3 * share
    for c, end in enumerate(ends, 1):
        hood[pl.ds(own - meta[5] + c * share, share), :] = end[...]
    from_last = own - meta[5] + (columns - 1) * share
    hood[pl.ds(jnp.where(column == 0, from_last, own - share), share), :] = before
    hood[own + share : own + 2 * share, :] = after
    head = after
    for c, end in enumerate(ends, 1):
        head = jnp.where(column == c, end[...], head)
    hood[pl.ds(own + jnp.clip(filled - base, 0, 2 * share), share), :] = head
    nothing = hood.shape[0] - SUB
    hood[nothing:, :] = jnp.zeros((SUB, width), jnp.float32)

    def run(weighted):
        def block(a, at):
            count, place_of = outer_range(plan, table, a)

            def fetch(t):
                place = place_of(t)
                value = hood[pl.ds(jnp.where(t < count, own + place, nothing), 1), :]
                if weighted:
                    value = value * factor(times, a, place)
                return wide(value)

            def pairs(values, carry):
                at, sums = carry
                result = []
                for here, total in zip(chunks, sums):
                    result.append(total + tree([tiles[at + t, here, :] * value for t, value in enumerate(values)]))
                return at + len(values), result

            _, sums = padded_sweep(count, fetch, pairs, (at, [rows_ref[a, here, :] for here in chunks]))
            for here, values in zip(chunks, sums):
                work[a, here, :] = values
            return at + count

        lax.fori_loop(0, meta[0], block, 0)

    either(again[0], run)
    return jnp.where(alive_rows(meta, share, width), lane_sums(work, share, width) + sub_sums(cols_ref), 0.0)


def apply_first(meta, table, plan, again, diagonal, times, *rest):
    *received, tiles, rows_ref, cols_ref, spill_ref, scaled_ref, work, hood = rest
    spill = apply_outer(meta, table, plan, again, received, times, tiles, rows_ref, cols_ref, work, hood)
    spill_ref[...] = spill
    scaled_ref[...] = spill / diagonal[...]


def apply_second(meta, table, plan, again, source, precond, spill, scaled, times, *rest):
    *received, tiles, rows_ref, cols_ref, twice_ref, sums_ref, work, hood = rest
    twice = apply_outer(meta, table, plan, again, received, times, tiles, rows_ref, cols_ref, work, hood)
    twice_ref[...] = twice
    share, width = twice.shape
    lane = lax.broadcasted_iota(jnp.int32, (1, width), 1)
    sums = jnp.zeros((1, width), jnp.float32)
    pairs = ((source[...], precond[...]), (spill[...], precond[...]), (spill[...], scaled[...]), (scaled[...], twice))
    for k, (first, second) in enumerate(pairs):
        along = jnp.sum(first * second, axis=0, keepdims=True)
        sums = jnp.where(lane == k, jnp.sum(along, axis=1, keepdims=True), sums)
    sums_ref[...] = wide(sums)


def finish(source, precond, spill, scaled, twice, *rest):
    *parts, solution_ref, residual_ref = rest
    sums = tree([ref[...] for ref in parts])

    def pick(k):
        return sums[0:1, k : k + 1]

    weighted, cross, square, last = pick(0), pick(1), pick(2), pick(3)
    part = cross / weighted
    advance = 1.0 / (1.0 - part)
    keep = -part * advance
    weighted_next = advance * advance * (square - cross * part)
    bent = keep * keep * cross + 2.0 * keep * advance * square + advance * advance * last
    blend = weighted_next / weighted
    advance_next = weighted_next / (weighted_next - bent - blend * weighted_next / advance)
    residual = keep * source[...] + advance * spill[...]
    next_precond = keep * precond[...] + advance * scaled[...]
    direction = next_precond + blend * precond[...]
    image = residual - keep * spill[...] - advance * twice[...] + blend * (source[...] - spill[...])
    solution_ref[...] = advance * precond[...] + advance_next * direction
    residual_ref[...] = residual - advance_next * image


def held(array):
    return pltpu.with_memory_space_constraint(array, pltpu.VMEM)


def body(positions, phase, neighbours, counts, phase_density, right_side):
    capacity, width = phase.shape
    columns = lax.axis_size("col")
    pieces = lax.axis_size("piece")
    share = capacity // columns
    f32 = jnp.float32
    vector = jax.ShapeDtypeStruct((share, width), f32)
    few = jax.ShapeDtypeStruct((SUB, width), f32)
    message = jax.ShapeDtypeStruct((4, share, width), f32)
    most_inner, most_outer = tile_bounds(share)
    inner_tiles = pltpu.VMEM((most_inner + 2 * GROUP, width, width), f32)
    outer_tiles = pltpu.VMEM((most_outer + 2 * GROUP, width, width), f32)
    ahead = pltpu.VMEM((GROUP, width, width), f32)
    square_more = pltpu.VMEM((share + 1, width, width), f32)
    narrow_more = pltpu.VMEM(((share + 1) * SUB, width), f32)
    square = pltpu.VMEM((share, width, width), f32)
    narrow = pltpu.VMEM((share * SUB, width), f32)
    table = jnp.asarray(FLAT)

    def call(kernel, args, outs, scratch=(), work=0, scalars=2, far=0, **more):
        return pl.pallas_call(
            kernel,
            out_shape=outs,
            in_specs=[SMEM] * scalars + [HBM] * far + [VMEM] * (len(args) - scalars - far),
            out_specs=[SMEM if getattr(o, "memory_space", None) == pltpu.SMEM else VMEM for o in outs],
            scratch_shapes=scratch,
            compiler_params=LIMIT,
            cost_estimate=pl.CostEstimate(flops=work * width * width, bytes_accessed=0, transcendentals=0),
            name=kernel.__name__,
            **more,
        )(*args)

    def swap(values, axis, step):
        return lax.ppermute(values, axis, [(i, i ^ step) for i in range(lax.axis_size(axis))])

    def away(array):
        return pltpu.with_memory_space_constraint(array, pltpu.HBM)

    around = jax.ShapeDtypeStruct((4, capacity + 2 * share, width), f32)
    near = jax.ShapeDtypeStruct((4, 2 * share, width), f32)
    far = [away(array) for array in (positions, phase, right_side, table, neighbours.T)]
    meta, table, around, near, density, source, first, second, own_lists = call(
        prepare,
        (away(counts), away(phase_density), *far),
        [pltpu.SMEM((8,), jnp.int32), pltpu.SMEM(table.shape, jnp.int32), around, near, vector, vector, message, message,
         jax.ShapeDtypeStruct(far[-1].shape, jnp.int32)],
        [pltpu.VMEM(phase.shape, jnp.int32), pltpu.VMEM((share, width), f32), pltpu.SemaphoreType.DMA((5,))],
        far=len(far),
    )
    meta, table = (pltpu.with_memory_space_constraint(array, pltpu.SMEM) for array in (meta, table))
    first = lax.ppermute(first, "piece", [(i, i ^ 1) for i in range(pieces)])
    axes = ("piece", "col")
    device = [(p, c) for p in range(pieces) for c in range(columns)]
    partner = [((p + (1 if p % 2 else -1)) % pieces, c) for p, c in device]
    second = lax.ppermute(second, axes, [(i, q * columns + d) for i, (q, d) in enumerate(partner)])

    col_steps = [(1 << k) | 1 for k in range(columns.bit_length() - 1)]
    lists = [own_lists]
    for step in col_steps:
        known = lists[0] if len(lists) == 1 else jnp.concatenate(lists, 0)
        lists = [known, swap(known, "col", step)]

    plan, runs, tiles_in, sides, middles, weights, rows, cols, selfs = call(
        build_inner,
        (meta, table, near),
        [pltpu.SMEM((share * FIELDS + 4,), jnp.int32), pltpu.SMEM((6 * share + 3,), jnp.int32), inner_tiles,
         pltpu.VMEM((2, share, width, width), jnp.bfloat16), pltpu.VMEM((3, share, width), f32), square,
         square_more, narrow_more, narrow],
        [pltpu.SMEM((3 * share + 3,), jnp.int32), ahead, ahead],
        16 * most_inner,
    )
    plan, runs = (pltpu.with_memory_space_constraint(array, pltpu.SMEM) for array in (plan, runs))
    again, tiles_out, diagonal, precond, times, alone = call(
        build_outer,
        (meta, table, plan, runs, around, first, second, density, source,
         held(tiles_in), held(sides), held(middles), held(weights), held(rows), held(cols), held(selfs), *lists),
        [pltpu.SMEM((1,), jnp.int32), outer_tiles, vector, vector, vector, vector],
        [pltpu.VMEM((4, capacity + 2 * share, width), f32), square_more]
        + [pltpu.VMEM((share, width), f32)] * 2 + [pltpu.VMEM((capacity, width), f32), ahead, ahead],
        16 * most_outer,
        scalars=4,
    )
    again = pltpu.with_memory_space_constraint(again, pltpu.SMEM)

    def inner(field):
        return call(
            apply_inner,
            (meta, table, plan, again, field, alone, times, held(tiles_in)),
            [square, narrow],
            [pltpu.VMEM((share, width, width), f32), pltpu.VMEM((share + SUB, width), f32), pltpu.VMEM((share, width), f32),
             pltpu.VMEM(((share + 1) * SUB, width), f32)],
            4 * most_inner,
            scalars=4,
        )

    def exchange(field):
        count = pieces * columns
        swaps = [[i ^ 1 for i in range(count)], [i - 1 if i % 2 == 0 else i + 1 for i in range(count)]]
        swaps[1][0], swaps[1][-1] = count - 1, 0
        for c in range(1, columns - 1):
            to = {}
            for p in range(pieces - 1):
                low, high = p * columns + c, (p + 1) * columns
                to[low], to[high] = high, low
            spare = {c % (columns - 1) + 1: [0], (c + 1) % (columns - 1) + 1: [(pieces - 1) * columns + c]}
            for p in range(0, pieces, 2):
                for d in range(1, columns):
                    if d != c:
                        ring = [p * columns + d, (p + 1) * columns + d]
                        ring += spare.get(d, []) if p == (0 if spare.get(d) == [0] else pieces - 2) else []
                        to.update(zip(ring, ring[1:] + ring[:1]))
            swaps.append([to[i] for i in range(count)])
        return [lax.ppermute(field, axes, list(enumerate(to))) for to in swaps]

    scratch = [pltpu.VMEM((share, width, width), f32), pltpu.VMEM((8 * share, width), f32)]

    received = exchange(precond)
    rows, cols = inner(precond)
    spill, scaled = call(
        apply_first,
        (meta, table, plan, again, diagonal, times, *received, held(tiles_out), held(rows), held(cols)),
        [vector, vector],
        scratch,
        2 * most_outer,
        scalars=4,
    )

    received = exchange(scaled)
    rows, cols = inner(scaled)
    twice, sums = call(
        apply_second,
        (meta, table, plan, again, source, precond, spill, scaled, times, *received, held(tiles_out), held(rows), held(cols)),
        [vector, few],
        scratch,
        2 * most_outer,
        scalars=4,
    )

    def together(values, axis, low, size):
        return tree([values] + [swap(values, axis, low * k) for k in range(1, size)])

    sums = together(sums, "piece", 1, 2)
    sums = together(sums, "col", 1, columns)
    step = 2
    while pieces // step > 4:
        sums = together(sums, "piece", step, 4)
        step *= 4
    others = [swap(sums, "piece", step * k) for k in range(1, pieces // step)]

    return tuple(call(
        finish,
        (source, precond, spill, scaled, twice, sums, *others),
        [vector, vector],
        scalars=0,
    ))


def solution(mesh):
    placed = (
        P(None, "piece", None),
        P("piece", None),
        P("piece", "col"),
        P(),
        P(),
        P(("piece", "col"), None),
    )
    return jax.shard_map(
        body,
        mesh=mesh,
        in_specs=placed,
        out_specs=(P(("piece", "col"), None), P(("piece", "col"), None)),
        check_vma=False,
    )
```

```python
import jax
import jax.numpy as jnp
import numpy as np
from jax import lax
from jax.experimental import pallas as pl
from jax.experimental.pallas import tpu as pltpu
from jax.sharding import PartitionSpec as P

ITERS = 2
SIDE = 4
LAYER = SIDE * SIDE
REACH = 2 * LAYER
SUB = 8
VMEM = pl.BlockSpec(memory_space=pltpu.VMEM)
SMEM = pl.BlockSpec(memory_space=pltpu.SMEM)
HBM = pl.BlockSpec(memory_space=pltpu.HBM)


def stencil_tables():
    levels = SIDE.bit_length() - 1

    def cell(code):
        across = sum((code >> (2 * level) & 1) << level for level in range(levels))
        along = sum((code >> (2 * level + 1) & 1) << level for level in range(levels))
        return across, along

    place = {cell(code): code for code in range(LAYER)}
    rows = []
    for code in range(LAYER):
        across, along = cell(code)
        rows.append(
            sorted(
                step_z * LAYER + place[across + step_x, along + step_y] - code
                for step_z in (-1, 0, 1)
                for step_y in (-1, 0, 1)
                for step_x in (-1, 0, 1)
                if (across + step_x, along + step_y) in place
            )
        )
    longest = max(len(row) for row in rows)
    offsets = np.zeros((LAYER, longest), np.int32)
    below = np.zeros((LAYER, 2 * REACH + 1), np.int32)
    for code, row in enumerate(rows):
        offsets[code, : len(row)] = row
        for t in range(-REACH, REACH + 1):
            below[code, t + REACH] = sum(offset < t for offset in row)
    return offsets, below


OFFSETS, BELOW = stencil_tables()
WIDEST = OFFSETS.shape[1]
TABLE = np.concatenate([OFFSETS, BELOW], 1)
STRIDE = TABLE.shape[1]
FLAT = np.concatenate([TABLE.reshape(-1), np.zeros(8, np.int32)])
LIMIT = pltpu.CompilerParams(vmem_limit_bytes=8 * 1024 * 1024)


def tile_bounds(share):
    inner = outer = 0
    for first in range(LAYER):
        for live in range(1, share + 1):
            near = far = 0
            for a in range(live):
                code = (first + a) % LAYER
                row = [int(o) for o in OFFSETS[code][: BELOW[code, -1]]]
                near += sum(0 <= a + o and o <= 0 for o in row)
                far += sum(a + o < 0 or a + o >= live for o in row)
            inner, outer = max(inner, near), max(outer, far)
    return inner, outer


def rank(table, code, t):
    return table[code * STRIDE + jnp.clip(t, -REACH, REACH) + REACH + WIDEST]


FIELDS = 6


def write_plan(meta, table, plan, a):
    code = lax.bitwise_and(meta[1] + a, LAYER - 1)
    place = meta[1] + a
    low, split, middle = rank(table, code, -place), rank(table, code, -a), rank(table, code, 0)
    resume, high = rank(table, code, meta[0] - a), rank(table, code, meta[2] - place)
    row = code * STRIDE
    ahead = split - low
    plan[a * FIELDS] = middle - split
    plan[a * FIELDS + 1] = row + split
    plan[a * FIELDS + 2] = ahead + jnp.maximum(high - resume, 0)
    plan[a * FIELDS + 3] = ahead
    plan[a * FIELDS + 4] = row + low
    plan[a * FIELDS + 5] = row + resume - ahead


def write_run(runs, at, a, start, count):
    runs[3 * at], runs[3 * at + 1], runs[3 * at + 2] = a, start, count
    return at + (count > 0).astype(jnp.int32)


def write_runs(meta, table, plan, inner_runs, outer_runs, share):
    inner = outer = total = far = jnp.int32(0)
    for a in range(share):
        write_plan(meta, table, plan, a)
        alive = a < meta[0]
        count, start, count_far, ahead, start_far, start_after = (plan[a * FIELDS + k] for k in range(FIELDS))
        inner = write_run(inner_runs, inner, a, start, jnp.where(alive, count + 1, 0))
        outer = write_run(outer_runs, outer, a, start_far, jnp.where(alive, ahead, 0))
        outer = write_run(outer_runs, outer, a, start_after + ahead, jnp.where(alive, count_far - ahead, 0))
        total = total + jnp.where(alive, count + 1, 0)
        far = far + jnp.where(alive, count_far, 0)
    for runs, at in ((inner_runs, inner), (outer_runs, outer)):
        write_run(runs, at, share, len(FLAT) - 8, jnp.int32(1))
    plan[share * FIELDS] = total
    plan[share * FIELDS + 1] = far
    plan[share * FIELDS + 2] = inner
    plan[share * FIELDS + 3] = outer


def inner_range(plan, table, a):
    start = plan[a * FIELDS + 1]
    return plan[a * FIELDS], lambda t: a + table[start + t]


def outer_range(plan, table, a):
    ahead, start, start_after = (plan[a * FIELDS + k] for k in (3, 4, 5))
    return plan[a * FIELDS + 2], lambda t: a + table[t + jnp.where(t < ahead, start, start_after)]


TURN = 3


def padded_sweep(count, fetch, step, carry):
    def turn(i, state):
        carry, *now = state
        later = [fetch(TURN * (i + 1) + k) for k in range(TURN)]
        return step(now, carry), *later

    state = (carry, *(fetch(k) for k in range(TURN)))
    return lax.fori_loop(0, lax.div(count + (TURN - 1), TURN), turn, state)[0]


def tree(terms):
    while len(terms) > 1:
        terms = [a + b for a, b in zip(terms[::2], terms[1::2])] + terms[len(terms) // 2 * 2 :]
    return terms[0]


def gather(partial, c, term):
    if c < len(partial):
        partial[c] = term
    else:
        partial[c % len(partial)] = partial[c % len(partial)] + term


def pieces_of(width):
    return [slice(c * SUB, (c + 1) * SUB) for c in range(width // SUB)]


def wide(row):
    return jnp.broadcast_to(row, (SUB, row.shape[1]))


def three_parts(values):
    high = values.astype(jnp.bfloat16).astype(jnp.float32)
    rest = values - high
    middle = rest.astype(jnp.bfloat16).astype(jnp.float32)
    return high, middle, rest - middle


def stacked(rows):
    sublane = lax.broadcasted_iota(jnp.int32, rows[0].shape, 0)
    result = jnp.zeros(rows[0].shape, jnp.float32)
    for k, row in enumerate(rows):
        result = jnp.where(sublane == k, row, result)
    return result


def half_size(x):
    return 0.5 - (x[0] * x[0] + x[1] * x[1] + x[2] * x[2])


def own_side(x):
    high, middle, low = three_parts(stacked([2.0 * x[0], 2.0 * x[1], 2.0 * x[2], jnp.ones_like(x[0])]))
    sizes = stacked(list(three_parts(half_size(x))))
    width = sizes.shape[1]
    rest = jnp.zeros((width - 7 * SUB, width), jnp.float32)
    return jnp.concatenate([high, high, middle, middle, high, low, sizes, rest], 0)


def other_sides(first, second):
    rows = [*first, half_size(first), *second, half_size(second)]
    high, middle, low = three_parts(stacked(rows))
    width = high.shape[1]
    ones = jnp.where(lax.broadcasted_iota(jnp.int32, (2 * SUB, width), 0) < 3, 1.0, 0.0).astype(jnp.bfloat16)
    front = jnp.concatenate([high, middle], 0).astype(jnp.bfloat16)
    back = jnp.concatenate([low, high], 0).astype(jnp.bfloat16)
    rest = jnp.zeros((width - 8 * SUB, width), jnp.bfloat16)
    return jnp.concatenate([front, front, back, ones, rest], 0)


GROUP = 10


def flat_tiles(count, runs, most, table, sides, middles, weights, other_at, buffers, tiles, rows_ref, cols_ref):
    share, width = rows_ref.shape[0] - 1, rows_ref.shape[2]
    chunks = pieces_of(width)

    def steps(state):
        found = []
        for _ in range(GROUP):
            run, t = state
            a, start, size = (runs[3 * run + k] for k in range(3))
            found.append((a, a + table[start + t]))
            over = t + 1 >= size
            state = jnp.minimum(run + over.astype(jnp.int32), most), jnp.where(over, 0, t + 1)
        return state, found

    def other_of(a, n):
        here = pl.ds(a, 1)
        return [wide(other_at(c, n)) - wide(middles[c, here, :]) for c in range(3)]

    def products(found, ahead):
        for k in range(0, GROUP, 2):
            (a, n), (b, m) = ((jnp.minimum(a, share - 1), n) for a, n in found[k : k + 2])
            own = jnp.concatenate([sides[0, a], sides[1, b]], 0)
            both = jnp.dot(own, other_sides(other_of(a, n), other_of(b, m)), preferred_element_type=jnp.float32)
            ahead[k] = both[:width]
            ahead[k + 1] = both[width:]

    def weigh(at, found, ahead):
        for k, (a, n) in enumerate(found):
            alone = a == n
            row = jnp.where(alone, share, a)
            own = jnp.minimum(a, share - 1)
            other = wide(other_at(3, n))
            down = [None] * 4
            for c, here in enumerate(chunks):
                left = ahead[k, here, :]
                rest = jnp.maximum(left, 0.0)
                inverse = pltpu.reciprocal((1.01 - left) * (weights[own, here, :] + other), approx=True)
                tile = rest * rest * inverse
                tiles[at + k, here, :] = tile
                rows_ref[row, here, :] = rows_ref[row, here, :] + tile
                if cols_ref is not None:
                    gather(down, c, tile)
            if cols_ref is not None:
                there = pl.ds(pl.multiple_of(jnp.where(alone, share, n) * SUB, SUB), SUB)
                cols_ref[there, :] = cols_ref[there, :] + tree(down)

    def turn(i, carry):
        state, found = carry
        at = i * (2 * GROUP)
        state, later = steps(state)
        products(later, buffers[1])
        weigh(at, found, buffers[0])
        state, last = steps(state)
        products(last, buffers[0])
        weigh(at + GROUP, later, buffers[1])
        return state, last

    state, found = steps((jnp.int32(0), jnp.int32(0)))
    products(found, buffers[0])
    lax.fori_loop(0, lax.div(count + (2 * GROUP - 1), 2 * GROUP), turn, (state, found))


def spread_columns(out, index, rows):
    count, width = rows.shape
    turned = rows.T
    for a in range(count):
        out[index(a)] = jnp.broadcast_to(turned[:, a : a + 1], (width, width))


def lane_sums(parts, count, width):
    lanes = lax.broadcasted_iota(jnp.int32, (width, width), 1)
    turned = jnp.zeros((width, width), jnp.float32)
    for a in range(count):
        turned = jnp.where(lanes == a, jnp.sum(parts[a], axis=1, keepdims=True), turned)
    return turned.T[:count]


def sub_sums(cols):
    return jnp.sum(cols[...].reshape(-1, SUB, cols.shape[1]), axis=1)


def alive_rows(meta, share, width):
    return lax.broadcasted_iota(jnp.int32, (share, width), 0) < meta[0]


def prepare(
    counts, densities, position_in, phase_in, right_side_in, table_in, lists_in,
    meta, table, hood, near, density, source, first_swap, second_swap, lists, phase, right_side, sems
):
    share, width = source.shape
    capacity = phase.shape[0]
    body_rows = pl.ds(share, capacity)
    copies = [
        pltpu.make_async_copy(phase_in, phase, sems.at[0]),
        pltpu.make_async_copy(position_in, hood.at[pl.ds(0, 3), body_rows, :], sems.at[1]),
        pltpu.make_async_copy(right_side_in, right_side, sems.at[2]),
        pltpu.make_async_copy(table_in, table, sems.at[3]),
        pltpu.make_async_copy(lists_in, lists, sems.at[4]),
    ]
    for copy in copies:
        copy.start()
    piece, column = lax.axis_index("piece"), lax.axis_index("col")
    filled = counts[piece]
    filled_before = counts[jnp.maximum(piece - 1, 0)]
    before = jnp.int32(0)
    total = jnp.int32(0)
    for p in range(counts.shape[0]):
        before = before + jnp.where(p < piece, counts[p], 0)
        total = total + counts[p]
    meta[0] = jnp.clip(filled - column * share, 0, share)
    meta[1] = before + column * share
    meta[2] = total
    meta[3] = column * share
    meta[4] = filled
    meta[5] = filled_before
    own_rows = pl.ds(pl.multiple_of(share + column * share, SUB), share)
    copies[0].wait()
    labels = phase[...]
    whole = sum(jnp.where(labels == k, densities[k], 0.0) for k in range(densities.shape[0]))
    hood[3, body_rows, :] = whole * (width / 2.0)
    density[...] = hood[3, own_rows, :] * (2.0 / width)
    copies[1].wait()
    even = lax.rem(piece, 2) == 0
    for k in range(4):
        tail, head = hood[k, pl.ds(filled, share), :], hood[k, share : 2 * share, :]
        first_swap[k] = jnp.where(even, tail, head)
        second_swap[k] = jnp.where(even, head, tail)
        near[k, 0:share, :] = hood[k, own_rows, :]
    for copy in copies[2:]:
        copy.wait()
    source[...] = jnp.where(alive_rows(meta, share, width), right_side[...], 0.0)


def finish_tiles(tiles, end):
    for t in range(TURN):
        tiles[end + t] = jnp.zeros(tiles.shape[1:], jnp.float32)


def build_inner(
    meta, table, near, plan, outer_runs, tiles, sides, middles, weights, rows_ref, cols_ref, self_ref,
    inner_runs, *buffers,
):
    share, width = weights.shape[:2]
    chunks = pieces_of(width)
    write_runs(meta, table, plan, inner_runs, outer_runs, share)
    for k in range(3):
        first = near[k, 0:share, 0:1]
        middles[k] = jnp.broadcast_to(jnp.floor(first) + 0.5, (share, width))
    parts = lax.broadcasted_iota(jnp.int32, (width, width), 1) < 6 * SUB
    for a in range(share):
        here = slice(a, a + 1)
        centred = [wide(near[k, here, :] - middles[k, here, :]) for k in range(3)]
        turned = own_side(centred).T
        sides[0, a] = turned.astype(jnp.bfloat16)
        sides[1, a] = jnp.where(parts, pltpu.roll(turned, SUB // 2, 1), turned).astype(jnp.bfloat16)
    spread_columns(weights, lambda a: a, near[3, 0:share, :])
    cols_ref[...] = jnp.zeros_like(cols_ref)
    rows_ref[...] = jnp.zeros_like(rows_ref)
    count = plan[share * FIELDS]
    flat_tiles(
        count, inner_runs, plan[share * FIELDS + 2], table, sides, middles, weights,
        lambda k, n: near[k, pl.ds(n, 1), :], buffers, tiles, rows_ref, cols_ref,
    )
    finish_tiles(tiles, count)
    lane = lax.broadcasted_iota(jnp.int32, (SUB, width), 1)
    sublane = lax.broadcasted_iota(jnp.int32, (SUB, width), 0)

    def block(a, at):
        at = at + plan[a * FIELDS]
        down = [None] * 4
        for c, here in enumerate(chunks):
            tile = jnp.where(lane == sublane + c * SUB, 0.0, tiles[at, here, :])
            tiles[at, here, :] = tile
            gather(down, c, tile)
        self_ref[pl.ds(pl.multiple_of(a * SUB, SUB), SUB), :] = tree(down)
        return at + 1

    lax.fori_loop(0, meta[0], block, 0)


def count_listed(meta, lists, width):
    capacity = lists[0].shape[1]
    filled, filled_before = meta[4], meta[5]
    start = lax.axis_index("piece") * capacity
    steps = lax.broadcasted_iota(jnp.int32, (2 * REACH, capacity), 0)
    partial = [None] * 4
    row = 0
    for ref in lists:
        ids = ref[...]
        slot = ids - start
        gap = jnp.where(slot < 0, capacity - filled_before, jnp.where(slot >= capacity, filled - capacity, 0))
        away = slot - lax.broadcasted_iota(jnp.int32, ids.shape, 1) + gap
        away = jnp.where(ids < 0, -REACH, away) + REACH
        for k in range(ids.shape[0]):
            gather(partial, row, jnp.where(steps == away[k : k + 1], 1.0, 0.0))
            row += 1
    return jnp.concatenate([tree(partial), jnp.zeros((width - 2 * REACH, capacity), jnp.float32)], 0).T


def factor(times, a, n):
    lane = lax.broadcasted_iota(jnp.int32, (1, times.shape[1]), 1)
    return jnp.sum(jnp.where(lane == n - a + REACH, times[pl.ds(a, 1), :], 0.0), axis=1, keepdims=True)


def either(flag, run):
    @pl.when(flag == 0)
    def _():
        run(False)

    @pl.when(flag != 0)
    def _():
        run(True)


TAIL = 13


def build_outer(
    meta, table, plan, runs, around, first, second, density, source, tiles_in, sides, middles, weights,
    rows_ref, cols_ref, self_ref, *rest
):
    lists, rest = rest[:-TAIL], rest[-TAIL:]
    again_ref, tiles, diagonal_ref, precond_ref, times, alone_ref, hood, work, sums_ref, extra, all_times, *buffers = rest
    share, width = diagonal_ref.shape
    base, filled = meta[3], meta[4]
    even = lax.rem(lax.axis_index("piece"), 2) == 0
    for k in range(4):
        hood[k, 0:share, :] = jnp.where(even, second[k], first[k])
        hood[k, share:, :] = around[k, share:, :]
        hood[k, pl.ds(share + filled, share), :] = jnp.where(even, first[k], second[k])
    alive = alive_rows(meta, share, width)
    all_times[...] = count_listed(meta, lists, width)
    often = jnp.where(alive, all_times[pl.ds(pl.multiple_of(base, SUB), share), :], 0.0)
    times[...] = often
    lane = lax.broadcasted_iota(jnp.int32, (share, width), 1)
    again = jnp.max(jnp.where((lane == REACH) | (lane == 0), 0.0, often)) > 1.5
    again_ref[0] = again.astype(jnp.int32)


    work[...] = jnp.zeros_like(work)
    count = plan[share * FIELDS + 1]
    flat_tiles(
        count, runs, plan[share * FIELDS + 3], table, sides, middles, weights,
        lambda k, n: hood[k, pl.ds(base + share + n, 1), :], buffers, tiles, work, None,
    )
    finish_tiles(tiles, count)
    sums_ref[...] = lane_sums([rows_ref[a] + work[a] for a in range(share)], share, width) + sub_sums(cols_ref)[0:share]

    @pl.when(again)
    def _():
        extra[...] = jnp.zeros_like(extra)
        work[...] = jnp.zeros_like(work)

        def block(a, state):
            count, place_of = inner_range(plan, table, a)

            def inner(t, at):
                n = place_of(t)
                tile = tiles_in[at]
                work[a] = work[a] + tile * factor(times, a, n)
                there = pl.ds(n, 1)
                down = jnp.sum(tile, axis=0, keepdims=True)
                extra[there, :] = extra[there, :] + down * factor(times, n, a)
                return at + 1

            at = lax.fori_loop(0, count, inner, state[0]) + 1
            count, place_far = outer_range(plan, table, a)

            def outer(t, at):
                work[a] = work[a] + tiles[at] * factor(times, a, place_far(t))
                return at + 1

            return at, lax.fori_loop(0, count, outer, state[1])

        lax.fori_loop(0, meta[0], block, (0, 0))
        sums_ref[...] = lane_sums(work, share, width) + extra[...]

    alone = jnp.sum(jnp.where(lane == REACH, often, 0.0), axis=1, keepdims=True)
    alone_ref[...] = jnp.broadcast_to(alone, (share, width))
    pairs = jnp.where(alive, sums_ref[...] + sub_sums(self_ref) * alone, 0.0)
    diagonal = 1.0 / density[...] + pairs
    diagonal_ref[...] = diagonal
    precond_ref[...] = source[...] / diagonal


def apply_inner(meta, table, plan, again, field, alone, times, tiles, rows_ref, cols_ref, spread, near, lone, cols):
    share, width = field.shape
    chunks = pieces_of(width)
    near[0:share, :] = field[...]
    near[share:, :] = jnp.zeros((SUB, width), jnp.float32)
    lone[...] = field[...] * alone[...]
    spread_columns(spread, lambda a: a, field[...])
    cols[...] = jnp.zeros_like(cols)

    def run(weighted):
        def block(a, at):
            count, place_of = inner_range(plan, table, a)

            def fetch(t):
                n = jnp.where(t < count, place_of(t), share)
                return n, wide(near[pl.ds(n, 1), :])

            def pairs(fetched, carry):
                at, sums = carry
                if weighted:
                    fetched = [(n, value * factor(times, a, jnp.minimum(n, share - 1))) for n, value in fetched]
                down = [[None] * 2 for _ in fetched]
                result = []
                for c, (here, total) in enumerate(zip(chunks, sums)):
                    own = spread[a, here, :]
                    found = []
                    for t, (_, value) in enumerate(fetched):
                        tile = tiles[at + t, here, :]
                        gather(down[t], c, tile * own)
                        found.append(tile * value)
                    result.append(total + tree(found))
                for (n, _), partial in zip(fetched, down):
                    there = pl.ds(pl.multiple_of(n * SUB, SUB), SUB)
                    partial = tree(partial)
                    if weighted:
                        partial = partial * factor(times, jnp.minimum(n, share - 1), a)
                    cols[there, :] = cols[there, :] + partial
                return at + len(fetched), result

            zero = jnp.zeros((SUB, width), jnp.float32)
            _, sums = padded_sweep(count, fetch, pairs, (at, [zero] * len(chunks)))
            at = at + count
            value = wide(lone[pl.ds(a, 1), :])
            for here, old in zip(chunks, sums):
                rows_ref[a, here, :] = old + tiles[at, here, :] * value
            return at + 1

        lax.fori_loop(0, meta[0], block, 0)

    either(again[0], run)
    cols_ref[...] = cols[0 : share * SUB, :]


def apply_outer(meta, table, plan, again, received, times, tiles, rows_ref, cols_ref, work, hood):
    first, second, *ends = received
    columns = len(received)
    share, width = first.shape
    chunks = pieces_of(width)
    base, filled = meta[3], meta[4]
    column = lax.div(base, share)
    odd = lax.rem(column, 2) == 1
    before = jnp.where(odd, first[...], second[...])
    after = jnp.where(odd, second[...], first[...])
    own = 3 * share
    for c, end in enumerate(ends, 1):
        hood[pl.ds(own - meta[5] + c * share, share), :] = end[...]
    from_last = own - meta[5] + (columns - 1) * share
    hood[pl.ds(jnp.where(column == 0, from_last, own - share), share), :] = before
    hood[own + share : own + 2 * share, :] = after
    head = after
    for c, end in enumerate(ends, 1):
        head = jnp.where(column == c, end[...], head)
    hood[pl.ds(own + jnp.clip(filled - base, 0, 2 * share), share), :] = head
    nothing = hood.shape[0] - SUB
    hood[nothing:, :] = jnp.zeros((SUB, width), jnp.float32)

    def run(weighted):
        def block(a, at):
            count, place_of = outer_range(plan, table, a)

            def fetch(t):
                place = place_of(t)
                value = hood[pl.ds(jnp.where(t < count, own + place, nothing), 1), :]
                if weighted:
                    value = value * factor(times, a, place)
                return wide(value)

            def pairs(values, carry):
                at, sums = carry
                result = []
                for here, total in zip(chunks, sums):
                    result.append(total + tree([tiles[at + t, here, :] * value for t, value in enumerate(values)]))
                return at + len(values), result

            _, sums = padded_sweep(count, fetch, pairs, (at, [rows_ref[a, here, :] for here in chunks]))
            for here, values in zip(chunks, sums):
                work[a, here, :] = values
            return at + count

        lax.fori_loop(0, meta[0], block, 0)

    either(again[0], run)
    return jnp.where(alive_rows(meta, share, width), lane_sums(work, share, width) + sub_sums(cols_ref), 0.0)


def apply_first(meta, table, plan, again, diagonal, times, *rest):
    *received, tiles, rows_ref, cols_ref, spill_ref, scaled_ref, work, hood = rest
    spill = apply_outer(meta, table, plan, again, received, times, tiles, rows_ref, cols_ref, work, hood)
    spill_ref[...] = spill
    scaled_ref[...] = spill / diagonal[...]


def apply_second(meta, table, plan, again, source, precond, spill, scaled, times, *rest):
    *received, tiles, rows_ref, cols_ref, twice_ref, sums_ref, work, hood = rest
    twice = apply_outer(meta, table, plan, again, received, times, tiles, rows_ref, cols_ref, work, hood)
    twice_ref[...] = twice
    share, width = twice.shape
    lane = lax.broadcasted_iota(jnp.int32, (1, width), 1)
    sums = jnp.zeros((1, width), jnp.float32)
    pairs = ((source[...], precond[...]), (spill[...], precond[...]), (spill[...], scaled[...]), (scaled[...], twice))
    for k, (first, second) in enumerate(pairs):
        along = jnp.sum(first * second, axis=0, keepdims=True)
        sums = jnp.where(lane == k, jnp.sum(along, axis=1, keepdims=True), sums)
    sums_ref[...] = wide(sums)


def finish(source, precond, spill, scaled, twice, *rest):
    *parts, solution_ref, residual_ref = rest
    sums = tree([ref[...] for ref in parts])

    def pick(k):
        return sums[0:1, k : k + 1]

    weighted, cross, square, last = pick(0), pick(1), pick(2), pick(3)
    part = cross / weighted
    advance = 1.0 / (1.0 - part)
    keep = -part * advance
    weighted_next = advance * advance * (square - cross * part)
    bent = keep * keep * cross + 2.0 * keep * advance * square + advance * advance * last
    blend = weighted_next / weighted
    advance_next = weighted_next / (weighted_next - bent - blend * weighted_next / advance)
    residual = keep * source[...] + advance * spill[...]
    next_precond = keep * precond[...] + advance * scaled[...]
    direction = next_precond + blend * precond[...]
    image = residual - keep * spill[...] - advance * twice[...] + blend * (source[...] - spill[...])
    solution_ref[...] = advance * precond[...] + advance_next * direction
    residual_ref[...] = residual - advance_next * image


def held(array):
    return pltpu.with_memory_space_constraint(array, pltpu.VMEM)


def body(positions, phase, neighbours, counts, phase_density, right_side):
    capacity, width = phase.shape
    columns = lax.axis_size("col")
    pieces = lax.axis_size("piece")
    share = capacity // columns
    f32 = jnp.float32
    vector = jax.ShapeDtypeStruct((share, width), f32)
    few = jax.ShapeDtypeStruct((SUB, width), f32)
    message = jax.ShapeDtypeStruct((4, share, width), f32)
    most_inner, most_outer = tile_bounds(share)
    inner_tiles = pltpu.VMEM((most_inner + 2 * GROUP, width, width), f32)
    outer_tiles = pltpu.VMEM((most_outer + 2 * GROUP, width, width), f32)
    ahead = pltpu.VMEM((GROUP, width, width), f32)
    square_more = pltpu.VMEM((share + 1, width, width), f32)
    narrow_more = pltpu.VMEM(((share + 1) * SUB, width), f32)
    square = pltpu.VMEM((share, width, width), f32)
    narrow = pltpu.VMEM((share * SUB, width), f32)
    table = jnp.asarray(FLAT)

    def call(kernel, args, outs, scratch=(), work=0, scalars=2, far=0, **more):
        return pl.pallas_call(
            kernel,
            out_shape=outs,
            in_specs=[SMEM] * scalars + [HBM] * far + [VMEM] * (len(args) - scalars - far),
            out_specs=[SMEM if getattr(o, "memory_space", None) == pltpu.SMEM else VMEM for o in outs],
            scratch_shapes=scratch,
            compiler_params=LIMIT,
            cost_estimate=pl.CostEstimate(flops=work * width * width, bytes_accessed=0, transcendentals=0),
            name=kernel.__name__,
            **more,
        )(*args)

    def swap(values, axis, step):
        return lax.ppermute(values, axis, [(i, i ^ step) for i in range(lax.axis_size(axis))])

    def away(array):
        return pltpu.with_memory_space_constraint(array, pltpu.HBM)

    around = jax.ShapeDtypeStruct((4, capacity + 2 * share, width), f32)
    near = jax.ShapeDtypeStruct((4, 2 * share, width), f32)
    far = [away(array) for array in (positions, phase, right_side, table, neighbours.T)]
    meta, table, around, near, density, source, first, second, own_lists = call(
        prepare,
        (away(counts), away(phase_density), *far),
        [pltpu.SMEM((8,), jnp.int32), pltpu.SMEM(table.shape, jnp.int32), around, near, vector, vector, message, message,
         jax.ShapeDtypeStruct(far[-1].shape, jnp.int32)],
        [pltpu.VMEM(phase.shape, jnp.int32), pltpu.VMEM((share, width), f32), pltpu.SemaphoreType.DMA((5,))],
        far=len(far),
    )
    meta, table = (pltpu.with_memory_space_constraint(array, pltpu.SMEM) for array in (meta, table))
    first = lax.ppermute(first, "piece", [(i, i ^ 1) for i in range(pieces)])
    axes = ("piece", "col")
    device = [(p, c) for p in range(pieces) for c in range(columns)]
    partner = [((p + (1 if p % 2 else -1)) % pieces, c) for p, c in device]
    second = lax.ppermute(second, axes, [(i, q * columns + d) for i, (q, d) in enumerate(partner)])

    col_steps = [(1 << k) | 1 for k in range(columns.bit_length() - 1)]
    lists = [own_lists]
    for step in col_steps:
        known = lists[0] if len(lists) == 1 else jnp.concatenate(lists, 0)
        lists = [known, swap(known, "col", step)]

    plan, runs, tiles_in, sides, middles, weights, rows, cols, selfs = call(
        build_inner,
        (meta, table, near),
        [pltpu.SMEM((share * FIELDS + 4,), jnp.int32), pltpu.SMEM((6 * share + 3,), jnp.int32), inner_tiles,
         pltpu.VMEM((2, share, width, width), jnp.bfloat16), pltpu.VMEM((3, share, width), f32), square,
         square_more, narrow_more, narrow],
        [pltpu.SMEM((3 * share + 3,), jnp.int32), ahead, ahead],
        16 * most_inner,
    )
    plan, runs = (pltpu.with_memory_space_constraint(array, pltpu.SMEM) for array in (plan, runs))
    again, tiles_out, diagonal, precond, times, alone = call(
        build_outer,
        (meta, table, plan, runs, around, first, second, density, source,
         held(tiles_in), held(sides), held(middles), held(weights), held(rows), held(cols), held(selfs), *lists),
        [pltpu.SMEM((1,), jnp.int32), outer_tiles, vector, vector, vector, vector],
        [pltpu.VMEM((4, capacity + 2 * share, width), f32), square_more]
        + [pltpu.VMEM((share, width), f32)] * 2 + [pltpu.VMEM((capacity, width), f32), ahead, ahead],
        16 * most_outer,
        scalars=4,
    )
    again = pltpu.with_memory_space_constraint(again, pltpu.SMEM)

    def inner(field):
        return call(
            apply_inner,
            (meta, table, plan, again, field, alone, times, held(tiles_in)),
            [square, narrow],
            [pltpu.VMEM((share, width, width), f32), pltpu.VMEM((share + SUB, width), f32), pltpu.VMEM((share, width), f32),
             pltpu.VMEM(((share + 1) * SUB, width), f32)],
            4 * most_inner,
            scalars=4,
        )

    def exchange(field):
        count = pieces * columns
        swaps = [[i ^ 1 for i in range(count)], [i - 1 if i % 2 == 0 else i + 1 for i in range(count)]]
        swaps[1][0], swaps[1][-1] = count - 1, 0
        for c in range(1, columns - 1):
            to = {}
            for p in range(pieces - 1):
                low, high = p * columns + c, (p + 1) * columns
                to[low], to[high] = high, low
            spare = {c % (columns - 1) + 1: [0], (c + 1) % (columns - 1) + 1: [(pieces - 1) * columns + c]}
            for p in range(0, pieces, 2):
                for d in range(1, columns):
                    if d != c:
                        ring = [p * columns + d, (p + 1) * columns + d]
                        ring += spare.get(d, []) if p == (0 if spare.get(d) == [0] else pieces - 2) else []
                        to.update(zip(ring, ring[1:] + ring[:1]))
            swaps.append([to[i] for i in range(count)])
        return [lax.ppermute(field, axes, list(enumerate(to))) for to in swaps]

    scratch = [pltpu.VMEM((share, width, width), f32), pltpu.VMEM((8 * share, width), f32)]

    received = exchange(precond)
    rows, cols = inner(precond)
    spill, scaled = call(
        apply_first,
        (meta, table, plan, again, diagonal, times, *received, held(tiles_out), held(rows), held(cols)),
        [vector, vector],
        scratch,
        2 * most_outer,
        scalars=4,
    )

    received = exchange(scaled)
    rows, cols = inner(scaled)
    twice, sums = call(
        apply_second,
        (meta, table, plan, again, source, precond, spill, scaled, times, *received, held(tiles_out), held(rows), held(cols)),
        [vector, few],
        scratch,
        2 * most_outer,
        scalars=4,
    )

    def together(values, axis, low, size):
        return tree([values] + [swap(values, axis, low * k) for k in range(1, size)])

    sums = together(sums, "piece", 1, 2)
    sums = together(sums, "col", 1, columns)
    step = 2
    while pieces // step > 4:
        sums = together(sums, "piece", step, 4)
        step *= 4
    others = [swap(sums, "piece", step * k) for k in range(1, pieces // step)]

    return tuple(call(
        finish,
        (source, precond, spill, scaled, twice, sums, *others),
        [vector, vector],
        scalars=0,
    ))


def solution(mesh):
    placed = (
        P(None, "piece", None),
        P("piece", None),
        P("piece", "col"),
        P(),
        P(),
        P(("piece", "col"), None),
    )
    return jax.shard_map(
        body,
        mesh=mesh,
        in_specs=placed,
        out_specs=(P(("piece", "col"), None), P(("piece", "col"), None)),
        check_vma=False,
    )
```
